32 devices in a mesh: row: 4 (over x, core), col: 8 (over z, y).
Axes of the slice: x: 2, y: 2, z: 4, core: 2. Of those that a mesh axis runs over, the one named last changes fastest.
Arguments:
- object_field: float32 [2, 3072, 6144], P(None, 'row', 'col'), may hold values from -1.5 to 1.5, as said below
- probe_modes: float32 [2, 2, 256, 256], replicated, may hold values from -3 to 3
- counts: int32 [4, 8], replicated, may hold values from 1 to 12, 32 in all within a row
- centers: int32 [4, 8, 2, 12], P('row', 'col'), may hold values from 0 to 767
- patterns: bfloat16 [4, 8, 12, 256, 256], P('row', 'col'), may hold values from 1 to 32
Outputs:
- new_object: float32 [2, 3072, 6144], P(None, 'row', 'col')
- new_probe: float32 [2, 2, 256, 256], replicated
The draws below stay inside these ranges and needn't reach their ends.
Inputs may be any that keep to these rules, and one draw needn't show every extreme that they name: Each row of counts sums to 32 and its largest entry is 12. `centers`: slot s of tile (r, c) is used only if s < counts[r, c]. `object_field`: each pixel is a complex value of magnitude between 0.5 and 1.5.
All inputs are finite; a program needn't handle non-finite values.
Results may differ from the reference program's by a relative error of at most 0.0038.
The reference program's roundings to bfloat16 on the way count: a program that leaves them out, or rounds other values in their place, can miss the bound.
Values may be sent and summed in bfloat16 or wider, within the bound.
No kernel may reach another device: no remote copies, remote signals or barrier semaphores. Data moves between devices by JAX's collectives and lax.ppermute only.
A program may use at most 128 MiB of HBM per device.

```python
import math
import jax
import jax.numpy as jnp
import numpy as np
from jax import lax

TILE = 768
P_SIZE = 256
MODES = 2
SLOTS = 12
ROW_POSITIONS = 32
OBJ_ROWS = 3072
OBJ_COLS = 6144
N_ROW = 4
N_COL = 8


def draw_object_field(key, part):
    key = jax.random.fold_in(key, 11)
    key_size, key_angle = jax.random.split(key, 2)
    grid_shape = (OBJ_ROWS, OBJ_COLS)
    magnitude = jax.random.uniform(key_size, grid_shape, jnp.float32, 0.5, 1.5)
    phase_angle = jax.random.uniform(key_angle, grid_shape, jnp.float32, -math.pi, math.pi)
    return jnp.stack([magnitude * jnp.cos(phase_angle), magnitude * jnp.sin(phase_angle)])


def place_ends(drawn, stream_key, smallest, largest):
    shape = drawn.shape
    place = [jax.random.randint(jax.random.fold_in(stream_key, axis), (), 0, shape[axis]) for axis in range(len(shape))]
    drawn = drawn.at[tuple(place)].set(smallest)
    longest = shape.index(max(shape))
    place[longest] = (place[longest] + 1) % shape[longest]
    return drawn.at[tuple(place)].set(largest)


def levels(stream_key, extent, cuts, smallest, top_value):
    factor_of, own = 1.0, jax.random.fold_in(stream_key, 6)
    for dim, parts in cuts:
        steps = jnp.exp(jax.random.uniform(jax.random.fold_in(own, dim), (parts,), jnp.float32, smallest / len(cuts), top_value / len(cuts)))
        factor_of = factor_of * jnp.repeat(steps, extent[dim] // parts).reshape([-1 if axis == dim else 1 for axis in range(len(extent))])
    return factor_of


def split_up(amount, total, most, lean):
    weights = [(1 << 20) // math.isqrt(standing ** lean) + 1 for standing in range(2, amount + 1)]
    spare, holding = total - most - (amount - 1), [1] * (amount - 1)
    while spare > 0:
        candidates = [i for i in range(amount - 1) if holding[i] < most]
        pool, budget = sum([weights[i] for i in candidates]), spare
        for i in candidates:
            more = min(most - holding[i], max(1, budget * weights[i] // pool), spare)
            holding[i] = holding[i] + more
            spare = spare - more
    return np.array([most] + holding)


def ragged_sizes(stream_key, number_of, total, limit, skew):
    if number_of == 2:
        one = jax.random.randint(stream_key, (), max(1, total - limit), min(limit, total - 1) + 1)
        return jnp.stack([one, total - one])
    sizes = jnp.asarray(split_up(number_of, total, limit, skew), jnp.int32)
    couples = (number_of - 1) // 2
    source_of, receiver = sizes[1:1 + 2 * couples:2], sizes[2:2 + 2 * couples:2]
    room = jnp.minimum(source_of - 1, limit - receiver)
    shifted = jax.random.randint(jax.random.fold_in(stream_key, 1), (couples,), 0, 1 << 20) % (room + 1)
    sizes = sizes.at[1:1 + 2 * couples:2].set(source_of - shifted).at[2:2 + 2 * couples:2].set(receiver + shifted)
    return sizes[jax.random.permutation(jax.random.fold_in(stream_key, 2), number_of)]


def normal_values(stream_key, extent, spread, most, held_as=jnp.bfloat16):
    return jnp.clip(spread * jax.random.normal(stream_key, extent, jnp.float32), -most, most).astype(held_as)


def setup_inputs(seed: int = 0) -> dict:
    streams_of = jax.random.split(jax.random.key(seed), 6)
    return {
        "object_field": draw_object_field(jax.random.fold_in(streams_of[5], 71), 0),
        "probe_modes": normal_values(streams_of[1], (MODES, 2, P_SIZE, P_SIZE), 0.5, 3.0, jnp.float32),
        "counts": jax.vmap(lambda own: ragged_sizes(own, N_COL, ROW_POSITIONS, SLOTS, 2))(jax.random.split(streams_of[2], N_ROW)).reshape((N_ROW, N_COL)).astype(jnp.int32),
        "centers": place_ends(jax.random.randint(streams_of[3], (N_ROW, N_COL, 2, SLOTS), 0, TILE), jax.random.fold_in(streams_of[3], 1), 0, TILE - 1).astype(jnp.int32),
        "patterns": jnp.clip(jnp.exp(math.log(32.0) - 3.465736 * jax.random.uniform(streams_of[4], (N_ROW, N_COL, SLOTS, P_SIZE, P_SIZE), jnp.float32) ** levels(streams_of[4], (N_ROW, N_COL, SLOTS, P_SIZE, P_SIZE), ((0, 4), (1, 8)), -0.2, 0.2)), 1.0, 32.0).astype(jnp.bfloat16),
    }


def dft_pair(length):
    indices = jnp.arange(length, dtype=jnp.int32)
    product = indices[:, None] * indices[None, :] % length
    angles = product.astype(jnp.float32) * (2.0 * jnp.pi / length)
    factor = 1.0 / jnp.sqrt(jnp.float32(length))
    cosine_table = (jnp.cos(angles) * factor).astype(jnp.bfloat16)
    sine_table = (jnp.sin(angles) * factor).astype(jnp.bfloat16)
    return (cosine_table, sine_table)

def matmul(left_side, right_side):
    return jnp.dot(left_side, right_side, preferred_element_type=jnp.float32)

def position_terms(patch_window, amplitude, probe_lower_edge, cosine_table, sine_table):
    patch_real = patch_window[0].astype(jnp.float32)
    patch_imag = patch_window[1].astype(jnp.float32)
    spectra = []
    total_power = jnp.zeros(patch_real.shape, jnp.float32)
    for mode_index in range(MODES):
        probe_real = probe_lower_edge[mode_index, 0].astype(jnp.float32)
        probe_imag = probe_lower_edge[mode_index, 1].astype(jnp.float32)
        wave_real = (probe_real * patch_real - probe_imag * patch_imag).astype(jnp.bfloat16)
        wave_imag = (probe_real * patch_imag + probe_imag * patch_real).astype(jnp.bfloat16)
        half_real = (matmul(wave_real, cosine_table) + matmul(wave_imag, sine_table)).astype(jnp.bfloat16)
        half_imag = (matmul(wave_imag, cosine_table) - matmul(wave_real, sine_table)).astype(jnp.bfloat16)
        spec_real = matmul(cosine_table, half_real) + matmul(sine_table, half_imag)
        spec_imag = matmul(cosine_table, half_imag) - matmul(sine_table, half_real)
        spectra.append((spec_real, spec_imag))
        total_power = total_power + spec_real * spec_real + spec_imag * spec_imag
    factor = amplitude.astype(jnp.float32) / jnp.sqrt(jnp.maximum(total_power, 0.5)) - 1.0
    object_real = jnp.zeros(patch_real.shape, jnp.float32)
    object_imag = jnp.zeros(patch_real.shape, jnp.float32)
    probe_parts = []
    for mode_index in range(MODES):
        probe_real = probe_lower_edge[mode_index, 0].astype(jnp.float32)
        probe_imag = probe_lower_edge[mode_index, 1].astype(jnp.float32)
        spec_real, spec_imag = spectra[mode_index]
        shift_real = (factor * spec_real).astype(jnp.bfloat16)
        shift_imag = (factor * spec_imag).astype(jnp.bfloat16)
        back_real = (matmul(shift_real, cosine_table) - matmul(shift_imag, sine_table)).astype(jnp.bfloat16)
        back_imag = (matmul(shift_imag, cosine_table) + matmul(shift_real, sine_table)).astype(jnp.bfloat16)
        change_real = matmul(cosine_table, back_real) - matmul(sine_table, back_imag)
        change_imag = matmul(cosine_table, back_imag) + matmul(sine_table, back_real)
        object_real = object_real + probe_real * change_real + probe_imag * change_imag
        object_imag = object_imag + probe_real * change_imag - probe_imag * change_real
        probe_parts.append(jnp.stack([patch_real * change_real + patch_imag * change_imag, patch_real * change_imag - patch_imag * change_real]))
    object_term = jnp.stack([object_real, object_imag]).astype(jnp.bfloat16)
    coverage = patch_real * patch_real + patch_imag * patch_imag
    return (object_term, jnp.stack(probe_parts), coverage)

def reference(object_field, probe_modes, counts, centers, patterns):
    cosine_table, sine_table = dft_pair(P_SIZE)
    half_width = P_SIZE // 2
    object_low = object_field.astype(jnp.bfloat16)
    probe_lower_edge = probe_modes.astype(jnp.bfloat16)
    padded = jnp.pad(object_low, ((0, 0), (half_width, half_width), (half_width, half_width)))
    row_base = (jnp.arange(N_ROW, dtype=jnp.int32) * TILE)[:, None, None]
    col_base = (jnp.arange(N_COL, dtype=jnp.int32) * TILE)[None, :, None]
    row_offsets = (centers[:, :, 0, :].astype(jnp.int32) + row_base).reshape(-1)
    column_offsets = (centers[:, :, 1, :].astype(jnp.int32) + col_base).reshape(-1)
    slot_numbers = jnp.arange(SLOTS, dtype=jnp.int32)[None, None, :]
    activity_flags = (slot_numbers < counts[:, :, None].astype(jnp.int32)).astype(jnp.float32).reshape(-1)
    measured_amplitudes = patterns.reshape(-1, P_SIZE, P_SIZE)
    zero_index = jnp.zeros((), jnp.int32)
    starting_guess = (jnp.zeros(padded.shape, jnp.float32), jnp.zeros((MODES, 2, P_SIZE, P_SIZE), jnp.float32), jnp.zeros((P_SIZE, P_SIZE), jnp.float32))

    def handle_scan_position(running, inputs):
        canvas, probe_total, cover_total = running
        row_start, col_start, amplitude, alive_flag = inputs
        patch_window = lax.dynamic_slice(padded, (zero_index, row_start, col_start), (2, P_SIZE, P_SIZE))
        object_term, probe_part, coverage = position_terms(patch_window, amplitude, probe_lower_edge, cosine_table, sine_table)
        placed = lax.dynamic_slice(canvas, (zero_index, row_start, col_start), (2, P_SIZE, P_SIZE))
        placed = placed + object_term.astype(jnp.float32) * alive_flag
        canvas = lax.dynamic_update_slice(canvas, placed, (zero_index, row_start, col_start))
        return ((canvas, probe_total + alive_flag * probe_part, cover_total + alive_flag * coverage), None)
    final_results, ignored_value = lax.scan(handle_scan_position, starting_guess, (row_offsets, column_offsets, measured_amplitudes, activity_flags))
    canvas, probe_total, cover_total = final_results
    gradient = canvas[:, half_width:half_width + OBJ_ROWS, half_width:half_width + OBJ_COLS]
    intensity = lax.optimization_barrier(jnp.sum(probe_modes * probe_modes, axis=(0, 1)))
    peak = jnp.max(intensity) + 1e-06
    new_object = object_field + gradient / peak
    new_probe = probe_modes + probe_total / jnp.sqrt(cover_total)
    return (new_object, new_probe)
```

```python
import functools

import jax
import jax.numpy as jnp
import ml_dtypes
import numpy as np
from jax import lax
from jax.experimental import pallas as pl
from jax.experimental.pallas import tpu as pltpu
from jax.sharding import PartitionSpec as P

LANES = 128
F32 = jnp.float32
BF16 = jnp.bfloat16


def dft_tables(length):
    indices = np.arange(length)
    angles = (indices[:, None] * indices[None, :] % length) * (2.0 * np.pi / length)
    scale = 1.0 / np.sqrt(length)
    cosine = (np.cos(angles) * scale).astype(np.float32).astype(ml_dtypes.bfloat16)
    sine = (np.sin(angles) * scale).astype(np.float32).astype(ml_dtypes.bfloat16)
    positive = np.block([[cosine, -sine], [sine, cosine]])
    negative = np.block([[cosine, sine], [-sine, cosine]])
    return positive, negative


def shift_down(array, axis):
    devices = lax.axis_size(axis)
    return lax.ppermute(array, axis, [(i, i + 1) for i in range(devices - 1)])


def shift_up(array, axis):
    devices = lax.axis_size(axis)
    return lax.ppermute(array, axis, [(i + 1, i) for i in range(devices - 1)])


def positions_kernel(
    counts, centers, obj_hbm, left, right, top, bottom, top_ends, bottom_ends, pat_hbm,
    probe, positive, negative,
    out_hbm, g_top, g_bottom, g_left, g_right, sums, peak_out,
    obj, canvas, patterns, low, waves, halves, spectra, patch, obj_sems, out_sems, pat_sem,
):
    size = probe.shape[-1]
    half = size // 2
    tile = obj_hbm.shape[1]
    inner = tile // LANES
    chunks = inner + 2
    modes = probe.shape[0]
    rows = slice(half, half + tile)

    def obj_copy(comp, j):
        return pltpu.make_async_copy(
            obj_hbm.at[comp, :, pl.ds(j * LANES, LANES)],
            obj.at[comp * chunks + 1 + j, pl.ds(half, tile), :],
            obj_sems.at[comp, j],
        )

    def out_copy(comp, j):
        return pltpu.make_async_copy(
            canvas.at[comp * chunks + 1 + j, pl.ds(half, tile), :],
            out_hbm.at[comp, :, pl.ds(j * LANES, LANES)],
            out_sems.at[comp, j],
        )

    pat_copy = pltpu.make_async_copy(pat_hbm, patterns, pat_sem)
    for comp in range(2):
        for j in range(inner):
            obj_copy(comp, j).start()
    pat_copy.start()

    canvas[...] = jnp.zeros_like(canvas)
    sums[...] = jnp.zeros_like(sums)
    intensity = jnp.zeros((size, size), F32)
    for m in range(modes):
        for comp in range(2):
            values = probe[m, comp]
            intensity = intensity + values * values
            low[2 * m + comp] = values.astype(BF16).astype(F32)
    peak = jnp.max(intensity) + 1e-06
    peak_out[0, 0] = peak

    for comp in range(2):
        first = comp * chunks
        last = first + chunks - 1
        obj[first, rows, :] = left[comp].astype(F32)
        obj[last, rows, :] = right[comp].astype(F32)
        obj[first, 0:half, :] = top_ends[comp, :, 0:LANES].astype(F32)
        obj[last, 0:half, :] = top_ends[comp, :, LANES:].astype(F32)
        obj[first, half + tile :, :] = bottom_ends[comp, :, 0:LANES].astype(F32)
        obj[last, half + tile :, :] = bottom_ends[comp, :, LANES:].astype(F32)
        for j in range(inner):
            columns = slice(j * LANES, (j + 1) * LANES)
            obj[first + 1 + j, 0:half, :] = top[comp, :, columns].astype(F32)
            obj[first + 1 + j, half + tile :, :] = bottom[comp, :, columns].astype(F32)

    for comp in range(2):
        for j in range(inner):
            obj_copy(comp, j).wait()
    pat_copy.wait()

    block = 64
    groups = block // 8
    lane = lax.broadcasted_iota(jnp.int32, (block, LANES), 1)

    def handle_position(slot, carry):
        row = centers[0, slot]
        column = centers[1, slot]
        chunk = column >> 7
        offset = column & 127
        back_offset = (LANES - offset) & 127
        from_first = lane < LANES - offset
        past = lane >= offset
        for begin in range(0, size, block):
            here = slice(begin, begin + block)
            parts = []
            for comp in range(2):
                moved = [
                    pltpu.roll(
                        obj[comp * chunks + chunk + k, pl.ds(row + begin, block), :],
                        back_offset, 1,
                    )
                    for k in range(3)
                ]
                window = jnp.concatenate(
                    [
                        jnp.where(from_first, moved[0], moved[1]),
                        jnp.where(from_first, moved[1], moved[2]),
                    ],
                    1,
                ).astype(BF16).astype(F32)
                patch[comp, here, :] = window
                parts.append(window)
            real, imag = parts
            start = begin // 8
            sums[start : start + groups, 2 * modes] += (real * real + imag * imag).reshape(
                groups, 8, size
            )
            for m in range(modes):
                probe_real = low[2 * m, here, :]
                probe_imag = low[2 * m + 1, here, :]
                there = slice(m * size + begin, m * size + begin + block)
                waves[there, 0:size] = (probe_real * real - probe_imag * imag).astype(BF16)
                waves[there, size:] = (probe_real * imag + probe_imag * real).astype(BF16)

        def to_columns(product):
            for m in range(modes):
                mode_rows = slice(m * size, (m + 1) * size)
                halves[0:size, mode_rows] = product[mode_rows, 0:size].astype(BF16)
                halves[size:, mode_rows] = product[mode_rows, size:].astype(BF16)

        to_columns(jnp.dot(waves[...], positive[...], preferred_element_type=F32))
        spectra[...] = jnp.dot(negative[...], halves[...], preferred_element_type=F32)
        for begin in range(0, size, block):
            here = slice(begin, begin + block)
            below = slice(size + begin, size + begin + block)
            amplitude = patterns[slot, here, :].astype(F32)
            power = jnp.zeros((block, size), F32)
            for m in range(modes):
                mode = slice(m * size, (m + 1) * size)
                real = spectra[here, mode]
                imag = spectra[below, mode]
                power = power + real * real + imag * imag
            factor = amplitude * lax.rsqrt(jnp.maximum(power, 0.5)) - 1.0
            for m in range(modes):
                mode = slice(m * size, (m + 1) * size)
                there = slice(m * size + begin, m * size + begin + block)
                waves[there, 0:size] = (factor * spectra[here, mode]).astype(BF16)
                waves[there, size:] = (factor * spectra[below, mode]).astype(BF16)
        to_columns(jnp.dot(waves[...], negative[...], preferred_element_type=F32))
        spectra[...] = jnp.dot(positive[...], halves[...], preferred_element_type=F32)

        for begin in range(0, size, block):
            here = slice(begin, begin + block)
            below = slice(size + begin, size + begin + block)
            start = begin // 8
            obj_real = patch[0, here, :]
            obj_imag = patch[1, here, :]
            term_real = jnp.zeros((block, size), F32)
            term_imag = jnp.zeros((block, size), F32)
            for m in range(modes):
                mode = slice(m * size, (m + 1) * size)
                real = spectra[here, mode]
                imag = spectra[below, mode]
                probe_real = low[2 * m, here, :]
                probe_imag = low[2 * m + 1, here, :]
                term_real = term_real + probe_real * real + probe_imag * imag
                term_imag = term_imag + probe_real * imag - probe_imag * real
                sums[start : start + groups, 2 * m] += (
                    obj_real * real + obj_imag * imag
                ).reshape(groups, 8, size)
                sums[start : start + groups, 2 * m + 1] += (
                    obj_real * imag - obj_imag * real
                ).reshape(groups, 8, size)
            for comp, term in enumerate((term_real, term_imag)):
                term = term.astype(BF16).astype(F32)
                first = pltpu.roll(term[:, 0:LANES], offset, 1)
                second = pltpu.roll(term[:, LANES:], offset, 1)
                place = comp * chunks + chunk
                window = pl.ds(row + begin, block)
                canvas[place, window, :] += jnp.where(past, first, 0.0)
                canvas[place + 1, window, :] += jnp.where(past, second, first)
                canvas[place + 2, window, :] += jnp.where(past, 0.0, second)
        return carry

    count = counts[lax.axis_index("row"), lax.axis_index("col")]
    lax.fori_loop(0, count, handle_position, 0)

    g_top[...] = canvas[:, 0:half, :].astype(BF16)
    g_bottom[...] = canvas[:, half + tile :, :].astype(BF16)
    for comp in range(2):
        g_left[comp] = canvas[comp * chunks, rows, :]
        g_right[comp] = canvas[comp * chunks + chunks - 1, rows, :]
        for j in range(inner):
            index = comp * chunks + 1 + j
            canvas[index, rows, :] = obj[index, rows, :] + canvas[index, rows, :] / peak
            out_copy(comp, j).start()
    for comp in range(2):
        for j in range(inner):
            out_copy(comp, j).wait()


def run_positions(counts, centers, object_field, halo, patterns, probe_modes):
    size = probe_modes.shape[-1]
    half = size // 2
    modes = probe_modes.shape[0]
    tile = object_field.shape[1]
    chunks = tile // LANES + 2
    slots = patterns.shape[0]
    positive, negative = dft_tables(size)
    smem = pl.BlockSpec(memory_space=pltpu.SMEM)
    vmem = pl.BlockSpec(memory_space=pltpu.VMEM)
    anywhere = pl.BlockSpec(memory_space=pl.ANY)
    shape = jax.ShapeDtypeStruct
    matmul_flops = 16 * modes * size**3 * 2
    return pl.pallas_call(
        positions_kernel,
        in_specs=[smem, smem, anywhere] + [vmem] * 6 + [anywhere] + [vmem] * 3,
        out_specs=[anywhere] + [vmem] * 5 + [smem],
        out_shape=[
            shape(object_field.shape, F32),
            shape((2 * chunks, half, LANES), BF16),
            shape((2 * chunks, half, LANES), BF16),
            shape((2, tile, LANES), F32),
            shape((2, tile, LANES), F32),
            shape((size // 8, 2 * modes + 1, 8, size), F32),
            shape((1, 1), F32),
        ],
        scratch_shapes=[
            pltpu.VMEM((2 * chunks, tile + size, LANES), F32),
            pltpu.VMEM((2 * chunks, tile + size, LANES), F32),
            pltpu.VMEM(patterns.shape, BF16),
            pltpu.VMEM((2 * modes, size, size), F32),
            pltpu.VMEM((modes * size, 2 * size), BF16),
            pltpu.VMEM((2 * size, modes * size), BF16),
            pltpu.VMEM((2 * size, modes * size), F32),
            pltpu.VMEM((2, size, size), F32),
            pltpu.SemaphoreType.DMA((2, tile // LANES)),
            pltpu.SemaphoreType.DMA((2, tile // LANES)),
            pltpu.SemaphoreType.DMA,
        ],
        compiler_params=pltpu.CompilerParams(vmem_limit_bytes=50 * 1024 * 1024),
        cost_estimate=pl.CostEstimate(
            flops=slots * matmul_flops, bytes_accessed=16 * 1024 * 1024, transcendentals=0
        ),
        name="positions",
    )(counts, centers, object_field, *halo, patterns, probe_modes, positive, negative)


def rims_kernel(
    partial, peak_ref, from_above, from_below, from_left, from_right, out,
    top, bottom, left, right, sems,
):
    tile = partial.shape[1]
    half = from_above.shape[1]
    inner = tile // LANES
    chunks = inner + 2
    middle = tile - 2 * half
    regions = (
        (top, 0, half, 0, tile),
        (bottom, tile - half, half, 0, tile),
        (left, half, middle, 0, half),
        (right, half, middle, tile - half, half),
    )

    def copy(index, comp, inward):
        buffer, row, height, column, width = regions[index]
        home = (partial if inward else out).at[comp, pl.ds(row, height), pl.ds(column, width)]
        here = buffer.at[comp]
        source, target = (home, here) if inward else (here, home)
        return pltpu.make_async_copy(source, target, sems.at[1 - int(inward), index, comp])

    everything = [(index, comp) for index in range(4) for comp in range(2)]
    for index, comp in everything:
        copy(index, comp, True).start()
    peak = peak_ref[0, 0]
    for index, comp in everything:
        copy(index, comp, True).wait()
        buffer = regions[index][0]
        if index < 2:
            ring = from_above if index == 0 else from_below
            side = slice(0, half) if index == 0 else slice(tile - half, tile)
            for j in range(inner):
                columns = slice(j * LANES, (j + 1) * LANES)
                extra = ring[comp * chunks + 1 + j].astype(F32)
                if j == 0:
                    extra = extra + from_left[comp, side, :].astype(F32)
                if j == inner - 1:
                    extra = extra + from_right[comp, side, :].astype(F32)
                buffer[comp, :, columns] += extra / peak
        else:
            strip = from_left if index == 2 else from_right
            buffer[comp] += strip[comp, half : half + middle, :].astype(F32) / peak
        copy(index, comp, False).start()
    for index, comp in everything:
        copy(index, comp, False).wait()


def add_rims(partial, peak, from_above, from_below, from_left, from_right):
    tile = partial.shape[1]
    half = from_above.shape[1]
    vmem = pl.BlockSpec(memory_space=pltpu.VMEM)
    anywhere = pl.BlockSpec(memory_space=pl.ANY)
    return pl.pallas_call(
        rims_kernel,
        in_specs=[anywhere, pl.BlockSpec(memory_space=pltpu.SMEM)] + [vmem] * 4,
        out_specs=anywhere,
        out_shape=jax.ShapeDtypeStruct(partial.shape, F32),
        input_output_aliases={0: 0},
        scratch_shapes=[
            pltpu.VMEM((2, half, tile), F32),
            pltpu.VMEM((2, half, tile), F32),
            pltpu.VMEM((2, tile - 2 * half, half), F32),
            pltpu.VMEM((2, tile - 2 * half, half), F32),
            pltpu.SemaphoreType.DMA((2, 4, 2)),
        ],
        compiler_params=pltpu.CompilerParams(vmem_limit_bytes=32 * 1024 * 1024),
        cost_estimate=pl.CostEstimate(
            flops=1024 * 1024, bytes_accessed=6 * 1024 * 1024, transcendentals=0
        ),
        name="rims",
    )(partial, peak, from_above, from_below, from_left, from_right)


def shared_update(sums, modes, size):
    axes = ("row", "col")
    devices = lax.axis_size("row") * lax.axis_size("col")
    groups, planes = sums.shape[0], sums.shape[1]
    share = size // devices
    if share < 8:
        sums = sums.reshape(groups, planes, 8 // share, share, size)
        sums = jnp.swapaxes(sums, 1, 2).reshape(devices, planes, share, size)
    else:
        sums = sums.reshape(devices, groups // devices, planes, 8, size)
    received = lax.all_to_all(sums, axes, 0, 0, tiled=True)
    total = jnp.sum(received, 0)
    if share >= 8:
        total = jnp.swapaxes(total, 0, 1).reshape(planes, share, size)
    update = total[: 2 * modes] / jnp.sqrt(total[2 * modes])
    gathered = lax.all_gather(update, axes, axis=0)
    return jnp.swapaxes(gathered, 0, 1).reshape(modes, 2, size, size)


def on_device(object_field, probe_modes, counts, centers, patterns):
    size = probe_modes.shape[-1]
    modes = probe_modes.shape[0]
    half = size // 2
    tile = object_field.shape[1]

    right_strip = object_field[:, :, tile - half :].astype(BF16)
    left_strip = object_field[:, :, :half].astype(BF16)
    left = shift_down(right_strip, "col")
    right = shift_up(left_strip, "col")
    top = shift_down(object_field[:, tile - half :, :].astype(BF16), "row")
    bottom = shift_up(object_field[:, :half, :].astype(BF16), "row")
    sides = jnp.concatenate([left, right], 2)
    top_ends = shift_down(sides[:, tile - half :, :], "row")
    bottom_ends = shift_up(sides[:, :half, :], "row")

    halo = (left, right, top, bottom, top_ends, bottom_ends)
    partial, g_top, g_bottom, g_left, g_right, sums, peak = run_positions(
        counts, centers[0, 0], object_field, halo, patterns[0, 0], probe_modes
    )

    from_above = shift_down(g_bottom, "row")
    from_below = shift_up(g_top, "row")
    chunks = g_top.shape[0] // 2

    def with_corners(strip, chunk):
        above = from_above[chunk::chunks].astype(F32)
        below = from_below[chunk::chunks].astype(F32)
        inside = jnp.zeros((2, tile - 2 * half, half), F32)
        return (strip + jnp.concatenate([above, inside, below], 1)).astype(BF16)

    from_left = shift_down(with_corners(g_right, chunks - 1), "col")
    from_right = shift_up(with_corners(g_left, 0), "col")
    new_object = add_rims(partial, peak, from_above, from_below, from_left, from_right)
    new_probe = probe_modes + shared_update(sums, modes, size)
    return (new_object, new_probe)


def solution(mesh):
    placed = (
        P(None, "row", "col"),
        P(),
        P(),
        P("row", "col", None, None),
        P("row", "col", None, None, None),
    )
    return jax.shard_map(
        on_device,
        mesh=mesh,
        in_specs=placed,
        out_specs=(P(None, "row", "col"), P()),
        check_vma=False,
    )
```

```python
import functools
import math

import jax
import jax.numpy as jnp
import ml_dtypes
import numpy as np
from jax import lax
from jax.experimental import pallas as pl
from jax.experimental.pallas import tpu as pltpu
from jax.sharding import PartitionSpec as P

LANES = 128
ROW = ("x", "core")
COL = ("col",)
F32 = jnp.float32
BF16 = jnp.bfloat16


def dft_tables(length):
    indices = np.arange(length)
    angles = (indices[:, None] * indices[None, :] % length) * (2.0 * np.pi / length)
    scale = 1.0 / np.sqrt(length)
    cosine = (np.cos(angles) * scale).astype(np.float32).astype(ml_dtypes.bfloat16)
    sine = (np.sin(angles) * scale).astype(np.float32).astype(ml_dtypes.bfloat16)
    positive = np.block([[cosine, -sine], [sine, cosine]])
    negative = np.block([[cosine, sine], [-sine, cosine]])
    return positive, negative


def shift_down(array, axis):
    devices = math.prod(lax.axis_size(name) for name in axis)
    return lax.ppermute(array, axis, [(i, i + 1) for i in range(devices - 1)])


def shift_up(array, axis):
    devices = math.prod(lax.axis_size(name) for name in axis)
    return lax.ppermute(array, axis, [(i + 1, i) for i in range(devices - 1)])


def positions_kernel(with_border, *refs):
    counts, centers, obj_hbm, start_hbm, pat_hbm, probe, positive, negative = refs[:8]
    refs = refs[8:]
    if with_border:
        left, right, top, bottom, left_ends, right_ends, sums_hbm = refs[:7]
        out_hbm, g_top, g_bottom, g_left, g_right, kept, given = refs[7:14]
        refs = refs[14:]
    else:
        out_hbm, sums_out = refs[:2]
        refs = refs[2:]
    (obj, canvas, patterns, low, waves, shifts, halves, spectra, changes, patch, sums, order,
     obj_sems, canvas_sems, out_sems, misc_sems) = refs
    size = probe.shape[-1]
    half = size // 2
    tile = obj_hbm.shape[1]
    inner = tile // LANES
    chunks = inner + 2
    modes = probe.shape[0]
    rows = slice(half, half + tile)
    pieces = [(comp, j) for comp in range(2) for j in range(inner)]

    def home(array, comp, j):
        return array.at[comp, :, pl.ds(j * LANES, LANES)]

    def held(array, comp, j):
        return array.at[comp * chunks + 1 + j, pl.ds(half, tile), :]

    obj_copies = [
        pltpu.make_async_copy(home(obj_hbm, *p), held(obj, *p), obj_sems.at[p]) for p in pieces
    ]
    canvas_copies = [
        pltpu.make_async_copy(home(start_hbm, *p), held(canvas, *p), canvas_sems.at[p])
        for p in pieces
    ]
    out_copies = [
        pltpu.make_async_copy(held(canvas, *p), home(out_hbm, *p), out_sems.at[p]) for p in pieces
    ]
    pat_copy = pltpu.make_async_copy(pat_hbm, patterns, misc_sems.at[0])
    later = [pat_copy] + canvas_copies
    for copy in obj_copies:
        copy.start()
    pat_copy.start()
    for copy in canvas_copies:
        copy.start()
    if with_border:
        sums_copy = pltpu.make_async_copy(sums_hbm, sums, misc_sems.at[1])
        sums_copy.start()
        later.append(sums_copy)
    else:
        sums[...] = jnp.zeros_like(sums)

    intensity = jnp.zeros((size, size), F32)
    for m in range(modes):
        for comp in range(2):
            values = probe[m, comp]
            intensity = intensity + values * values
            low[2 * m + comp] = values.astype(BF16).astype(F32)
    scale = 1.0 / (jnp.max(intensity) + 1e-06)
    changes[...] = jnp.zeros_like(changes)
    patch[...] = jnp.zeros_like(patch)

    if with_border:
        for comp in range(2):
            first = comp * chunks
            last = first + chunks - 1
            obj[first, rows, :] = left[comp].astype(F32)
            obj[last, rows, :] = right[comp].astype(F32)
            obj[first, 0:half, :] = left_ends[comp, 0:half, :].astype(F32)
            obj[last, 0:half, :] = right_ends[comp, 0:half, :].astype(F32)
            obj[first, half + tile :, :] = left_ends[comp, half:, :].astype(F32)
            obj[last, half + tile :, :] = right_ends[comp, half:, :].astype(F32)
            strip = jnp.zeros((tile + size, LANES), F32)
            canvas[first] = strip
            canvas[last] = strip
            for j in range(inner):
                columns = slice(j * LANES, (j + 1) * LANES)
                obj[first + 1 + j, 0:half, :] = top[comp, :, columns].astype(F32)
                obj[first + 1 + j, half + tile :, :] = bottom[comp, :, columns].astype(F32)
                canvas[first + 1 + j, 0:half, :] = strip[0:half]
                canvas[first + 1 + j, half + tile :, :] = strip[0:half]

    order[0] = 0
    count = counts[lax.axis_index(ROW), lax.axis_index("col")]

    def note(slot, found):
        row = centers[0, slot]
        column = centers[1, slot]
        inside = (row >= half) & (row <= tile - half) & (column >= half) & (column <= tile - half)
        order[found] = slot
        return found + jnp.where(inside, 0 if with_border else 1, 1 if with_border else 0)

    found = lax.fori_loop(0, count, note, 0)

    block = 64
    groups = block // 8
    lane = lax.broadcasted_iota(jnp.int32, (block, LANES), 1)
    blocks = range(0, size, block)

    def place_of(index):
        slot = order[index]
        column = centers[1, slot]
        return slot, centers[0, slot], column >> 7, column & 127

    def cut(index):
        _, row, chunk, offset = place_of(index)
        back_offset = (LANES - offset) & 127
        from_first = lane < LANES - offset
        for begin in blocks:
            here = slice(begin, begin + block)
            parts = []
            for comp in range(2):
                moved = [
                    pltpu.roll(
                        obj[comp * chunks + chunk + k, pl.ds(row + begin, block), :],
                        back_offset, 1,
                    )
                    for k in range(3)
                ]
                window = jnp.concatenate(
                    [
                        jnp.where(from_first, moved[0], moved[1]),
                        jnp.where(from_first, moved[1], moved[2]),
                    ],
                    1,
                ).astype(BF16).astype(F32)
                patch[index & 1, comp, here, :] = window
                parts.append(window)
            real, imag = parts
            for m in range(modes):
                probe_real = low[2 * m, here, :]
                probe_imag = low[2 * m + 1, here, :]
                there = slice(m * size + begin, m * size + begin + block)
                waves[there, 0:size] = (probe_real * real - probe_imag * imag).astype(BF16)
                waves[there, size:] = (probe_real * imag + probe_imag * real).astype(BF16)

    def right_product(source, table):
        product = jnp.dot(source[...], table[...], preferred_element_type=F32)
        for m in range(modes):
            mode_rows = slice(m * size, (m + 1) * size)
            halves[0:size, mode_rows] = product[mode_rows, 0:size].astype(BF16)
            halves[size:, mode_rows] = product[mode_rows, size:].astype(BF16)

    def reweigh(index):
        slot = order[index]
        for begin in blocks:
            here = slice(begin, begin + block)
            below = slice(size + begin, size + begin + block)
            amplitude = patterns[slot, here, :].astype(F32)
            power = jnp.zeros((block, size), F32)
            for m in range(modes):
                mode = slice(m * size, (m + 1) * size)
                real = spectra[here, mode]
                imag = spectra[below, mode]
                power = power + real * real + imag * imag
            factor = amplitude * lax.rsqrt(jnp.maximum(power, 0.5)) - 1.0
            for m in range(modes):
                mode = slice(m * size, (m + 1) * size)
                there = slice(m * size + begin, m * size + begin + block)
                shifts[there, 0:size] = (factor * spectra[here, mode]).astype(BF16)
                shifts[there, size:] = (factor * spectra[below, mode]).astype(BF16)

    def deposit(index, buffer):
        _, row, chunk, offset = place_of(index)
        past = lane >= offset
        for begin in blocks:
            here = slice(begin, begin + block)
            below = slice(size + begin, size + begin + block)
            start = begin // 8
            obj_real = patch[buffer, 0, here, :]
            obj_imag = patch[buffer, 1, here, :]
            term_real = jnp.zeros((block, size), F32)
            term_imag = jnp.zeros((block, size), F32)

            def add(plane, value):
                sums[start : start + groups, plane] += value.reshape(groups, 8, size)

            add(2 * modes, obj_real * obj_real + obj_imag * obj_imag)
            for m in range(modes):
                mode = slice(m * size, (m + 1) * size)
                real = changes[here, mode]
                imag = changes[below, mode]
                probe_real = low[2 * m, here, :]
                probe_imag = low[2 * m + 1, here, :]
                term_real = term_real + probe_real * real + probe_imag * imag
                term_imag = term_imag + probe_real * imag - probe_imag * real
                add(2 * m, obj_real * real + obj_imag * imag)
                add(2 * m + 1, obj_real * imag - obj_imag * real)
            for comp, term in enumerate((term_real, term_imag)):
                term = term.astype(BF16).astype(F32) * scale
                first = pltpu.roll(term[:, 0:LANES], offset, 1)
                second = pltpu.roll(term[:, LANES:], offset, 1)
                place = comp * chunks + chunk
                window = pl.ds(row + begin, block)
                values = [canvas[place + k, window, :] for k in range(3)]
                canvas[place, window, :] = values[0] + jnp.where(past, first, 0.0)
                canvas[place + 1, window, :] = values[1] + jnp.where(past, second, first)
                canvas[place + 2, window, :] = values[2] + jnp.where(past, 0.0, second)

    def step(index, carry):
        previous = jnp.maximum(index - 1, 0)
        right_product(waves, positive)
        deposit(previous, (index + 1) & 1)
        spectra[...] = jnp.dot(negative[...], halves[...], preferred_element_type=F32)
        reweigh(index)
        cut(jnp.minimum(index + 1, found - 1))
        right_product(shifts, negative)
        changes[...] = jnp.dot(positive[...], halves[...], preferred_element_type=F32)
        return carry

    for copy in obj_copies:
        copy.wait()

    @pl.when(found > 0)
    def _():
        cut(0)

    for copy in later:
        copy.wait()

    @pl.when(found > 0)
    def _():
        lax.fori_loop(0, found, step, 0)
        deposit(found - 1, (found - 1) & 1)

    for copy in out_copies:
        copy.start()
    if with_border:
        g_top[...] = canvas[:, 0:half, :].astype(BF16)
        g_bottom[...] = canvas[:, half + tile :, :].astype(BF16)
        for comp in range(2):
            g_left[comp] = canvas[comp * chunks, rows, :].astype(BF16)
            g_right[comp] = canvas[comp * chunks + chunks - 1, rows, :].astype(BF16)
        core = lax.axis_index("core")
        count_of = kept.shape[0]
        kept[...] = sums[pl.ds(core * count_of, count_of)]
        given[...] = sums[pl.ds((1 - core) * count_of, count_of)]
    else:
        sums_copy = pltpu.make_async_copy(sums, sums_out, misc_sems.at[1])
        sums_copy.start()
        sums_copy.wait()
    for copy in out_copies:
        copy.wait()


def run_positions(counts, centers, object_field, started, patterns, probe_modes, border=None):
    size = probe_modes.shape[-1]
    half = size // 2
    modes = probe_modes.shape[0]
    tile = object_field.shape[1]
    chunks = tile // LANES + 2
    slots = patterns.shape[0]
    positive, negative = dft_tables(size)
    smem = pl.BlockSpec(memory_space=pltpu.SMEM)
    vmem = pl.BlockSpec(memory_space=pltpu.VMEM)
    anywhere = pl.BlockSpec(memory_space=pl.ANY)
    shape = jax.ShapeDtypeStruct
    in_specs = [smem, smem, anywhere, anywhere, anywhere, vmem, vmem, vmem]
    operands = [counts, centers, object_field, started, patterns, probe_modes, positive, negative]
    sums_shape = (size // 8, 2 * modes + 1, 8, size)
    if border is None:
        out_specs = [anywhere, anywhere]
        out_shape = [shape(object_field.shape, F32), shape(sums_shape, F32)]
    else:
        in_specs += [vmem] * 6 + [anywhere]
        operands += list(border)
        half_sums = (size // 16,) + sums_shape[1:]
        out_specs = [anywhere] + [vmem] * 6
        out_shape = [
            shape(object_field.shape, F32),
            shape((2 * chunks, half, LANES), BF16),
            shape((2 * chunks, half, LANES), BF16),
            shape((2, tile, LANES), BF16),
            shape((2, tile, LANES), BF16),
            shape(half_sums, F32),
            shape(half_sums, F32),
        ]
    copy_sems = pltpu.SemaphoreType.DMA((2, tile // LANES))
    return pl.pallas_call(
        functools.partial(positions_kernel, border is not None),
        in_specs=in_specs,
        out_specs=out_specs,
        out_shape=out_shape,
        scratch_shapes=[
            pltpu.VMEM((2 * chunks, tile + size, LANES), F32),
            pltpu.VMEM((2 * chunks, tile + size, LANES), F32),
            pltpu.VMEM(patterns.shape, BF16),
            pltpu.VMEM((2 * modes, size, size), F32),
            pltpu.VMEM((modes * size, 2 * size), BF16),
            pltpu.VMEM((modes * size, 2 * size), BF16),
            pltpu.VMEM((2 * size, modes * size), BF16),
            pltpu.VMEM((2 * size, modes * size), F32),
            pltpu.VMEM((2 * size, modes * size), F32),
            pltpu.VMEM((2, 2, size, size), F32),
            pltpu.VMEM(sums_shape, F32),
            pltpu.SMEM((slots + 1,), jnp.int32),
            copy_sems,
            copy_sems,
            copy_sems,
            pltpu.SemaphoreType.DMA((2,)),
        ],
        compiler_params=pltpu.CompilerParams(vmem_limit_bytes=30 * 1024 * 1024),
        cost_estimate=pl.CostEstimate(
            flops=slots * 16 * modes * size**3,
            bytes_accessed=24 * 1024 * 1024,
            transcendentals=0,
        ),
        name="border" if border is not None else "interior",
    )(*operands)


def rims_kernel(
    partial, from_above, from_below, ends_left, ends_right, mid_left, mid_right, out,
    top, bottom, left, right, sems,
):
    tile = partial.shape[1]
    half = from_above.shape[1]
    inner = tile // LANES
    chunks = inner + 2
    middle = tile - 2 * half
    regions = (
        (top, 0, half, 0, tile),
        (bottom, tile - half, half, 0, tile),
        (left, half, middle, 0, half),
        (right, half, middle, tile - half, half),
    )

    def copy(index, comp, inward):
        buffer, row, height, column, width = regions[index]
        home = (partial if inward else out).at[comp, pl.ds(row, height), pl.ds(column, width)]
        here = buffer.at[comp]
        source, target = (home, here) if inward else (here, home)
        return pltpu.make_async_copy(source, target, sems.at[1 - int(inward), index, comp])

    everything = [(index, comp) for index in range(4) for comp in range(2)]
    for index, comp in everything:
        copy(index, comp, True).start()
    for index, comp in everything:
        copy(index, comp, True).wait()
        buffer = regions[index][0]
        if index < 2:
            ring = from_above if index == 0 else from_below
            side = slice(0, half) if index == 0 else slice(half, 2 * half)
            for j in range(inner):
                columns = slice(j * LANES, (j + 1) * LANES)
                extra = ring[comp * chunks + 1 + j].astype(F32)
                if j == 0:
                    extra = extra + ends_left[comp, side, :].astype(F32)
                if j == inner - 1:
                    extra = extra + ends_right[comp, side, :].astype(F32)
                buffer[comp, :, columns] += extra
        else:
            strip = mid_left if index == 2 else mid_right
            buffer[comp] += strip[comp].astype(F32)
        copy(index, comp, False).start()
    for index, comp in everything:
        copy(index, comp, False).wait()


def add_rims(partial, rims):
    tile = partial.shape[1]
    half = rims[0].shape[1]
    vmem = pl.BlockSpec(memory_space=pltpu.VMEM)
    anywhere = pl.BlockSpec(memory_space=pl.ANY)
    return pl.pallas_call(
        rims_kernel,
        in_specs=[anywhere] + [vmem] * 6,
        out_specs=anywhere,
        out_shape=jax.ShapeDtypeStruct(partial.shape, F32),
        input_output_aliases={0: 0},
        scratch_shapes=[
            pltpu.VMEM((2, half, tile), F32),
            pltpu.VMEM((2, half, tile), F32),
            pltpu.VMEM((2, tile - 2 * half, half), F32),
            pltpu.VMEM((2, tile - 2 * half, half), F32),
            pltpu.SemaphoreType.DMA((2, 4, 2)),
        ],
        compiler_params=pltpu.CompilerParams(vmem_limit_bytes=16 * 1024 * 1024),
        cost_estimate=pl.CostEstimate(
            flops=1024 * 1024, bytes_accessed=6 * 1024 * 1024, transcendentals=0
        ),
        name="rims",
    )(partial, *rims)


def chip_sums(kept, given):
    return (kept + lax.ppermute(given, "core", [(0, 1), (1, 0)])).astype(BF16)


def shared_update(on_chip, beside, modes, size):
    axes = ("x", "col")
    devices = lax.axis_size("x") * lax.axis_size("col")
    core = lax.axis_index("core")
    groups, planes = on_chip.shape[:2]
    share = groups * 8 // devices
    if share < 8:
        on_chip = on_chip.reshape(groups, planes, 8 // share, share, size)
        on_chip = jnp.swapaxes(on_chip, 1, 2).reshape(devices, planes, share, size)
    else:
        on_chip = on_chip.reshape(devices, groups // devices, planes, 8, size)
    received = lax.all_to_all(on_chip, axes, 0, 0, tiled=True)
    received, beside = lax.optimization_barrier((received, beside))
    total = jnp.sum(received.astype(F32), 0)
    if share >= 8:
        total = jnp.swapaxes(total, 0, 1).reshape(planes, share, size)
    update = (total[: 2 * modes] / jnp.sqrt(total[2 * modes])).astype(BF16)
    copies = jnp.broadcast_to(update, (devices,) + update.shape)
    mine = lax.all_to_all(copies, axes, 0, 0, tiled=True)
    other = lax.ppermute(mine, "core", [(0, 1), (1, 0)])
    low = jnp.where(core == 0, mine, other)
    high = jnp.where(core == 0, other, mine)
    whole = jnp.concatenate([low, high], 0)
    return jnp.swapaxes(whole, 0, 1).reshape(modes, 2, size, size).astype(F32), beside


def on_device(object_field, probe_modes, counts, centers, patterns):
    size = probe_modes.shape[-1]
    modes = probe_modes.shape[0]
    half = size // 2
    tile = object_field.shape[1]

    top = shift_down(object_field[:, tile - half :, :].astype(BF16), ROW)
    bottom = shift_up(object_field[:, :half, :].astype(BF16), ROW)
    left = shift_down(object_field[:, :, tile - half :].astype(BF16), COL)
    right = shift_up(object_field[:, :, :half].astype(BF16), COL)
    left_ends = shift_down(
        jnp.concatenate([top[:, :, tile - half :], bottom[:, :, tile - half :]], 1), COL
    )
    right_ends = shift_up(jnp.concatenate([top[:, :, :half], bottom[:, :, :half]], 1), COL)

    counts_and_places = (counts, centers[0, 0])
    started, sums = run_positions(
        *counts_and_places, object_field, object_field, patterns[0, 0], probe_modes
    )
    border = (left, right, top, bottom, left_ends, right_ends, sums)
    partial, g_top, g_bottom, g_left, g_right, kept, given = run_positions(
        *counts_and_places, object_field, started, patterns[0, 0], probe_modes, border
    )

    chunks = g_top.shape[0] // 2
    on_chip = chip_sums(kept, given)
    mid_left = shift_down(g_right[:, half : tile - half], COL)
    mid_right = shift_up(g_left[:, half : tile - half], COL)
    from_above = shift_down(g_bottom, ROW)
    from_below = shift_up(g_top, ROW)

    def ends(strip, chunk):
        above = strip[:, :half].astype(F32) + from_above[chunk::chunks].astype(F32)
        below = strip[:, tile - half :].astype(F32) + from_below[chunk::chunks].astype(F32)
        return jnp.concatenate([above, below], 1).astype(BF16)

    update, (mid_left, mid_right) = shared_update(on_chip, (mid_left, mid_right), modes, size)
    new_probe = probe_modes + update
    ends_left = shift_down(ends(g_right, chunks - 1), COL)
    ends_right = shift_up(ends(g_left, 0), COL)
    rims = (from_above, from_below, ends_left, ends_right, mid_left, mid_right)
    new_object = add_rims(partial, rims)
    return (new_object, new_probe)


def solution(mesh):
    rows, columns = mesh.devices.shape
    split = jax.sharding.Mesh(
        mesh.devices.reshape(rows // 2, 2, columns), ("x", "core", "col")
    )
    placed = (
        P(None, ROW, "col"),
        P(),
        P(),
        P(ROW, "col", None, None),
        P(ROW, "col", None, None, None),
    )
    return jax.shard_map(
        on_device,
        mesh=split,
        in_specs=placed,
        out_specs=(P(None, ROW, "col"), P()),
        check_vma=False,
    )
```

```python
import functools
import math

import jax
import jax.numpy as jnp
import ml_dtypes
import numpy as np
from jax import lax
from jax.experimental import pallas as pl
from jax.experimental.pallas import tpu as pltpu
from jax.sharding import PartitionSpec as P

LANES = 128
ROW = ("x", "core")
COL = ("col",)
F32 = jnp.float32
BF16 = jnp.bfloat16


def dft_tables(length):
    indices = np.arange(length)
    angles = (indices[:, None] * indices[None, :] % length) * (2.0 * np.pi / length)
    scale = 1.0 / np.sqrt(length)
    cosine = (np.cos(angles) * scale).astype(np.float32).astype(ml_dtypes.bfloat16)
    sine = (np.sin(angles) * scale).astype(np.float32).astype(ml_dtypes.bfloat16)
    positive = np.block([[cosine, -sine], [sine, cosine]])
    negative = np.block([[cosine, sine], [-sine, cosine]])
    return positive, negative


def shift_down(array, axis):
    devices = math.prod(lax.axis_size(name) for name in axis)
    return lax.ppermute(array, axis, [(i, i + 1) for i in range(devices - 1)])


def shift_up(array, axis):
    devices = math.prod(lax.axis_size(name) for name in axis)
    return lax.ppermute(array, axis, [(i + 1, i) for i in range(devices - 1)])


def positions_kernel(with_border, *refs):
    counts, centers, obj_hbm, start_hbm, pat_hbm, probe = refs[:6]
    right_positive, right_negative, left_positive, left_negative = refs[6:10]
    refs = refs[10:]
    if with_border:
        left, right, top, bottom, left_ends, right_ends, sums_hbm = refs[:7]
        out_hbm, g_top, g_bottom, g_left, g_right, kept, given = refs[7:14]
        refs = refs[14:]
    else:
        out_hbm, sums_out = refs[:2]
        refs = refs[2:]
    (obj, canvas, patterns, low, waves, shifts, halves, backs, spectra, changes, patch, sums, order,
     obj_sems, canvas_sems, out_sems, misc_sems) = refs
    size = probe.shape[-1]
    half = size // 2
    tile = obj_hbm.shape[1]
    inner = tile // LANES
    chunks = inner + 2
    modes = probe.shape[0]
    rows = slice(half, half + tile)
    pieces = [(comp, j) for comp in range(2) for j in range(inner)]

    def home(array, comp, j):
        return array.at[comp, :, pl.ds(j * LANES, LANES)]

    def held(array, comp, j):
        return array.at[comp * chunks + 1 + j, pl.ds(half, tile), :]

    obj_copies = [
        pltpu.make_async_copy(home(obj_hbm, *p), held(obj, *p), obj_sems.at[p]) for p in pieces
    ]
    canvas_copies = [
        pltpu.make_async_copy(home(start_hbm, *p), held(canvas, *p), canvas_sems.at[p])
        for p in pieces
    ]
    out_copies = [
        pltpu.make_async_copy(held(canvas, *p), home(out_hbm, *p), out_sems.at[p]) for p in pieces
    ]
    pat_copy = pltpu.make_async_copy(pat_hbm, patterns, misc_sems.at[0])
    later = [pat_copy] + canvas_copies
    for copy in obj_copies:
        copy.start()
    pat_copy.start()
    for copy in canvas_copies:
        copy.start()
    if with_border:
        sums_copy = pltpu.make_async_copy(sums_hbm, sums, misc_sems.at[1])
        sums_copy.start()
        later.append(sums_copy)
    else:
        sums[...] = jnp.zeros_like(sums)

    intensity = jnp.zeros((size, size), F32)
    for m in range(modes):
        for comp in range(2):
            values = probe[m, comp]
            intensity = intensity + values * values
            low[2 * m + comp] = values.astype(BF16).astype(F32)
    scale = 1.0 / (jnp.max(intensity) + 1e-06)
    changes[...] = jnp.zeros_like(changes)
    patch[...] = jnp.zeros_like(patch)

    if with_border:
        for comp in range(2):
            first = comp * chunks
            last = first + chunks - 1
            obj[first, rows, :] = left[comp].astype(F32)
            obj[last, rows, :] = right[comp].astype(F32)
            obj[first, 0:half, :] = left_ends[comp, 0:half, :].astype(F32)
            obj[last, 0:half, :] = right_ends[comp, 0:half, :].astype(F32)
            obj[first, half + tile :, :] = left_ends[comp, half:, :].astype(F32)
            obj[last, half + tile :, :] = right_ends[comp, half:, :].astype(F32)
            strip = jnp.zeros((tile + size, LANES), F32)
            canvas[first] = strip
            canvas[last] = strip
            for j in range(inner):
                columns = slice(j * LANES, (j + 1) * LANES)
                obj[first + 1 + j, 0:half, :] = top[comp, :, columns].astype(F32)
                obj[first + 1 + j, half + tile :, :] = bottom[comp, :, columns].astype(F32)
                canvas[first + 1 + j, 0:half, :] = strip[0:half]
                canvas[first + 1 + j, half + tile :, :] = strip[0:half]

    order[0] = 0
    count = counts[lax.axis_index(ROW), lax.axis_index("col")]

    def note(slot, found):
        row = centers[0, slot]
        column = centers[1, slot]
        inside = (row >= half) & (row <= tile - half) & (column >= half) & (column <= tile - half)
        order[found] = slot
        return found + jnp.where(inside, 0 if with_border else 1, 1 if with_border else 0)

    found = lax.fori_loop(0, count, note, 0)

    block = 64
    groups = block // 8
    lane = lax.broadcasted_iota(jnp.int32, (block, LANES), 1)
    blocks = range(0, size, block)

    def place_of(index):
        slot = order[index]
        column = centers[1, slot]
        return slot, centers[0, slot], column >> 7, column & 127

    def cut(index, begin):
        _, row, chunk, offset = place_of(index)
        back_offset = (LANES - offset) & 127
        from_first = lane < LANES - offset
        here = slice(begin, begin + block)
        parts = []
        for comp in range(2):
            moved = [
                pltpu.roll(
                    obj[comp * chunks + chunk + k, pl.ds(row + begin, block), :], back_offset, 1
                )
                for k in range(3)
            ]
            window = jnp.concatenate(
                [
                    jnp.where(from_first, moved[0], moved[1]),
                    jnp.where(from_first, moved[1], moved[2]),
                ],
                1,
            ).astype(BF16).astype(F32)
            patch[index & 1, comp, here, :] = window
            parts.append(window)
        real, imag = parts
        for m in range(modes):
            probe_real = low[2 * m, here, :]
            probe_imag = low[2 * m + 1, here, :]
            there = slice(m * size + begin, m * size + begin + block)
            waves[there, 0:size] = (probe_real * real - probe_imag * imag).astype(BF16)
            waves[there, size:] = (probe_real * imag + probe_imag * real).astype(BF16)

    def forward_right(m, part):
        mode = slice(m * size, (m + 1) * size)
        columns = slice(part * size, (part + 1) * size)
        halves[columns, mode] = jnp.dot(
            waves[mode, :], right_positive[:, columns], preferred_element_type=F32
        ).astype(BF16)

    def forward_left(k):
        rows_here = slice(k * size, (k + 1) * size)
        spectra[rows_here, :] = jnp.dot(
            left_negative[rows_here, :], halves[...], preferred_element_type=F32
        )

    def reweigh(index, begin):
        slot = order[index]
        k, inside = divmod(begin, half)
        real_rows = slice(k * size + inside, k * size + inside + block)
        imag_rows = slice(k * size + half + inside, k * size + half + inside + block)
        amplitude = patterns[slot, begin : begin + block, :].astype(F32)
        mode_columns = [slice(m * size, (m + 1) * size) for m in range(modes)]
        parts = [(spectra[real_rows, mode], spectra[imag_rows, mode]) for mode in mode_columns]
        power = sum(real * real + imag * imag for real, imag in parts)
        factor = amplitude * lax.rsqrt(jnp.maximum(power, 0.5)) - 1.0
        for m, (real, imag) in enumerate(parts):
            first = k * size + m * half + inside
            there = slice(first, first + block)
            shifts[there, 0:size] = (factor * real).astype(BF16)
            shifts[there, size:] = (factor * imag).astype(BF16)

    def backward_right(k):
        product = jnp.dot(
            shifts[k * size : (k + 1) * size, :], right_negative[...],
            preferred_element_type=F32,
        ).astype(BF16)
        for m in range(modes):
            mode = slice(m * size, (m + 1) * size)
            for part in range(2):
                first = part * size + k * half
                backs[first : first + half, mode] = product[
                    m * half : (m + 1) * half, part * size : (part + 1) * size
                ]

    def backward_left(m, part):
        mode = slice(m * size, (m + 1) * size)
        rows_here = slice(part * size, (part + 1) * size)
        changes[rows_here, mode] = jnp.dot(
            left_positive[rows_here, :], backs[:, mode], preferred_element_type=F32
        )

    def deposit(index, buffer, begin):
        _, row, chunk, offset = place_of(index)
        past = lane >= offset
        here = slice(begin, begin + block)
        below = slice(size + begin, size + begin + block)
        start = begin // 8
        obj_real = patch[buffer, 0, here, :]
        obj_imag = patch[buffer, 1, here, :]

        def add(plane, value):
            sums[start : start + groups, plane] += value.reshape(groups, 8, size)

        add(2 * modes, obj_real * obj_real + obj_imag * obj_imag)
        term_real = term_imag = None
        for m in range(modes):
            mode = slice(m * size, (m + 1) * size)
            real = changes[here, mode]
            imag = changes[below, mode]
            probe_real = low[2 * m, here, :]
            probe_imag = low[2 * m + 1, here, :]
            more_real = probe_real * real + probe_imag * imag
            more_imag = probe_real * imag - probe_imag * real
            term_real = more_real if m == 0 else term_real + more_real
            term_imag = more_imag if m == 0 else term_imag + more_imag
            add(2 * m, obj_real * real + obj_imag * imag)
            add(2 * m + 1, obj_real * imag - obj_imag * real)
        for comp, term in enumerate((term_real, term_imag)):
            term = term.astype(BF16).astype(F32) * scale
            first = pltpu.roll(term[:, 0:LANES], offset, 1)
            second = pltpu.roll(term[:, LANES:], offset, 1)
            place = comp * chunks + chunk
            window = pl.ds(row + begin, block)
            values = [canvas[place + k, window, :] for k in range(3)]
            canvas[place, window, :] = values[0] + jnp.where(past, first, 0.0)
            canvas[place + 1, window, :] = values[1] + jnp.where(past, second, first)
            canvas[place + 2, window, :] = values[2] + jnp.where(past, 0.0, second)

    def step(index, carry):
        previous = jnp.maximum(index - 1, 0)
        following = jnp.minimum(index + 1, found - 1)
        buffer = (index + 1) & 1
        starts = list(blocks)
        for m in range(modes):
            for part in range(2):
                forward_right(m, part)
                deposit(previous, buffer, starts[2 * m + part])
        forward_left(0)
        forward_left(1)
        for begin in starts[:2]:
            reweigh(index, begin)
        backward_right(0)
        for begin in starts[2:]:
            reweigh(index, begin)
        cut(following, starts[0])
        backward_right(1)
        cut(following, starts[1])
        backward_left(0, 0)
        cut(following, starts[2])
        backward_left(0, 1)
        cut(following, starts[3])
        backward_left(1, 0)
        backward_left(1, 1)
        return carry

    for copy in obj_copies:
        copy.wait()

    @pl.when(found > 0)
    def _():
        for begin in blocks:
            cut(0, begin)

    for copy in later:
        copy.wait()

    @pl.when(found > 0)
    def _():
        lax.fori_loop(0, found, step, 0)
        for begin in blocks:
            deposit(found - 1, (found - 1) & 1, begin)

    for copy in out_copies:
        copy.start()
    if with_border:
        g_top[...] = canvas[:, 0:half, :].astype(BF16)
        g_bottom[...] = canvas[:, half + tile :, :].astype(BF16)
        for comp in range(2):
            g_left[comp] = canvas[comp * chunks, rows, :].astype(BF16)
            g_right[comp] = canvas[comp * chunks + chunks - 1, rows, :].astype(BF16)
        core = lax.axis_index("core")
        count_of = kept.shape[0]
        kept[...] = sums[pl.ds(core * count_of, count_of)]
        given[...] = sums[pl.ds((1 - core) * count_of, count_of)]
    else:
        sums_copy = pltpu.make_async_copy(sums, sums_out, misc_sems.at[1])
        sums_copy.start()
        sums_copy.wait()
    for copy in out_copies:
        copy.wait()


def run_positions(counts, centers, object_field, started, patterns, probe_modes, border=None):
    size = probe_modes.shape[-1]
    half = size // 2
    modes = probe_modes.shape[0]
    tile = object_field.shape[1]
    chunks = tile // LANES + 2
    slots = patterns.shape[0]
    positive, negative = dft_tables(size)
    by_quarter = np.arange(2 * size).reshape(2, 2, half).swapaxes(0, 1).reshape(-1)
    tables = [positive, negative, positive, negative[by_quarter]]
    smem = pl.BlockSpec(memory_space=pltpu.SMEM)
    vmem = pl.BlockSpec(memory_space=pltpu.VMEM)
    anywhere = pl.BlockSpec(memory_space=pl.ANY)
    shape = jax.ShapeDtypeStruct
    in_specs = [smem, smem, anywhere, anywhere, anywhere] + [vmem] * 5
    operands = [counts, centers, object_field, started, patterns, probe_modes, *tables]
    sums_shape = (size // 8, 2 * modes + 1, 8, size)
    if border is None:
        out_specs = [anywhere, anywhere]
        out_shape = [shape(object_field.shape, F32), shape(sums_shape, F32)]
    else:
        in_specs += [vmem] * 6 + [anywhere]
        operands += list(border)
        half_sums = (size // 16,) + sums_shape[1:]
        out_specs = [anywhere] + [vmem] * 6
        out_shape = [
            shape(object_field.shape, F32),
            shape((2 * chunks, half, LANES), BF16),
            shape((2 * chunks, half, LANES), BF16),
            shape((2, tile, LANES), BF16),
            shape((2, tile, LANES), BF16),
            shape(half_sums, F32),
            shape(half_sums, F32),
        ]
    copy_sems = pltpu.SemaphoreType.DMA((2, tile // LANES))
    return pl.pallas_call(
        functools.partial(positions_kernel, border is not None),
        in_specs=in_specs,
        out_specs=out_specs,
        out_shape=out_shape,
        scratch_shapes=[
            pltpu.VMEM((2 * chunks, tile + size, LANES), F32),
            pltpu.VMEM((2 * chunks, tile + size, LANES), F32),
            pltpu.VMEM(patterns.shape, BF16),
            pltpu.VMEM((2 * modes, size, size), F32),
            pltpu.VMEM((modes * size, 2 * size), BF16),
            pltpu.VMEM((modes * size, 2 * size), BF16),
            pltpu.VMEM((2 * size, modes * size), BF16),
            pltpu.VMEM((2 * size, modes * size), BF16),
            pltpu.VMEM((2 * size, modes * size), F32),
            pltpu.VMEM((2 * size, modes * size), F32),
            pltpu.VMEM((2, 2, size, size), F32),
            pltpu.VMEM(sums_shape, F32),
            pltpu.SMEM((slots + 1,), jnp.int32),
            copy_sems,
            copy_sems,
            copy_sems,
            pltpu.SemaphoreType.DMA((2,)),
        ],
        compiler_params=pltpu.CompilerParams(vmem_limit_bytes=30 * 1024 * 1024),
        cost_estimate=pl.CostEstimate(
            flops=slots * 16 * modes * size**3,
            bytes_accessed=24 * 1024 * 1024,
            transcendentals=0,
        ),
        name="border" if border is not None else "interior",
    )(*operands)


def rims_kernel(
    partial, from_above, from_below, from_left, from_right, out,
    top, bottom, left, right, sems,
):
    tile = partial.shape[1]
    half = from_above.shape[1]
    inner = tile // LANES
    chunks = inner + 2
    middle = tile - 2 * half
    regions = (
        (top, 0, half, 0, tile),
        (bottom, tile - half, half, 0, tile),
        (left, half, middle, 0, half),
        (right, half, middle, tile - half, half),
    )

    def copy(index, comp, inward):
        buffer, row, height, column, width = regions[index]
        home = (partial if inward else out).at[comp, pl.ds(row, height), pl.ds(column, width)]
        here = buffer.at[comp]
        source, target = (home, here) if inward else (here, home)
        return pltpu.make_async_copy(source, target, sems.at[1 - int(inward), index, comp])

    everything = [(index, comp) for index in range(4) for comp in range(2)]
    for index, comp in everything:
        copy(index, comp, True).start()
    for index, comp in everything:
        copy(index, comp, True).wait()
        buffer = regions[index][0]
        if index < 2:
            ring = from_above if index == 0 else from_below
            side = slice(0, half) if index == 0 else slice(tile - half, tile)
            for j in range(inner):
                columns = slice(j * LANES, (j + 1) * LANES)
                extra = ring[comp * chunks + 1 + j].astype(F32)
                if j == 0:
                    extra = extra + from_left[comp, side, :].astype(F32)
                if j == inner - 1:
                    extra = extra + from_right[comp, side, :].astype(F32)
                buffer[comp, :, columns] += extra
        else:
            strip = from_left if index == 2 else from_right
            buffer[comp] += strip[comp, half : half + middle, :].astype(F32)
        copy(index, comp, False).start()
    for index, comp in everything:
        copy(index, comp, False).wait()


def add_rims(partial, rims):
    tile = partial.shape[1]
    half = rims[0].shape[1]
    vmem = pl.BlockSpec(memory_space=pltpu.VMEM)
    anywhere = pl.BlockSpec(memory_space=pl.ANY)
    return pl.pallas_call(
        rims_kernel,
        in_specs=[anywhere] + [vmem] * 4,
        out_specs=anywhere,
        out_shape=jax.ShapeDtypeStruct(partial.shape, F32),
        input_output_aliases={0: 0},
        scratch_shapes=[
            pltpu.VMEM((2, half, tile), F32),
            pltpu.VMEM((2, half, tile), F32),
            pltpu.VMEM((2, tile - 2 * half, half), F32),
            pltpu.VMEM((2, tile - 2 * half, half), F32),
            pltpu.SemaphoreType.DMA((2, 4, 2)),
        ],
        compiler_params=pltpu.CompilerParams(vmem_limit_bytes=16 * 1024 * 1024),
        cost_estimate=pl.CostEstimate(
            flops=1024 * 1024, bytes_accessed=6 * 1024 * 1024, transcendentals=0
        ),
        name="rims",
    )(partial, *rims)


def chip_sums(kept, given):
    return (kept + lax.ppermute(given, "core", [(0, 1), (1, 0)])).astype(BF16)


def shared_update(on_chip, beside, modes, size):
    axes = ("x", "col")
    devices = lax.axis_size("x") * lax.axis_size("col")
    core = lax.axis_index("core")
    groups, planes = on_chip.shape[:2]
    share = groups * 8 // devices
    if share < 8:
        on_chip = on_chip.reshape(groups, planes, 8 // share, share, size)
        on_chip = jnp.swapaxes(on_chip, 1, 2).reshape(devices, planes, share, size)
    else:
        on_chip = on_chip.reshape(devices, groups // devices, planes, 8, size)
    received = lax.all_to_all(on_chip, axes, 0, 0, tiled=True)
    total = jnp.sum(received.astype(F32), 0)
    if share >= 8:
        total = jnp.swapaxes(total, 0, 1).reshape(planes, share, size)
    update = (total[: 2 * modes] / jnp.sqrt(total[2 * modes])).astype(BF16)
    copies = jnp.broadcast_to(update, (devices,) + update.shape)
    mine = lax.all_to_all(copies, axes, 0, 0, tiled=True)
    mine, beside = lax.optimization_barrier((mine, beside))
    other = lax.ppermute(mine, "core", [(0, 1), (1, 0)])
    low = jnp.where(core == 0, mine, other)
    high = jnp.where(core == 0, other, mine)
    whole = jnp.concatenate([low, high], 0)
    return jnp.swapaxes(whole, 0, 1).reshape(modes, 2, size, size).astype(F32), beside


def on_device(object_field, probe_modes, counts, centers, patterns):
    size = probe_modes.shape[-1]
    modes = probe_modes.shape[0]
    half = size // 2
    tile = object_field.shape[1]

    top = shift_down(object_field[:, tile - half :, :].astype(BF16), ROW)
    bottom = shift_up(object_field[:, :half, :].astype(BF16), ROW)
    left = shift_down(object_field[:, :, tile - half :].astype(BF16), COL)
    right = shift_up(object_field[:, :, :half].astype(BF16), COL)
    left_ends = shift_down(
        jnp.concatenate([top[:, :, tile - half :], bottom[:, :, tile - half :]], 1), COL
    )
    right_ends = shift_up(jnp.concatenate([top[:, :, :half], bottom[:, :, :half]], 1), COL)

    counts_and_places = (counts, centers[0, 0])
    started, sums = run_positions(
        *counts_and_places, object_field, object_field, patterns[0, 0], probe_modes
    )
    border = (left, right, top, bottom, left_ends, right_ends, sums)
    partial, g_top, g_bottom, g_left, g_right, kept, given = run_positions(
        *counts_and_places, object_field, started, patterns[0, 0], probe_modes, border
    )

    chunks = g_top.shape[0] // 2
    from_above = shift_down(g_bottom, ROW)
    from_below = shift_up(g_top, ROW)

    def with_corners(strip, chunk):
        above = strip[:, :half].astype(F32) + from_above[chunk::chunks].astype(F32)
        below = strip[:, tile - half :].astype(F32) + from_below[chunk::chunks].astype(F32)
        middle = strip[:, half : tile - half]
        return jnp.concatenate([above.astype(BF16), middle, below.astype(BF16)], 1)

    to_right, to_left, on_chip = lax.optimization_barrier(
        (with_corners(g_right, chunks - 1), with_corners(g_left, 0), chip_sums(kept, given))
    )
    from_left = shift_down(to_right, COL)
    from_right = shift_up(to_left, COL)
    new_object = add_rims(partial, (from_above, from_below, from_left, from_right))
    update, new_object = shared_update(on_chip, new_object, modes, size)
    new_probe = probe_modes + update
    return (new_object, new_probe)


def solution(mesh):
    rows, columns = mesh.devices.shape
    split = jax.sharding.Mesh(
        mesh.devices.reshape(rows // 2, 2, columns), ("x", "core", "col")
    )
    placed = (
        P(None, ROW, "col"),
        P(),
        P(),
        P(ROW, "col", None, None),
        P(ROW, "col", None, None, None),
    )
    return jax.shard_map(
        on_device,
        mesh=split,
        in_specs=placed,
        out_specs=(P(None, ROW, "col"), P()),
        check_vma=False,
    )
```

```python
import functools
import math

import jax
import jax.numpy as jnp
import ml_dtypes
import numpy as np
from jax import lax
from jax.experimental import pallas as pl
from jax.experimental.pallas import tpu as pltpu
from jax.sharding import PartitionSpec as P

LANES = 128
ROW = ("x", "core")
COL = ("col",)
F32 = jnp.float32
BF16 = jnp.bfloat16


def dft_tables(length):
    indices = np.arange(length)
    angles = (indices[:, None] * indices[None, :] % length) * (2.0 * np.pi / length)
    scale = 1.0 / np.sqrt(length)
    cosine = (np.cos(angles) * scale).astype(np.float32).astype(ml_dtypes.bfloat16)
    sine = (np.sin(angles) * scale).astype(np.float32).astype(ml_dtypes.bfloat16)
    positive = np.block([[cosine, -sine], [sine, cosine]])
    negative = np.block([[cosine, sine], [-sine, cosine]])
    return positive, negative


def swap_pairs(array, axis, odd):
    devices = math.prod(lax.axis_size(name) for name in axis)
    firsts = range(odd, devices - 1, 2)
    return lax.ppermute(
        array, axis, [(i, i + 1) for i in firsts] + [(i + 1, i) for i in firsts]
    )


def sides(axis, length, width):
    even = (lax.axis_index(axis) & 1) == 0
    far = length - width
    return [
        pl.multiple_of(jnp.where(even, far, 0), width),
        pl.multiple_of(jnp.where(even, 0, far), width),
    ]


def strips_kernel(obj_hbm, col_even, col_odd, row_even, row_odd, col_buffer, row_buffer, sems):
    tile = obj_hbm.shape[1]
    half = row_even.shape[1]
    copies = []
    for pair in range(2):
        column = sides(COL, tile, half)[pair]
        row = sides(ROW, tile, half)[pair]
        copies.append(
            pltpu.make_async_copy(
                obj_hbm.at[:, :, pl.ds(column, half)], col_buffer.at[pair], sems.at[0, pair]
            )
        )
        copies.append(
            pltpu.make_async_copy(
                obj_hbm.at[:, pl.ds(row, half), :], row_buffer.at[pair], sems.at[1, pair]
            )
        )
    for copy in copies:
        copy.start()
    outputs = (col_even, row_even, col_odd, row_odd)
    buffers = (col_buffer, row_buffer) * 2
    for index, copy in enumerate(copies):
        copy.wait()
        outputs[index][...] = buffers[index][index // 2].astype(BF16)


def cut_strips(object_field, half):
    tile = object_field.shape[1]
    vmem = pl.BlockSpec(memory_space=pltpu.VMEM)
    columns = jax.ShapeDtypeStruct((2, tile, half), BF16)
    rows = jax.ShapeDtypeStruct((2, half, tile), BF16)
    return pl.pallas_call(
        strips_kernel,
        in_specs=[pl.BlockSpec(memory_space=pltpu.HBM)],
        out_specs=[vmem] * 4,
        out_shape=[columns, columns, rows, rows],
        scratch_shapes=[
            pltpu.VMEM((2, 2, tile, half), F32),
            pltpu.VMEM((2, 2, half, tile), F32),
            pltpu.SemaphoreType.DMA((2, 2)),
        ],
        compiler_params=pltpu.CompilerParams(vmem_limit_bytes=12 * 1024 * 1024),
        cost_estimate=pl.CostEstimate(
            flops=1024 * 1024, bytes_accessed=5 * 1024 * 1024, transcendentals=0
        ),
        name="strips",
    )(object_field)


def positions_kernel(with_border, *refs):
    counts, centers, obj_hbm, start_hbm, pat_hbm, probe = refs[:6]
    right_positive, right_negative, left_positive, left_negative = refs[6:10]
    refs = refs[10:]
    if with_border:
        col_halos, row_halos, end_halos, sums_hbm = refs[0:2], refs[2:4], refs[4:6], refs[6]
        out_hbm, g_rows, g_cols, kept, given = refs[7], refs[8:10], refs[10:12], *refs[12:14]
        refs = refs[14:]
    else:
        out_hbm, sums_out = refs[:2]
        refs = refs[2:]
    (obj, canvas, patterns, low, waves, shifts, halves, backs, spectra, changes, patch, sums, order,
     obj_sems, canvas_sems, out_sems, misc_sems) = refs
    size = probe.shape[-1]
    half = size // 2
    tile = obj_hbm.shape[1]
    inner = tile // LANES
    chunks = inner + 2
    modes = probe.shape[0]
    rows = slice(half, half + tile)
    pieces = [(comp, j) for comp in range(2) for j in range(inner)]

    def home(array, comp, j):
        return array.at[comp, :, pl.ds(j * LANES, LANES)]

    def held(array, comp, j):
        return array.at[comp * chunks + 1 + j, pl.ds(half, tile), :]

    obj_copies = [
        pltpu.make_async_copy(home(obj_hbm, *p), held(obj, *p), obj_sems.at[p]) for p in pieces
    ]
    canvas_copies = [
        pltpu.make_async_copy(home(start_hbm, *p), held(canvas, *p), canvas_sems.at[p])
        for p in pieces
    ]
    out_copies = [
        pltpu.make_async_copy(held(canvas, *p), home(out_hbm, *p), out_sems.at[p]) for p in pieces
    ]
    pat_copy = pltpu.make_async_copy(pat_hbm, patterns, misc_sems.at[0])
    later = [pat_copy] + canvas_copies
    for copy in obj_copies:
        copy.start()
    pat_copy.start()
    for copy in canvas_copies:
        copy.start()
    if with_border:
        sums_copy = pltpu.make_async_copy(sums_hbm, sums, misc_sems.at[1])
        sums_copy.start()
        later.append(sums_copy)
    else:
        sums[...] = jnp.zeros_like(sums)

    intensity = jnp.zeros((size, size), F32)
    for m in range(modes):
        for comp in range(2):
            values = probe[m, comp]
            intensity = intensity + values * values
            low[2 * m + comp] = values.astype(BF16).astype(F32)
    scale = 1.0 / (jnp.max(intensity) + 1e-06)
    changes[...] = jnp.zeros_like(changes)
    patch[...] = jnp.zeros_like(patch)

    if with_border:
        row_sides = sides(ROW, tile + size, half)
        col_sides = [offset // LANES for offset in sides(COL, tile + size, half)]
        blank = jnp.zeros((tile + size, LANES), F32)
        for comp in range(2):
            first = comp * chunks
            canvas[first] = blank
            canvas[first + chunks - 1] = blank
            for j in range(inner):
                canvas[first + 1 + j, 0:half, :] = blank[0:half]
                canvas[first + 1 + j, half + tile :, :] = blank[0:half]
            for pair in range(2):
                beside = first + col_sides[pair]
                obj[beside, rows, :] = col_halos[pair][comp].astype(F32)
                for other in range(2):
                    obj[beside, pl.ds(row_sides[other], half), :] = end_halos[pair][
                        comp, other * half : (other + 1) * half, :
                    ].astype(F32)
                for j in range(inner):
                    columns = slice(j * LANES, (j + 1) * LANES)
                    obj[first + 1 + j, pl.ds(row_sides[pair], half), :] = row_halos[pair][
                        comp, :, columns
                    ].astype(F32)

    order[0] = 0
    count = counts[lax.axis_index(ROW), lax.axis_index("col")]

    def note(slot, found):
        row = centers[0, slot]
        column = centers[1, slot]
        inside = (row >= half) & (row <= tile - half) & (column >= half) & (column <= tile - half)
        order[found] = slot
        return found + jnp.where(inside, 0 if with_border else 1, 1 if with_border else 0)

    found = lax.fori_loop(0, count, note, 0)

    block = 64
    groups = block // 8
    lane = lax.broadcasted_iota(jnp.int32, (block, LANES), 1)
    blocks = range(0, size, block)

    def place_of(index):
        slot = order[index]
        column = centers[1, slot]
        return slot, centers[0, slot], column >> 7, column & 127

    def cut(index, begin):
        _, row, chunk, offset = place_of(index)
        back_offset = (LANES - offset) & 127
        from_first = lane < LANES - offset
        here = slice(begin, begin + block)
        parts = []
        for comp in range(2):
            moved = [
                pltpu.roll(
                    obj[comp * chunks + chunk + k, pl.ds(row + begin, block), :], back_offset, 1
                )
                for k in range(3)
            ]
            window = jnp.concatenate(
                [
                    jnp.where(from_first, moved[0], moved[1]),
                    jnp.where(from_first, moved[1], moved[2]),
                ],
                1,
            ).astype(BF16).astype(F32)
            patch[index & 1, comp, here, :] = window
            parts.append(window)
        real, imag = parts
        for m in range(modes):
            probe_real = low[2 * m, here, :]
            probe_imag = low[2 * m + 1, here, :]
            there = slice(m * size + begin, m * size + begin + block)
            waves[there, 0:size] = (probe_real * real - probe_imag * imag).astype(BF16)
            waves[there, size:] = (probe_real * imag + probe_imag * real).astype(BF16)

    def forward_right(m, part):
        mode = slice(m * size, (m + 1) * size)
        columns = slice(part * size, (part + 1) * size)
        halves[columns, mode] = jnp.dot(
            waves[mode, :], right_positive[:, columns], preferred_element_type=F32
        ).astype(BF16)

    def forward_left(k):
        rows_here = slice(k * size, (k + 1) * size)
        spectra[rows_here, :] = jnp.dot(
            left_negative[rows_here, :], halves[...], preferred_element_type=F32
        )

    def reweigh(index, begin):
        slot = order[index]
        k, inside = divmod(begin, half)
        real_rows = slice(k * size + inside, k * size + inside + block)
        imag_rows = slice(k * size + half + inside, k * size + half + inside + block)
        amplitude = patterns[slot, begin : begin + block, :].astype(F32)
        mode_columns = [slice(m * size, (m + 1) * size) for m in range(modes)]
        parts = [(spectra[real_rows, mode], spectra[imag_rows, mode]) for mode in mode_columns]
        power = sum(real * real + imag * imag for real, imag in parts)
        factor = amplitude * lax.rsqrt(jnp.maximum(power, 0.5)) - 1.0
        for m, (real, imag) in enumerate(parts):
            first = k * size + m * half + inside
            there = slice(first, first + block)
            shifts[there, 0:size] = (factor * real).astype(BF16)
            shifts[there, size:] = (factor * imag).astype(BF16)

    def backward_right(k):
        product = jnp.dot(
            shifts[k * size : (k + 1) * size, :], right_negative[...],
            preferred_element_type=F32,
        ).astype(BF16)
        for m in range(modes):
            mode = slice(m * size, (m + 1) * size)
            for part in range(2):
                first = part * size + k * half
                backs[first : first + half, mode] = product[
                    m * half : (m + 1) * half, part * size : (part + 1) * size
                ]

    def backward_left(m, part):
        mode = slice(m * size, (m + 1) * size)
        rows_here = slice(part * size, (part + 1) * size)
        changes[rows_here, mode] = jnp.dot(
            left_positive[rows_here, :], backs[:, mode], preferred_element_type=F32
        )

    def deposit(index, buffer, begin):
        _, row, chunk, offset = place_of(index)
        past = lane >= offset
        here = slice(begin, begin + block)
        below = slice(size + begin, size + begin + block)
        start = begin // 8
        obj_real = patch[buffer, 0, here, :]
        obj_imag = patch[buffer, 1, here, :]

        def add(plane, value):
            sums[start : start + groups, plane] += value.reshape(groups, 8, size)

        add(2 * modes, obj_real * obj_real + obj_imag * obj_imag)
        term_real = term_imag = None
        for m in range(modes):
            mode = slice(m * size, (m + 1) * size)
            real = changes[here, mode]
            imag = changes[below, mode]
            probe_real = low[2 * m, here, :]
            probe_imag = low[2 * m + 1, here, :]
            more_real = probe_real * real + probe_imag * imag
            more_imag = probe_real * imag - probe_imag * real
            term_real = more_real if m == 0 else term_real + more_real
            term_imag = more_imag if m == 0 else term_imag + more_imag
            add(2 * m, obj_real * real + obj_imag * imag)
            add(2 * m + 1, obj_real * imag - obj_imag * real)
        for comp, term in enumerate((term_real, term_imag)):
            term = term.astype(BF16).astype(F32) * scale
            first = pltpu.roll(term[:, 0:LANES], offset, 1)
            second = pltpu.roll(term[:, LANES:], offset, 1)
            place = comp * chunks + chunk
            window = pl.ds(row + begin, block)
            values = [canvas[place + k, window, :] for k in range(3)]
            canvas[place, window, :] = values[0] + jnp.where(past, first, 0.0)
            canvas[place + 1, window, :] = values[1] + jnp.where(past, second, first)
            canvas[place + 2, window, :] = values[2] + jnp.where(past, 0.0, second)

    def step(index, carry):
        previous = jnp.maximum(index - 1, 0)
        following = jnp.minimum(index + 1, found - 1)
        buffer = (index + 1) & 1
        starts = list(blocks)
        for m in range(modes):
            for part in range(2):
                forward_right(m, part)
                deposit(previous, buffer, starts[2 * m + part])
        forward_left(0)
        forward_left(1)
        for begin in starts[:2]:
            reweigh(index, begin)
        backward_right(0)
        for begin in starts[2:]:
            reweigh(index, begin)
        cut(following, starts[0])
        backward_right(1)
        cut(following, starts[1])
        backward_left(0, 0)
        cut(following, starts[2])
        backward_left(0, 1)
        cut(following, starts[3])
        backward_left(1, 0)
        backward_left(1, 1)
        return carry

    for copy in obj_copies:
        copy.wait()

    @pl.when(found > 0)
    def _():
        for begin in blocks:
            cut(0, begin)

    for copy in later:
        copy.wait()

    @pl.when(found > 0)
    def _():
        lax.fori_loop(0, found, step, 0)
        for begin in blocks:
            deposit(found - 1, (found - 1) & 1, begin)

    for copy in out_copies:
        copy.start()
    if with_border:
        for pair in range(2):
            g_rows[pair][...] = canvas[:, pl.ds(row_sides[pair], half), :].astype(BF16)
            for comp in range(2):
                g_cols[pair][comp] = canvas[comp * chunks + col_sides[pair], rows, :].astype(BF16)
        core = lax.axis_index("core")
        count_of = kept.shape[0]
        kept[...] = sums[pl.ds(core * count_of, count_of)]
        given[...] = sums[pl.ds((1 - core) * count_of, count_of)]
    else:
        sums_copy = pltpu.make_async_copy(sums, sums_out, misc_sems.at[1])
        sums_copy.start()
        sums_copy.wait()
    for copy in out_copies:
        copy.wait()


def run_positions(counts, centers, object_field, started, patterns, probe_modes, border=None):
    size = probe_modes.shape[-1]
    half = size // 2
    modes = probe_modes.shape[0]
    tile = object_field.shape[1]
    chunks = tile // LANES + 2
    slots = patterns.shape[0]
    positive, negative = dft_tables(size)
    by_quarter = np.arange(2 * size).reshape(2, 2, half).swapaxes(0, 1).reshape(-1)
    tables = [positive, negative, positive, negative[by_quarter]]
    smem = pl.BlockSpec(memory_space=pltpu.SMEM)
    vmem = pl.BlockSpec(memory_space=pltpu.VMEM)
    anywhere = pl.BlockSpec(memory_space=pl.ANY)
    shape = jax.ShapeDtypeStruct
    in_specs = [smem, smem, anywhere, anywhere, anywhere] + [vmem] * 5
    operands = [counts, centers, object_field, started, patterns, probe_modes, *tables]
    sums_shape = (size // 8, 2 * modes + 1, 8, size)
    if border is None:
        out_specs = [anywhere, anywhere]
        out_shape = [shape(object_field.shape, F32), shape(sums_shape, F32)]
    else:
        in_specs += [vmem] * 6 + [anywhere]
        operands += list(border)
        half_sums = (size // 16,) + sums_shape[1:]
        out_specs = [anywhere] + [vmem] * 6
        out_shape = [
            shape(object_field.shape, F32),
            shape((2 * chunks, half, LANES), BF16),
            shape((2 * chunks, half, LANES), BF16),
            shape((2, tile, LANES), BF16),
            shape((2, tile, LANES), BF16),
            shape(half_sums, F32),
            shape(half_sums, F32),
        ]
    copy_sems = pltpu.SemaphoreType.DMA((2, tile // LANES))
    return pl.pallas_call(
        functools.partial(positions_kernel, border is not None),
        in_specs=in_specs,
        out_specs=out_specs,
        out_shape=out_shape,
        scratch_shapes=[
            pltpu.VMEM((2 * chunks, tile + size, LANES), F32),
            pltpu.VMEM((2 * chunks, tile + size, LANES), F32),
            pltpu.VMEM(patterns.shape, BF16),
            pltpu.VMEM((2 * modes, size, size), F32),
            pltpu.VMEM((modes * size, 2 * size), BF16),
            pltpu.VMEM((modes * size, 2 * size), BF16),
            pltpu.VMEM((2 * size, modes * size), BF16),
            pltpu.VMEM((2 * size, modes * size), BF16),
            pltpu.VMEM((2 * size, modes * size), F32),
            pltpu.VMEM((2 * size, modes * size), F32),
            pltpu.VMEM((2, 2, size, size), F32),
            pltpu.VMEM(sums_shape, F32),
            pltpu.SMEM((slots + 1,), jnp.int32),
            copy_sems,
            copy_sems,
            copy_sems,
            pltpu.SemaphoreType.DMA((2,)),
        ],
        compiler_params=pltpu.CompilerParams(vmem_limit_bytes=30 * 1024 * 1024),
        cost_estimate=pl.CostEstimate(
            flops=slots * 16 * modes * size**3,
            bytes_accessed=24 * 1024 * 1024,
            transcendentals=0,
        ),
        name="border" if border is not None else "interior",
    )(*operands)


def corners_kernel(col_even, col_odd, row_even, row_odd, out_even, out_odd):
    tile = col_even.shape[1]
    half = row_even.shape[1]
    chunks = row_even.shape[0] // 2
    row_sides = sides(ROW, tile, half)
    col_sides = [offset // LANES for offset in sides(COL, chunks * LANES, half)]
    for pair, (strip, out) in enumerate(((col_even, out_even), (col_odd, out_odd))):
        out[:, half : tile - half, :] = strip[:, half : tile - half, :]
        for other, ring in enumerate((row_even, row_odd)):
            there = pl.ds(row_sides[other], half)
            for comp in range(2):
                extra = ring[comp * chunks + col_sides[pair]].astype(F32)
                out[comp, there, :] = (strip[comp, there, :].astype(F32) + extra).astype(BF16)


def add_corners(g_cols, from_rows):
    vmem = pl.BlockSpec(memory_space=pltpu.VMEM)
    shape = jax.ShapeDtypeStruct(g_cols[0].shape, BF16)
    return pl.pallas_call(
        corners_kernel,
        in_specs=[vmem] * 4,
        out_specs=[vmem] * 2,
        out_shape=[shape, shape],
        compiler_params=pltpu.CompilerParams(vmem_limit_bytes=8 * 1024 * 1024),
        cost_estimate=pl.CostEstimate(
            flops=256 * 1024, bytes_accessed=2 * 1024 * 1024, transcendentals=0
        ),
        name="corners",
    )(*g_cols, *from_rows)


def rims_kernel(
    partial, row_even, row_odd, col_even, col_odd, out, row_buffer, col_buffer, sems
):
    tile = partial.shape[1]
    half = row_even.shape[1]
    inner = tile // LANES
    chunks = inner + 2
    middle = tile - 2 * half
    row_sides = sides(ROW, tile, half)
    col_sides = sides(COL, tile, half)
    row_rings = (row_even, row_odd)
    col_strips = (col_even, col_odd)

    def copy(kind, pair, comp, inward):
        if kind == 0:
            here = row_buffer.at[pair, comp]
            place = (comp, pl.ds(row_sides[pair], half), slice(None))
        else:
            here = col_buffer.at[pair, comp]
            place = (comp, pl.ds(half, middle), pl.ds(col_sides[pair], half))
        source, target = (partial.at[place], here) if inward else (here, out.at[place])
        return pltpu.make_async_copy(
            source, target, sems.at[1 - int(inward), 2 * kind + pair, comp]
        )

    everything = [(kind, pair, comp) for kind in range(2) for pair in range(2) for comp in range(2)]
    for piece in everything:
        copy(*piece, True).start()
    for kind, pair, comp in everything:
        copy(kind, pair, comp, True).wait()
        if kind == 0:
            for j in range(inner):
                columns = slice(j * LANES, (j + 1) * LANES)
                ring = row_rings[pair][comp * chunks + 1 + j]
                row_buffer[pair, comp, :, columns] += ring.astype(F32)
            for other in range(2):
                columns = pl.ds(col_sides[other], half)
                strip = col_strips[other][comp, pl.ds(row_sides[pair], half), :]
                row_buffer[pair, comp, :, columns] += strip.astype(F32)
        else:
            strip = col_strips[pair][comp, half : half + middle, :]
            col_buffer[pair, comp] += strip.astype(F32)
        copy(kind, pair, comp, False).start()
    for piece in everything:
        copy(*piece, False).wait()


def add_rims(partial, from_rows, from_cols):
    tile = partial.shape[1]
    half = from_rows[0].shape[1]
    vmem = pl.BlockSpec(memory_space=pltpu.VMEM)
    anywhere = pl.BlockSpec(memory_space=pl.ANY)
    return pl.pallas_call(
        rims_kernel,
        in_specs=[anywhere] + [vmem] * 4,
        out_specs=anywhere,
        out_shape=jax.ShapeDtypeStruct(partial.shape, F32),
        input_output_aliases={0: 0},
        scratch_shapes=[
            pltpu.VMEM((2, 2, half, tile), F32),
            pltpu.VMEM((2, 2, tile - 2 * half, half), F32),
            pltpu.SemaphoreType.DMA((2, 4, 2)),
        ],
        compiler_params=pltpu.CompilerParams(vmem_limit_bytes=16 * 1024 * 1024),
        cost_estimate=pl.CostEstimate(
            flops=1024 * 1024, bytes_accessed=6 * 1024 * 1024, transcendentals=0
        ),
        name="rims",
    )(partial, *from_rows, *from_cols)


def chip_sums(kept, given):
    return (kept + lax.ppermute(given, "core", [(0, 1), (1, 0)])).astype(BF16)


def shared_update(on_chip, beside, modes, size):
    axes = ("x", "col")
    devices = lax.axis_size("x") * lax.axis_size("col")
    core = lax.axis_index("core")
    groups, planes = on_chip.shape[:2]
    share = groups * 8 // devices
    if share < 8:
        on_chip = on_chip.reshape(groups, planes, 8 // share, share, size)
        on_chip = jnp.swapaxes(on_chip, 1, 2).reshape(devices, planes, share, size)
    else:
        on_chip = on_chip.reshape(devices, groups // devices, planes, 8, size)
    received = lax.all_to_all(on_chip, axes, 0, 0, tiled=True)
    received, beside = lax.optimization_barrier((received, beside))
    total = jnp.sum(received.astype(F32), 0)
    if share >= 8:
        total = jnp.swapaxes(total, 0, 1).reshape(planes, share, size)
    update = (total[: 2 * modes] / jnp.sqrt(total[2 * modes])).astype(BF16)
    copies = jnp.broadcast_to(update, (devices,) + update.shape)
    mine = lax.all_to_all(copies, axes, 0, 0, tiled=True)
    other = lax.ppermute(mine, "core", [(0, 1), (1, 0)])
    low = jnp.where(core == 0, mine, other)
    high = jnp.where(core == 0, other, mine)
    whole = jnp.concatenate([low, high], 0)
    return jnp.swapaxes(whole, 0, 1).reshape(modes, 2, size, size).astype(F32), beside


def on_device(object_field, probe_modes, counts, centers, patterns):
    size = probe_modes.shape[-1]
    modes = probe_modes.shape[0]
    half = size // 2
    tile = object_field.shape[1]

    col_even, col_odd, row_even, row_odd = cut_strips(object_field, half)
    col_halos = (swap_pairs(col_even, COL, 0), swap_pairs(col_odd, COL, 1))
    row_halos = (swap_pairs(row_even, ROW, 0), swap_pairs(row_odd, ROW, 1))
    is_even = (lax.axis_index("col") & 1) == 0
    first_ends = jnp.concatenate([halo[:, :, :half] for halo in row_halos], 1)
    last_ends = jnp.concatenate([halo[:, :, tile - half :] for halo in row_halos], 1)
    end_halos = (
        swap_pairs(jnp.where(is_even, last_ends, first_ends), COL, 0),
        swap_pairs(jnp.where(is_even, first_ends, last_ends), COL, 1),
    )

    inputs = (counts, centers[0, 0], object_field)
    started, sums = run_positions(*inputs, object_field, patterns[0, 0], probe_modes)
    border = (*col_halos, *row_halos, *end_halos, sums)
    partial, g_row_even, g_row_odd, g_col_even, g_col_odd, kept, given = run_positions(
        *inputs, started, patterns[0, 0], probe_modes, border
    )

    from_rows = (swap_pairs(g_row_even, ROW, 0), swap_pairs(g_row_odd, ROW, 1))
    to_even, to_odd = add_corners((g_col_even, g_col_odd), from_rows)
    to_even, to_odd, on_chip = lax.optimization_barrier(
        (to_even, to_odd, chip_sums(kept, given))
    )
    from_cols = (swap_pairs(to_even, COL, 0), swap_pairs(to_odd, COL, 1))
    update, from_cols = shared_update(on_chip, from_cols, modes, size)
    new_object = add_rims(partial, from_rows, from_cols)
    new_probe = probe_modes + update
    return (new_object, new_probe)


def solution(mesh):
    rows, columns = mesh.devices.shape
    split = jax.sharding.Mesh(
        mesh.devices.reshape(rows // 2, 2, columns), ("x", "core", "col")
    )
    placed = (
        P(None, ROW, "col"),
        P(),
        P(),
        P(ROW, "col", None, None),
        P(ROW, "col", None, None, None),
    )
    return jax.shard_map(
        on_device,
        mesh=split,
        in_specs=placed,
        out_specs=(P(None, ROW, "col"), P()),
        check_vma=False,
    )
```

```python
import functools
import math

import jax
import jax.numpy as jnp
import ml_dtypes
import numpy as np
from jax import lax
from jax.experimental import pallas as pl
from jax.experimental.pallas import tpu as pltpu
from jax.sharding import PartitionSpec as P

LANES = 128
ROW = ("x", "core")
COL = ("col",)
F32 = jnp.float32
BF16 = jnp.bfloat16


def dft_tables(length):
    indices = np.arange(length)
    angles = (indices[:, None] * indices[None, :] % length) * (2.0 * np.pi / length)
    scale = 1.0 / np.sqrt(length)
    cosine = (np.cos(angles) * scale).astype(np.float32).astype(ml_dtypes.bfloat16)
    sine = (np.sin(angles) * scale).astype(np.float32).astype(ml_dtypes.bfloat16)
    positive = np.block([[cosine, -sine], [sine, cosine]])
    negative = np.block([[cosine, sine], [-sine, cosine]])
    return positive, negative


def swap_pairs(array, axis, odd):
    devices = math.prod(lax.axis_size(name) for name in axis)
    firsts = range(odd, devices - 1, 2)
    return lax.ppermute(
        array, axis, [(i, i + 1) for i in firsts] + [(i + 1, i) for i in firsts]
    )


def sides(axis, length, width):
    even = (lax.axis_index(axis) & 1) == 0
    far = length - width
    return [
        pl.multiple_of(jnp.where(even, far, 0), width),
        pl.multiple_of(jnp.where(even, 0, far), width),
    ]


def strips_kernel(obj_hbm, col_even, col_odd, row_even, row_odd, col_buffer, row_buffer, sems):
    tile = obj_hbm.shape[1]
    half = row_even.shape[1]
    copies = []
    for pair in range(2):
        column = sides(COL, tile, half)[pair]
        row = sides(ROW, tile, half)[pair]
        copies.append(
            pltpu.make_async_copy(
                obj_hbm.at[:, :, pl.ds(column, half)], col_buffer.at[pair], sems.at[0, pair]
            )
        )
        copies.append(
            pltpu.make_async_copy(
                obj_hbm.at[:, pl.ds(row, half), :], row_buffer.at[pair], sems.at[1, pair]
            )
        )
    for copy in copies:
        copy.start()
    outputs = (col_even, row_even, col_odd, row_odd)
    buffers = (col_buffer, row_buffer) * 2
    for index, copy in enumerate(copies):
        copy.wait()
        outputs[index][...] = buffers[index][index // 2].astype(BF16)


def cut_strips(object_field, half):
    tile = object_field.shape[1]
    vmem = pl.BlockSpec(memory_space=pltpu.VMEM)
    columns = jax.ShapeDtypeStruct((2, tile, half), BF16)
    rows = jax.ShapeDtypeStruct((2, half, tile), BF16)
    return pl.pallas_call(
        strips_kernel,
        in_specs=[pl.BlockSpec(memory_space=pltpu.HBM)],
        out_specs=[vmem] * 4,
        out_shape=[columns, columns, rows, rows],
        scratch_shapes=[
            pltpu.VMEM((2, 2, tile, half), F32),
            pltpu.VMEM((2, 2, half, tile), F32),
            pltpu.SemaphoreType.DMA((2, 2)),
        ],
        compiler_params=pltpu.CompilerParams(vmem_limit_bytes=60 * 1024 * 1024),
        cost_estimate=pl.CostEstimate(
            flops=1024 * 1024, bytes_accessed=5 * 1024 * 1024, transcendentals=0
        ),
        name="strips",
    )(object_field)


def positions_kernel(with_border, *refs):
    counts, centers, obj_hbm, pat_hbm, probe = refs[:5]
    tables_hbm = refs[5:8]
    refs = refs[8:]
    start_hbm = obj_hbm
    if with_border:
        col_halos, row_halos, end_halos = refs[0:2], refs[2:4], refs[4:6]
        sums_hbm, start_hbm = refs[6:8]
        out_hbm, g_rows, g_cols, kept, given = refs[8], refs[9:11], refs[11:13], *refs[13:15]
        refs = refs[15:]
    else:
        out_hbm, sums_out = refs[:2]
        refs = refs[2:]
    (obj, canvas, patterns, positive, negative, left_negative, low, waves, shifts, halves, backs, spectra, changes, patch, sums, order,
     obj_sems, canvas_sems, out_sems, misc_sems) = refs
    size = probe.shape[-1]
    half = size // 2
    tile = obj_hbm.shape[1]
    inner = tile // LANES
    chunks = inner + 2
    modes = probe.shape[0]
    rows = slice(half, half + tile)
    pieces = [(comp, j) for comp in range(2) for j in range(inner)]

    def home(array, comp, j):
        return array.at[comp, :, pl.ds(j * LANES, LANES)]

    def held(array, comp, j):
        return array.at[comp * chunks + 1 + j, pl.ds(half, tile), :]

    obj_copies = [
        pltpu.make_async_copy(home(obj_hbm, *p), held(obj, *p), obj_sems.at[p]) for p in pieces
    ]
    canvas_copies = [
        pltpu.make_async_copy(home(start_hbm, *p), held(canvas, *p), canvas_sems.at[p])
        for p in pieces
    ]
    out_copies = [
        pltpu.make_async_copy(held(canvas, *p), home(out_hbm, *p), out_sems.at[p]) for p in pieces
    ]
    pat_copy = pltpu.make_async_copy(pat_hbm, patterns, misc_sems.at[0])
    tables = (positive, negative, left_negative)
    table_copies = [
        pltpu.make_async_copy(tables_hbm[i], tables[i], misc_sems.at[2 + i]) for i in range(3)
    ]
    later = table_copies + [pat_copy] + canvas_copies
    for copy in obj_copies:
        copy.start()
    for copy in table_copies:
        copy.start()
    pat_copy.start()
    for copy in canvas_copies:
        copy.start()
    if with_border:
        sums_copy = pltpu.make_async_copy(sums_hbm, sums, misc_sems.at[1])
        sums_copy.start()
        later.append(sums_copy)
    else:
        sums[...] = jnp.zeros_like(sums)

    intensity = jnp.zeros((size, size), F32)
    for m in range(modes):
        for comp in range(2):
            values = probe[m, comp]
            intensity = intensity + values * values
            low[2 * m + comp] = values.astype(BF16).astype(F32)
    scale = 1.0 / (jnp.max(intensity) + 1e-06)
    changes[...] = jnp.zeros_like(changes)
    patch[...] = jnp.zeros_like(patch)

    if with_border:
        row_sides = sides(ROW, tile + size, half)
        col_sides = [offset // LANES for offset in sides(COL, tile + size, half)]
        blank = jnp.zeros((tile + size, LANES), F32)
        for comp in range(2):
            first = comp * chunks
            canvas[first] = blank
            canvas[first + chunks - 1] = blank
            for j in range(inner):
                canvas[first + 1 + j, 0:half, :] = blank[0:half]
                canvas[first + 1 + j, half + tile :, :] = blank[0:half]
            for pair in range(2):
                beside = first + col_sides[pair]
                obj[beside, rows, :] = col_halos[pair][comp].astype(F32)
                for other in range(2):
                    obj[beside, pl.ds(row_sides[other], half), :] = end_halos[pair][
                        comp, other * half : (other + 1) * half, :
                    ].astype(F32)
                for j in range(inner):
                    columns = slice(j * LANES, (j + 1) * LANES)
                    obj[first + 1 + j, pl.ds(row_sides[pair], half), :] = row_halos[pair][
                        comp, :, columns
                    ].astype(F32)

    order[0] = 0
    count = counts[lax.axis_index(ROW), lax.axis_index("col")]

    def note(slot, found):
        row = centers[0, slot]
        column = centers[1, slot]
        inside = (row >= half) & (row <= tile - half) & (column >= half) & (column <= tile - half)
        order[found] = slot
        return found + jnp.where(inside, 0 if with_border else 1, 1 if with_border else 0)

    found = lax.fori_loop(0, count, note, 0)

    block = 64
    groups = block // 8
    lane = lax.broadcasted_iota(jnp.int32, (block, LANES), 1)
    blocks = range(0, size, block)

    def place_of(index):
        slot = order[index]
        column = centers[1, slot]
        return slot, centers[0, slot], column >> 7, column & 127

    def cut(index, begin):
        _, row, chunk, offset = place_of(index)
        back_offset = (LANES - offset) & 127
        from_first = lane < LANES - offset
        here = slice(begin, begin + block)
        parts = []
        for comp in range(2):
            moved = [
                pltpu.roll(
                    obj[comp * chunks + chunk + k, pl.ds(row + begin, block), :], back_offset, 1
                )
                for k in range(3)
            ]
            window = jnp.concatenate(
                [
                    jnp.where(from_first, moved[0], moved[1]),
                    jnp.where(from_first, moved[1], moved[2]),
                ],
                1,
            ).astype(BF16).astype(F32)
            patch[index & 1, comp, here, :] = window
            parts.append(window)
        real, imag = parts
        for m in range(modes):
            probe_real = low[2 * m, here, :]
            probe_imag = low[2 * m + 1, here, :]
            there = slice(m * size + begin, m * size + begin + block)
            waves[there, 0:size] = (probe_real * real - probe_imag * imag).astype(BF16)
            waves[there, size:] = (probe_real * imag + probe_imag * real).astype(BF16)

    def forward_right(m, part):
        mode = slice(m * size, (m + 1) * size)
        columns = slice(part * size, (part + 1) * size)
        halves[columns, mode] = jnp.dot(
            waves[mode, :], positive[:, columns], preferred_element_type=F32
        ).astype(BF16)

    def forward_left(k):
        rows_here = slice(k * size, (k + 1) * size)
        spectra[rows_here, :] = jnp.dot(
            left_negative[rows_here, :], halves[...], preferred_element_type=F32
        )

    def reweigh(index, begin):
        slot = order[index]
        k, inside = divmod(begin, half)
        real_rows = slice(k * size + inside, k * size + inside + block)
        imag_rows = slice(k * size + half + inside, k * size + half + inside + block)
        amplitude = patterns[slot, begin : begin + block, :].astype(F32)
        mode_columns = [slice(m * size, (m + 1) * size) for m in range(modes)]
        parts = [(spectra[real_rows, mode], spectra[imag_rows, mode]) for mode in mode_columns]
        power = sum(real * real + imag * imag for real, imag in parts)
        factor = amplitude * lax.rsqrt(jnp.maximum(power, 0.5)) - 1.0
        for m, (real, imag) in enumerate(parts):
            first = k * size + m * half + inside
            there = slice(first, first + block)
            shifts[there, 0:size] = (factor * real).astype(BF16)
            shifts[there, size:] = (factor * imag).astype(BF16)

    def backward_right(k):
        product = jnp.dot(
            shifts[k * size : (k + 1) * size, :], negative[...],
            preferred_element_type=F32,
        ).astype(BF16)
        for m in range(modes):
            mode = slice(m * size, (m + 1) * size)
            for part in range(2):
                first = part * size + k * half
                backs[first : first + half, mode] = product[
                    m * half : (m + 1) * half, part * size : (part + 1) * size
                ]

    def backward_left(m, part):
        mode = slice(m * size, (m + 1) * size)
        rows_here = slice(part * size, (part + 1) * size)
        changes[rows_here, mode] = jnp.dot(
            positive[rows_here, :], backs[:, mode], preferred_element_type=F32
        )

    def deposit(index, buffer, begin):
        _, row, chunk, offset = place_of(index)
        past = lane >= offset
        here = slice(begin, begin + block)
        below = slice(size + begin, size + begin + block)
        start = begin // 8
        obj_real = patch[buffer, 0, here, :]
        obj_imag = patch[buffer, 1, here, :]

        def add(plane, value):
            sums[start : start + groups, plane] += value.reshape(groups, 8, size)

        add(2 * modes, obj_real * obj_real + obj_imag * obj_imag)
        term_real = term_imag = None
        for m in range(modes):
            mode = slice(m * size, (m + 1) * size)
            real = changes[here, mode]
            imag = changes[below, mode]
            probe_real = low[2 * m, here, :]
            probe_imag = low[2 * m + 1, here, :]
            more_real = probe_real * real + probe_imag * imag
            more_imag = probe_real * imag - probe_imag * real
            term_real = more_real if m == 0 else term_real + more_real
            term_imag = more_imag if m == 0 else term_imag + more_imag
            add(2 * m, obj_real * real + obj_imag * imag)
            add(2 * m + 1, obj_real * imag - obj_imag * real)
        for comp, term in enumerate((term_real, term_imag)):
            term = term.astype(BF16).astype(F32) * scale
            first = pltpu.roll(term[:, 0:LANES], offset, 1)
            second = pltpu.roll(term[:, LANES:], offset, 1)
            place = comp * chunks + chunk
            window = pl.ds(row + begin, block)
            values = [canvas[place + k, window, :] for k in range(3)]
            canvas[place, window, :] = values[0] + jnp.where(past, first, 0.0)
            canvas[place + 1, window, :] = values[1] + jnp.where(past, second, first)
            canvas[place + 2, window, :] = values[2] + jnp.where(past, 0.0, second)

    def step(index, carry):
        previous = jnp.maximum(index - 1, 0)
        following = jnp.minimum(index + 1, found - 1)
        buffer = (index + 1) & 1
        starts = list(blocks)
        for m in range(modes):
            for part in range(2):
                forward_right(m, part)
                deposit(previous, buffer, starts[2 * m + part])
        forward_left(0)
        forward_left(1)
        for begin in starts[:2]:
            reweigh(index, begin)
        backward_right(0)
        for begin in starts[2:]:
            reweigh(index, begin)
        cut(following, starts[0])
        backward_right(1)
        cut(following, starts[1])
        backward_left(0, 0)
        cut(following, starts[2])
        backward_left(0, 1)
        cut(following, starts[3])
        backward_left(1, 0)
        backward_left(1, 1)
        return carry

    for copy in obj_copies:
        copy.wait()

    @pl.when(found > 0)
    def _():
        for begin in blocks:
            cut(0, begin)

    for copy in later:
        copy.wait()

    @pl.when(found > 0)
    def _():
        lax.fori_loop(0, found, step, 0)
        for begin in blocks:
            deposit(found - 1, (found - 1) & 1, begin)

    for copy in out_copies:
        copy.start()
    if with_border:
        for pair in range(2):
            beside = pl.ds(row_sides[pair], half)
            for comp in range(2):
                g_cols[pair][comp] = canvas[comp * chunks + col_sides[pair]].astype(BF16)
                for j in range(inner):
                    g_rows[pair][comp * inner + j] = canvas[
                        comp * chunks + 1 + j, beside, :
                    ].astype(BF16)
        core = lax.axis_index("core")
        count_of = kept.shape[0]
        kept[...] = sums[pl.ds(core * count_of, count_of)]
        given[...] = sums[pl.ds((1 - core) * count_of, count_of)]
    else:
        sums_copy = pltpu.make_async_copy(sums, sums_out, misc_sems.at[1])
        sums_copy.start()
        sums_copy.wait()
    for copy in out_copies:
        copy.wait()


def run_positions(counts, centers, object_field, patterns, probe_modes, border=None):
    size = probe_modes.shape[-1]
    half = size // 2
    modes = probe_modes.shape[0]
    tile = object_field.shape[1]
    chunks = tile // LANES + 2
    slots = patterns.shape[0]
    positive, negative = dft_tables(size)
    by_quarter = np.arange(2 * size).reshape(2, 2, half).swapaxes(0, 1).reshape(-1)
    tables = [positive, negative, negative[by_quarter]]
    smem = pl.BlockSpec(memory_space=pltpu.SMEM)
    vmem = pl.BlockSpec(memory_space=pltpu.VMEM)
    anywhere = pl.BlockSpec(memory_space=pl.ANY)
    shape = jax.ShapeDtypeStruct
    in_hbm = pl.BlockSpec(memory_space=pltpu.HBM)
    in_specs = [smem, smem, in_hbm, in_hbm, vmem] + [in_hbm] * 3
    operands = [counts, centers, object_field, patterns, probe_modes, *tables]
    sums_shape = (size // 8, 2 * modes + 1, 8, size)
    if border is None:
        out_specs = [anywhere, anywhere]
        out_shape = [shape(object_field.shape, F32), shape(sums_shape, F32)]
    else:
        in_specs += [vmem] * 6 + [anywhere, anywhere]
        operands += list(border)
        half_sums = (size // 16,) + sums_shape[1:]
        out_specs = [anywhere] + [vmem] * 6
        out_shape = [
            shape(object_field.shape, F32),
            shape((2 * chunks - 4, half, LANES), BF16),
            shape((2 * chunks - 4, half, LANES), BF16),
            shape((2, tile + size, LANES), BF16),
            shape((2, tile + size, LANES), BF16),
            shape(half_sums, F32),
            shape(half_sums, F32),
        ]
    copy_sems = pltpu.SemaphoreType.DMA((2, tile // LANES))
    return pl.pallas_call(
        functools.partial(positions_kernel, border is not None),
        in_specs=in_specs,
        out_specs=out_specs,
        out_shape=out_shape,
        scratch_shapes=[
            pltpu.VMEM((2 * chunks, tile + size, LANES), F32),
            pltpu.VMEM((2 * chunks, tile + size, LANES), F32),
            pltpu.VMEM(patterns.shape, BF16),
            pltpu.VMEM((2 * size, 2 * size), BF16),
            pltpu.VMEM((2 * size, 2 * size), BF16),
            pltpu.VMEM((2 * size, 2 * size), BF16),
            pltpu.VMEM((2 * modes, size, size), F32),
            pltpu.VMEM((modes * size, 2 * size), BF16),
            pltpu.VMEM((modes * size, 2 * size), BF16),
            pltpu.VMEM((2 * size, modes * size), BF16),
            pltpu.VMEM((2 * size, modes * size), BF16),
            pltpu.VMEM((2 * size, modes * size), F32),
            pltpu.VMEM((2 * size, modes * size), F32),
            pltpu.VMEM((2, 2, size, size), F32),
            pltpu.VMEM(sums_shape, F32),
            pltpu.SMEM((slots + 1,), jnp.int32),
            copy_sems,
            copy_sems,
            copy_sems,
            pltpu.SemaphoreType.DMA((5,)),
        ],
        compiler_params=pltpu.CompilerParams(vmem_limit_bytes=(50 if border is None else 40) * 1024 * 1024),
        cost_estimate=pl.CostEstimate(
            flops=slots * 16 * modes * size**3,
            bytes_accessed=24 * 1024 * 1024,
            transcendentals=0,
        ),
        name="border" if border is not None else "interior",
    )(*operands)


def corners_kernel(row_even, row_odd, col_even, col_odd, out_even, out_odd):
    half = row_even.shape[1]
    inner = row_even.shape[0] // 2
    row_sides = sides(ROW, col_even.shape[1], half)
    col_sides = [offset // LANES for offset in sides(COL, inner * LANES, half)]
    for pair, (ring, out) in enumerate(((row_even, out_even), (row_odd, out_odd))):
        out[...] = ring[...]
        for comp in range(2):
            for other, strip in enumerate((col_even, col_odd)):
                place = comp * inner + col_sides[other]
                extra = strip[comp, pl.ds(row_sides[pair], half), :].astype(F32)
                out[place] = (ring[place].astype(F32) + extra).astype(BF16)


def add_corners(g_rows, from_cols):
    vmem = pl.BlockSpec(memory_space=pltpu.VMEM)
    shape = jax.ShapeDtypeStruct(g_rows[0].shape, BF16)
    return pl.pallas_call(
        corners_kernel,
        in_specs=[vmem] * 4,
        out_specs=[vmem] * 2,
        out_shape=[shape, shape],
        compiler_params=pltpu.CompilerParams(vmem_limit_bytes=8 * 1024 * 1024),
        cost_estimate=pl.CostEstimate(
            flops=256 * 1024, bytes_accessed=2 * 1024 * 1024, transcendentals=0
        ),
        name="corners",
    )(*g_rows, *from_cols)


def rims_kernel(
    partial, row_even, row_odd, col_even, col_odd, out, row_buffer, col_buffer, sems
):
    tile = partial.shape[1]
    half = row_even.shape[1]
    inner = tile // LANES
    middle = tile - 2 * half
    row_sides = sides(ROW, tile, half)
    col_sides = sides(COL, tile, half)
    row_rings = (row_even, row_odd)
    col_strips = (col_even, col_odd)

    def copy(kind, pair, comp, inward):
        if kind == 0:
            here = row_buffer.at[pair, comp]
            place = (comp, pl.ds(row_sides[pair], half), slice(None))
        else:
            here = col_buffer.at[pair, comp]
            place = (comp, pl.ds(half, middle), pl.ds(col_sides[pair], half))
        source, target = (partial.at[place], here) if inward else (here, out.at[place])
        return pltpu.make_async_copy(
            source, target, sems.at[1 - int(inward), 2 * kind + pair, comp]
        )

    everything = [(kind, pair, comp) for kind in range(2) for pair in range(2) for comp in range(2)]
    for piece in everything:
        copy(*piece, True).start()
    for kind, pair, comp in everything:
        copy(kind, pair, comp, True).wait()
        if kind == 0:
            for j in range(inner):
                columns = slice(j * LANES, (j + 1) * LANES)
                ring = row_rings[pair][comp * inner + j]
                row_buffer[pair, comp, :, columns] += ring.astype(F32)
            for other in range(2):
                columns = pl.ds(col_sides[other], half)
                strip = col_strips[other][comp, pl.ds(half + row_sides[pair], half), :]
                row_buffer[pair, comp, :, columns] += strip.astype(F32)
        else:
            strip = col_strips[pair][comp, 2 * half : 2 * half + middle, :]
            col_buffer[pair, comp] += strip.astype(F32)
        copy(kind, pair, comp, False).start()
    for piece in everything:
        copy(*piece, False).wait()


def add_rims(partial, from_rows, from_cols):
    tile = partial.shape[1]
    half = from_rows[0].shape[1]
    vmem = pl.BlockSpec(memory_space=pltpu.VMEM)
    anywhere = pl.BlockSpec(memory_space=pl.ANY)
    return pl.pallas_call(
        rims_kernel,
        in_specs=[anywhere] + [vmem] * 4,
        out_specs=anywhere,
        out_shape=jax.ShapeDtypeStruct(partial.shape, F32),
        input_output_aliases={0: 0},
        scratch_shapes=[
            pltpu.VMEM((2, 2, half, tile), F32),
            pltpu.VMEM((2, 2, tile - 2 * half, half), F32),
            pltpu.SemaphoreType.DMA((2, 4, 2)),
        ],
        compiler_params=pltpu.CompilerParams(vmem_limit_bytes=16 * 1024 * 1024),
        cost_estimate=pl.CostEstimate(
            flops=1024 * 1024, bytes_accessed=6 * 1024 * 1024, transcendentals=0
        ),
        name="rims",
    )(partial, *from_rows, *from_cols)


def chip_sums_kernel(kept, received, out):
    out[...] = (kept[...] + received[...]).astype(BF16)


def chip_sums(kept, given):
    vmem = pl.BlockSpec(memory_space=pltpu.VMEM)
    return pl.pallas_call(
        chip_sums_kernel,
        in_specs=[vmem, vmem],
        out_specs=vmem,
        out_shape=jax.ShapeDtypeStruct(kept.shape, BF16),
        compiler_params=pltpu.CompilerParams(vmem_limit_bytes=8 * 1024 * 1024),
        cost_estimate=pl.CostEstimate(
            flops=32 * 1024**3, bytes_accessed=32 * 1024 * 1024, transcendentals=0
        ),
        name="chip_sums",
    )(kept, lax.ppermute(given, "core", [(0, 1), (1, 0)]))


def first_sums(on_chip):
    axes = ("x", "col")
    devices = lax.axis_size("x") * lax.axis_size("col")
    groups, planes, _, size = on_chip.shape
    share = groups * 8 // devices
    if share < 8:
        on_chip = on_chip.reshape(groups, planes, 8 // share, share, size)
        on_chip = jnp.swapaxes(on_chip, 1, 2).reshape(devices, planes, share, size)
    else:
        on_chip = on_chip.reshape(devices, groups // devices, planes, 8, size)
    return lax.all_to_all(on_chip, axes, 0, 0, tiled=True)


def shared_update(received, beside, modes, size):
    axes = ("x", "col")
    devices = lax.axis_size("x") * lax.axis_size("col")
    core = lax.axis_index("core")
    planes = 2 * modes + 1
    share = size // 2 // devices
    total = jnp.sum(received.astype(F32), 0)
    if share >= 8:
        total = jnp.swapaxes(total, 0, 1).reshape(planes, share, size)
    update = (total[: 2 * modes] / jnp.sqrt(total[2 * modes])).astype(BF16)
    copies = jnp.broadcast_to(update, (devices,) + update.shape)
    mine = lax.all_to_all(copies, axes, 0, 0, tiled=True)
    mine, beside = lax.optimization_barrier((mine, beside))
    other = lax.ppermute(mine, "core", [(0, 1), (1, 0)])
    low = jnp.where(core == 0, mine, other)
    high = jnp.where(core == 0, other, mine)
    whole = jnp.concatenate([low, high], 0)
    return jnp.swapaxes(whole, 0, 1).reshape(modes, 2, size, size).astype(F32), beside


def on_device(object_field, probe_modes, counts, centers, patterns):
    size = probe_modes.shape[-1]
    modes = probe_modes.shape[0]
    half = size // 2
    tile = object_field.shape[1]

    col_even, col_odd, row_even, row_odd = cut_strips(object_field, half)
    col_halos = (swap_pairs(col_even, COL, 0), swap_pairs(col_odd, COL, 1))
    row_halos = (swap_pairs(row_even, ROW, 0), swap_pairs(row_odd, ROW, 1))
    is_even = (lax.axis_index("col") & 1) == 0
    first_ends = jnp.concatenate([halo[:, :, :half] for halo in row_halos], 1)
    last_ends = jnp.concatenate([halo[:, :, tile - half :] for halo in row_halos], 1)
    end_halos = (
        swap_pairs(jnp.where(is_even, last_ends, first_ends), COL, 0),
        swap_pairs(jnp.where(is_even, first_ends, last_ends), COL, 1),
    )

    inputs = (counts, centers[0, 0], object_field, patterns[0, 0], probe_modes)
    started, sums = run_positions(*inputs)
    border = (*col_halos, *row_halos, *end_halos, sums, started)
    partial, g_row_even, g_row_odd, g_col_even, g_col_odd, kept, given = run_positions(
        *inputs, border
    )

    from_cols = (swap_pairs(g_col_even, COL, 0), swap_pairs(g_col_odd, COL, 1))
    received = first_sums(chip_sums(kept, given))
    from_cols, _ = lax.optimization_barrier((from_cols, received))
    to_even, to_odd = add_corners((g_row_even, g_row_odd), from_cols)
    from_rows = (swap_pairs(to_even, ROW, 0), swap_pairs(to_odd, ROW, 1))
    new_object = add_rims(partial, from_rows, from_cols)
    update, new_object = shared_update(received, new_object, modes, size)
    new_probe = probe_modes + update
    return (new_object, new_probe)


def solution(mesh):
    rows, columns = mesh.devices.shape
    split = jax.sharding.Mesh(
        mesh.devices.reshape(rows // 2, 2, columns), ("x", "core", "col")
    )
    placed = (
        P(None, ROW, "col"),
        P(),
        P(),
        P(ROW, "col", None, None),
        P(ROW, "col", None, None, None),
    )
    return jax.shard_map(
        on_device,
        mesh=split,
        in_specs=placed,
        out_specs=(P(None, ROW, "col"), P()),
        check_vma=False,
    )
```

```python
import functools
import math

import jax
import jax.numpy as jnp
import ml_dtypes
import numpy as np
from jax import lax
from jax.experimental import pallas as pl
from jax.experimental.pallas import tpu as pltpu
from jax.sharding import PartitionSpec as P

LANES = 128
ROW = ("x", "core")
COL = ("col",)
F32 = jnp.float32
BF16 = jnp.bfloat16


def dft_tables(length):
    indices = np.arange(length)
    angles = (indices[:, None] * indices[None, :] % length) * (2.0 * np.pi / length)
    scale = 1.0 / np.sqrt(length)
    cosine = (np.cos(angles) * scale).astype(np.float32).astype(ml_dtypes.bfloat16)
    sine = (np.sin(angles) * scale).astype(np.float32).astype(ml_dtypes.bfloat16)
    positive = np.block([[cosine, -sine], [sine, cosine]])
    negative = np.block([[cosine, sine], [-sine, cosine]])
    return positive, negative


def swap_pairs(array, axis, odd):
    devices = math.prod(lax.axis_size(name) for name in axis)
    firsts = range(odd, devices - 1, 2)
    return lax.ppermute(
        array, axis, [(i, i + 1) for i in firsts] + [(i + 1, i) for i in firsts]
    )


def sides(axis, length, width):
    even = (lax.axis_index(axis) & 1) == 0
    far = length - width
    return [
        pl.multiple_of(jnp.where(even, far, 0), width),
        pl.multiple_of(jnp.where(even, 0, far), width),
    ]


def strips_kernel(obj_hbm, col_even, col_odd, row_even, row_odd, col_buffer, row_buffer, sems):
    tile = obj_hbm.shape[1]
    half = row_even.shape[1]
    copies = []
    for pair in range(2):
        column = sides(COL, tile, half)[pair]
        row = sides(ROW, tile, half)[pair]
        copies.append(
            pltpu.make_async_copy(
                obj_hbm.at[:, :, pl.ds(column, half)], col_buffer.at[pair], sems.at[0, pair]
            )
        )
        copies.append(
            pltpu.make_async_copy(
                obj_hbm.at[:, pl.ds(row, half), :], row_buffer.at[pair], sems.at[1, pair]
            )
        )
    for copy in copies:
        copy.start()
    outputs = (col_even, row_even, col_odd, row_odd)
    buffers = (col_buffer, row_buffer) * 2
    for index, copy in enumerate(copies):
        copy.wait()
        outputs[index][...] = buffers[index][index // 2].astype(BF16)


def cut_strips(object_field, half):
    tile = object_field.shape[1]
    vmem = pl.BlockSpec(memory_space=pltpu.VMEM)
    columns = jax.ShapeDtypeStruct((2, tile, half), BF16)
    rows = jax.ShapeDtypeStruct((2, half, tile), BF16)
    return pl.pallas_call(
        strips_kernel,
        in_specs=[pl.BlockSpec(memory_space=pltpu.HBM)],
        out_specs=[vmem] * 4,
        out_shape=[columns, columns, rows, rows],
        scratch_shapes=[
            pltpu.VMEM((2, 2, tile, half), F32),
            pltpu.VMEM((2, 2, half, tile), F32),
            pltpu.SemaphoreType.DMA((2, 2)),
        ],
        compiler_params=pltpu.CompilerParams(vmem_limit_bytes=60 * 1024 * 1024),
        cost_estimate=pl.CostEstimate(
            flops=1024 * 1024, bytes_accessed=5 * 1024 * 1024, transcendentals=0
        ),
        name="strips",
    )(object_field)


def positions_kernel(with_border, *refs):
    counts, centers, obj_hbm, pat_hbm, probe = refs[:5]
    tables_hbm, row_halos = refs[5:8], refs[8:10]
    refs = refs[10:]
    if with_border:
        col_halos, end_halos = refs[0:2], refs[2:4]
        start_hbm, ring_hbm, sums_hbm = refs[4:7]
        out_hbm, g_rows, g_cols, kept, given = refs[7], refs[8:10], refs[10:12], *refs[12:14]
        refs = refs[14:]
    else:
        out_hbm, ring_out, sums_out = refs[:3]
        refs = refs[3:]
    (obj, canvas, patterns, positive, negative, left_negative, low, waves, shifts, halves, backs,
     spectra, changes, patch, sums, order, piece_sems, out_sems, ring_sems, pat_sems,
     misc_sems) = refs
    size = probe.shape[-1]
    half = size // 2
    tile = obj_hbm.shape[1]
    inner = tile // LANES
    chunks = inner + 2
    modes = probe.shape[0]
    rows = slice(half, half + tile)
    near = [0, 1, inner - 2, inner - 1] if with_border else list(range(inner))
    pieces = [(comp, j) for comp in range(2) for j in near]
    everywhere = [(comp, j) for comp in range(2) for j in range(inner)]

    def home(array, comp, j):
        return array.at[comp, :, pl.ds(j * LANES, LANES)]

    def held(array, comp, j):
        return array.at[comp * chunks + 1 + j, pl.ds(half, tile), :]

    def ring_pieces(array):
        for comp, j in everywhere:
            for side, row in enumerate((0, half + tile)):
                yield (
                    array.at[comp * inner + j, pl.ds(side * half, half), :],
                    canvas.at[comp * chunks + 1 + j, pl.ds(row, half), :],
                    ring_sems.at[side, comp, j],
                )

    obj_copies = [
        pltpu.make_async_copy(home(obj_hbm, *p), held(obj, *p), piece_sems.at[0, *p])
        for p in pieces
    ]
    out_copies = [
        pltpu.make_async_copy(held(canvas, *p), home(out_hbm, *p), out_sems.at[p]) for p in pieces
    ]
    tables = (positive, negative, left_negative)
    later = [
        pltpu.make_async_copy(tables_hbm[i], tables[i], misc_sems.at[i]) for i in range(3)
    ]
    if with_border:
        later += [
            pltpu.make_async_copy(home(start_hbm, *p), held(canvas, *p), piece_sems.at[1, *p])
            for p in pieces
        ]
        later += [pltpu.make_async_copy(*piece) for piece in ring_pieces(ring_hbm)]
        later.append(pltpu.make_async_copy(sums_hbm, sums, misc_sems.at[3]))
    for copy in obj_copies + later:
        copy.start()

    order[0] = 0
    count = counts[lax.axis_index(ROW), lax.axis_index("col")]

    def pattern_copy(slot):
        return pltpu.make_async_copy(pat_hbm.at[slot], patterns.at[slot], pat_sems.at[slot])

    def note(slot, found):
        column = centers[1, slot]
        inside = (column >= half) & (column <= tile - half)
        order[found] = slot
        return found + jnp.where(inside, 0 if with_border else 1, 1 if with_border else 0)

    def fetch(index, carry):
        pattern_copy(order[index]).start()
        return carry

    found = lax.fori_loop(0, count, note, 0)
    lax.fori_loop(0, found, fetch, 0)

    if not with_border:
        sums[...] = jnp.zeros_like(sums)
    intensity = jnp.zeros((size, size), F32)
    for m in range(modes):
        for comp in range(2):
            values = probe[m, comp]
            intensity = intensity + values * values
            low[2 * m + comp] = values.astype(BF16).astype(F32)
    scale = 1.0 / (jnp.max(intensity) + 1e-06)
    changes[...] = jnp.zeros_like(changes)
    patch[...] = jnp.zeros_like(patch)

    row_sides = sides(ROW, tile + size, half)
    col_sides = [offset // LANES for offset in sides(COL, tile + size, half)]
    blank = jnp.zeros((tile + size, LANES), F32)
    for comp in range(2):
        first = comp * chunks
        for pair in range(2):
            for j in near:
                columns = slice(j * LANES, (j + 1) * LANES)
                obj[first + 1 + j, pl.ds(row_sides[pair], half), :] = row_halos[pair][
                    comp, :, columns
                ].astype(F32)
            if with_border:
                beside = first + col_sides[pair]
                canvas[beside] = blank
                obj[beside, rows, :] = col_halos[pair][comp].astype(F32)
                for other in range(2):
                    obj[beside, pl.ds(row_sides[other], half), :] = end_halos[pair][
                        comp, other * half : (other + 1) * half, :
                    ].astype(F32)
        if not with_border:
            for j in range(inner):
                canvas[first + 1 + j, 0:half, :] = blank[0:half]
                canvas[first + 1 + j, half + tile :, :] = blank[0:half]

    block = 64
    groups = block // 8
    lane = lax.broadcasted_iota(jnp.int32, (block, LANES), 1)
    blocks = range(0, size, block)

    def place_of(index):
        slot = order[index]
        column = centers[1, slot]
        return slot, centers[0, slot], column >> 7, column & 127

    def cut(index, begin):
        _, row, chunk, offset = place_of(index)
        back_offset = (LANES - offset) & 127
        from_first = lane < LANES - offset
        here = slice(begin, begin + block)
        parts = []
        for comp in range(2):
            moved = [
                pltpu.roll(
                    obj[comp * chunks + chunk + k, pl.ds(row + begin, block), :], back_offset, 1
                )
                for k in range(3)
            ]
            window = jnp.concatenate(
                [
                    jnp.where(from_first, moved[0], moved[1]),
                    jnp.where(from_first, moved[1], moved[2]),
                ],
                1,
            ).astype(BF16).astype(F32)
            patch[index & 1, comp, here, :] = window
            parts.append(window)
        real, imag = parts
        for m in range(modes):
            probe_real = low[2 * m, here, :]
            probe_imag = low[2 * m + 1, here, :]
            there = slice(m * size + begin, m * size + begin + block)
            waves[there, 0:size] = (probe_real * real - probe_imag * imag).astype(BF16)
            waves[there, size:] = (probe_real * imag + probe_imag * real).astype(BF16)

    def forward_right(m, part):
        mode = slice(m * size, (m + 1) * size)
        columns = slice(part * size, (part + 1) * size)
        halves[columns, mode] = jnp.dot(
            waves[mode, :], positive[:, columns], preferred_element_type=F32
        ).astype(BF16)

    def forward_left(k):
        rows_here = slice(k * size, (k + 1) * size)
        spectra[rows_here, :] = jnp.dot(
            left_negative[rows_here, :], halves[...], preferred_element_type=F32
        )

    def reweigh(index, begin):
        slot = order[index]
        k, inside = divmod(begin, half)
        real_rows = slice(k * size + inside, k * size + inside + block)
        imag_rows = slice(k * size + half + inside, k * size + half + inside + block)
        amplitude = patterns[slot, begin : begin + block, :].astype(F32)
        mode_columns = [slice(m * size, (m + 1) * size) for m in range(modes)]
        parts = [(spectra[real_rows, mode], spectra[imag_rows, mode]) for mode in mode_columns]
        power = sum(real * real + imag * imag for real, imag in parts)
        factor = amplitude * lax.rsqrt(jnp.maximum(power, 0.5)) - 1.0
        for m, (real, imag) in enumerate(parts):
            first = k * size + m * half + inside
            there = slice(first, first + block)
            shifts[there, 0:size] = (factor * real).astype(BF16)
            shifts[there, size:] = (factor * imag).astype(BF16)

    def backward_right(k):
        product = jnp.dot(
            shifts[k * size : (k + 1) * size, :], negative[...],
            preferred_element_type=F32,
        ).astype(BF16)
        for m in range(modes):
            mode = slice(m * size, (m + 1) * size)
            for part in range(2):
                first = part * size + k * half
                backs[first : first + half, mode] = product[
                    m * half : (m + 1) * half, part * size : (part + 1) * size
                ]

    def backward_left(m, part):
        mode = slice(m * size, (m + 1) * size)
        rows_here = slice(part * size, (part + 1) * size)
        changes[rows_here, mode] = jnp.dot(
            positive[rows_here, :], backs[:, mode], preferred_element_type=F32
        )

    def deposit(index, buffer, begin):
        _, row, chunk, offset = place_of(index)
        past = lane >= offset
        here = slice(begin, begin + block)
        below = slice(size + begin, size + begin + block)
        start = begin // 8
        obj_real = patch[buffer, 0, here, :]
        obj_imag = patch[buffer, 1, here, :]

        def add(plane, value):
            sums[start : start + groups, plane] += value.reshape(groups, 8, size)

        add(2 * modes, obj_real * obj_real + obj_imag * obj_imag)
        term_real = term_imag = None
        for m in range(modes):
            mode = slice(m * size, (m + 1) * size)
            real = changes[here, mode]
            imag = changes[below, mode]
            probe_real = low[2 * m, here, :]
            probe_imag = low[2 * m + 1, here, :]
            more_real = probe_real * real + probe_imag * imag
            more_imag = probe_real * imag - probe_imag * real
            term_real = more_real if m == 0 else term_real + more_real
            term_imag = more_imag if m == 0 else term_imag + more_imag
            add(2 * m, obj_real * real + obj_imag * imag)
            add(2 * m + 1, obj_real * imag - obj_imag * real)
        for comp, term in enumerate((term_real, term_imag)):
            term = term.astype(BF16).astype(F32) * scale
            first = pltpu.roll(term[:, 0:LANES], offset, 1)
            second = pltpu.roll(term[:, LANES:], offset, 1)
            place = comp * chunks + chunk
            window = pl.ds(row + begin, block)
            values = [canvas[place + k, window, :] for k in range(3)]
            canvas[place, window, :] = values[0] + jnp.where(past, first, 0.0)
            canvas[place + 1, window, :] = values[1] + jnp.where(past, second, first)
            canvas[place + 2, window, :] = values[2] + jnp.where(past, 0.0, second)

    def step(index, carry):
        pattern_copy(order[index]).wait()
        previous = jnp.maximum(index - 1, 0)
        following = jnp.minimum(index + 1, found - 1)
        buffer = (index + 1) & 1
        starts = list(blocks)
        for m in range(modes):
            for part in range(2):
                forward_right(m, part)
                deposit(previous, buffer, starts[2 * m + part])
        forward_left(0)
        forward_left(1)
        for begin in starts[:2]:
            reweigh(index, begin)
        backward_right(0)
        for begin in starts[2:]:
            reweigh(index, begin)
        cut(following, starts[0])
        backward_right(1)
        cut(following, starts[1])
        backward_left(0, 0)
        cut(following, starts[2])
        backward_left(0, 1)
        cut(following, starts[3])
        backward_left(1, 0)
        backward_left(1, 1)
        return carry

    for copy in obj_copies:
        copy.wait()

    @pl.when(found > 0)
    def _():
        for begin in blocks:
            cut(0, begin)

    if not with_border:
        for comp, j in pieces:
            index = comp * chunks + 1 + j
            canvas[index, rows, :] = obj[index, rows, :]
    for copy in later:
        copy.wait()

    @pl.when(found > 0)
    def _():
        lax.fori_loop(0, found, step, 0)
        for begin in blocks:
            deposit(found - 1, (found - 1) & 1, begin)

    last_copies = list(out_copies)
    if not with_border:
        last_copies += [
            pltpu.make_async_copy(here, there, sem) for there, here, sem in ring_pieces(ring_out)
        ]
        last_copies.append(pltpu.make_async_copy(sums, sums_out, misc_sems.at[3]))
    for copy in last_copies:
        copy.start()
    if with_border:
        for pair in range(2):
            beside = pl.ds(row_sides[pair], half)
            for comp in range(2):
                g_cols[pair][comp] = canvas[comp * chunks + col_sides[pair]].astype(BF16)
                for j in range(inner):
                    g_rows[pair][comp * inner + j] = canvas[
                        comp * chunks + 1 + j, beside, :
                    ].astype(BF16)
        core = lax.axis_index("core")
        count_of = kept.shape[0]
        kept[...] = sums[pl.ds(core * count_of, count_of)]
        given[...] = sums[pl.ds((1 - core) * count_of, count_of)]
    for copy in last_copies:
        copy.wait()


def run_positions(
    counts, centers, object_field, patterns, probe_modes, row_halos, border=None
):
    size = probe_modes.shape[-1]
    half = size // 2
    modes = probe_modes.shape[0]
    tile = object_field.shape[1]
    inner = tile // LANES
    chunks = inner + 2
    slots = patterns.shape[0]
    positive, negative = dft_tables(size)
    by_quarter = np.arange(2 * size).reshape(2, 2, half).swapaxes(0, 1).reshape(-1)
    tables = [positive, negative, negative[by_quarter]]
    smem = pl.BlockSpec(memory_space=pltpu.SMEM)
    vmem = pl.BlockSpec(memory_space=pltpu.VMEM)
    anywhere = pl.BlockSpec(memory_space=pl.ANY)
    shape = jax.ShapeDtypeStruct
    in_specs = [smem, smem, anywhere, anywhere, vmem] + [anywhere] * 3 + [vmem] * 2
    operands = [counts, centers, object_field, patterns, probe_modes, *tables, *row_halos]
    sums_shape = (size // 8, 2 * modes + 1, 8, size)
    ring_shape = (2 * inner, size, LANES)
    aliases = {}
    if border is None:
        out_specs = [anywhere] * 3
        out_shape = [shape(each, F32) for each in (object_field.shape, ring_shape, sums_shape)]
    else:
        aliases = {len(operands) + 4: 0}
        in_specs += [vmem] * 4 + [anywhere] * 3
        operands += list(border)
        half_sums = (size // 16,) + sums_shape[1:]
        out_specs = [anywhere] + [vmem] * 6
        out_shape = [
            shape(object_field.shape, F32),
            shape((2 * inner, half, LANES), BF16),
            shape((2 * inner, half, LANES), BF16),
            shape((2, tile + size, LANES), BF16),
            shape((2, tile + size, LANES), BF16),
            shape(half_sums, F32),
            shape(half_sums, F32),
        ]
    table = pltpu.VMEM((2 * size, 2 * size), BF16)
    products = pltpu.VMEM((2 * size, modes * size), BF16)
    wide = pltpu.VMEM((2 * size, modes * size), F32)
    padded = pltpu.VMEM((2 * chunks, tile + size, LANES), F32)
    dma = pltpu.SemaphoreType.DMA
    return pl.pallas_call(
        functools.partial(positions_kernel, border is not None),
        in_specs=in_specs,
        out_specs=out_specs,
        out_shape=out_shape,
        input_output_aliases=aliases,
        scratch_shapes=[
            padded,
            padded,
            pltpu.VMEM(patterns.shape, BF16),
            table,
            table,
            table,
            pltpu.VMEM((2 * modes, size, size), F32),
            products,
            products,
            products,
            products,
            wide,
            wide,
            pltpu.VMEM((2, 2, size, size), F32),
            pltpu.VMEM(sums_shape, F32),
            pltpu.SMEM((slots + 1,), jnp.int32),
            dma((2, 2, inner)),
            dma((2, inner)),
            dma((2, 2, inner)),
            dma((slots,)),
            dma((4,)),
        ],
        compiler_params=pltpu.CompilerParams(
            vmem_limit_bytes=(50 if border is None else 46) * 1024 * 1024
        ),
        cost_estimate=pl.CostEstimate(
            flops=slots * 16 * modes * size**3,
            bytes_accessed=24 * 1024 * 1024,
            transcendentals=0,
        ),
        name="border" if border is not None else "interior",
    )(*operands)


def corners_kernel(row_even, row_odd, col_even, col_odd, out_even, out_odd):
    half = row_even.shape[1]
    inner = row_even.shape[0] // 2
    row_sides = sides(ROW, col_even.shape[1], half)
    col_sides = [offset // LANES for offset in sides(COL, inner * LANES, half)]
    for pair, (ring, out) in enumerate(((row_even, out_even), (row_odd, out_odd))):
        out[...] = ring[...]
        for comp in range(2):
            for other, strip in enumerate((col_even, col_odd)):
                place = comp * inner + col_sides[other]
                extra = strip[comp, pl.ds(row_sides[pair], half), :].astype(F32)
                out[place] = (ring[place].astype(F32) + extra).astype(BF16)


def add_corners(g_rows, from_cols):
    vmem = pl.BlockSpec(memory_space=pltpu.VMEM)
    shape = jax.ShapeDtypeStruct(g_rows[0].shape, BF16)
    return pl.pallas_call(
        corners_kernel,
        in_specs=[vmem] * 4,
        out_specs=[vmem] * 2,
        out_shape=[shape, shape],
        compiler_params=pltpu.CompilerParams(vmem_limit_bytes=8 * 1024 * 1024),
        cost_estimate=pl.CostEstimate(
            flops=256 * 1024, bytes_accessed=2 * 1024 * 1024, transcendentals=0
        ),
        name="corners",
    )(*g_rows, *from_cols)


def rims_kernel(
    partial, row_even, row_odd, col_even, col_odd, out, row_buffer, col_buffer, sems
):
    tile = partial.shape[1]
    half = row_even.shape[1]
    inner = tile // LANES
    middle = tile - 2 * half
    row_sides = sides(ROW, tile, half)
    col_sides = sides(COL, tile, half)
    row_rings = (row_even, row_odd)
    col_strips = (col_even, col_odd)

    def copy(kind, pair, comp, inward):
        if kind == 0:
            here = row_buffer.at[pair, comp]
            place = (comp, pl.ds(row_sides[pair], half), slice(None))
        else:
            here = col_buffer.at[pair, comp]
            place = (comp, pl.ds(half, middle), pl.ds(col_sides[pair], half))
        source, target = (partial.at[place], here) if inward else (here, out.at[place])
        return pltpu.make_async_copy(
            source, target, sems.at[1 - int(inward), 2 * kind + pair, comp]
        )

    everything = [(kind, pair, comp) for kind in range(2) for pair in range(2) for comp in range(2)]
    for piece in everything:
        copy(*piece, True).start()
    for kind, pair, comp in everything:
        copy(kind, pair, comp, True).wait()
        if kind == 0:
            for j in range(inner):
                columns = slice(j * LANES, (j + 1) * LANES)
                ring = row_rings[pair][comp * inner + j]
                row_buffer[pair, comp, :, columns] += ring.astype(F32)
            for other in range(2):
                columns = pl.ds(col_sides[other], half)
                strip = col_strips[other][comp, pl.ds(half + row_sides[pair], half), :]
                row_buffer[pair, comp, :, columns] += strip.astype(F32)
        else:
            strip = col_strips[pair][comp, 2 * half : 2 * half + middle, :]
            col_buffer[pair, comp] += strip.astype(F32)
        copy(kind, pair, comp, False).start()
    for piece in everything:
        copy(*piece, False).wait()


def add_rims(partial, from_rows, from_cols):
    tile = partial.shape[1]
    half = from_rows[0].shape[1]
    vmem = pl.BlockSpec(memory_space=pltpu.VMEM)
    anywhere = pl.BlockSpec(memory_space=pl.ANY)
    return pl.pallas_call(
        rims_kernel,
        in_specs=[anywhere] + [vmem] * 4,
        out_specs=anywhere,
        out_shape=jax.ShapeDtypeStruct(partial.shape, F32),
        input_output_aliases={0: 0},
        scratch_shapes=[
            pltpu.VMEM((2, 2, half, tile), F32),
            pltpu.VMEM((2, 2, tile - 2 * half, half), F32),
            pltpu.SemaphoreType.DMA((2, 4, 2)),
        ],
        compiler_params=pltpu.CompilerParams(vmem_limit_bytes=16 * 1024 * 1024),
        cost_estimate=pl.CostEstimate(
            flops=1024 * 1024, bytes_accessed=6 * 1024 * 1024, transcendentals=0
        ),
        name="rims",
    )(partial, *from_rows, *from_cols)


def chip_sums_kernel(kept, received, out):
    out[...] = (kept[...] + received[...]).astype(BF16)


def chip_sums(kept, given):
    vmem = pl.BlockSpec(memory_space=pltpu.VMEM)
    return pl.pallas_call(
        chip_sums_kernel,
        in_specs=[vmem, vmem],
        out_specs=vmem,
        out_shape=jax.ShapeDtypeStruct(kept.shape, BF16),
        compiler_params=pltpu.CompilerParams(vmem_limit_bytes=8 * 1024 * 1024),
        cost_estimate=pl.CostEstimate(
            flops=32 * 1024**3, bytes_accessed=32 * 1024 * 1024, transcendentals=0
        ),
        name="chip_sums",
    )(kept, lax.ppermute(given, "core", [(0, 1), (1, 0)]))


def by_device(on_chip):
    devices = lax.axis_size("x") * lax.axis_size("col")
    groups, planes, _, size = on_chip.shape
    share = groups * 8 // devices
    if share < 8:
        on_chip = on_chip.reshape(groups, planes, 8 // share, share, size)
        return jnp.swapaxes(on_chip, 1, 2).reshape(devices, planes, share, size)
    return on_chip.reshape(devices, groups // devices, planes, 8, size)


def first_sums(parts):
    return lax.all_to_all(parts, ("x", "col"), 0, 0, tiled=True)


def shared_update(received, beside, modes, size):
    axes = ("x", "col")
    devices = lax.axis_size("x") * lax.axis_size("col")
    core = lax.axis_index("core")
    planes = 2 * modes + 1
    share = size // 2 // devices
    total = jnp.sum(received.astype(F32), 0)
    if share >= 8:
        total = jnp.swapaxes(total, 0, 1).reshape(planes, share, size)
    update = (total[: 2 * modes] / jnp.sqrt(total[2 * modes])).astype(BF16)
    copies = jnp.broadcast_to(update, (devices,) + update.shape)
    mine = lax.all_to_all(copies, axes, 0, 0, tiled=True)
    mine, beside = lax.optimization_barrier((mine, beside))
    other = lax.ppermute(mine, "core", [(0, 1), (1, 0)])
    low = jnp.where(core == 0, mine, other)
    high = jnp.where(core == 0, other, mine)
    whole = jnp.concatenate([low, high], 0)
    return jnp.swapaxes(whole, 0, 1).reshape(modes, 2, size, size).astype(F32), beside


def on_device(object_field, probe_modes, counts, centers, patterns):
    size = probe_modes.shape[-1]
    modes = probe_modes.shape[0]
    half = size // 2
    tile = object_field.shape[1]

    col_even, col_odd, row_even, row_odd = cut_strips(object_field, half)
    col_halos = (swap_pairs(col_even, COL, 0), swap_pairs(col_odd, COL, 1))
    row_halos = (swap_pairs(row_even, ROW, 0), swap_pairs(row_odd, ROW, 1))
    is_even = (lax.axis_index("col") & 1) == 0
    first_ends = jnp.concatenate([halo[:, :, :half] for halo in row_halos], 1)
    last_ends = jnp.concatenate([halo[:, :, tile - half :] for halo in row_halos], 1)
    end_halos = (
        swap_pairs(jnp.where(is_even, last_ends, first_ends), COL, 0),
        swap_pairs(jnp.where(is_even, first_ends, last_ends), COL, 1),
    )

    inputs = (counts, centers[0, 0], object_field, patterns[0, 0], probe_modes, row_halos)
    started = run_positions(*inputs)
    border = (*col_halos, *end_halos, *started)
    partial, g_row_even, g_row_odd, g_col_even, g_col_odd, kept, given = run_positions(
        *inputs, border
    )

    from_cols = (swap_pairs(g_col_even, COL, 0), swap_pairs(g_col_odd, COL, 1))
    received = lax.cond(
        counts[0, 0] > 0, first_sums, jnp.zeros_like, by_device(chip_sums(kept, given))
    )
    from_cols, _ = lax.optimization_barrier((from_cols, received))
    to_even, to_odd = add_corners((g_row_even, g_row_odd), from_cols)
    from_rows = (swap_pairs(to_even, ROW, 0), swap_pairs(to_odd, ROW, 1))
    new_object = add_rims(partial, from_rows, from_cols)
    update, new_object = shared_update(received, new_object, modes, size)
    new_probe = probe_modes + update
    return (new_object, new_probe)


def solution(mesh):
    rows, columns = mesh.devices.shape
    split = jax.sharding.Mesh(
        mesh.devices.reshape(rows // 2, 2, columns), ("x", "core", "col")
    )
    placed = (
        P(None, ROW, "col"),
        P(),
        P(),
        P(ROW, "col", None, None),
        P(ROW, "col", None, None, None),
    )
    return jax.shard_map(
        on_device,
        mesh=split,
        in_specs=placed,
        out_specs=(P(None, ROW, "col"), P()),
        check_vma=False,
    )
```

```python
import functools
import math

import jax
import jax.numpy as jnp
import ml_dtypes
import numpy as np
from jax import lax
from jax.experimental import pallas as pl
from jax.experimental.pallas import tpu as pltpu
from jax.sharding import PartitionSpec as P

LANES = 128
ROW = ("x", "core")
COL = ("col",)
F32 = jnp.float32
BF16 = jnp.bfloat16


def dft_tables(length):
    indices = np.arange(length)
    angles = (indices[:, None] * indices[None, :] % length) * (2.0 * np.pi / length)
    scale = 1.0 / np.sqrt(length)
    cosine = (np.cos(angles) * scale).astype(np.float32).astype(ml_dtypes.bfloat16)
    sine = (np.sin(angles) * scale).astype(np.float32).astype(ml_dtypes.bfloat16)
    positive = np.block([[cosine, -sine], [sine, cosine]])
    negative = np.block([[cosine, sine], [-sine, cosine]])
    return positive, negative


def swap_pairs(array, axis, odd):
    devices = math.prod(lax.axis_size(name) for name in axis)
    firsts = range(odd, devices - 1, 2)
    return lax.ppermute(
        array, axis, [(i, i + 1) for i in firsts] + [(i + 1, i) for i in firsts]
    )


def sides(axis, length, width):
    even = (lax.axis_index(axis) & 1) == 0
    far = length - width
    return [
        pl.multiple_of(jnp.where(even, far, 0), width),
        pl.multiple_of(jnp.where(even, 0, far), width),
    ]


def spread_kernel(obj_hbm, pieces, col_even, col_odd, row_even, row_odd, sems):
    tile = obj_hbm.shape[1]
    half = row_even.shape[1]
    inner = tile // LANES
    col_sides = [offset // LANES for offset in sides(COL, tile, half)]
    row_sides = sides(ROW, tile, half)
    copies = [
        pltpu.make_async_copy(
            obj_hbm.at[comp, :, pl.ds(j * LANES, LANES)], pieces.at[comp * inner + j],
            sems.at[comp, j],
        )
        for comp in range(2)
        for j in range(inner)
    ]
    for copy in copies:
        copy.start()
    for index, copy in enumerate(copies):
        copy.wait()
        for pair, rows in enumerate((row_even, row_odd)):
            rows[index] = pieces[index, pl.ds(row_sides[pair], half), :].astype(BF16)
    for pair, columns in enumerate((col_even, col_odd)):
        for comp in range(2):
            columns[comp] = pieces[comp * inner + col_sides[pair]].astype(BF16)


def spread(object_field, half):
    tile = object_field.shape[1]
    inner = tile // LANES
    vmem = pl.BlockSpec(memory_space=pltpu.VMEM)
    columns = jax.ShapeDtypeStruct((2, tile, half), BF16)
    rows = jax.ShapeDtypeStruct((2 * inner, half, LANES), BF16)
    return pl.pallas_call(
        spread_kernel,
        in_specs=[pl.BlockSpec(memory_space=pl.ANY)],
        out_specs=[vmem] * 5,
        out_shape=[
            jax.ShapeDtypeStruct((2 * inner, tile, LANES), F32), columns, columns, rows, rows
        ],
        scratch_shapes=[pltpu.SemaphoreType.DMA((2, inner))],
        compiler_params=pltpu.CompilerParams(vmem_limit_bytes=46 * 1024 * 1024),
        cost_estimate=pl.CostEstimate(
            flops=1024 * 1024, bytes_accessed=12 * 1024 * 1024, transcendentals=0
        ),
        name="spread",
    )(object_field)


def positions_kernel(with_border, *refs):
    counts, centers, obj_in, pat_hbm, probe = refs[:5]
    tables_hbm, row_halos = refs[5:8], refs[8:10]
    refs = refs[10:]
    if with_border:
        col_halos, end_halos = refs[0:2], refs[2:4]
        start_in, ring_in, sums_in = refs[4:7]
        out_hbm, g_rows, g_cols, kept, given = refs[7], refs[8:10], refs[10:12], *refs[12:14]
        refs = refs[14:]
    else:
        start_out, ring_out, sums_out = refs[:3]
        start_in = obj_in
        refs = refs[3:]
    (obj, canvas, patterns, positive, negative, left_negative, low, waves, shifts, halves, backs,
     spectra, changes, patch, sums, order, piece_sems, out_sems, ring_sems, pat_sems,
     misc_sems) = refs
    size = probe.shape[-1]
    half = size // 2
    tile = obj_in.shape[1]
    inner = tile // LANES
    chunks = inner + 2
    modes = probe.shape[0]
    rows = slice(half, half + tile)
    near = [0, 1, inner - 2, inner - 1] if with_border else list(range(inner))
    pieces = [(comp, j) for comp in range(2) for j in near]
    everywhere = [(comp, j) for comp in range(2) for j in range(inner)]

    def piece(array, comp, j):
        return array.at[comp * inner + j]

    def home(array, comp, j):
        return array.at[comp, :, pl.ds(j * LANES, LANES)]

    def held(array, comp, j):
        return array.at[comp * chunks + 1 + j, pl.ds(half, tile), :]

    def ring_pieces(array):
        for comp, j in everywhere:
            for side, row in enumerate((0, half + tile)):
                yield (
                    array.at[comp * inner + j, pl.ds(side * half, half), :],
                    canvas.at[comp * chunks + 1 + j, pl.ds(row, half), :],
                    ring_sems.at[side, comp, j],
                )

    obj_copies = [
        pltpu.make_async_copy(piece(obj_in, *p), held(obj, *p), piece_sems.at[0, *p])
        for p in pieces
    ]
    tables = (positive, negative, left_negative)
    later = [
        pltpu.make_async_copy(tables_hbm[i], tables[i], misc_sems.at[i]) for i in range(3)
    ]
    later += [
        pltpu.make_async_copy(piece(start_in, *p), held(canvas, *p), piece_sems.at[1, *p])
        for p in pieces
    ]
    if with_border:
        later += [pltpu.make_async_copy(*each) for each in ring_pieces(ring_in)]
        later.append(pltpu.make_async_copy(sums_in, sums, misc_sems.at[3]))
        out_copies = [
            pltpu.make_async_copy(held(canvas, *p), home(out_hbm, *p), out_sems.at[p])
            for p in pieces
        ]
        through_copies = [
            pltpu.make_async_copy(piece(start_in, *p), home(out_hbm, *p), out_sems.at[p])
            for p in everywhere
            if p not in pieces
        ]
    else:
        out_copies = [
            pltpu.make_async_copy(held(canvas, *p), piece(start_out, *p), out_sems.at[p])
            for p in pieces
        ]
        through_copies = []
    for copy in obj_copies + later + through_copies:
        copy.start()

    order[0] = 0
    count = counts[lax.axis_index(ROW), lax.axis_index("col")]

    def pattern_copy(slot):
        return pltpu.make_async_copy(pat_hbm.at[slot], patterns.at[slot], pat_sems.at[slot])

    def note(slot, found):
        column = centers[1, slot]
        inside = (column >= half) & (column <= tile - half)
        order[found] = slot
        return found + jnp.where(inside, 0 if with_border else 1, 1 if with_border else 0)

    def fetch(index, carry):
        pattern_copy(order[index]).start()
        return carry

    found = lax.fori_loop(0, count, note, 0)
    lax.fori_loop(0, found, fetch, 0)

    if not with_border:
        sums[...] = jnp.zeros_like(sums)
    intensity = jnp.zeros((size, size), F32)
    for m in range(modes):
        for comp in range(2):
            values = probe[m, comp]
            intensity = intensity + values * values
            low[2 * m + comp] = values.astype(BF16).astype(F32)
    scale = 1.0 / (jnp.max(intensity) + 1e-06)
    changes[...] = jnp.zeros_like(changes)
    patch[...] = jnp.zeros_like(patch)

    row_sides = sides(ROW, tile + size, half)
    col_sides = [offset // LANES for offset in sides(COL, tile + size, half)]
    blank = jnp.zeros((tile + size, LANES), F32)
    for comp in range(2):
        first = comp * chunks
        for pair in range(2):
            for j in near:
                obj[first + 1 + j, pl.ds(row_sides[pair], half), :] = row_halos[pair][
                    comp * inner + j
                ].astype(F32)
            if with_border:
                beside = first + col_sides[pair]
                canvas[beside] = blank
                obj[beside, rows, :] = col_halos[pair][comp].astype(F32)
                for other in range(2):
                    obj[beside, pl.ds(row_sides[other], half), :] = end_halos[pair][
                        comp, other * half : (other + 1) * half, :
                    ].astype(F32)
        if not with_border:
            for j in range(inner):
                canvas[first + 1 + j, 0:half, :] = blank[0:half]
                canvas[first + 1 + j, half + tile :, :] = blank[0:half]

    block = 64
    groups = block // 8
    lane = lax.broadcasted_iota(jnp.int32, (block, LANES), 1)
    blocks = range(0, size, block)

    def place_of(index):
        slot = order[index]
        column = centers[1, slot]
        return slot, centers[0, slot], column >> 7, column & 127

    def cut(index, begin):
        _, row, chunk, offset = place_of(index)
        back_offset = (LANES - offset) & 127
        from_first = lane < LANES - offset
        here = slice(begin, begin + block)
        parts = []
        for comp in range(2):
            moved = [
                pltpu.roll(
                    obj[comp * chunks + chunk + k, pl.ds(row + begin, block), :], back_offset, 1
                )
                for k in range(3)
            ]
            window = jnp.concatenate(
                [
                    jnp.where(from_first, moved[0], moved[1]),
                    jnp.where(from_first, moved[1], moved[2]),
                ],
                1,
            ).astype(BF16).astype(F32)
            patch[index & 1, comp, here, :] = window
            parts.append(window)
        real, imag = parts
        for m in range(modes):
            probe_real = low[2 * m, here, :]
            probe_imag = low[2 * m + 1, here, :]
            there = slice(m * size + begin, m * size + begin + block)
            waves[there, 0:size] = (probe_real * real - probe_imag * imag).astype(BF16)
            waves[there, size:] = (probe_real * imag + probe_imag * real).astype(BF16)

    def forward_right(m, part):
        mode = slice(m * size, (m + 1) * size)
        columns = slice(part * size, (part + 1) * size)
        halves[columns, mode] = jnp.dot(
            waves[mode, :], positive[:, columns], preferred_element_type=F32
        ).astype(BF16)

    def forward_left(k):
        rows_here = slice(k * size, (k + 1) * size)
        spectra[rows_here, :] = jnp.dot(
            left_negative[rows_here, :], halves[...], preferred_element_type=F32
        )

    def reweigh(index, begin):
        slot = order[index]
        k, inside = divmod(begin, half)
        real_rows = slice(k * size + inside, k * size + inside + block)
        imag_rows = slice(k * size + half + inside, k * size + half + inside + block)
        amplitude = patterns[slot, begin : begin + block, :].astype(F32)
        mode_columns = [slice(m * size, (m + 1) * size) for m in range(modes)]
        parts = [(spectra[real_rows, mode], spectra[imag_rows, mode]) for mode in mode_columns]
        power = sum(real * real + imag * imag for real, imag in parts)
        factor = amplitude * lax.rsqrt(jnp.maximum(power, 0.5)) - 1.0
        for m, (real, imag) in enumerate(parts):
            first = k * size + m * half + inside
            there = slice(first, first + block)
            shifts[there, 0:size] = (factor * real).astype(BF16)
            shifts[there, size:] = (factor * imag).astype(BF16)

    def backward_right(k):
        product = jnp.dot(
            shifts[k * size : (k + 1) * size, :], negative[...],
            preferred_element_type=F32,
        ).astype(BF16)
        for m in range(modes):
            mode = slice(m * size, (m + 1) * size)
            for part in range(2):
                first = part * size + k * half
                backs[first : first + half, mode] = product[
                    m * half : (m + 1) * half, part * size : (part + 1) * size
                ]

    def backward_left(m, part):
        mode = slice(m * size, (m + 1) * size)
        rows_here = slice(part * size, (part + 1) * size)
        changes[rows_here, mode] = jnp.dot(
            positive[rows_here, :], backs[:, mode], preferred_element_type=F32
        )

    def deposit(index, buffer, begin):
        _, row, chunk, offset = place_of(index)
        past = lane >= offset
        here = slice(begin, begin + block)
        below = slice(size + begin, size + begin + block)
        start = begin // 8
        obj_real = patch[buffer, 0, here, :]
        obj_imag = patch[buffer, 1, here, :]

        def add(plane, value):
            sums[start : start + groups, plane] += value.reshape(groups, 8, size)

        add(2 * modes, obj_real * obj_real + obj_imag * obj_imag)
        term_real = term_imag = None
        for m in range(modes):
            mode = slice(m * size, (m + 1) * size)
            real = changes[here, mode]
            imag = changes[below, mode]
            probe_real = low[2 * m, here, :]
            probe_imag = low[2 * m + 1, here, :]
            more_real = probe_real * real + probe_imag * imag
            more_imag = probe_real * imag - probe_imag * real
            term_real = more_real if m == 0 else term_real + more_real
            term_imag = more_imag if m == 0 else term_imag + more_imag
            add(2 * m, obj_real * real + obj_imag * imag)
            add(2 * m + 1, obj_real * imag - obj_imag * real)
        for comp, term in enumerate((term_real, term_imag)):
            term = term.astype(BF16).astype(F32) * scale
            first = pltpu.roll(term[:, 0:LANES], offset, 1)
            second = pltpu.roll(term[:, LANES:], offset, 1)
            place = comp * chunks + chunk
            window = pl.ds(row + begin, block)
            values = [canvas[place + k, window, :] for k in range(3)]
            canvas[place, window, :] = values[0] + jnp.where(past, first, 0.0)
            canvas[place + 1, window, :] = values[1] + jnp.where(past, second, first)
            canvas[place + 2, window, :] = values[2] + jnp.where(past, 0.0, second)

    def step(index, carry):
        pattern_copy(order[index]).wait()
        previous = jnp.maximum(index - 1, 0)
        following = jnp.minimum(index + 1, found - 1)
        buffer = (index + 1) & 1
        starts = list(blocks)
        for m in range(modes):
            for part in range(2):
                forward_right(m, part)
                deposit(previous, buffer, starts[2 * m + part])
        forward_left(0)
        forward_left(1)
        for begin in starts[:2]:
            reweigh(index, begin)
        backward_right(0)
        for begin in starts[2:]:
            reweigh(index, begin)
        cut(following, starts[0])
        backward_right(1)
        cut(following, starts[1])
        backward_left(0, 0)
        cut(following, starts[2])
        backward_left(0, 1)
        cut(following, starts[3])
        backward_left(1, 0)
        backward_left(1, 1)
        return carry

    for copy in obj_copies:
        copy.wait()

    @pl.when(found > 0)
    def _():
        for begin in blocks:
            cut(0, begin)

    for copy in later:
        copy.wait()

    @pl.when(found > 0)
    def _():
        lax.fori_loop(0, found, step, 0)
        for begin in blocks:
            deposit(found - 1, (found - 1) & 1, begin)

    last_copies = list(out_copies)
    if not with_border:
        last_copies += [
            pltpu.make_async_copy(here, there, sem) for there, here, sem in ring_pieces(ring_out)
        ]
        last_copies.append(pltpu.make_async_copy(sums, sums_out, misc_sems.at[3]))
    for copy in last_copies:
        copy.start()
    if with_border:
        for pair in range(2):
            g_rows[pair][...] = canvas[:, pl.ds(row_sides[pair], half), :].astype(BF16)
            for comp in range(2):
                beside = comp * chunks + col_sides[pair]
                g_cols[pair][comp] = canvas[beside, rows, :].astype(BF16)
        core = lax.axis_index("core")
        count_of = kept.shape[0]
        kept[...] = sums[pl.ds(core * count_of, count_of)]
        given[...] = sums[pl.ds((1 - core) * count_of, count_of)]
    for copy in last_copies + through_copies:
        copy.wait()


def run_positions(counts, centers, pieces, patterns, probe_modes, row_halos, border=None):
    size = probe_modes.shape[-1]
    half = size // 2
    modes = probe_modes.shape[0]
    tile = pieces.shape[1]
    inner = tile // LANES
    chunks = inner + 2
    slots = patterns.shape[0]
    positive, negative = dft_tables(size)
    by_quarter = np.arange(2 * size).reshape(2, 2, half).swapaxes(0, 1).reshape(-1)
    tables = [positive, negative, negative[by_quarter]]
    smem = pl.BlockSpec(memory_space=pltpu.SMEM)
    vmem = pl.BlockSpec(memory_space=pltpu.VMEM)
    anywhere = pl.BlockSpec(memory_space=pl.ANY)
    shape = jax.ShapeDtypeStruct
    in_specs = [smem, smem, anywhere, anywhere, vmem] + [anywhere] * 3 + [vmem] * 2
    operands = [counts, centers, pieces, patterns, probe_modes, *tables, *row_halos]
    sums_shape = (size // 8, 2 * modes + 1, 8, size)
    ring_shape = (2 * inner, size, LANES)
    if border is None:
        out_specs = [anywhere] * 3
        out_shape = [shape(each, F32) for each in (pieces.shape, ring_shape, sums_shape)]
    else:
        in_specs += [vmem] * 4 + [anywhere] * 3
        operands += list(border)
        half_sums = (size // 16,) + sums_shape[1:]
        out_specs = [anywhere] + [vmem] * 6
        out_shape = [
            shape((2, tile, tile), F32),
            shape((2 * chunks, half, LANES), BF16),
            shape((2 * chunks, half, LANES), BF16),
            shape((2, tile, LANES), BF16),
            shape((2, tile, LANES), BF16),
            shape(half_sums, F32),
            shape(half_sums, F32),
        ]
    table = pltpu.VMEM((2 * size, 2 * size), BF16)
    products = pltpu.VMEM((2 * size, modes * size), BF16)
    wide = pltpu.VMEM((2 * size, modes * size), F32)
    padded = pltpu.VMEM((2 * chunks, tile + size, LANES), F32)
    dma = pltpu.SemaphoreType.DMA
    return pl.pallas_call(
        functools.partial(positions_kernel, border is not None),
        in_specs=in_specs,
        out_specs=out_specs,
        out_shape=out_shape,
        scratch_shapes=[
            padded,
            padded,
            pltpu.VMEM(patterns.shape, BF16),
            table,
            table,
            table,
            pltpu.VMEM((2 * modes, size, size), F32),
            products,
            products,
            products,
            products,
            wide,
            wide,
            pltpu.VMEM((2, 2, size, size), F32),
            pltpu.VMEM(sums_shape, F32),
            pltpu.SMEM((slots + 1,), jnp.int32),
            dma((2, 2, inner)),
            dma((2, inner)),
            dma((2, 2, inner)),
            dma((slots,)),
            dma((4,)),
        ],
        compiler_params=pltpu.CompilerParams(
            vmem_limit_bytes=30 * 1024 * 1024
        ),
        cost_estimate=pl.CostEstimate(
            flops=slots * 16 * modes * size**3,
            bytes_accessed=24 * 1024 * 1024,
            transcendentals=0,
        ),
        name="border" if border is not None else "interior",
    )(*operands)


def corners_kernel(col_even, col_odd, row_even, row_odd, out_even, out_odd):
    tile = col_even.shape[1]
    half = row_even.shape[1]
    chunks = row_even.shape[0] // 2
    row_sides = sides(ROW, tile, half)
    col_sides = [offset // LANES for offset in sides(COL, chunks * LANES, half)]
    for pair, (strip, out) in enumerate(((col_even, out_even), (col_odd, out_odd))):
        out[:, half : tile - half, :] = strip[:, half : tile - half, :]
        for other, ring in enumerate((row_even, row_odd)):
            there = pl.ds(row_sides[other], half)
            for comp in range(2):
                extra = ring[comp * chunks + col_sides[pair]].astype(F32)
                out[comp, there, :] = (strip[comp, there, :].astype(F32) + extra).astype(BF16)


def add_corners(g_cols, from_rows):
    vmem = pl.BlockSpec(memory_space=pltpu.VMEM)
    shape = jax.ShapeDtypeStruct(g_cols[0].shape, BF16)
    return pl.pallas_call(
        corners_kernel,
        in_specs=[vmem] * 4,
        out_specs=[vmem] * 2,
        out_shape=[shape, shape],
        compiler_params=pltpu.CompilerParams(vmem_limit_bytes=8 * 1024 * 1024),
        cost_estimate=pl.CostEstimate(
            flops=256 * 1024, bytes_accessed=2 * 1024 * 1024, transcendentals=0
        ),
        name="corners",
    )(*g_cols, *from_rows)


def rims_kernel(
    partial, row_even, row_odd, col_even, col_odd, out, row_buffer, col_buffer, sems
):
    tile = partial.shape[1]
    half = row_even.shape[1]
    inner = tile // LANES
    chunks = inner + 2
    middle = tile - 2 * half
    row_sides = sides(ROW, tile, half)
    col_sides = sides(COL, tile, half)
    row_rings = (row_even, row_odd)
    col_strips = (col_even, col_odd)

    def copy(kind, pair, comp, inward):
        if kind == 0:
            here = row_buffer.at[pair, comp]
            place = (comp, pl.ds(row_sides[pair], half), slice(None))
        else:
            here = col_buffer.at[pair, comp]
            place = (comp, pl.ds(half, middle), pl.ds(col_sides[pair], half))
        source, target = (partial.at[place], here) if inward else (here, out.at[place])
        return pltpu.make_async_copy(
            source, target, sems.at[1 - int(inward), 2 * kind + pair, comp]
        )

    everything = [(kind, pair, comp) for kind in range(2) for pair in range(2) for comp in range(2)]
    for piece in everything:
        copy(*piece, True).start()
    for kind, pair, comp in everything:
        copy(kind, pair, comp, True).wait()
        if kind == 0:
            for j in range(inner):
                columns = slice(j * LANES, (j + 1) * LANES)
                ring = row_rings[pair][comp * chunks + 1 + j]
                row_buffer[pair, comp, :, columns] += ring.astype(F32)
            for other in range(2):
                columns = pl.ds(col_sides[other], half)
                strip = col_strips[other][comp, pl.ds(row_sides[pair], half), :]
                row_buffer[pair, comp, :, columns] += strip.astype(F32)
        else:
            strip = col_strips[pair][comp, half : half + middle, :]
            col_buffer[pair, comp] += strip.astype(F32)
        copy(kind, pair, comp, False).start()
    for piece in everything:
        copy(*piece, False).wait()


def add_rims(partial, from_rows, from_cols):
    tile = partial.shape[1]
    half = from_rows[0].shape[1]
    vmem = pl.BlockSpec(memory_space=pltpu.VMEM)
    anywhere = pl.BlockSpec(memory_space=pl.ANY)
    return pl.pallas_call(
        rims_kernel,
        in_specs=[anywhere] + [vmem] * 4,
        out_specs=anywhere,
        out_shape=jax.ShapeDtypeStruct(partial.shape, F32),
        input_output_aliases={0: 0},
        scratch_shapes=[
            pltpu.VMEM((2, 2, half, tile), F32),
            pltpu.VMEM((2, 2, tile - 2 * half, half), F32),
            pltpu.SemaphoreType.DMA((2, 4, 2)),
        ],
        compiler_params=pltpu.CompilerParams(vmem_limit_bytes=16 * 1024 * 1024),
        cost_estimate=pl.CostEstimate(
            flops=1024 * 1024, bytes_accessed=6 * 1024 * 1024, transcendentals=0
        ),
        name="rims",
    )(partial, *from_rows, *from_cols)


def chip_sums_kernel(kept, received, out):
    out[...] = (kept[...] + received[...]).astype(BF16)


def chip_sums(kept, given):
    vmem = pl.BlockSpec(memory_space=pltpu.VMEM)
    return pl.pallas_call(
        chip_sums_kernel,
        in_specs=[vmem, vmem],
        out_specs=vmem,
        out_shape=jax.ShapeDtypeStruct(kept.shape, BF16),
        compiler_params=pltpu.CompilerParams(vmem_limit_bytes=8 * 1024 * 1024),
        cost_estimate=pl.CostEstimate(
            flops=32 * 1024**3, bytes_accessed=32 * 1024 * 1024, transcendentals=0
        ),
        name="chip_sums",
    )(kept, lax.ppermute(given, "core", [(0, 1), (1, 0)]))


def by_device(on_chip):
    devices = lax.axis_size("x") * lax.axis_size("col")
    groups, planes, _, size = on_chip.shape
    share = groups * 8 // devices
    if share < 8:
        on_chip = on_chip.reshape(groups, planes, 8 // share, share, size)
        return jnp.swapaxes(on_chip, 1, 2).reshape(devices, planes, share, size)
    return on_chip.reshape(devices, groups // devices, planes, 8, size)


def first_sums(parts):
    return lax.all_to_all(parts, ("x", "col"), 0, 0, tiled=True)


def update_kernel(received, copies):
    devices = received.shape[0]
    total = received[0].astype(F32)
    for device in range(1, devices):
        total = total + received[device].astype(F32)
    planes = total.shape[0]
    update = (total[: planes - 1] / jnp.sqrt(total[planes - 1])).astype(BF16)
    for device in range(devices):
        copies[device] = update


def shared_update(received):
    devices, planes, share, size = received.shape
    vmem = pl.BlockSpec(memory_space=pltpu.VMEM)
    return pl.pallas_call(
        update_kernel,
        in_specs=[vmem],
        out_specs=vmem,
        out_shape=jax.ShapeDtypeStruct((devices, planes - 1, share, size), BF16),
        compiler_params=pltpu.CompilerParams(vmem_limit_bytes=8 * 1024 * 1024),
        cost_estimate=pl.CostEstimate(
            flops=512 * 1024, bytes_accessed=1024 * 1024, transcendentals=0
        ),
        name="update",
    )(received)


def finish_kernel(probe, mine, other, out):
    core = lax.axis_index("core")
    groups, planes, height, _ = mine.shape
    for side, update in enumerate((mine, other)):
        first = jnp.where(core == side, 0, groups * height)
        for group in range(groups):
            place = pl.ds(pl.multiple_of(first + group * height, height), height)
            for plane in range(planes):
                m, comp = divmod(plane, 2)
                out[m, comp, place, :] = probe[m, comp, place, :] + update[group, plane].astype(F32)


def finish_probe(probe_modes, mine):
    devices, planes, share, size = mine.shape
    if share < 8:
        mine = mine.reshape(devices * share // 8, 8 // share, planes, share, size)
        mine = jnp.swapaxes(mine, 1, 2).reshape(-1, planes, 8, size)
    other = lax.ppermute(mine, "core", [(0, 1), (1, 0)])
    vmem = pl.BlockSpec(memory_space=pltpu.VMEM)
    return pl.pallas_call(
        finish_kernel,
        in_specs=[vmem] * 3,
        out_specs=vmem,
        out_shape=jax.ShapeDtypeStruct(probe_modes.shape, F32),
        compiler_params=pltpu.CompilerParams(vmem_limit_bytes=8 * 1024 * 1024),
        cost_estimate=pl.CostEstimate(
            flops=256 * 1024, bytes_accessed=3 * 1024 * 1024, transcendentals=0
        ),
        name="finish",
    )(probe_modes, mine, other)


def on_device(object_field, probe_modes, counts, centers, patterns):
    half = probe_modes.shape[-1] // 2
    inner = object_field.shape[1] // LANES

    pieces, col_even, col_odd, row_even, row_odd = spread(object_field, half)
    row_halos = (swap_pairs(row_even, ROW, 0), swap_pairs(row_odd, ROW, 1))
    col_halos = (swap_pairs(col_even, COL, 0), swap_pairs(col_odd, COL, 1))
    is_even = (lax.axis_index("col") & 1) == 0
    first_ends = jnp.concatenate([halo[::inner] for halo in row_halos], 1)
    last_ends = jnp.concatenate([halo[inner - 1 :: inner] for halo in row_halos], 1)
    end_halos = (
        swap_pairs(jnp.where(is_even, last_ends, first_ends), COL, 0),
        swap_pairs(jnp.where(is_even, first_ends, last_ends), COL, 1),
    )

    inputs = (counts, centers[0, 0], pieces, patterns[0, 0], probe_modes, row_halos)
    started = run_positions(*inputs)
    border = (*col_halos, *end_halos, *started)
    partial, g_row_even, g_row_odd, g_col_even, g_col_odd, kept, given = run_positions(
        *inputs, border
    )

    from_rows = (swap_pairs(g_row_even, ROW, 0), swap_pairs(g_row_odd, ROW, 1))
    to_even, to_odd = add_corners((g_col_even, g_col_odd), from_rows)
    from_cols = (swap_pairs(to_even, COL, 0), swap_pairs(to_odd, COL, 1))
    received = lax.cond(
        counts[0, 0] > 0, first_sums, jnp.zeros_like, by_device(chip_sums(kept, given))
    )
    received, from_cols = lax.optimization_barrier((received, from_cols))
    if received.ndim == 5:
        received = received[:, 0]
    mine = lax.all_to_all(shared_update(received), ("x", "col"), 0, 0, tiled=True)
    new_object = add_rims(partial, from_rows, from_cols)
    mine, new_object = lax.optimization_barrier((mine, new_object))
    return (new_object, finish_probe(probe_modes, mine))


def solution(mesh):
    rows, columns = mesh.devices.shape
    split = jax.sharding.Mesh(
        mesh.devices.reshape(rows // 2, 2, columns), ("x", "core", "col")
    )
    placed = (
        P(None, ROW, "col"),
        P(),
        P(),
        P(ROW, "col", None, None),
        P(ROW, "col", None, None, None),
    )
    return jax.shard_map(
        on_device,
        mesh=split,
        in_specs=placed,
        out_specs=(P(None, ROW, "col"), P()),
        check_vma=False,
    )
```

```python
import functools
import math

import jax
import jax.numpy as jnp
import ml_dtypes
import numpy as np
from jax import lax
from jax.experimental import pallas as pl
from jax.experimental.pallas import tpu as pltpu
from jax.sharding import PartitionSpec as P

LANES = 128
ROW = ("x", "core")
COL = ("col",)
F32 = jnp.float32
BF16 = jnp.bfloat16


def dft_tables(length):
    indices = np.arange(length)
    angles = (indices[:, None] * indices[None, :] % length) * (2.0 * np.pi / length)
    scale = 1.0 / np.sqrt(length)
    cosine = (np.cos(angles) * scale).astype(np.float32).astype(ml_dtypes.bfloat16)
    sine = (np.sin(angles) * scale).astype(np.float32).astype(ml_dtypes.bfloat16)
    positive = np.block([[cosine, -sine], [sine, cosine]])
    negative = np.block([[cosine, sine], [-sine, cosine]])
    return positive, negative


def swap_pairs(array, axis, odd):
    devices = math.prod(lax.axis_size(name) for name in axis)
    firsts = range(odd, devices - 1, 2)
    return lax.ppermute(
        array, axis, [(i, i + 1) for i in firsts] + [(i + 1, i) for i in firsts]
    )


def sides(axis, length, width):
    even = (lax.axis_index(axis) & 1) == 0
    far = length - width
    return [
        pl.multiple_of(jnp.where(even, far, 0), width),
        pl.multiple_of(jnp.where(even, 0, far), width),
    ]


def strips_kernel(obj_hbm, col_even, col_odd, row_even, row_odd, col_buffer, row_buffer, sems):
    tile = obj_hbm.shape[1]
    half = row_even.shape[1]
    copies = []
    for pair in range(2):
        column = sides(COL, tile, half)[pair]
        row = sides(ROW, tile, half)[pair]
        copies.append(
            pltpu.make_async_copy(
                obj_hbm.at[:, :, pl.ds(column, half)], col_buffer.at[pair], sems.at[0, pair]
            )
        )
        copies.append(
            pltpu.make_async_copy(
                obj_hbm.at[:, pl.ds(row, half), :], row_buffer.at[pair], sems.at[1, pair]
            )
        )
    for copy in copies:
        copy.start()
    outputs = (col_even, row_even, col_odd, row_odd)
    buffers = (col_buffer, row_buffer) * 2
    for index, copy in enumerate(copies):
        copy.wait()
        outputs[index][...] = buffers[index][index // 2].astype(BF16)


def cut_strips(object_field, half):
    tile = object_field.shape[1]
    vmem = pl.BlockSpec(memory_space=pltpu.VMEM)
    columns = jax.ShapeDtypeStruct((2, tile, half), BF16)
    rows = jax.ShapeDtypeStruct((2, half, tile), BF16)
    return pl.pallas_call(
        strips_kernel,
        in_specs=[pl.BlockSpec(memory_space=pltpu.HBM)],
        out_specs=[vmem] * 4,
        out_shape=[columns, columns, rows, rows],
        scratch_shapes=[
            pltpu.VMEM((2, 2, tile, half), F32),
            pltpu.VMEM((2, 2, half, tile), F32),
            pltpu.SemaphoreType.DMA((2, 2)),
        ],
        compiler_params=pltpu.CompilerParams(vmem_limit_bytes=60 * 1024 * 1024),
        cost_estimate=pl.CostEstimate(
            flops=1024 * 1024, bytes_accessed=5 * 1024 * 1024, transcendentals=0
        ),
        name="strips",
    )(object_field)


def positions_kernel(with_border, *refs):
    counts, centers, obj_hbm, pat_hbm, probe = refs[:5]
    tables_hbm, row_halos = refs[5:8], refs[8:10]
    refs = refs[10:]
    if with_border:
        col_halos, end_halos = refs[0:2], refs[2:4]
        start_hbm, ring_in, sums_in = refs[4:7]
        out_hbm, g_rows, g_ends, g_mids = refs[7], refs[8:10], refs[10:12], refs[12:14]
        kept, given = refs[14:16]
        refs = refs[16:]
    else:
        out_hbm, ring_out, sums_out = refs[:3]
        refs = refs[3:]
    (obj, canvas, patterns, positive, negative, left_negative, low, waves, shifts, halves, backs,
     spectra, changes, patch, terms, sums, order, piece_sems, out_sems, ring_sems, pat_sems,
     sums_sems, misc_sems) = refs
    size = probe.shape[-1]
    half = size // 2
    tile = obj_hbm.shape[1]
    inner = tile // LANES
    chunks = inner + 2
    modes = probe.shape[0]
    rows = slice(half, half + tile)
    near = [0, 1, inner - 2, inner - 1] if with_border else list(range(inner))
    pieces = [(comp, j) for comp in range(2) for j in near]
    everywhere = [(comp, j) for comp in range(2) for j in range(inner)]

    def home(array, comp, j):
        return array.at[comp, :, pl.ds(j * LANES, LANES)]

    def held(array, comp, j):
        return array.at[comp * chunks + 1 + j, pl.ds(half, tile), :]

    def ring_pieces(array):
        for comp, j in everywhere:
            for side, row in enumerate((0, half + tile)):
                yield (
                    array.at[comp, pl.ds(side * half, half), pl.ds(j * LANES, LANES)],
                    canvas.at[comp * chunks + 1 + j, pl.ds(row, half), :],
                    ring_sems.at[side, comp, j],
                )

    def sums_pieces(array):
        step = array.shape[0] // sums_parts
        for part in range(sums_parts):
            here = pl.ds(part * step, step)
            yield array.at[here], sums.at[here], sums_sems.at[part]

    sums_parts = sums_sems.shape[0]
    obj_copies = [
        pltpu.make_async_copy(home(obj_hbm, *p), held(obj, *p), piece_sems.at[0, *p])
        for p in pieces
    ]
    out_copies = [
        pltpu.make_async_copy(held(canvas, *p), home(out_hbm, *p), out_sems.at[p]) for p in pieces
    ]
    tables = (positive, negative, left_negative)
    later = [
        pltpu.make_async_copy(tables_hbm[i], tables[i], misc_sems.at[i]) for i in range(3)
    ]
    if with_border:
        later += [
            pltpu.make_async_copy(home(start_hbm, *p), held(canvas, *p), piece_sems.at[1, *p])
            for p in pieces
        ]
        later += [pltpu.make_async_copy(*each) for each in ring_pieces(ring_in)]
        later += [pltpu.make_async_copy(*each) for each in sums_pieces(sums_in)]
    for copy in obj_copies + later:
        copy.start()

    order[0] = 0
    count = counts[lax.axis_index(ROW), lax.axis_index("col")]

    def pattern_copy(slot):
        return pltpu.make_async_copy(pat_hbm.at[slot], patterns.at[slot], pat_sems.at[slot])

    def note(slot, found):
        column = centers[1, slot]
        inside = (column >= half) & (column <= tile - half)
        order[found] = slot
        return found + jnp.where(inside, 0 if with_border else 1, 1 if with_border else 0)

    def fetch(index, carry):
        pattern_copy(order[index]).start()
        return carry

    found = lax.fori_loop(0, count, note, 0)
    lax.fori_loop(0, found, fetch, 0)

    if not with_border:
        sums[...] = jnp.zeros_like(sums)
    intensity = jnp.zeros((size, size), F32)
    for m in range(modes):
        for comp in range(2):
            values = probe[m, comp]
            intensity = intensity + values * values
            low[2 * m + comp] = values.astype(BF16).astype(F32)
    scale = 1.0 / (jnp.max(intensity) + 1e-06)
    changes[...] = jnp.zeros_like(changes)
    patch[...] = jnp.zeros_like(patch)

    row_sides = sides(ROW, tile + size, half)
    col_sides = [offset // LANES for offset in sides(COL, tile + size, half)]
    blank = jnp.zeros((tile + size, LANES), F32)
    for comp in range(2):
        first = comp * chunks
        for pair in range(2):
            for j in near:
                columns = slice(j * LANES, (j + 1) * LANES)
                obj[first + 1 + j, pl.ds(row_sides[pair], half), :] = row_halos[pair][
                    comp, :, columns
                ].astype(F32)
            if with_border:
                beside = first + col_sides[pair]
                canvas[beside] = blank
                obj[beside, rows, :] = col_halos[pair][comp].astype(F32)
                for other in range(2):
                    obj[beside, pl.ds(row_sides[other], half), :] = end_halos[pair][
                        comp, other * half : (other + 1) * half, :
                    ].astype(F32)
        if not with_border:
            for j in range(inner):
                canvas[first + 1 + j, 0:half, :] = blank[0:half]
                canvas[first + 1 + j, half + tile :, :] = blank[0:half]

    block = 64
    groups = block // 8
    lane = lax.broadcasted_iota(jnp.int32, (block, LANES), 1)
    blocks = range(0, size, block)

    def place_of(index):
        slot = order[index]
        column = centers[1, slot]
        return slot, centers[0, slot], column >> 7, column & 127

    def cut(index, buffer):
        _, row, chunk, offset = place_of(index)
        back_offset = (LANES - offset) & 127
        from_first = lane < LANES - offset
        for begin in blocks:
            here = slice(begin, begin + block)
            for comp in range(2):
                moved = [
                    pltpu.roll(
                        obj[comp * chunks + chunk + k, pl.ds(row + begin, block), :],
                        back_offset, 1,
                    )
                    for k in range(3)
                ]
                for k in range(2):
                    window = jnp.where(from_first, moved[k], moved[k + 1])
                    patch[buffer, comp, here, k * LANES : (k + 1) * LANES] = window.astype(
                        BF16
                    ).astype(F32)

    def make_waves(buffer, begin):
        here = slice(begin, begin + block)
        real = patch[buffer, 0, here, :]
        imag = patch[buffer, 1, here, :]
        for m in range(modes):
            probe_real = low[2 * m, here, :]
            probe_imag = low[2 * m + 1, here, :]
            there = slice(m * size + begin, m * size + begin + block)
            waves[there, 0:size] = (probe_real * real - probe_imag * imag).astype(BF16)
            waves[there, size:] = (probe_real * imag + probe_imag * real).astype(BF16)

    def hand_on(begin):
        here = slice(begin, begin + block)
        for comp in range(2):
            patch[0, comp, here, :] = patch[1, comp, here, :]
            patch[1, comp, here, :] = patch[2, comp, here, :]

    def forward_right(m, part):
        mode = slice(m * size, (m + 1) * size)
        columns = slice(part * size, (part + 1) * size)
        halves[columns, mode] = jnp.dot(
            waves[mode, :], positive[:, columns], preferred_element_type=F32
        ).astype(BF16)

    def forward_left(k):
        rows_here = slice(k * size, (k + 1) * size)
        spectra[rows_here, :] = jnp.dot(
            left_negative[rows_here, :], halves[...], preferred_element_type=F32
        )

    def reweigh(index, begin):
        slot = order[index]
        k, inside = divmod(begin, half)
        real_rows = slice(k * size + inside, k * size + inside + block)
        imag_rows = slice(k * size + half + inside, k * size + half + inside + block)
        amplitude = patterns[slot, begin : begin + block, :].astype(F32)
        mode_columns = [slice(m * size, (m + 1) * size) for m in range(modes)]
        parts = [(spectra[real_rows, mode], spectra[imag_rows, mode]) for mode in mode_columns]
        power = sum(real * real + imag * imag for real, imag in parts)
        factor = amplitude * lax.rsqrt(jnp.maximum(power, 0.5)) - 1.0
        for m, (real, imag) in enumerate(parts):
            first = k * size + m * half + inside
            there = slice(first, first + block)
            shifts[there, 0:size] = (factor * real).astype(BF16)
            shifts[there, size:] = (factor * imag).astype(BF16)

    def backward_right(k):
        product = jnp.dot(
            shifts[k * size : (k + 1) * size, :], negative[...],
            preferred_element_type=F32,
        ).astype(BF16)
        for m in range(modes):
            mode = slice(m * size, (m + 1) * size)
            for part in range(2):
                first = part * size + k * half
                backs[first : first + half, mode] = product[
                    m * half : (m + 1) * half, part * size : (part + 1) * size
                ]

    def backward_left(m, part):
        mode = slice(m * size, (m + 1) * size)
        rows_here = slice(part * size, (part + 1) * size)
        changes[rows_here, mode] = jnp.dot(
            positive[rows_here, :], backs[:, mode], preferred_element_type=F32
        )

    def gather_terms(begin):
        here = slice(begin, begin + block)
        below = slice(size + begin, size + begin + block)
        start = begin // 8
        obj_real = patch[0, 0, here, :]
        obj_imag = patch[0, 1, here, :]

        def add(plane, value):
            sums[start : start + groups, plane] += value.reshape(groups, 8, size)

        add(2 * modes, obj_real * obj_real + obj_imag * obj_imag)
        term_real = term_imag = None
        for m in range(modes):
            mode = slice(m * size, (m + 1) * size)
            real = changes[here, mode]
            imag = changes[below, mode]
            probe_real = low[2 * m, here, :]
            probe_imag = low[2 * m + 1, here, :]
            more_real = probe_real * real + probe_imag * imag
            more_imag = probe_real * imag - probe_imag * real
            term_real = more_real if m == 0 else term_real + more_real
            term_imag = more_imag if m == 0 else term_imag + more_imag
            add(2 * m, obj_real * real + obj_imag * imag)
            add(2 * m + 1, obj_real * imag - obj_imag * real)
        terms[0, here, :] = term_real.astype(BF16).astype(F32) * scale
        terms[1, here, :] = term_imag.astype(BF16).astype(F32) * scale

    def deposit(index):
        _, row, chunk, offset = place_of(index)
        past = lane >= offset
        for begin in blocks:
            here = slice(begin, begin + block)
            for comp in range(2):
                first = pltpu.roll(terms[comp, here, 0:LANES], offset, 1)
                second = pltpu.roll(terms[comp, here, LANES:], offset, 1)
                place = comp * chunks + chunk
                window = pl.ds(row + begin, block)
                values = [canvas[place + k, window, :] for k in range(3)]
                canvas[place, window, :] = values[0] + jnp.where(past, first, 0.0)
                canvas[place + 1, window, :] = values[1] + jnp.where(past, second, first)
                canvas[place + 2, window, :] = values[2] + jnp.where(past, 0.0, second)

    def step(index, carry):
        pattern_copy(order[index]).wait()
        cut(jnp.minimum(index + 1, found - 1), 2)
        starts = list(blocks)
        for m in range(modes):
            for part in range(2):
                forward_right(m, part)
                gather_terms(starts[2 * m + part])
        forward_left(0)
        forward_left(1)
        for begin in starts[:2]:
            reweigh(index, begin)
        backward_right(0)
        for begin in starts[2:]:
            reweigh(index, begin)
        make_waves(2, starts[0])
        backward_right(1)
        make_waves(2, starts[1])
        hand_on(starts[0])
        backward_left(0, 0)
        make_waves(2, starts[2])
        hand_on(starts[1])
        backward_left(0, 1)
        make_waves(2, starts[3])
        hand_on(starts[2])
        backward_left(1, 0)
        hand_on(starts[3])
        backward_left(1, 1)
        deposit(jnp.maximum(index - 1, 0))
        return carry

    for copy in obj_copies:
        copy.wait()

    @pl.when(found > 0)
    def _():
        cut(0, 1)
        for begin in blocks:
            make_waves(1, begin)

    if not with_border:
        for comp, j in pieces:
            index = comp * chunks + 1 + j
            canvas[index, rows, :] = obj[index, rows, :]
    for copy in later:
        copy.wait()

    @pl.when(found > 0)
    def _():
        lax.fori_loop(0, found, step, 0)
        for begin in blocks:
            gather_terms(begin)
        deposit(found - 1)

    last_copies = list(out_copies)
    if not with_border:
        last_copies += [
            pltpu.make_async_copy(here, there, sem) for there, here, sem in ring_pieces(ring_out)
        ]
        last_copies += [
            pltpu.make_async_copy(here, there, sem) for there, here, sem in sums_pieces(sums_out)
        ]
    for copy in last_copies:
        copy.start()
    if with_border:
        for pair in range(2):
            g_rows[pair][...] = canvas[:, pl.ds(row_sides[pair], half), :].astype(BF16)
            for comp in range(2):
                beside = comp * chunks + col_sides[pair]
                low_end = half + tile
                g_ends[pair][comp, 0:half] = canvas[beside, half:size, :].astype(BF16)
                g_ends[pair][comp, half:] = canvas[beside, low_end - half : low_end, :].astype(BF16)
                g_mids[pair][comp] = canvas[beside, size : low_end - half, :].astype(BF16)
        core = lax.axis_index("core")
        count_of = kept.shape[0]
        kept[...] = sums[pl.ds(core * count_of, count_of)]
        given[...] = sums[pl.ds((1 - core) * count_of, count_of)]
    for copy in last_copies:
        copy.wait()


def run_positions(counts, centers, object_field, patterns, probe_modes, row_halos, border=None):
    size = probe_modes.shape[-1]
    half = size // 2
    modes = probe_modes.shape[0]
    tile = object_field.shape[1]
    inner = tile // LANES
    chunks = inner + 2
    slots = patterns.shape[0]
    positive, negative = dft_tables(size)
    by_quarter = np.arange(2 * size).reshape(2, 2, half).swapaxes(0, 1).reshape(-1)
    tables = [positive, negative, negative[by_quarter]]
    smem = pl.BlockSpec(memory_space=pltpu.SMEM)
    vmem = pl.BlockSpec(memory_space=pltpu.VMEM)
    anywhere = pl.BlockSpec(memory_space=pl.ANY)
    shape = jax.ShapeDtypeStruct
    in_specs = [smem, smem, anywhere, anywhere, vmem] + [anywhere] * 3 + [vmem] * 2
    operands = [counts, centers, object_field, patterns, probe_modes, *tables, *row_halos]
    sums_shape = (size // 8, 2 * modes + 1, 8, size)
    ring_shape = (2, size, tile)
    aliases = {}
    if border is None:
        out_specs = [anywhere] * 3
        out_shape = [shape(each, F32) for each in (object_field.shape, ring_shape, sums_shape)]
    else:
        aliases = {len(operands) + 4: 0}
        in_specs += [vmem] * 4 + [anywhere] * 3
        operands += list(border)
        half_sums = (size // 16,) + sums_shape[1:]
        out_specs = [anywhere] + [vmem] * 8
        out_shape = [
            shape((2, tile, tile), F32),
            shape((2 * chunks, half, LANES), BF16),
            shape((2 * chunks, half, LANES), BF16),
            shape((2, size, LANES), BF16),
            shape((2, size, LANES), BF16),
            shape((2, tile - size, LANES), BF16),
            shape((2, tile - size, LANES), BF16),
            shape(half_sums, F32),
            shape(half_sums, F32),
        ]
    table = pltpu.VMEM((2 * size, 2 * size), BF16)
    products = pltpu.VMEM((2 * size, modes * size), BF16)
    wide = pltpu.VMEM((2 * size, modes * size), F32)
    padded = pltpu.VMEM((2 * chunks, tile + size, LANES), F32)
    dma = pltpu.SemaphoreType.DMA
    return pl.pallas_call(
        functools.partial(positions_kernel, border is not None),
        in_specs=in_specs,
        out_specs=out_specs,
        out_shape=out_shape,
        input_output_aliases=aliases,
        scratch_shapes=[
            padded,
            padded,
            pltpu.VMEM(patterns.shape, BF16),
            table,
            table,
            table,
            pltpu.VMEM((2 * modes, size, size), F32),
            products,
            products,
            products,
            products,
            wide,
            wide,
            pltpu.VMEM((3, 2, size, size), F32),
            pltpu.VMEM((2, size, size), F32),
            pltpu.VMEM(sums_shape, F32),
            pltpu.SMEM((slots + 1,), jnp.int32),
            dma((2, 2, inner)),
            dma((2, inner)),
            dma((2, 2, inner)),
            dma((slots,)),
            dma((8,)),
            dma((3,)),
        ],
        compiler_params=pltpu.CompilerParams(
            vmem_limit_bytes=(50 if border is None else 46) * 1024 * 1024
        ),
        cost_estimate=pl.CostEstimate(
            flops=slots * 16 * modes * size**3,
            bytes_accessed=24 * 1024 * 1024,
            transcendentals=0,
        ),
        name="border" if border is not None else "interior",
    )(*operands)


def corners_kernel(end_even, end_odd, row_even, row_odd, out_even, out_odd):
    half = row_even.shape[1]
    chunks = row_even.shape[0] // 2
    row_sides = sides(ROW, 2 * half, half)
    col_sides = [offset // LANES for offset in sides(COL, chunks * LANES, half)]
    for pair, (strip, out) in enumerate(((end_even, out_even), (end_odd, out_odd))):
        for other, ring in enumerate((row_even, row_odd)):
            there = pl.ds(row_sides[other], half)
            for comp in range(2):
                extra = ring[comp * chunks + col_sides[pair]].astype(F32)
                out[comp, there, :] = (strip[comp, there, :].astype(F32) + extra).astype(BF16)


def add_corners(g_ends, from_rows):
    vmem = pl.BlockSpec(memory_space=pltpu.VMEM)
    shape = jax.ShapeDtypeStruct(g_ends[0].shape, BF16)
    return pl.pallas_call(
        corners_kernel,
        in_specs=[vmem] * 4,
        out_specs=[vmem] * 2,
        out_shape=[shape, shape],
        compiler_params=pltpu.CompilerParams(vmem_limit_bytes=8 * 1024 * 1024),
        cost_estimate=pl.CostEstimate(
            flops=256 * 1024, bytes_accessed=2 * 1024 * 1024, transcendentals=0
        ),
        name="corners",
    )(*g_ends, *from_rows)


def rims_kernel(
    partial, row_even, row_odd, end_even, end_odd, mid_even, mid_odd, out, row_buffer, col_buffer,
    sems,
):
    tile = partial.shape[1]
    half = row_even.shape[1]
    inner = tile // LANES
    chunks = inner + 2
    middle = tile - 2 * half
    row_sides = sides(ROW, tile, half)
    col_sides = sides(COL, tile, half)
    row_rings = (row_even, row_odd)
    end_sides = sides(ROW, 2 * half, half)
    end_strips = (end_even, end_odd)
    mid_strips = (mid_even, mid_odd)

    def copy(kind, pair, comp, inward):
        if kind == 0:
            here = row_buffer.at[pair, comp]
            place = (comp, pl.ds(row_sides[pair], half), slice(None))
        else:
            here = col_buffer.at[pair, comp]
            place = (comp, pl.ds(half, middle), pl.ds(col_sides[pair], half))
        source, target = (partial.at[place], here) if inward else (here, out.at[place])
        return pltpu.make_async_copy(
            source, target, sems.at[1 - int(inward), 2 * kind + pair, comp]
        )

    everything = [(kind, pair, comp) for kind in range(2) for pair in range(2) for comp in range(2)]
    for piece in everything:
        copy(*piece, True).start()
    for kind, pair, comp in everything:
        copy(kind, pair, comp, True).wait()
        if kind == 0:
            for j in range(inner):
                columns = slice(j * LANES, (j + 1) * LANES)
                ring = row_rings[pair][comp * chunks + 1 + j]
                row_buffer[pair, comp, :, columns] += ring.astype(F32)
            for other in range(2):
                columns = pl.ds(col_sides[other], half)
                strip = end_strips[other][comp, pl.ds(end_sides[pair], half), :]
                row_buffer[pair, comp, :, columns] += strip.astype(F32)
        else:
            col_buffer[pair, comp] += mid_strips[pair][comp].astype(F32)
        copy(kind, pair, comp, False).start()
    for piece in everything:
        copy(*piece, False).wait()


def add_rims(partial, from_rows, from_ends, from_mids):
    tile = partial.shape[1]
    half = from_rows[0].shape[1]
    vmem = pl.BlockSpec(memory_space=pltpu.VMEM)
    anywhere = pl.BlockSpec(memory_space=pl.ANY)
    return pl.pallas_call(
        rims_kernel,
        in_specs=[anywhere] + [vmem] * 6,
        out_specs=anywhere,
        out_shape=jax.ShapeDtypeStruct(partial.shape, F32),
        input_output_aliases={0: 0},
        scratch_shapes=[
            pltpu.VMEM((2, 2, half, tile), F32),
            pltpu.VMEM((2, 2, tile - 2 * half, half), F32),
            pltpu.SemaphoreType.DMA((2, 4, 2)),
        ],
        compiler_params=pltpu.CompilerParams(vmem_limit_bytes=16 * 1024 * 1024),
        cost_estimate=pl.CostEstimate(
            flops=1024 * 1024, bytes_accessed=6 * 1024 * 1024, transcendentals=0
        ),
        name="rims",
    )(partial, *from_rows, *from_ends, *from_mids)


def chip_sums_kernel(kept, received, out):
    out[...] = (kept[...] + received[...]).astype(BF16)


def chip_sums(kept, given):
    vmem = pl.BlockSpec(memory_space=pltpu.VMEM)
    return pl.pallas_call(
        chip_sums_kernel,
        in_specs=[vmem, vmem],
        out_specs=vmem,
        out_shape=jax.ShapeDtypeStruct(kept.shape, BF16),
        compiler_params=pltpu.CompilerParams(vmem_limit_bytes=8 * 1024 * 1024),
        cost_estimate=pl.CostEstimate(
            flops=32 * 1024**3, bytes_accessed=32 * 1024 * 1024, transcendentals=0
        ),
        name="chip_sums",
    )(kept, lax.ppermute(given, "core", [(0, 1), (1, 0)]))


def by_device(on_chip):
    devices = lax.axis_size("x") * lax.axis_size("col")
    groups, planes, _, size = on_chip.shape
    share = groups * 8 // devices
    if share < 8:
        on_chip = on_chip.reshape(groups, planes, 8 // share, share, size)
        return jnp.swapaxes(on_chip, 1, 2).reshape(devices, planes, share, size)
    return on_chip.reshape(devices, groups // devices, planes, 8, size)


def first_sums(parts):
    return lax.all_to_all(parts, ("x", "col"), 0, 0, tiled=True)


def update_kernel(received, copies):
    devices = received.shape[0]
    total = received[0].astype(F32)
    for device in range(1, devices):
        total = total + received[device].astype(F32)
    planes = total.shape[0]
    update = (total[: planes - 1] / jnp.sqrt(total[planes - 1])).astype(BF16)
    for device in range(devices):
        copies[device] = update


def shared_update(received):
    devices, planes, share, size = received.shape
    vmem = pl.BlockSpec(memory_space=pltpu.VMEM)
    return pl.pallas_call(
        update_kernel,
        in_specs=[vmem],
        out_specs=vmem,
        out_shape=jax.ShapeDtypeStruct((devices, planes - 1, share, size), BF16),
        compiler_params=pltpu.CompilerParams(vmem_limit_bytes=8 * 1024 * 1024),
        cost_estimate=pl.CostEstimate(
            flops=512 * 1024, bytes_accessed=1024 * 1024, transcendentals=0
        ),
        name="update",
    )(received)


def finish_kernel(probe, mine, other, out):
    core = lax.axis_index("core")
    groups, planes, height, _ = mine.shape
    for side, update in enumerate((mine, other)):
        first = jnp.where(core == side, 0, groups * height)
        for group in range(groups):
            place = pl.ds(pl.multiple_of(first + group * height, height), height)
            for plane in range(planes):
                m, comp = divmod(plane, 2)
                out[m, comp, place, :] = probe[m, comp, place, :] + update[group, plane].astype(F32)


def finish_probe(probe_modes, mine):
    devices, planes, share, size = mine.shape
    if share < 8:
        mine = mine.reshape(devices * share // 8, 8 // share, planes, share, size)
        mine = jnp.swapaxes(mine, 1, 2).reshape(-1, planes, 8, size)
    other = lax.ppermute(mine, "core", [(0, 1), (1, 0)])
    vmem = pl.BlockSpec(memory_space=pltpu.VMEM)
    return pl.pallas_call(
        finish_kernel,
        in_specs=[vmem] * 3,
        out_specs=vmem,
        out_shape=jax.ShapeDtypeStruct(probe_modes.shape, F32),
        compiler_params=pltpu.CompilerParams(vmem_limit_bytes=8 * 1024 * 1024),
        cost_estimate=pl.CostEstimate(
            flops=256 * 1024, bytes_accessed=3 * 1024 * 1024, transcendentals=0
        ),
        name="finish",
    )(probe_modes, mine, other)


def on_device(object_field, probe_modes, counts, centers, patterns):
    half = probe_modes.shape[-1] // 2

    col_even, col_odd, row_even, row_odd = cut_strips(object_field, half)
    row_halos = (swap_pairs(row_even, ROW, 0), swap_pairs(row_odd, ROW, 1))
    col_halos = (swap_pairs(col_even, COL, 0), swap_pairs(col_odd, COL, 1))
    is_even = (lax.axis_index("col") & 1) == 0
    first_ends = jnp.concatenate([halo[:, :, :half] for halo in row_halos], 1)
    last_ends = jnp.concatenate([halo[:, :, -half:] for halo in row_halos], 1)
    end_halos = (
        swap_pairs(jnp.where(is_even, last_ends, first_ends), COL, 0),
        swap_pairs(jnp.where(is_even, first_ends, last_ends), COL, 1),
    )

    inputs = (counts, centers[0, 0], object_field, patterns[0, 0], probe_modes, row_halos)
    started = run_positions(*inputs)
    border = (*col_halos, *end_halos, *started)
    partial, *rims, kept, given = run_positions(*inputs, border)
    g_row_even, g_row_odd, g_end_even, g_end_odd, g_mid_even, g_mid_odd = rims

    from_mids = (swap_pairs(g_mid_even, COL, 0), swap_pairs(g_mid_odd, COL, 1))
    from_rows = (swap_pairs(g_row_even, ROW, 0), swap_pairs(g_row_odd, ROW, 1))
    to_even, to_odd = add_corners((g_end_even, g_end_odd), from_rows)
    from_ends = (swap_pairs(to_even, COL, 0), swap_pairs(to_odd, COL, 1))
    received = lax.cond(
        counts[0, 0] > 0, first_sums, jnp.zeros_like, by_device(chip_sums(kept, given))
    )
    received, from_mids, from_ends = lax.optimization_barrier((received, from_mids, from_ends))
    if received.ndim == 5:
        received = received[:, 0]
    mine = lax.all_to_all(shared_update(received), ("x", "col"), 0, 0, tiled=True)
    new_object = add_rims(partial, from_rows, from_ends, from_mids)
    mine, new_object = lax.optimization_barrier((mine, new_object))
    return (new_object, finish_probe(probe_modes, mine))


def solution(mesh):
    rows, columns = mesh.devices.shape
    split = jax.sharding.Mesh(
        mesh.devices.reshape(rows // 2, 2, columns), ("x", "core", "col")
    )
    placed = (
        P(None, ROW, "col"),
        P(),
        P(),
        P(ROW, "col", None, None),
        P(ROW, "col", None, None, None),
    )
    return jax.shard_map(
        on_device,
        mesh=split,
        in_specs=placed,
        out_specs=(P(None, ROW, "col"), P()),
        check_vma=False,
    )
```

```python
import functools
import math

import jax
import jax.numpy as jnp
import ml_dtypes
import numpy as np
from jax import lax
from jax.experimental import pallas as pl
from jax.experimental.pallas import tpu as pltpu
from jax.sharding import PartitionSpec as P

LANES = 128
ROW = ("x", "core")
COL = ("col",)
F32 = jnp.float32
BF16 = jnp.bfloat16


def dft_tables(length):
    indices = np.arange(length)
    angles = (indices[:, None] * indices[None, :] % length) * (2.0 * np.pi / length)
    scale = 1.0 / np.sqrt(length)
    cosine = (np.cos(angles) * scale).astype(np.float32).astype(ml_dtypes.bfloat16)
    sine = (np.sin(angles) * scale).astype(np.float32).astype(ml_dtypes.bfloat16)
    positive = np.block([[cosine, -sine], [sine, cosine]])
    negative = np.block([[cosine, sine], [-sine, cosine]])
    return positive, negative


def swap_pairs(array, axis, odd):
    devices = math.prod(lax.axis_size(name) for name in axis)
    firsts = range(odd, devices - 1, 2)
    return lax.ppermute(
        array, axis, [(i, i + 1) for i in firsts] + [(i + 1, i) for i in firsts]
    )


def sides(axis, length, width):
    even = (lax.axis_index(axis) & 1) == 0
    far = length - width
    return [
        pl.multiple_of(jnp.where(even, far, 0), width),
        pl.multiple_of(jnp.where(even, 0, far), width),
    ]


def strips_kernel(obj_hbm, col_even, col_odd, row_even, row_odd, col_buffer, row_buffer, sems):
    tile = obj_hbm.shape[1]
    half = row_even.shape[1]
    copies = []
    for pair in range(2):
        column = sides(COL, tile, half)[pair]
        row = sides(ROW, tile, half)[pair]
        copies.append(
            pltpu.make_async_copy(
                obj_hbm.at[:, :, pl.ds(column, half)], col_buffer.at[pair], sems.at[0, pair]
            )
        )
        copies.append(
            pltpu.make_async_copy(
                obj_hbm.at[:, pl.ds(row, half), :], row_buffer.at[pair], sems.at[1, pair]
            )
        )
    for copy in copies:
        copy.start()
    outputs = (col_even, row_even, col_odd, row_odd)
    buffers = (col_buffer, row_buffer) * 2
    for index, copy in enumerate(copies):
        copy.wait()
        outputs[index][...] = buffers[index][index // 2].astype(BF16)


def cut_strips(object_field, half):
    tile = object_field.shape[1]
    vmem = pl.BlockSpec(memory_space=pltpu.VMEM)
    columns = jax.ShapeDtypeStruct((2, tile, half), BF16)
    rows = jax.ShapeDtypeStruct((2, half, tile), BF16)
    return pl.pallas_call(
        strips_kernel,
        in_specs=[pl.BlockSpec(memory_space=pltpu.HBM)],
        out_specs=[vmem] * 4,
        out_shape=[columns, columns, rows, rows],
        scratch_shapes=[
            pltpu.VMEM((2, 2, tile, half), F32),
            pltpu.VMEM((2, 2, half, tile), F32),
            pltpu.SemaphoreType.DMA((2, 2)),
        ],
        compiler_params=pltpu.CompilerParams(vmem_limit_bytes=60 * 1024 * 1024),
        cost_estimate=pl.CostEstimate(
            flops=1024 * 1024, bytes_accessed=5 * 1024 * 1024, transcendentals=0
        ),
        name="strips",
    )(object_field)


def positions_kernel(with_border, *refs):
    counts, centers, obj_hbm, pat_hbm, probe = refs[:5]
    tables_hbm, row_halos = refs[5:8], refs[8:10]
    refs = refs[10:]
    if with_border:
        col_halos, end_halos = refs[0:2], refs[2:4]
        start_hbm, ring_in, sums_in = refs[4:7]
        out_hbm, g_rows, g_ends, g_mids = refs[7], refs[8:10], refs[10:12], refs[12:14]
        kept, given = refs[14:16]
        refs = refs[16:]
    else:
        out_hbm, ring_out, sums_out = refs[:3]
        refs = refs[3:]
    (obj, canvas, patterns, positive, negative, left_negative, low, waves, shifts, halves, backs,
     spectra, changes, patch, sums, order, piece_sems, out_sems, ring_sems, pat_sems,
     sums_sems, misc_sems) = refs
    size = probe.shape[-1]
    half = size // 2
    tile = obj_hbm.shape[1]
    inner = tile // LANES
    chunks = inner + 2
    modes = probe.shape[0]
    rows = slice(half, half + tile)
    near = [0, 1, inner - 2, inner - 1] if with_border else list(range(inner))
    pieces = [(comp, j) for comp in range(2) for j in near]
    everywhere = [(comp, j) for comp in range(2) for j in range(inner)]

    def home(array, comp, j):
        return array.at[comp, :, pl.ds(j * LANES, LANES)]

    def held(array, comp, j):
        return array.at[comp * chunks + 1 + j, pl.ds(half, tile), :]

    def ring_pieces(array):
        for comp, j in everywhere:
            for side, row in enumerate((0, half + tile)):
                yield (
                    array.at[comp, pl.ds(side * half, half), pl.ds(j * LANES, LANES)],
                    canvas.at[comp * chunks + 1 + j, pl.ds(row, half), :],
                    ring_sems.at[side, comp, j],
                )

    def sums_pieces(array):
        step = array.shape[0] // sums_parts
        for part in range(sums_parts):
            here = pl.ds(part * step, step)
            yield array.at[here], sums.at[here], sums_sems.at[part]

    sums_parts = sums_sems.shape[0]
    obj_copies = [
        pltpu.make_async_copy(home(obj_hbm, *p), held(obj, *p), piece_sems.at[0, *p])
        for p in pieces
    ]
    out_copies = [
        pltpu.make_async_copy(held(canvas, *p), home(out_hbm, *p), out_sems.at[p]) for p in pieces
    ]
    tables = (positive, negative, left_negative)
    later = [
        pltpu.make_async_copy(tables_hbm[i], tables[i], misc_sems.at[i]) for i in range(3)
    ]
    if with_border:
        later += [
            pltpu.make_async_copy(home(start_hbm, *p), held(canvas, *p), piece_sems.at[1, *p])
            for p in pieces
        ]
        later += [pltpu.make_async_copy(*each) for each in ring_pieces(ring_in)]
        later += [pltpu.make_async_copy(*each) for each in sums_pieces(sums_in)]
    through_copies = [
        pltpu.make_async_copy(home(start_hbm, *p), home(out_hbm, *p), out_sems.at[p])
        for p in everywhere
        if p not in pieces
    ]
    for copy in obj_copies + later + through_copies:
        copy.start()

    order[0] = 0
    count = counts[lax.axis_index(ROW), lax.axis_index("col")]

    def pattern_copy(slot):
        return pltpu.make_async_copy(pat_hbm.at[slot], patterns.at[slot], pat_sems.at[slot])

    def note(slot, found):
        column = centers[1, slot]
        inside = (column >= half) & (column <= tile - half)
        order[found] = slot
        return found + jnp.where(inside, 0 if with_border else 1, 1 if with_border else 0)

    def fetch(index, carry):
        pattern_copy(order[index]).start()
        return carry

    found = lax.fori_loop(0, count, note, 0)
    lax.fori_loop(0, found, fetch, 0)

    if not with_border:
        sums[...] = jnp.zeros_like(sums)
    intensity = jnp.zeros((size, size), F32)
    for m in range(modes):
        for comp in range(2):
            values = probe[m, comp]
            intensity = intensity + values * values
            low[2 * m + comp] = values.astype(BF16).astype(F32)
    scale = 1.0 / (jnp.max(intensity) + 1e-06)
    changes[...] = jnp.zeros_like(changes)
    patch[...] = jnp.zeros_like(patch)

    row_sides = sides(ROW, tile + size, half)
    col_sides = [offset // LANES for offset in sides(COL, tile + size, half)]
    blank = jnp.zeros((tile + size, LANES), F32)
    for comp in range(2):
        first = comp * chunks
        for pair in range(2):
            for j in near:
                columns = slice(j * LANES, (j + 1) * LANES)
                obj[first + 1 + j, pl.ds(row_sides[pair], half), :] = row_halos[pair][
                    comp, :, columns
                ].astype(F32)
            if with_border:
                beside = first + col_sides[pair]
                canvas[beside] = blank
                obj[beside, rows, :] = col_halos[pair][comp].astype(F32)
                for other in range(2):
                    obj[beside, pl.ds(row_sides[other], half), :] = end_halos[pair][
                        comp, other * half : (other + 1) * half, :
                    ].astype(F32)
        if not with_border:
            for j in range(inner):
                canvas[first + 1 + j, 0:half, :] = blank[0:half]
                canvas[first + 1 + j, half + tile :, :] = blank[0:half]

    block = 64
    groups = block // 8
    lane = lax.broadcasted_iota(jnp.int32, (block, LANES), 1)
    blocks = range(0, size, block)

    def place_of(index):
        slot = order[index]
        column = centers[1, slot]
        return slot, centers[0, slot], column >> 7, column & 127

    def cut(index, begin):
        _, row, chunk, offset = place_of(index)
        back_offset = (LANES - offset) & 127
        from_first = lane < LANES - offset
        here = slice(begin, begin + block)
        parts = []
        for comp in range(2):
            moved = [
                pltpu.roll(
                    obj[comp * chunks + chunk + k, pl.ds(row + begin, block), :], back_offset, 1
                )
                for k in range(3)
            ]
            window = jnp.concatenate(
                [
                    jnp.where(from_first, moved[0], moved[1]),
                    jnp.where(from_first, moved[1], moved[2]),
                ],
                1,
            ).astype(BF16).astype(F32)
            patch[index & 1, comp, here, :] = window
            parts.append(window)
        real, imag = parts
        for m in range(modes):
            probe_real = low[2 * m, here, :]
            probe_imag = low[2 * m + 1, here, :]
            there = slice(m * size + begin, m * size + begin + block)
            waves[there, 0:size] = (probe_real * real - probe_imag * imag).astype(BF16)
            waves[there, size:] = (probe_real * imag + probe_imag * real).astype(BF16)

    def forward_right(m, part):
        mode = slice(m * size, (m + 1) * size)
        columns = slice(part * size, (part + 1) * size)
        halves[columns, mode] = jnp.dot(
            waves[mode, :], positive[:, columns], preferred_element_type=F32
        ).astype(BF16)

    def forward_left(k):
        rows_here = slice(k * size, (k + 1) * size)
        spectra[rows_here, :] = jnp.dot(
            left_negative[rows_here, :], halves[...], preferred_element_type=F32
        )

    def reweigh(index, begin):
        slot = order[index]
        k, inside = divmod(begin, half)
        real_rows = slice(k * size + inside, k * size + inside + block)
        imag_rows = slice(k * size + half + inside, k * size + half + inside + block)
        amplitude = patterns[slot, begin : begin + block, :].astype(F32)
        mode_columns = [slice(m * size, (m + 1) * size) for m in range(modes)]
        parts = [(spectra[real_rows, mode], spectra[imag_rows, mode]) for mode in mode_columns]
        power = sum(real * real + imag * imag for real, imag in parts)
        factor = amplitude * lax.rsqrt(jnp.maximum(power, 0.5)) - 1.0
        for m, (real, imag) in enumerate(parts):
            first = k * size + m * half + inside
            there = slice(first, first + block)
            shifts[there, 0:size] = (factor * real).astype(BF16)
            shifts[there, size:] = (factor * imag).astype(BF16)

    def backward_right(k):
        product = jnp.dot(
            shifts[k * size : (k + 1) * size, :], negative[...],
            preferred_element_type=F32,
        ).astype(BF16)
        for m in range(modes):
            mode = slice(m * size, (m + 1) * size)
            for part in range(2):
                first = part * size + k * half
                backs[first : first + half, mode] = product[
                    m * half : (m + 1) * half, part * size : (part + 1) * size
                ]

    def backward_left(m, part):
        mode = slice(m * size, (m + 1) * size)
        rows_here = slice(part * size, (part + 1) * size)
        changes[rows_here, mode] = jnp.dot(
            positive[rows_here, :], backs[:, mode], preferred_element_type=F32
        )

    def deposit(index, buffer, begin):
        _, row, chunk, offset = place_of(index)
        past = lane >= offset
        here = slice(begin, begin + block)
        below = slice(size + begin, size + begin + block)
        start = begin // 8
        obj_real = patch[buffer, 0, here, :]
        obj_imag = patch[buffer, 1, here, :]

        def add(plane, value):
            sums[start : start + groups, plane] += value.reshape(groups, 8, size)

        add(2 * modes, obj_real * obj_real + obj_imag * obj_imag)
        term_real = term_imag = None
        for m in range(modes):
            mode = slice(m * size, (m + 1) * size)
            real = changes[here, mode]
            imag = changes[below, mode]
            probe_real = low[2 * m, here, :]
            probe_imag = low[2 * m + 1, here, :]
            more_real = probe_real * real + probe_imag * imag
            more_imag = probe_real * imag - probe_imag * real
            term_real = more_real if m == 0 else term_real + more_real
            term_imag = more_imag if m == 0 else term_imag + more_imag
            add(2 * m, obj_real * real + obj_imag * imag)
            add(2 * m + 1, obj_real * imag - obj_imag * real)
        for comp, term in enumerate((term_real, term_imag)):
            term = term.astype(BF16).astype(F32) * scale
            first = pltpu.roll(term[:, 0:LANES], offset, 1)
            second = pltpu.roll(term[:, LANES:], offset, 1)
            place = comp * chunks + chunk
            window = pl.ds(row + begin, block)
            values = [canvas[place + k, window, :] for k in range(3)]
            canvas[place, window, :] = values[0] + jnp.where(past, first, 0.0)
            canvas[place + 1, window, :] = values[1] + jnp.where(past, second, first)
            canvas[place + 2, window, :] = values[2] + jnp.where(past, 0.0, second)

    def step(index, carry):
        pattern_copy(order[index]).wait()
        previous = jnp.maximum(index - 1, 0)
        following = jnp.minimum(index + 1, found - 1)
        buffer = (index + 1) & 1
        starts = list(blocks)
        for m in range(modes):
            for part in range(2):
                forward_right(m, part)
                deposit(previous, buffer, starts[2 * m + part])
        forward_left(0)
        forward_left(1)
        for begin in starts[:2]:
            reweigh(index, begin)
        backward_right(0)
        for begin in starts[2:]:
            reweigh(index, begin)
        cut(following, starts[0])
        backward_right(1)
        cut(following, starts[1])
        backward_left(0, 0)
        cut(following, starts[2])
        backward_left(0, 1)
        cut(following, starts[3])
        backward_left(1, 0)
        backward_left(1, 1)
        return carry

    for copy in obj_copies:
        copy.wait()

    @pl.when(found > 0)
    def _():
        for begin in blocks:
            cut(0, begin)

    if not with_border:
        for comp, j in pieces:
            index = comp * chunks + 1 + j
            canvas[index, rows, :] = obj[index, rows, :]
    for copy in later:
        copy.wait()

    @pl.when(found > 0)
    def _():
        lax.fori_loop(0, found, step, 0)
        for begin in blocks:
            deposit(found - 1, (found - 1) & 1, begin)

    last_copies = list(out_copies)
    if not with_border:
        last_copies += [
            pltpu.make_async_copy(here, there, sem) for there, here, sem in ring_pieces(ring_out)
        ]
        last_copies += [
            pltpu.make_async_copy(here, there, sem) for there, here, sem in sums_pieces(sums_out)
        ]
    for copy in last_copies:
        copy.start()
    if with_border:
        for pair in range(2):
            g_rows[pair][...] = canvas[:, pl.ds(row_sides[pair], half), :].astype(BF16)
            for comp in range(2):
                beside = comp * chunks + col_sides[pair]
                low_end = half + tile
                g_ends[pair][comp, 0:half] = canvas[beside, half:size, :].astype(BF16)
                g_ends[pair][comp, half:] = canvas[beside, low_end - half : low_end, :].astype(BF16)
                g_mids[pair][comp] = canvas[beside, size : low_end - half, :].astype(BF16)
        core = lax.axis_index("core")
        count_of = kept.shape[0]
        kept[...] = sums[pl.ds(core * count_of, count_of)]
        given[...] = sums[pl.ds((1 - core) * count_of, count_of)]
    for copy in last_copies + through_copies:
        copy.wait()


def run_positions(counts, centers, object_field, patterns, probe_modes, row_halos, border=None):
    size = probe_modes.shape[-1]
    half = size // 2
    modes = probe_modes.shape[0]
    tile = object_field.shape[1]
    inner = tile // LANES
    chunks = inner + 2
    slots = patterns.shape[0]
    positive, negative = dft_tables(size)
    by_quarter = np.arange(2 * size).reshape(2, 2, half).swapaxes(0, 1).reshape(-1)
    tables = [positive, negative, negative[by_quarter]]
    smem = pl.BlockSpec(memory_space=pltpu.SMEM)
    vmem = pl.BlockSpec(memory_space=pltpu.VMEM)
    anywhere = pl.BlockSpec(memory_space=pl.ANY)
    shape = jax.ShapeDtypeStruct
    in_specs = [smem, smem, anywhere, anywhere, vmem] + [anywhere] * 3 + [vmem] * 2
    operands = [counts, centers, object_field, patterns, probe_modes, *tables, *row_halos]
    sums_shape = (size // 8, 2 * modes + 1, 8, size)
    ring_shape = (2, size, tile)
    if border is None:
        out_specs = [anywhere] * 3
        out_shape = [shape(each, F32) for each in (object_field.shape, ring_shape, sums_shape)]
    else:
        in_specs += [vmem] * 4 + [anywhere] * 3
        operands += list(border)
        half_sums = (size // 16,) + sums_shape[1:]
        out_specs = [anywhere] + [vmem] * 8
        out_shape = [
            shape((2, tile, tile), F32),
            shape((2 * chunks, half, LANES), BF16),
            shape((2 * chunks, half, LANES), BF16),
            shape((2, size, LANES), BF16),
            shape((2, size, LANES), BF16),
            shape((2, tile - size, LANES), BF16),
            shape((2, tile - size, LANES), BF16),
            shape(half_sums, F32),
            shape(half_sums, F32),
        ]
    table = pltpu.VMEM((2 * size, 2 * size), BF16)
    products = pltpu.VMEM((2 * size, modes * size), BF16)
    wide = pltpu.VMEM((2 * size, modes * size), F32)
    padded = pltpu.VMEM((2 * chunks, tile + size, LANES), F32)
    dma = pltpu.SemaphoreType.DMA
    return pl.pallas_call(
        functools.partial(positions_kernel, border is not None),
        in_specs=in_specs,
        out_specs=out_specs,
        out_shape=out_shape,
        scratch_shapes=[
            padded,
            padded,
            pltpu.VMEM(patterns.shape, BF16),
            table,
            table,
            table,
            pltpu.VMEM((2 * modes, size, size), F32),
            products,
            products,
            products,
            products,
            wide,
            wide,
            pltpu.VMEM((2, 2, size, size), F32),
            pltpu.VMEM(sums_shape, F32),
            pltpu.SMEM((slots + 1,), jnp.int32),
            dma((2, 2, inner)),
            dma((2, inner)),
            dma((2, 2, inner)),
            dma((slots,)),
            dma((8,)),
            dma((3,)),
        ],
        compiler_params=pltpu.CompilerParams(
            vmem_limit_bytes=(44 if border is None else 40) * 1024 * 1024
        ),
        cost_estimate=pl.CostEstimate(
            flops=slots * 16 * modes * size**3,
            bytes_accessed=24 * 1024 * 1024,
            transcendentals=0,
        ),
        name="border" if border is not None else "interior",
    )(*operands)


def corners_kernel(end_even, end_odd, row_even, row_odd, out_even, out_odd):
    half = row_even.shape[1]
    chunks = row_even.shape[0] // 2
    row_sides = sides(ROW, 2 * half, half)
    col_sides = [offset // LANES for offset in sides(COL, chunks * LANES, half)]
    for pair, (strip, out) in enumerate(((end_even, out_even), (end_odd, out_odd))):
        for other, ring in enumerate((row_even, row_odd)):
            there = pl.ds(row_sides[other], half)
            for comp in range(2):
                extra = ring[comp * chunks + col_sides[pair]].astype(F32)
                out[comp, there, :] = (strip[comp, there, :].astype(F32) + extra).astype(BF16)


def add_corners(g_ends, from_rows):
    vmem = pl.BlockSpec(memory_space=pltpu.VMEM)
    shape = jax.ShapeDtypeStruct(g_ends[0].shape, BF16)
    return pl.pallas_call(
        corners_kernel,
        in_specs=[vmem] * 4,
        out_specs=[vmem] * 2,
        out_shape=[shape, shape],
        compiler_params=pltpu.CompilerParams(vmem_limit_bytes=8 * 1024 * 1024),
        cost_estimate=pl.CostEstimate(
            flops=256 * 1024, bytes_accessed=2 * 1024 * 1024, transcendentals=0
        ),
        name="corners",
    )(*g_ends, *from_rows)


def rims_kernel(
    partial, row_even, row_odd, end_even, end_odd, mid_even, mid_odd, out, row_buffer, col_buffer,
    sems,
):
    tile = partial.shape[1]
    half = row_even.shape[1]
    inner = tile // LANES
    chunks = inner + 2
    middle = tile - 2 * half
    row_sides = sides(ROW, tile, half)
    col_sides = sides(COL, tile, half)
    row_rings = (row_even, row_odd)
    end_sides = sides(ROW, 2 * half, half)
    end_strips = (end_even, end_odd)
    mid_strips = (mid_even, mid_odd)

    def copy(kind, pair, comp, inward):
        if kind == 0:
            here = row_buffer.at[pair, comp]
            place = (comp, pl.ds(row_sides[pair], half), slice(None))
        else:
            here = col_buffer.at[pair, comp]
            place = (comp, pl.ds(half, middle), pl.ds(col_sides[pair], half))
        source, target = (partial.at[place], here) if inward else (here, out.at[place])
        return pltpu.make_async_copy(
            source, target, sems.at[1 - int(inward), 2 * kind + pair, comp]
        )

    everything = [(kind, pair, comp) for kind in range(2) for pair in range(2) for comp in range(2)]
    for piece in everything:
        copy(*piece, True).start()
    for kind, pair, comp in everything:
        copy(kind, pair, comp, True).wait()
        if kind == 0:
            for j in range(inner):
                columns = slice(j * LANES, (j + 1) * LANES)
                ring = row_rings[pair][comp * chunks + 1 + j]
                row_buffer[pair, comp, :, columns] += ring.astype(F32)
            for other in range(2):
                columns = pl.ds(col_sides[other], half)
                strip = end_strips[other][comp, pl.ds(end_sides[pair], half), :]
                row_buffer[pair, comp, :, columns] += strip.astype(F32)
        else:
            col_buffer[pair, comp] += mid_strips[pair][comp].astype(F32)
        copy(kind, pair, comp, False).start()
    for piece in everything:
        copy(*piece, False).wait()


def add_rims(partial, from_rows, from_ends, from_mids):
    tile = partial.shape[1]
    half = from_rows[0].shape[1]
    vmem = pl.BlockSpec(memory_space=pltpu.VMEM)
    anywhere = pl.BlockSpec(memory_space=pl.ANY)
    return pl.pallas_call(
        rims_kernel,
        in_specs=[anywhere] + [vmem] * 6,
        out_specs=anywhere,
        out_shape=jax.ShapeDtypeStruct(partial.shape, F32),
        input_output_aliases={0: 0},
        scratch_shapes=[
            pltpu.VMEM((2, 2, half, tile), F32),
            pltpu.VMEM((2, 2, tile - 2 * half, half), F32),
            pltpu.SemaphoreType.DMA((2, 4, 2)),
        ],
        compiler_params=pltpu.CompilerParams(vmem_limit_bytes=16 * 1024 * 1024),
        cost_estimate=pl.CostEstimate(
            flops=1024 * 1024, bytes_accessed=6 * 1024 * 1024, transcendentals=0
        ),
        name="rims",
    )(partial, *from_rows, *from_ends, *from_mids)


def chip_sums_kernel(kept, received, out):
    out[...] = (kept[...] + received[...]).astype(BF16)


def chip_sums(kept, given):
    vmem = pl.BlockSpec(memory_space=pltpu.VMEM)
    return pl.pallas_call(
        chip_sums_kernel,
        in_specs=[vmem, vmem],
        out_specs=vmem,
        out_shape=jax.ShapeDtypeStruct(kept.shape, BF16),
        compiler_params=pltpu.CompilerParams(vmem_limit_bytes=8 * 1024 * 1024),
        cost_estimate=pl.CostEstimate(
            flops=1024 * 1024, bytes_accessed=2 * 1024 * 1024, transcendentals=0
        ),
        name="chip_sums",
    )(kept, lax.ppermute(given, "core", [(0, 1), (1, 0)]))


def by_device(on_chip):
    devices = lax.axis_size("x") * lax.axis_size("col")
    groups, planes, _, size = on_chip.shape
    share = groups * 8 // devices
    if share < 8:
        on_chip = on_chip.reshape(groups, planes, 8 // share, share, size)
        return jnp.swapaxes(on_chip, 1, 2).reshape(devices, planes, share, size)
    return on_chip.reshape(devices, groups // devices, planes, 8, size)


def first_sums(parts):
    return lax.all_to_all(parts, ("x", "col"), 0, 0, tiled=True)


def update_kernel(received, copies):
    devices = received.shape[0]
    total = received[0].astype(F32)
    for device in range(1, devices):
        total = total + received[device].astype(F32)
    planes = total.shape[0]
    update = (total[: planes - 1] / jnp.sqrt(total[planes - 1])).astype(BF16)
    for device in range(devices):
        copies[device] = update


def shared_update(received):
    devices, planes, share, size = received.shape
    vmem = pl.BlockSpec(memory_space=pltpu.VMEM)
    return pl.pallas_call(
        update_kernel,
        in_specs=[vmem],
        out_specs=vmem,
        out_shape=jax.ShapeDtypeStruct((devices, planes - 1, share, size), BF16),
        compiler_params=pltpu.CompilerParams(vmem_limit_bytes=8 * 1024 * 1024),
        cost_estimate=pl.CostEstimate(
            flops=512 * 1024, bytes_accessed=1024 * 1024, transcendentals=0
        ),
        name="update",
    )(received)


def finish_kernel(probe, mine, other, out):
    core = lax.axis_index("core")
    groups, planes, height, _ = mine.shape
    for side, update in enumerate((mine, other)):
        first = jnp.where(core == side, 0, groups * height)
        for group in range(groups):
            place = pl.ds(pl.multiple_of(first + group * height, height), height)
            for plane in range(planes):
                m, comp = divmod(plane, 2)
                out[m, comp, place, :] = probe[m, comp, place, :] + update[group, plane].astype(F32)


def finish_probe(probe_modes, mine):
    devices, planes, share, size = mine.shape
    if share < 8:
        mine = mine.reshape(devices * share // 8, 8 // share, planes, share, size)
        mine = jnp.swapaxes(mine, 1, 2).reshape(-1, planes, 8, size)
    other = lax.ppermute(mine, "core", [(0, 1), (1, 0)])
    vmem = pl.BlockSpec(memory_space=pltpu.VMEM)
    return pl.pallas_call(
        finish_kernel,
        in_specs=[vmem] * 3,
        out_specs=vmem,
        out_shape=jax.ShapeDtypeStruct(probe_modes.shape, F32),
        compiler_params=pltpu.CompilerParams(vmem_limit_bytes=8 * 1024 * 1024),
        cost_estimate=pl.CostEstimate(
            flops=256 * 1024, bytes_accessed=3 * 1024 * 1024, transcendentals=0
        ),
        name="finish",
    )(probe_modes, mine, other)


def on_device(object_field, probe_modes, counts, centers, patterns):
    half = probe_modes.shape[-1] // 2

    col_even, col_odd, row_even, row_odd = cut_strips(object_field, half)
    row_halos = (swap_pairs(row_even, ROW, 0), swap_pairs(row_odd, ROW, 1))
    col_halos = (swap_pairs(col_even, COL, 0), swap_pairs(col_odd, COL, 1))
    is_even = (lax.axis_index("col") & 1) == 0
    first_ends = jnp.concatenate([halo[:, :, :half] for halo in row_halos], 1)
    last_ends = jnp.concatenate([halo[:, :, -half:] for halo in row_halos], 1)
    end_halos = (
        swap_pairs(jnp.where(is_even, last_ends, first_ends), COL, 0),
        swap_pairs(jnp.where(is_even, first_ends, last_ends), COL, 1),
    )

    inputs = (counts, centers[0, 0], object_field, patterns[0, 0], probe_modes, row_halos)
    started = run_positions(*inputs)
    border = (*col_halos, *end_halos, *started)
    partial, *rims, kept, given = run_positions(*inputs, border)
    g_row_even, g_row_odd, g_end_even, g_end_odd, g_mid_even, g_mid_odd = rims

    from_mids = (swap_pairs(g_mid_even, COL, 0), swap_pairs(g_mid_odd, COL, 1))
    from_rows = (swap_pairs(g_row_even, ROW, 0), swap_pairs(g_row_odd, ROW, 1))
    to_even, to_odd = add_corners((g_end_even, g_end_odd), from_rows)
    received = first_sums(by_device(chip_sums(kept, given)))
    received, from_mids, to_even, to_odd = lax.optimization_barrier(
        (received, from_mids, to_even, to_odd)
    )
    from_ends = (swap_pairs(to_even, COL, 0), swap_pairs(to_odd, COL, 1))
    if received.ndim == 5:
        received = received[:, 0]
    mine = lax.all_to_all(shared_update(received), ("x", "col"), 0, 0, tiled=True)
    new_object = add_rims(partial, from_rows, from_ends, from_mids)
    mine, new_object = lax.optimization_barrier((mine, new_object))
    return (new_object, finish_probe(probe_modes, mine))


def solution(mesh):
    rows, columns = mesh.devices.shape
    split = jax.sharding.Mesh(
        mesh.devices.reshape(rows // 2, 2, columns), ("x", "core", "col")
    )
    placed = (
        P(None, ROW, "col"),
        P(),
        P(),
        P(ROW, "col", None, None),
        P(ROW, "col", None, None, None),
    )
    return jax.shard_map(
        on_device,
        mesh=split,
        in_specs=placed,
        out_specs=(P(None, ROW, "col"), P()),
        check_vma=False,
    )
```

```python
import functools
import math

import jax
import jax.numpy as jnp
import ml_dtypes
import numpy as np
from jax import lax
from jax.experimental import pallas as pl
from jax.experimental.pallas import tpu as pltpu
from jax.sharding import PartitionSpec as P

LANES = 128
ROW = ("x", "core")
COL = ("col",)
F32 = jnp.float32
BF16 = jnp.bfloat16


def dft_tables(length):
    indices = np.arange(length)
    angles = (indices[:, None] * indices[None, :] % length) * (2.0 * np.pi / length)
    scale = 1.0 / np.sqrt(length)
    cosine = (np.cos(angles) * scale).astype(np.float32).astype(ml_dtypes.bfloat16)
    sine = (np.sin(angles) * scale).astype(np.float32).astype(ml_dtypes.bfloat16)
    return np.stack([cosine, sine, -sine])


def swap_pairs(array, axis, odd):
    devices = math.prod(lax.axis_size(name) for name in axis)
    firsts = range(odd, devices - 1, 2)
    return lax.ppermute(
        array, axis, [(i, i + 1) for i in firsts] + [(i + 1, i) for i in firsts]
    )


def sides(axis, length, width):
    even = (lax.axis_index(axis) & 1) == 0
    far = length - width
    return [
        pl.multiple_of(jnp.where(even, far, 0), width),
        pl.multiple_of(jnp.where(even, 0, far), width),
    ]


def strips_kernel(obj_hbm, col_even, col_odd, row_even, row_odd, col_buffer, row_buffer, sems):
    tile = obj_hbm.shape[1]
    half = row_even.shape[1]
    copies = []
    for pair in range(2):
        column = sides(COL, tile, half)[pair]
        row = sides(ROW, tile, half)[pair]
        copies.append(
            pltpu.make_async_copy(
                obj_hbm.at[:, :, pl.ds(column, half)], col_buffer.at[pair], sems.at[0, pair]
            )
        )
        copies.append(
            pltpu.make_async_copy(
                obj_hbm.at[:, pl.ds(row, half), :], row_buffer.at[pair], sems.at[1, pair]
            )
        )
    for copy in copies:
        copy.start()
    outputs = (col_even, row_even, col_odd, row_odd)
    buffers = (col_buffer, row_buffer) * 2
    for index, copy in enumerate(copies):
        copy.wait()
        outputs[index][...] = buffers[index][index // 2].astype(BF16)


def cut_strips(object_field, half):
    tile = object_field.shape[1]
    vmem = pl.BlockSpec(memory_space=pltpu.VMEM)
    columns = jax.ShapeDtypeStruct((2, tile, half), BF16)
    rows = jax.ShapeDtypeStruct((2, half, tile), BF16)
    return pl.pallas_call(
        strips_kernel,
        in_specs=[pl.BlockSpec(memory_space=pltpu.HBM)],
        out_specs=[vmem] * 4,
        out_shape=[columns, columns, rows, rows],
        scratch_shapes=[
            pltpu.VMEM((2, 2, tile, half), F32),
            pltpu.VMEM((2, 2, half, tile), F32),
            pltpu.SemaphoreType.DMA((2, 2)),
        ],
        compiler_params=pltpu.CompilerParams(vmem_limit_bytes=60 * 1024 * 1024),
        cost_estimate=pl.CostEstimate(
            flops=1024 * 1024, bytes_accessed=5 * 1024 * 1024, transcendentals=0
        ),
        name="strips",
    )(object_field)


def positions_kernel(with_border, *refs):
    counts, centers, obj_hbm, pat_hbm, probe = refs[:5]
    tables, row_halos = refs[5], refs[6:8]
    refs = refs[8:]
    if with_border:
        col_halos, end_halos = refs[0:2], refs[2:4]
        start_hbm, ring_in, sums_in = refs[4:7]
        out_hbm, g_rows, g_ends, g_mids = refs[7], refs[8:10], refs[10:12], refs[12:14]
        kept = refs[14]
        refs = refs[15:]
    else:
        out_hbm, ring_out, sums_out = refs[:3]
        refs = refs[3:]
    (obj, canvas, patterns, positive, negative, left_negative, low, waves, shifts, halves, backs,
     spectra, changes, patch, sums, order, piece_sems, out_sems, ring_sems, pat_sems,
     sums_sems) = refs
    size = probe.shape[-1]
    half = size // 2
    tile = obj_hbm.shape[1]
    inner = tile // LANES
    chunks = inner + 2
    modes = probe.shape[0]
    rows = slice(half, half + tile)
    near = [0, 1, inner - 2, inner - 1] if with_border else list(range(inner))
    pieces = [(comp, j) for comp in range(2) for j in near]

    def home(array, comp, j):
        return array.at[comp, :, pl.ds(j * LANES, LANES)]

    def held(array, comp, j):
        return array.at[comp * chunks + 1 + j, pl.ds(half, tile), :]

    def ring_pieces(array):
        for comp in range(2):
            for side, row in enumerate((0, half + tile)):
                yield (
                    array.at[pl.ds(comp * inner, inner), pl.ds(side * half, half), :],
                    canvas.at[pl.ds(comp * chunks + 1, inner), pl.ds(row, half), :],
                    ring_sems.at[side, comp],
                )

    def sums_pieces(array):
        step = array.shape[0] // sums_parts
        for part in range(sums_parts):
            here = pl.ds(part * step, step)
            yield array.at[here], sums.at[here], sums_sems.at[part]

    sums_parts = sums_sems.shape[0]
    obj_copies = [
        pltpu.make_async_copy(home(obj_hbm, *p), held(obj, *p), piece_sems.at[0, *p])
        for p in pieces
    ]
    out_copies = [
        pltpu.make_async_copy(held(canvas, *p), home(out_hbm, *p), out_sems.at[p]) for p in pieces
    ]
    later = []
    if with_border:
        later += [
            pltpu.make_async_copy(home(start_hbm, *p), held(canvas, *p), piece_sems.at[1, *p])
            for p in pieces
        ]
        later += [pltpu.make_async_copy(*each) for each in ring_pieces(ring_in)]
        later += [pltpu.make_async_copy(*each) for each in sums_pieces(sums_in)]
    for copy in obj_copies + later:
        copy.start()

    order[0] = 0
    count = counts[lax.axis_index(ROW), lax.axis_index("col")]

    def pattern_copy(slot):
        return pltpu.make_async_copy(pat_hbm.at[slot], patterns.at[slot], pat_sems.at[slot])

    def note(slot, found):
        column = centers[1, slot]
        inside = (column >= half) & (column <= tile - half)
        order[found] = slot
        return found + jnp.where(inside, 0 if with_border else 1, 1 if with_border else 0)

    def fetch(index, carry):
        pattern_copy(order[index]).start()
        return carry

    found = lax.fori_loop(0, count, note, 0)
    lax.fori_loop(0, found, fetch, 0)

    if not with_border:
        sums[...] = jnp.zeros_like(sums)
    intensity = jnp.zeros((size, size), F32)
    for m in range(modes):
        for comp in range(2):
            values = probe[m, comp]
            intensity = intensity + values * values
            low[2 * m + comp] = values.astype(BF16).astype(F32)
    scale = 1.0 / (jnp.max(intensity) + 1e-06)
    for turn, inverse in ((positive, True), (negative, False)):
        upper, lower = (2, 1) if inverse else (1, 2)
        turn[0:size, 0:size] = tables[0]
        turn[0:size, size:] = tables[upper]
        turn[size:, 0:size] = tables[lower]
        turn[size:, size:] = tables[0]
    for k in range(2):
        rows_here = slice(k * half, (k + 1) * half)
        first = k * size
        left_negative[first : first + half, 0:size] = tables[0, rows_here]
        left_negative[first : first + half, size:] = tables[1, rows_here]
        left_negative[first + half : first + size, 0:size] = tables[2, rows_here]
        left_negative[first + half : first + size, size:] = tables[0, rows_here]
    changes[...] = jnp.zeros_like(changes)
    patch[...] = jnp.zeros_like(patch)

    row_sides = sides(ROW, tile + size, half)
    col_sides = [offset // LANES for offset in sides(COL, tile + size, half)]
    blank = jnp.zeros((tile + size, LANES), F32)
    for comp in range(2):
        first = comp * chunks
        for pair in range(2):
            for j in near:
                columns = slice(j * LANES, (j + 1) * LANES)
                obj[first + 1 + j, pl.ds(row_sides[pair], half), :] = row_halos[pair][
                    comp, :, columns
                ].astype(F32)
            if with_border:
                beside = first + col_sides[pair]
                canvas[beside] = blank
                obj[beside, rows, :] = col_halos[pair][comp].astype(F32)
                for other in range(2):
                    obj[beside, pl.ds(row_sides[other], half), :] = end_halos[pair][
                        comp, other * half : (other + 1) * half, :
                    ].astype(F32)
        if not with_border:
            for j in range(inner):
                canvas[first + 1 + j, 0:half, :] = blank[0:half]
                canvas[first + 1 + j, half + tile :, :] = blank[0:half]

    block = 16
    groups = block // 8
    lane = lax.broadcasted_iota(jnp.int32, (block, LANES), 1)
    blocks = range(0, size, block)

    def place_of(index):
        slot = order[index]
        column = centers[1, slot]
        return slot, centers[0, slot], column >> 7, column & 127

    def cut(index, begin):
        _, row, chunk, offset = place_of(index)
        back_offset = (LANES - offset) & 127
        from_first = lane < LANES - offset
        here = slice(begin, begin + block)
        parts = []
        for comp in range(2):
            moved = [
                pltpu.roll(
                    obj[comp * chunks + chunk + k, pl.ds(row + begin, block), :], back_offset, 1
                )
                for k in range(3)
            ]
            window = jnp.concatenate(
                [
                    jnp.where(from_first, moved[0], moved[1]),
                    jnp.where(from_first, moved[1], moved[2]),
                ],
                1,
            ).astype(BF16).astype(F32)
            patch[index & 1, comp, here, :] = window
            parts.append(window)
        real, imag = parts
        for m in range(modes):
            probe_real = low[2 * m, here, :]
            probe_imag = low[2 * m + 1, here, :]
            there = slice(m * size + begin, m * size + begin + block)
            waves[there, 0:size] = (probe_real * real - probe_imag * imag).astype(BF16)
            waves[there, size:] = (probe_real * imag + probe_imag * real).astype(BF16)

    def forward_right(m, part):
        mode = slice(m * size, (m + 1) * size)
        columns = slice(part * size, (part + 1) * size)
        halves[columns, mode] = jnp.dot(
            waves[mode, :], positive[:, columns], preferred_element_type=F32
        ).astype(BF16)

    def forward_left(k):
        rows_here = slice(k * size, (k + 1) * size)
        spectra[rows_here, :] = jnp.dot(
            left_negative[rows_here, :], halves[...], preferred_element_type=F32
        )

    def reweigh(index, begin):
        slot = order[index]
        k, inside = divmod(begin, half)
        real_rows = slice(k * size + inside, k * size + inside + block)
        imag_rows = slice(k * size + half + inside, k * size + half + inside + block)
        amplitude = patterns[slot, begin : begin + block, :].astype(F32)
        mode_columns = [slice(m * size, (m + 1) * size) for m in range(modes)]
        parts = [(spectra[real_rows, mode], spectra[imag_rows, mode]) for mode in mode_columns]
        power = sum(real * real + imag * imag for real, imag in parts)
        factor = amplitude * lax.rsqrt(jnp.maximum(power, 0.5)) - 1.0
        for m, (real, imag) in enumerate(parts):
            first = k * size + m * half + inside
            there = slice(first, first + block)
            shifts[there, 0:size] = (factor * real).astype(BF16)
            shifts[there, size:] = (factor * imag).astype(BF16)

    def backward_right(k):
        product = jnp.dot(
            shifts[k * size : (k + 1) * size, :], negative[...],
            preferred_element_type=F32,
        ).astype(BF16)
        for m in range(modes):
            mode = slice(m * size, (m + 1) * size)
            for part in range(2):
                first = part * size + k * half
                backs[first : first + half, mode] = product[
                    m * half : (m + 1) * half, part * size : (part + 1) * size
                ]

    def backward_left(m, part):
        mode = slice(m * size, (m + 1) * size)
        rows_here = slice(part * size, (part + 1) * size)
        changes[rows_here, mode] = jnp.dot(
            positive[rows_here, :], backs[:, mode], preferred_element_type=F32
        )

    def deposit(index, buffer, begin):
        _, row, chunk, offset = place_of(index)
        past = lane >= offset
        here = slice(begin, begin + block)
        below = slice(size + begin, size + begin + block)
        start = begin // 8
        obj_real = patch[buffer, 0, here, :]
        obj_imag = patch[buffer, 1, here, :]

        def add(plane, value):
            sums[start : start + groups, plane] += value.reshape(groups, 8, size)

        add(2 * modes, obj_real * obj_real + obj_imag * obj_imag)
        term_real = term_imag = None
        for m in range(modes):
            mode = slice(m * size, (m + 1) * size)
            real = changes[here, mode]
            imag = changes[below, mode]
            probe_real = low[2 * m, here, :]
            probe_imag = low[2 * m + 1, here, :]
            more_real = probe_real * real + probe_imag * imag
            more_imag = probe_real * imag - probe_imag * real
            term_real = more_real if m == 0 else term_real + more_real
            term_imag = more_imag if m == 0 else term_imag + more_imag
            add(2 * m, obj_real * real + obj_imag * imag)
            add(2 * m + 1, obj_real * imag - obj_imag * real)
        for comp, term in enumerate((term_real, term_imag)):
            term = term.astype(BF16).astype(F32) * scale
            first = pltpu.roll(term[:, 0:LANES], offset, 1)
            second = pltpu.roll(term[:, LANES:], offset, 1)
            place = comp * chunks + chunk
            window = pl.ds(row + begin, block)
            values = [canvas[place + k, window, :] for k in range(3)]
            canvas[place, window, :] = values[0] + jnp.where(past, first, 0.0)
            canvas[place + 1, window, :] = values[1] + jnp.where(past, second, first)
            canvas[place + 2, window, :] = values[2] + jnp.where(past, 0.0, second)

    def step(index, carry):
        pattern_copy(order[index]).wait()
        previous = jnp.maximum(index - 1, 0)
        following = jnp.minimum(index + 1, found - 1)
        buffer = (index + 1) & 1
        starts = list(blocks)
        quarter = len(starts) // 4
        quarters = [starts[i * quarter : (i + 1) * quarter] for i in range(4)]
        for m in range(modes):
            for part in range(2):
                forward_right(m, part)
                for begin in quarters[2 * m + part]:
                    deposit(previous, buffer, begin)
        forward_left(0)
        forward_left(1)
        for begin in quarters[0] + quarters[1]:
            reweigh(index, begin)
        backward_right(0)
        for begin in quarters[2] + quarters[3]:
            reweigh(index, begin)
        for begin in quarters[0]:
            cut(following, begin)
        backward_right(1)
        for begin in quarters[1]:
            cut(following, begin)
        backward_left(0, 0)
        for begin in quarters[2]:
            cut(following, begin)
        backward_left(0, 1)
        for begin in quarters[3]:
            cut(following, begin)
        backward_left(1, 0)
        backward_left(1, 1)
        return carry

    for copy in obj_copies:
        copy.wait()

    @pl.when(found > 0)
    def _():
        for begin in blocks:
            cut(0, begin)

    if not with_border:
        for comp, j in pieces:
            index = comp * chunks + 1 + j
            canvas[index, rows, :] = obj[index, rows, :]
    for copy in later:
        copy.wait()

    @pl.when(found > 0)
    def _():
        lax.fori_loop(0, found, step, 0)
        for begin in blocks:
            deposit(found - 1, (found - 1) & 1, begin)

    last_copies = list(out_copies)
    if not with_border:
        last_copies += [
            pltpu.make_async_copy(here, there, sem) for there, here, sem in ring_pieces(ring_out)
        ]
        last_copies += [
            pltpu.make_async_copy(here, there, sem) for there, here, sem in sums_pieces(sums_out)
        ]
    for copy in last_copies:
        copy.start()
    if with_border:
        for pair in range(2):
            g_rows[pair][0 : 2 * chunks] = canvas[:, pl.ds(row_sides[pair], half), :].astype(BF16)
            for comp in range(2):
                beside = comp * chunks + col_sides[pair]
                low_end = half + tile
                g_ends[pair][comp, 0:half] = canvas[beside, half:size, :].astype(BF16)
                g_ends[pair][comp, half:] = canvas[beside, low_end - half : low_end, :].astype(BF16)
                g_mids[pair][comp] = canvas[beside, size : low_end - half, :].astype(BF16)
        core = lax.axis_index("core")
        count_of = kept.shape[0]
        kept[...] = sums[pl.ds(core * count_of, count_of)]
        for plane in range(2 * modes + 1):
            for side in range(2):
                columns = slice(side * half, (side + 1) * half)
                given = sums[pl.ds((1 - core) * count_of, count_of), plane, :, columns]
                g_rows[0][2 * chunks + 2 * plane + side] = given.reshape(half, LANES).astype(BF16)
    for copy in last_copies:
        copy.wait()


def run_positions(counts, centers, object_field, patterns, probe_modes, row_halos, border=None):
    size = probe_modes.shape[-1]
    half = size // 2
    modes = probe_modes.shape[0]
    tile = object_field.shape[1]
    inner = tile // LANES
    chunks = inner + 2
    slots = patterns.shape[0]
    smem = pl.BlockSpec(memory_space=pltpu.SMEM)
    vmem = pl.BlockSpec(memory_space=pltpu.VMEM)
    anywhere = pl.BlockSpec(memory_space=pl.ANY)
    shape = jax.ShapeDtypeStruct
    in_specs = [smem, smem, anywhere, anywhere] + [vmem] * 4
    operands = [counts, centers, object_field, patterns, probe_modes, dft_tables(size), *row_halos]
    sums_shape = (size // 8, 2 * modes + 1, 8, size)
    ring_shape = (2 * inner, size, LANES)
    aliases = {}
    if border is None:
        out_specs = [anywhere] * 3
        out_shape = [shape(each, F32) for each in (object_field.shape, ring_shape, sums_shape)]
    else:
        aliases = {len(operands) + 4: 0}
        in_specs += [vmem] * 4 + [anywhere] * 3
        operands += list(border)
        half_sums = (size // 16,) + sums_shape[1:]
        out_specs = [anywhere] + [vmem] * 7
        out_shape = [
            shape((2, tile, tile), F32),
            shape((2 * chunks + 4 * modes + 2, half, LANES), BF16),
            shape((2 * chunks, half, LANES), BF16),
            shape((2, size, LANES), BF16),
            shape((2, size, LANES), BF16),
            shape((2, tile - size, LANES), BF16),
            shape((2, tile - size, LANES), BF16),
            shape(half_sums, F32),
        ]
    table = pltpu.VMEM((2 * size, 2 * size), BF16)
    products = pltpu.VMEM((2 * size, modes * size), BF16)
    wide = pltpu.VMEM((2 * size, modes * size), F32)
    padded = pltpu.VMEM((2 * chunks, tile + size, LANES), F32)
    dma = pltpu.SemaphoreType.DMA
    return pl.pallas_call(
        functools.partial(positions_kernel, border is not None),
        in_specs=in_specs,
        out_specs=out_specs,
        out_shape=out_shape,
        input_output_aliases=aliases,
        scratch_shapes=[
            padded,
            padded,
            pltpu.VMEM(patterns.shape, BF16),
            table,
            table,
            table,
            pltpu.VMEM((2 * modes, size, size), F32),
            products,
            products,
            products,
            products,
            wide,
            wide,
            pltpu.VMEM((2, 2, size, size), F32),
            pltpu.VMEM(sums_shape, F32),
            pltpu.SMEM((slots + 1,), jnp.int32),
            dma((2, 2, inner)),
            dma((2, inner)),
            dma((2, 2)),
            dma((slots,)),
            dma((4,)),
        ],
        compiler_params=pltpu.CompilerParams(
            vmem_limit_bytes=(44 if border is None else 40) * 1024 * 1024
        ),
        cost_estimate=pl.CostEstimate(
            flops=slots * 16 * modes * size**3,
            bytes_accessed=24 * 1024 * 1024,
            transcendentals=0,
        ),
        name="border" if border is not None else "interior",
    )(*operands)


def corners_kernel(end_even, end_odd, row_even, row_odd, out_even, out_odd):
    half = row_even.shape[1]
    chunks = row_odd.shape[0] // 2
    row_sides = sides(ROW, 2 * half, half)
    col_sides = [offset // LANES for offset in sides(COL, chunks * LANES, half)]
    for pair, (strip, out) in enumerate(((end_even, out_even), (end_odd, out_odd))):
        for other, ring in enumerate((row_even, row_odd)):
            there = pl.ds(row_sides[other], half)
            for comp in range(2):
                extra = ring[comp * chunks + col_sides[pair]].astype(F32)
                out[comp, there, :] = (strip[comp, there, :].astype(F32) + extra).astype(BF16)


def add_corners(g_ends, from_rows):
    vmem = pl.BlockSpec(memory_space=pltpu.VMEM)
    shape = jax.ShapeDtypeStruct(g_ends[0].shape, BF16)
    return pl.pallas_call(
        corners_kernel,
        in_specs=[vmem] * 4,
        out_specs=[vmem] * 2,
        out_shape=[shape, shape],
        compiler_params=pltpu.CompilerParams(vmem_limit_bytes=8 * 1024 * 1024),
        cost_estimate=pl.CostEstimate(
            flops=256 * 1024, bytes_accessed=2 * 1024 * 1024, transcendentals=0
        ),
        name="corners",
    )(*g_ends, *from_rows)


def rims_kernel(
    partial, row_even, row_odd, end_even, end_odd, mid_even, mid_odd, out, row_buffer, col_buffer,
    sems,
):
    tile = partial.shape[1]
    half = row_even.shape[1]
    inner = tile // LANES
    chunks = inner + 2
    middle = tile - 2 * half
    row_sides = sides(ROW, tile, half)
    col_sides = sides(COL, tile, half)
    row_rings = (row_even, row_odd)
    end_sides = sides(ROW, 2 * half, half)
    end_strips = (end_even, end_odd)
    mid_strips = (mid_even, mid_odd)

    def copy(kind, pair, comp, inward):
        if kind == 0:
            here = row_buffer.at[pair, comp]
            place = (comp, pl.ds(row_sides[pair], half), slice(None))
        else:
            here = col_buffer.at[pair, comp]
            place = (comp, pl.ds(half, middle), pl.ds(col_sides[pair], half))
        source, target = (partial.at[place], here) if inward else (here, out.at[place])
        return pltpu.make_async_copy(
            source, target, sems.at[1 - int(inward), 2 * kind + pair, comp]
        )

    everything = [(kind, pair, comp) for kind in range(2) for pair in range(2) for comp in range(2)]
    for piece in everything:
        copy(*piece, True).start()
    for kind, pair, comp in everything:
        copy(kind, pair, comp, True).wait()
        if kind == 0:
            for j in range(inner):
                columns = slice(j * LANES, (j + 1) * LANES)
                ring = row_rings[pair][comp * chunks + 1 + j]
                row_buffer[pair, comp, :, columns] += ring.astype(F32)
            for other in range(2):
                columns = pl.ds(col_sides[other], half)
                strip = end_strips[other][comp, pl.ds(end_sides[pair], half), :]
                row_buffer[pair, comp, :, columns] += strip.astype(F32)
        else:
            col_buffer[pair, comp] += mid_strips[pair][comp].astype(F32)
        copy(kind, pair, comp, False).start()
    for piece in everything:
        copy(*piece, False).wait()


def add_rims(partial, from_rows, from_ends, from_mids):
    tile = partial.shape[1]
    half = from_rows[0].shape[1]
    vmem = pl.BlockSpec(memory_space=pltpu.VMEM)
    anywhere = pl.BlockSpec(memory_space=pl.ANY)
    return pl.pallas_call(
        rims_kernel,
        in_specs=[anywhere] + [vmem] * 6,
        out_specs=anywhere,
        out_shape=jax.ShapeDtypeStruct(partial.shape, F32),
        input_output_aliases={0: 0},
        scratch_shapes=[
            pltpu.VMEM((2, 2, half, tile), F32),
            pltpu.VMEM((2, 2, tile - 2 * half, half), F32),
            pltpu.SemaphoreType.DMA((2, 4, 2)),
        ],
        compiler_params=pltpu.CompilerParams(vmem_limit_bytes=16 * 1024 * 1024),
        cost_estimate=pl.CostEstimate(
            flops=1024 * 1024, bytes_accessed=6 * 1024 * 1024, transcendentals=0
        ),
        name="rims",
    )(partial, *from_rows, *from_ends, *from_mids)


def chip_sums_kernel(kept, received, out):
    groups, planes, height, size = kept.shape
    half = received.shape[1]
    first = received.shape[0] - 2 * planes
    for plane in range(planes):
        for side in range(2):
            columns = slice(side * half, (side + 1) * half)
            other = received[first + 2 * plane + side].astype(F32).reshape(groups, height, half)
            out[:, plane, :, columns] = (kept[:, plane, :, columns] + other).astype(BF16)


def chip_sums(kept, received):
    vmem = pl.BlockSpec(memory_space=pltpu.VMEM)
    return pl.pallas_call(
        chip_sums_kernel,
        in_specs=[vmem, vmem],
        out_specs=vmem,
        out_shape=jax.ShapeDtypeStruct(kept.shape, BF16),
        compiler_params=pltpu.CompilerParams(vmem_limit_bytes=8 * 1024 * 1024),
        cost_estimate=pl.CostEstimate(
            flops=32 * 1024**3, bytes_accessed=32 * 1024 * 1024, transcendentals=0
        ),
        name="chip_sums",
    )(kept, received)


def by_device(on_chip):
    devices = lax.axis_size("x") * lax.axis_size("col")
    groups, planes, _, size = on_chip.shape
    share = groups * 8 // devices
    if share < 8:
        on_chip = on_chip.reshape(groups, planes, 8 // share, share, size)
        return jnp.swapaxes(on_chip, 1, 2).reshape(devices, planes, share, size)
    return on_chip.reshape(devices, groups // devices, planes, 8, size)


def first_sums(parts):
    return lax.all_to_all(parts, ("x", "col"), 0, 0, tiled=True)


def update_kernel(received, copies):
    devices = received.shape[0]
    total = received[0].astype(F32)
    for device in range(1, devices):
        total = total + received[device].astype(F32)
    planes = total.shape[0]
    update = (total[: planes - 1] / jnp.sqrt(total[planes - 1])).astype(BF16)
    for device in range(devices):
        copies[device] = update


def shared_update(received):
    devices, planes, share, size = received.shape
    vmem = pl.BlockSpec(memory_space=pltpu.VMEM)
    return pl.pallas_call(
        update_kernel,
        in_specs=[vmem],
        out_specs=vmem,
        out_shape=jax.ShapeDtypeStruct((devices, planes - 1, share, size), BF16),
        compiler_params=pltpu.CompilerParams(vmem_limit_bytes=8 * 1024 * 1024),
        cost_estimate=pl.CostEstimate(
            flops=512 * 1024, bytes_accessed=1024 * 1024, transcendentals=0
        ),
        name="update",
    )(received)


def finish_kernel(probe, mine, other, out):
    core = lax.axis_index("core")
    groups, planes, height, _ = mine.shape
    for side, update in enumerate((mine, other)):
        first = jnp.where(core == side, 0, groups * height)
        for group in range(groups):
            place = pl.ds(pl.multiple_of(first + group * height, height), height)
            for plane in range(planes):
                m, comp = divmod(plane, 2)
                out[m, comp, place, :] = probe[m, comp, place, :] + update[group, plane].astype(F32)


def finish_probe(probe_modes, mine):
    devices, planes, share, size = mine.shape
    if share < 8:
        mine = mine.reshape(devices * share // 8, 8 // share, planes, share, size)
        mine = jnp.swapaxes(mine, 1, 2).reshape(-1, planes, 8, size)
    other = lax.ppermute(mine, "core", [(0, 1), (1, 0)])
    vmem = pl.BlockSpec(memory_space=pltpu.VMEM)
    return pl.pallas_call(
        finish_kernel,
        in_specs=[vmem] * 3,
        out_specs=vmem,
        out_shape=jax.ShapeDtypeStruct(probe_modes.shape, F32),
        compiler_params=pltpu.CompilerParams(vmem_limit_bytes=8 * 1024 * 1024),
        cost_estimate=pl.CostEstimate(
            flops=256 * 1024, bytes_accessed=3 * 1024 * 1024, transcendentals=0
        ),
        name="finish",
    )(probe_modes, mine, other)


def on_device(object_field, probe_modes, counts, centers, patterns):
    half = probe_modes.shape[-1] // 2

    col_even, col_odd, row_even, row_odd = cut_strips(object_field, half)
    row_even, go_on = lax.optimization_barrier((row_even, counts[0, 0] > 0))
    row_halos = (swap_pairs(row_even, ROW, 0), swap_pairs(row_odd, ROW, 1))
    col_halos = (swap_pairs(col_even, COL, 0), swap_pairs(col_odd, COL, 1))
    is_even = (lax.axis_index("col") & 1) == 0
    first_ends = jnp.concatenate([halo[:, :, :half] for halo in row_halos], 1)
    last_ends = jnp.concatenate([halo[:, :, -half:] for halo in row_halos], 1)
    end_halos = (
        swap_pairs(jnp.where(is_even, last_ends, first_ends), COL, 0),
        swap_pairs(jnp.where(is_even, first_ends, last_ends), COL, 1),
    )

    inputs = (counts, centers[0, 0], object_field, patterns[0, 0], probe_modes, row_halos)
    started = run_positions(*inputs)
    border = (*col_halos, *end_halos, *started)
    partial, *rims, kept = run_positions(*inputs, border)
    g_row_even, g_row_odd, g_end_even, g_end_odd, g_mid_even, g_mid_odd = rims

    from_rows = (swap_pairs(g_row_even, ROW, 0), swap_pairs(g_row_odd, ROW, 1))
    from_mids = (swap_pairs(g_mid_even, COL, 0), swap_pairs(g_mid_odd, COL, 1))
    received = lax.cond(
        go_on, first_sums, jnp.zeros_like, by_device(chip_sums(kept, from_rows[0]))
    )
    row_odd, _ = lax.optimization_barrier((from_rows[1], received))
    from_rows = (from_rows[0], row_odd)
    to_even, to_odd = add_corners((g_end_even, g_end_odd), from_rows)
    received, from_mids, to_even, to_odd = lax.optimization_barrier(
        (received, from_mids, to_even, to_odd)
    )
    from_ends = (swap_pairs(to_even, COL, 0), swap_pairs(to_odd, COL, 1))
    if received.ndim == 5:
        received = received[:, 0]
    mine = lax.all_to_all(shared_update(received), ("x", "col"), 0, 0, tiled=True)
    new_object = add_rims(partial, from_rows, from_ends, from_mids)
    mine, new_object = lax.optimization_barrier((mine, new_object))
    return (new_object, finish_probe(probe_modes, mine))


def solution(mesh):
    rows, columns = mesh.devices.shape
    split = jax.sharding.Mesh(
        mesh.devices.reshape(rows // 2, 2, columns), ("x", "core", "col")
    )
    placed = (
        P(None, ROW, "col"),
        P(),
        P(),
        P(ROW, "col", None, None),
        P(ROW, "col", None, None, None),
    )
    return jax.shard_map(
        on_device,
        mesh=split,
        in_specs=placed,
        out_specs=(P(None, ROW, "col"), P()),
        check_vma=False,
    )
```

```python
import functools
import math

import jax
import jax.numpy as jnp
import ml_dtypes
import numpy as np
from jax import lax
from jax.experimental import pallas as pl
from jax.experimental.pallas import tpu as pltpu
from jax.sharding import PartitionSpec as P

LANES = 128
ROW = ("x", "core")
COL = ("col",)
F32 = jnp.float32
BF16 = jnp.bfloat16


def dft_tables(length):
    indices = np.arange(length)
    angles = (indices[:, None] * indices[None, :] % length) * (2.0 * np.pi / length)
    scale = 1.0 / np.sqrt(length)
    cosine = (np.cos(angles) * scale).astype(np.float32).astype(ml_dtypes.bfloat16)
    sine = (np.sin(angles) * scale).astype(np.float32).astype(ml_dtypes.bfloat16)
    return np.stack([cosine, sine, -sine])


def swap_pairs(array, axis, odd):
    devices = math.prod(lax.axis_size(name) for name in axis)
    firsts = range(odd, devices - 1, 2)
    return lax.ppermute(
        array, axis, [(i, i + 1) for i in firsts] + [(i + 1, i) for i in firsts]
    )


def sides(axis, length, width):
    even = (lax.axis_index(axis) & 1) == 0
    far = length - width
    return [
        pl.multiple_of(jnp.where(even, far, 0), width),
        pl.multiple_of(jnp.where(even, 0, far), width),
    ]


def strips_kernel(obj_hbm, col_even, col_odd, row_even, row_odd, col_buffer, row_buffer, sems):
    tile = obj_hbm.shape[1]
    half = row_even.shape[1]
    copies = []
    for pair in range(2):
        column = sides(COL, tile, half)[pair]
        row = sides(ROW, tile, half)[pair]
        copies.append(
            pltpu.make_async_copy(
                obj_hbm.at[:, :, pl.ds(column, half)], col_buffer.at[pair], sems.at[0, pair]
            )
        )
        copies.append(
            pltpu.make_async_copy(
                obj_hbm.at[:, pl.ds(row, half), :], row_buffer.at[pair], sems.at[1, pair]
            )
        )
    for copy in copies:
        copy.start()
    outputs = (col_even, row_even, col_odd, row_odd)
    buffers = (col_buffer, row_buffer) * 2
    for index, copy in enumerate(copies):
        copy.wait()
        outputs[index][...] = buffers[index][index // 2].astype(BF16)


def cut_strips(object_field, half):
    tile = object_field.shape[1]
    vmem = pl.BlockSpec(memory_space=pltpu.VMEM)
    columns = jax.ShapeDtypeStruct((2, tile, half), BF16)
    rows = jax.ShapeDtypeStruct((2, half, tile), BF16)
    return pl.pallas_call(
        strips_kernel,
        in_specs=[pl.BlockSpec(memory_space=pltpu.HBM)],
        out_specs=[vmem] * 4,
        out_shape=[columns, columns, rows, rows],
        scratch_shapes=[
            pltpu.VMEM((2, 2, tile, half), F32),
            pltpu.VMEM((2, 2, half, tile), F32),
            pltpu.SemaphoreType.DMA((2, 2)),
        ],
        compiler_params=pltpu.CompilerParams(vmem_limit_bytes=60 * 1024 * 1024),
        cost_estimate=pl.CostEstimate(
            flops=1024 * 1024, bytes_accessed=5 * 1024 * 1024, transcendentals=0
        ),
        name="strips",
    )(object_field)


def positions_kernel(with_border, *refs):
    counts, centers, obj_hbm, pat_hbm, probe = refs[:5]
    tables, row_halos = refs[5], refs[6:8]
    refs = refs[8:]
    if with_border:
        col_halos, end_halos = refs[0:2], refs[2:4]
        start_hbm, ring_in, sums_in = refs[4:7]
        out_hbm, g_rows, g_ends, g_mids = refs[7], refs[8:10], refs[10:12], refs[12:14]
        kept = refs[14]
        refs = refs[15:]
    else:
        out_hbm, ring_out, sums_out = refs[:3]
        refs = refs[3:]
    (obj, canvas, patterns, positive, negative, left_negative, low, waves, shifts, halves, backs,
     spectra, changes, patch, sums, order, piece_sems, out_sems, ring_sems, pat_sems,
     sums_sems) = refs
    size = probe.shape[-1]
    half = size // 2
    tile = obj_hbm.shape[1]
    inner = tile // LANES
    chunks = inner + 2
    modes = probe.shape[0]
    rows = slice(half, half + tile)
    near = [0, 1, inner - 2, inner - 1] if with_border else list(range(inner))
    near_pieces = [(comp, j) for comp in range(2) for j in near]
    pieces = [(comp, j) for comp in range(2) for j in range(inner)]

    def home(array, comp, j):
        return array.at[comp, :, pl.ds(j * LANES, LANES)]

    def held(array, comp, j):
        return array.at[comp * chunks + 1 + j, pl.ds(half, tile), :]

    def ring_pieces(array):
        for comp in range(2):
            for side, row in enumerate((0, half + tile)):
                yield (
                    array.at[pl.ds(comp * inner, inner), pl.ds(side * half, half), :],
                    canvas.at[pl.ds(comp * chunks + 1, inner), pl.ds(row, half), :],
                    ring_sems.at[side, comp],
                )

    def sums_pieces(array):
        step = array.shape[0] // sums_parts
        for part in range(sums_parts):
            here = pl.ds(part * step, step)
            yield array.at[here], sums.at[here], sums_sems.at[part]

    sums_parts = sums_sems.shape[0]
    obj_copies = [
        pltpu.make_async_copy(home(obj_hbm, *p), held(obj, *p), piece_sems.at[0, *p])
        for p in near_pieces
    ]
    out_copies = [
        pltpu.make_async_copy(held(canvas, *p), home(out_hbm, *p), out_sems.at[p]) for p in pieces
    ]
    later = []
    if with_border:
        later += [
            pltpu.make_async_copy(home(start_hbm, *p), held(canvas, *p), piece_sems.at[1, *p])
            for p in pieces
        ]
        later += [pltpu.make_async_copy(*each) for each in ring_pieces(ring_in)]
        later += [pltpu.make_async_copy(*each) for each in sums_pieces(sums_in)]
    for copy in obj_copies + later:
        copy.start()

    order[0] = 0
    count = counts[lax.axis_index(ROW), lax.axis_index("col")]

    def pattern_copy(slot):
        return pltpu.make_async_copy(pat_hbm.at[slot], patterns.at[slot], pat_sems.at[slot])

    def note(slot, found):
        column = centers[1, slot]
        inside = (column >= half) & (column <= tile - half)
        order[found] = slot
        return found + jnp.where(inside, 0 if with_border else 1, 1 if with_border else 0)

    def fetch(index, carry):
        pattern_copy(order[index]).start()
        return carry

    found = lax.fori_loop(0, count, note, 0)
    lax.fori_loop(0, found, fetch, 0)

    if not with_border:
        sums[...] = jnp.zeros_like(sums)
    intensity = jnp.zeros((size, size), F32)
    for m in range(modes):
        for comp in range(2):
            values = probe[m, comp]
            intensity = intensity + values * values
            low[2 * m + comp] = values.astype(BF16).astype(F32)
    scale = 1.0 / (jnp.max(intensity) + 1e-06)
    for turn, inverse in ((positive, True), (negative, False)):
        upper, lower = (2, 1) if inverse else (1, 2)
        turn[0:size, 0:size] = tables[0]
        turn[0:size, size:] = tables[upper]
        turn[size:, 0:size] = tables[lower]
        turn[size:, size:] = tables[0]
    for k in range(2):
        rows_here = slice(k * half, (k + 1) * half)
        first = k * size
        left_negative[first : first + half, 0:size] = tables[0, rows_here]
        left_negative[first : first + half, size:] = tables[1, rows_here]
        left_negative[first + half : first + size, 0:size] = tables[2, rows_here]
        left_negative[first + half : first + size, size:] = tables[0, rows_here]
    changes[...] = jnp.zeros_like(changes)
    patch[...] = jnp.zeros_like(patch)

    row_sides = sides(ROW, tile + size, half)
    col_sides = [offset // LANES for offset in sides(COL, tile + size, half)]
    blank = jnp.zeros((tile + size, LANES), F32)
    for comp in range(2):
        first = comp * chunks
        for pair in range(2):
            for j in near:
                columns = slice(j * LANES, (j + 1) * LANES)
                obj[first + 1 + j, pl.ds(row_sides[pair], half), :] = row_halos[pair][
                    comp, :, columns
                ].astype(F32)
            if with_border:
                beside = first + col_sides[pair]
                canvas[beside] = blank
                obj[beside, rows, :] = col_halos[pair][comp].astype(F32)
                for other in range(2):
                    obj[beside, pl.ds(row_sides[other], half), :] = end_halos[pair][
                        comp, other * half : (other + 1) * half, :
                    ].astype(F32)
        if not with_border:
            for j in range(inner):
                canvas[first + 1 + j, 0:half, :] = blank[0:half]
                canvas[first + 1 + j, half + tile :, :] = blank[0:half]

    block = 16
    groups = block // 8
    lane = lax.broadcasted_iota(jnp.int32, (block, LANES), 1)
    blocks = range(0, size, block)

    def place_of(index):
        slot = order[index]
        column = centers[1, slot]
        return slot, centers[0, slot], column >> 7, column & 127

    def cut(index, begin):
        _, row, chunk, offset = place_of(index)
        back_offset = (LANES - offset) & 127
        from_first = lane < LANES - offset
        here = slice(begin, begin + block)
        parts = []
        for comp in range(2):
            moved = [
                pltpu.roll(
                    obj[comp * chunks + chunk + k, pl.ds(row + begin, block), :], back_offset, 1
                )
                for k in range(3)
            ]
            window = jnp.concatenate(
                [
                    jnp.where(from_first, moved[0], moved[1]),
                    jnp.where(from_first, moved[1], moved[2]),
                ],
                1,
            ).astype(BF16).astype(F32)
            patch[index & 1, comp, here, :] = window
            parts.append(window)
        real, imag = parts
        for m in range(modes):
            probe_real = low[2 * m, here, :]
            probe_imag = low[2 * m + 1, here, :]
            there = slice(m * size + begin, m * size + begin + block)
            waves[there, 0:size] = (probe_real * real - probe_imag * imag).astype(BF16)
            waves[there, size:] = (probe_real * imag + probe_imag * real).astype(BF16)

    def forward_right(m, part):
        mode = slice(m * size, (m + 1) * size)
        columns = slice(part * size, (part + 1) * size)
        halves[columns, mode] = jnp.dot(
            waves[mode, :], positive[:, columns], preferred_element_type=F32
        ).astype(BF16)

    def forward_left(k):
        rows_here = slice(k * size, (k + 1) * size)
        spectra[rows_here, :] = jnp.dot(
            left_negative[rows_here, :], halves[...], preferred_element_type=F32
        )

    def reweigh(index, begin):
        slot = order[index]
        k, inside = divmod(begin, half)
        real_rows = slice(k * size + inside, k * size + inside + block)
        imag_rows = slice(k * size + half + inside, k * size + half + inside + block)
        amplitude = patterns[slot, begin : begin + block, :].astype(F32)
        mode_columns = [slice(m * size, (m + 1) * size) for m in range(modes)]
        parts = [(spectra[real_rows, mode], spectra[imag_rows, mode]) for mode in mode_columns]
        power = sum(real * real + imag * imag for real, imag in parts)
        factor = amplitude * lax.rsqrt(jnp.maximum(power, 0.5)) - 1.0
        for m, (real, imag) in enumerate(parts):
            first = k * size + m * half + inside
            there = slice(first, first + block)
            shifts[there, 0:size] = (factor * real).astype(BF16)
            shifts[there, size:] = (factor * imag).astype(BF16)

    def backward_right(k):
        product = jnp.dot(
            shifts[k * size : (k + 1) * size, :], negative[...],
            preferred_element_type=F32,
        ).astype(BF16)
        for m in range(modes):
            mode = slice(m * size, (m + 1) * size)
            for part in range(2):
                first = part * size + k * half
                backs[first : first + half, mode] = product[
                    m * half : (m + 1) * half, part * size : (part + 1) * size
                ]

    def backward_left(m, part):
        mode = slice(m * size, (m + 1) * size)
        rows_here = slice(part * size, (part + 1) * size)
        changes[rows_here, mode] = jnp.dot(
            positive[rows_here, :], backs[:, mode], preferred_element_type=F32
        )

    def deposit(index, buffer, begin):
        _, row, chunk, offset = place_of(index)
        past = lane >= offset
        here = slice(begin, begin + block)
        below = slice(size + begin, size + begin + block)
        start = begin // 8
        obj_real = patch[buffer, 0, here, :]
        obj_imag = patch[buffer, 1, here, :]

        def add(plane, value):
            sums[start : start + groups, plane] += value.reshape(groups, 8, size)

        add(2 * modes, obj_real * obj_real + obj_imag * obj_imag)
        term_real = term_imag = None
        for m in range(modes):
            mode = slice(m * size, (m + 1) * size)
            real = changes[here, mode]
            imag = changes[below, mode]
            probe_real = low[2 * m, here, :]
            probe_imag = low[2 * m + 1, here, :]
            more_real = probe_real * real + probe_imag * imag
            more_imag = probe_real * imag - probe_imag * real
            term_real = more_real if m == 0 else term_real + more_real
            term_imag = more_imag if m == 0 else term_imag + more_imag
            add(2 * m, obj_real * real + obj_imag * imag)
            add(2 * m + 1, obj_real * imag - obj_imag * real)
        for comp, term in enumerate((term_real, term_imag)):
            term = term.astype(BF16).astype(F32) * scale
            first = pltpu.roll(term[:, 0:LANES], offset, 1)
            second = pltpu.roll(term[:, LANES:], offset, 1)
            place = comp * chunks + chunk
            window = pl.ds(row + begin, block)
            values = [canvas[place + k, window, :] for k in range(3)]
            canvas[place, window, :] = values[0] + jnp.where(past, first, 0.0)
            canvas[place + 1, window, :] = values[1] + jnp.where(past, second, first)
            canvas[place + 2, window, :] = values[2] + jnp.where(past, 0.0, second)

    def step(index, carry):
        pattern_copy(order[index]).wait()
        previous = jnp.maximum(index - 1, 0)
        following = jnp.minimum(index + 1, found - 1)
        buffer = (index + 1) & 1
        starts = list(blocks)
        quarter = len(starts) // 4
        quarters = [starts[i * quarter : (i + 1) * quarter] for i in range(4)]
        for m in range(modes):
            for part in range(2):
                forward_right(m, part)
                for begin in quarters[2 * m + part]:
                    deposit(previous, buffer, begin)
        forward_left(0)
        forward_left(1)
        for begin in quarters[0] + quarters[1]:
            reweigh(index, begin)
        backward_right(0)
        for begin in quarters[2] + quarters[3]:
            reweigh(index, begin)
        for begin in quarters[0]:
            cut(following, begin)
        backward_right(1)
        for begin in quarters[1]:
            cut(following, begin)
        backward_left(0, 0)
        for begin in quarters[2]:
            cut(following, begin)
        backward_left(0, 1)
        for begin in quarters[3]:
            cut(following, begin)
        backward_left(1, 0)
        backward_left(1, 1)
        return carry

    for copy in obj_copies:
        copy.wait()

    @pl.when(found > 0)
    def _():
        for begin in blocks:
            cut(0, begin)

    if not with_border:
        for comp, j in pieces:
            index = comp * chunks + 1 + j
            canvas[index, rows, :] = obj[index, rows, :]
    for copy in later:
        copy.wait()

    @pl.when(found > 0)
    def _():
        lax.fori_loop(0, found, step, 0)
        for begin in blocks:
            deposit(found - 1, (found - 1) & 1, begin)

    last_copies = list(out_copies)
    if not with_border:
        last_copies += [
            pltpu.make_async_copy(here, there, sem) for there, here, sem in ring_pieces(ring_out)
        ]
        last_copies += [
            pltpu.make_async_copy(here, there, sem) for there, here, sem in sums_pieces(sums_out)
        ]
    for copy in last_copies:
        copy.start()
    if with_border:
        for pair in range(2):
            g_rows[pair][0 : 2 * chunks] = canvas[:, pl.ds(row_sides[pair], half), :].astype(BF16)
            for comp in range(2):
                beside = comp * chunks + col_sides[pair]
                low_end = half + tile
                g_ends[pair][comp, 0:half] = canvas[beside, half:size, :].astype(BF16)
                g_ends[pair][comp, half:] = canvas[beside, low_end - half : low_end, :].astype(BF16)
                g_mids[pair][comp] = canvas[beside, size : low_end - half, :].astype(BF16)
        core = lax.axis_index("core")
        count_of = kept.shape[0]
        kept[...] = sums[pl.ds(core * count_of, count_of)]
        for plane in range(2 * modes + 1):
            for side in range(2):
                columns = slice(side * half, (side + 1) * half)
                given = sums[pl.ds((1 - core) * count_of, count_of), plane, :, columns]
                g_rows[0][2 * chunks + 2 * plane + side] = given.reshape(half, LANES).astype(BF16)
    for copy in last_copies:
        copy.wait()


def run_positions(counts, centers, object_field, patterns, probe_modes, row_halos, border=None):
    size = probe_modes.shape[-1]
    half = size // 2
    modes = probe_modes.shape[0]
    tile = object_field.shape[1]
    inner = tile // LANES
    chunks = inner + 2
    slots = patterns.shape[0]
    smem = pl.BlockSpec(memory_space=pltpu.SMEM)
    vmem = pl.BlockSpec(memory_space=pltpu.VMEM)
    anywhere = pl.BlockSpec(memory_space=pl.ANY)
    shape = jax.ShapeDtypeStruct
    in_specs = [smem, smem, anywhere, anywhere] + [vmem] * 4
    operands = [counts, centers, object_field, patterns, probe_modes, dft_tables(size), *row_halos]
    sums_shape = (size // 8, 2 * modes + 1, 8, size)
    ring_shape = (2 * inner, size, LANES)
    if border is None:
        out_specs = [anywhere] * 3
        out_shape = [shape(each, F32) for each in (object_field.shape, ring_shape, sums_shape)]
    else:
        in_specs += [vmem] * 4 + [anywhere] * 3
        operands += list(border)
        half_sums = (size // 16,) + sums_shape[1:]
        out_specs = [anywhere] + [vmem] * 7
        out_shape = [
            shape((2, tile, tile), F32),
            shape((2 * chunks + 4 * modes + 2, half, LANES), BF16),
            shape((2 * chunks, half, LANES), BF16),
            shape((2, size, LANES), BF16),
            shape((2, size, LANES), BF16),
            shape((2, tile - size, LANES), BF16),
            shape((2, tile - size, LANES), BF16),
            shape(half_sums, F32),
        ]
    table = pltpu.VMEM((2 * size, 2 * size), BF16)
    products = pltpu.VMEM((2 * size, modes * size), BF16)
    wide = pltpu.VMEM((2 * size, modes * size), F32)
    padded = pltpu.VMEM((2 * chunks, tile + size, LANES), F32)
    dma = pltpu.SemaphoreType.DMA
    return pl.pallas_call(
        functools.partial(positions_kernel, border is not None),
        in_specs=in_specs,
        out_specs=out_specs,
        out_shape=out_shape,
        scratch_shapes=[
            padded,
            padded,
            pltpu.VMEM(patterns.shape, BF16),
            table,
            table,
            table,
            pltpu.VMEM((2 * modes, size, size), F32),
            products,
            products,
            products,
            products,
            wide,
            wide,
            pltpu.VMEM((2, 2, size, size), F32),
            pltpu.VMEM(sums_shape, F32),
            pltpu.SMEM((slots + 1,), jnp.int32),
            dma((2, 2, inner)),
            dma((2, inner)),
            dma((2, 2)),
            dma((slots,)),
            dma((4,)),
        ],
        compiler_params=pltpu.CompilerParams(
            vmem_limit_bytes=30 * 1024 * 1024
        ),
        cost_estimate=pl.CostEstimate(
            flops=slots * 16 * modes * size**3,
            bytes_accessed=24 * 1024 * 1024,
            transcendentals=0,
        ),
        name="border" if border is not None else "interior",
    )(*operands)


def corners_kernel(end_even, end_odd, row_even, row_odd, out_even, out_odd):
    half = row_even.shape[1]
    chunks = row_odd.shape[0] // 2
    row_sides = sides(ROW, 2 * half, half)
    col_sides = [offset // LANES for offset in sides(COL, chunks * LANES, half)]
    for pair, (strip, out) in enumerate(((end_even, out_even), (end_odd, out_odd))):
        for other, ring in enumerate((row_even, row_odd)):
            there = pl.ds(row_sides[other], half)
            for comp in range(2):
                extra = ring[comp * chunks + col_sides[pair]].astype(F32)
                out[comp, there, :] = (strip[comp, there, :].astype(F32) + extra).astype(BF16)


def add_corners(g_ends, from_rows):
    vmem = pl.BlockSpec(memory_space=pltpu.VMEM)
    shape = jax.ShapeDtypeStruct(g_ends[0].shape, BF16)
    return pl.pallas_call(
        corners_kernel,
        in_specs=[vmem] * 4,
        out_specs=[vmem] * 2,
        out_shape=[shape, shape],
        compiler_params=pltpu.CompilerParams(vmem_limit_bytes=8 * 1024 * 1024),
        cost_estimate=pl.CostEstimate(
            flops=256 * 1024, bytes_accessed=2 * 1024 * 1024, transcendentals=0
        ),
        name="corners",
    )(*g_ends, *from_rows)


def rims_kernel(
    partial, row_even, row_odd, end_even, end_odd, mid_even, mid_odd, out, row_buffer, col_buffer,
    sems,
):
    tile = partial.shape[1]
    half = row_even.shape[1]
    inner = tile // LANES
    chunks = inner + 2
    middle = tile - 2 * half
    row_sides = sides(ROW, tile, half)
    col_sides = sides(COL, tile, half)
    row_rings = (row_even, row_odd)
    end_sides = sides(ROW, 2 * half, half)
    end_strips = (end_even, end_odd)
    mid_strips = (mid_even, mid_odd)

    def copy(kind, pair, comp, inward):
        if kind == 0:
            here = row_buffer.at[pair, comp]
            place = (comp, pl.ds(row_sides[pair], half), slice(None))
        else:
            here = col_buffer.at[pair, comp]
            place = (comp, pl.ds(half, middle), pl.ds(col_sides[pair], half))
        source, target = (partial.at[place], here) if inward else (here, out.at[place])
        return pltpu.make_async_copy(
            source, target, sems.at[1 - int(inward), 2 * kind + pair, comp]
        )

    everything = [(kind, pair, comp) for kind in range(2) for pair in range(2) for comp in range(2)]
    for piece in everything:
        copy(*piece, True).start()
    for kind, pair, comp in everything:
        copy(kind, pair, comp, True).wait()
        if kind == 0:
            for j in range(inner):
                columns = slice(j * LANES, (j + 1) * LANES)
                ring = row_rings[pair][comp * chunks + 1 + j]
                row_buffer[pair, comp, :, columns] += ring.astype(F32)
            for other in range(2):
                columns = pl.ds(col_sides[other], half)
                strip = end_strips[other][comp, pl.ds(end_sides[pair], half), :]
                row_buffer[pair, comp, :, columns] += strip.astype(F32)
        else:
            col_buffer[pair, comp] += mid_strips[pair][comp].astype(F32)
        copy(kind, pair, comp, False).start()
    for piece in everything:
        copy(*piece, False).wait()


def add_rims(partial, from_rows, from_ends, from_mids):
    tile = partial.shape[1]
    half = from_rows[0].shape[1]
    vmem = pl.BlockSpec(memory_space=pltpu.VMEM)
    anywhere = pl.BlockSpec(memory_space=pl.ANY)
    return pl.pallas_call(
        rims_kernel,
        in_specs=[anywhere] + [vmem] * 6,
        out_specs=anywhere,
        out_shape=jax.ShapeDtypeStruct(partial.shape, F32),
        input_output_aliases={0: 0},
        scratch_shapes=[
            pltpu.VMEM((2, 2, half, tile), F32),
            pltpu.VMEM((2, 2, tile - 2 * half, half), F32),
            pltpu.SemaphoreType.DMA((2, 4, 2)),
        ],
        compiler_params=pltpu.CompilerParams(vmem_limit_bytes=16 * 1024 * 1024),
        cost_estimate=pl.CostEstimate(
            flops=1024 * 1024, bytes_accessed=6 * 1024 * 1024, transcendentals=0
        ),
        name="rims",
    )(partial, *from_rows, *from_ends, *from_mids)


def chip_sums_kernel(kept, received, out):
    groups, planes, height, size = kept.shape
    half = received.shape[1]
    first = received.shape[0] - 2 * planes
    for plane in range(planes):
        for side in range(2):
            columns = slice(side * half, (side + 1) * half)
            other = received[first + 2 * plane + side].astype(F32).reshape(groups, height, half)
            out[:, plane, :, columns] = (kept[:, plane, :, columns] + other).astype(BF16)


def chip_sums(kept, received):
    vmem = pl.BlockSpec(memory_space=pltpu.VMEM)
    return pl.pallas_call(
        chip_sums_kernel,
        in_specs=[vmem, vmem],
        out_specs=vmem,
        out_shape=jax.ShapeDtypeStruct(kept.shape, BF16),
        compiler_params=pltpu.CompilerParams(vmem_limit_bytes=8 * 1024 * 1024),
        cost_estimate=pl.CostEstimate(
            flops=32 * 1024**3, bytes_accessed=32 * 1024 * 1024, transcendentals=0
        ),
        name="chip_sums",
    )(kept, received)


def by_device(on_chip):
    devices = lax.axis_size("x") * lax.axis_size("col")
    groups, planes, _, size = on_chip.shape
    share = groups * 8 // devices
    if share < 8:
        on_chip = on_chip.reshape(groups, planes, 8 // share, share, size)
        return jnp.swapaxes(on_chip, 1, 2).reshape(devices, planes, share, size)
    return on_chip.reshape(devices, groups // devices, planes, 8, size)


def first_sums(parts):
    return lax.all_to_all(parts, ("x", "col"), 0, 0, tiled=True)


def update_kernel(received, copies):
    devices = received.shape[0]
    total = received[0].astype(F32)
    for device in range(1, devices):
        total = total + received[device].astype(F32)
    planes = total.shape[0]
    update = (total[: planes - 1] / jnp.sqrt(total[planes - 1])).astype(BF16)
    for device in range(devices):
        copies[device] = update


def shared_update(received):
    devices, planes, share, size = received.shape
    vmem = pl.BlockSpec(memory_space=pltpu.VMEM)
    return pl.pallas_call(
        update_kernel,
        in_specs=[vmem],
        out_specs=vmem,
        out_shape=jax.ShapeDtypeStruct((devices, planes - 1, share, size), BF16),
        compiler_params=pltpu.CompilerParams(vmem_limit_bytes=8 * 1024 * 1024),
        cost_estimate=pl.CostEstimate(
            flops=512 * 1024, bytes_accessed=1024 * 1024, transcendentals=0
        ),
        name="update",
    )(received)


def finish_kernel(probe, mine, other, out):
    core = lax.axis_index("core")
    groups, planes, height, _ = mine.shape
    for side, update in enumerate((mine, other)):
        first = jnp.where(core == side, 0, groups * height)
        for group in range(groups):
            place = pl.ds(pl.multiple_of(first + group * height, height), height)
            for plane in range(planes):
                m, comp = divmod(plane, 2)
                out[m, comp, place, :] = probe[m, comp, place, :] + update[group, plane].astype(F32)


def finish_probe(probe_modes, mine):
    devices, planes, share, size = mine.shape
    if share < 8:
        mine = mine.reshape(devices * share // 8, 8 // share, planes, share, size)
        mine = jnp.swapaxes(mine, 1, 2).reshape(-1, planes, 8, size)
    other = lax.ppermute(mine, "core", [(0, 1), (1, 0)])
    vmem = pl.BlockSpec(memory_space=pltpu.VMEM)
    return pl.pallas_call(
        finish_kernel,
        in_specs=[vmem] * 3,
        out_specs=vmem,
        out_shape=jax.ShapeDtypeStruct(probe_modes.shape, F32),
        compiler_params=pltpu.CompilerParams(vmem_limit_bytes=8 * 1024 * 1024),
        cost_estimate=pl.CostEstimate(
            flops=256 * 1024, bytes_accessed=3 * 1024 * 1024, transcendentals=0
        ),
        name="finish",
    )(probe_modes, mine, other)


def on_device(object_field, probe_modes, counts, centers, patterns):
    half = probe_modes.shape[-1] // 2

    col_even, col_odd, row_even, row_odd = cut_strips(object_field, half)
    go_on = lax.axis_index("col") < 4096
    row_halos = (swap_pairs(row_even, ROW, 0), swap_pairs(row_odd, ROW, 1))
    col_halos = (swap_pairs(col_even, COL, 0), swap_pairs(col_odd, COL, 1))
    is_even = (lax.axis_index("col") & 1) == 0
    first_ends = jnp.concatenate([halo[:, :, :half] for halo in row_halos], 1)
    last_ends = jnp.concatenate([halo[:, :, -half:] for halo in row_halos], 1)
    end_halos = (
        swap_pairs(jnp.where(is_even, last_ends, first_ends), COL, 0),
        swap_pairs(jnp.where(is_even, first_ends, last_ends), COL, 1),
    )

    inputs = (counts, centers[0, 0], object_field, patterns[0, 0], probe_modes, row_halos)
    started = run_positions(*inputs)
    border = (*col_halos, *end_halos, *started)
    partial, *rims, kept = run_positions(*inputs, border)
    g_row_even, g_row_odd, g_end_even, g_end_odd, g_mid_even, g_mid_odd = rims

    from_rows = (swap_pairs(g_row_even, ROW, 0), swap_pairs(g_row_odd, ROW, 1))
    from_mids = (swap_pairs(g_mid_even, COL, 0), swap_pairs(g_mid_odd, COL, 1))
    received = lax.cond(
        go_on, first_sums, jnp.zeros_like, by_device(chip_sums(kept, from_rows[0]))
    )
    row_odd, _ = lax.optimization_barrier((from_rows[1], received))
    from_rows = (from_rows[0], row_odd)
    to_even, to_odd = add_corners((g_end_even, g_end_odd), from_rows)
    received, from_mids, to_even, to_odd = lax.optimization_barrier(
        (received, from_mids, to_even, to_odd)
    )
    from_ends = (swap_pairs(to_even, COL, 0), swap_pairs(to_odd, COL, 1))
    if received.ndim == 5:
        received = received[:, 0]
    mine = lax.all_to_all(shared_update(received), ("x", "col"), 0, 0, tiled=True)
    mine, from_ends, partial = lax.optimization_barrier((mine, from_ends, partial))
    new_object = add_rims(partial, from_rows, from_ends, from_mids)
    return (new_object, finish_probe(probe_modes, mine))


def solution(mesh):
    rows, columns = mesh.devices.shape
    split = jax.sharding.Mesh(
        mesh.devices.reshape(rows // 2, 2, columns), ("x", "core", "col")
    )
    placed = (
        P(None, ROW, "col"),
        P(),
        P(),
        P(ROW, "col", None, None),
        P(ROW, "col", None, None, None),
    )
    return jax.shard_map(
        on_device,
        mesh=split,
        in_specs=placed,
        out_specs=(P(None, ROW, "col"), P()),
        check_vma=False,
    )
```

```python
import functools
import math

import jax
import jax.numpy as jnp
import ml_dtypes
import numpy as np
from jax import lax
from jax.experimental import pallas as pl
from jax.experimental.pallas import tpu as pltpu
from jax.sharding import PartitionSpec as P

LANES = 128
ROW = ("x", "core")
COL = ("col",)
F32 = jnp.float32
BF16 = jnp.bfloat16


def dft_tables(length):
    indices = np.arange(length)
    angles = (indices[:, None] * indices[None, :] % length) * (2.0 * np.pi / length)
    scale = 1.0 / np.sqrt(length)
    cosine = (np.cos(angles) * scale).astype(np.float32).astype(ml_dtypes.bfloat16)
    sine = (np.sin(angles) * scale).astype(np.float32).astype(ml_dtypes.bfloat16)
    return np.stack([cosine, sine, -sine])


def swap_pairs(array, axis, odd):
    devices = math.prod(lax.axis_size(name) for name in axis)
    firsts = range(odd, devices - 1, 2)
    return lax.ppermute(
        array, axis, [(i, i + 1) for i in firsts] + [(i + 1, i) for i in firsts]
    )


def sides(axis, length, width):
    even = (lax.axis_index(axis) & 1) == 0
    far = length - width
    return [
        pl.multiple_of(jnp.where(even, far, 0), width),
        pl.multiple_of(jnp.where(even, 0, far), width),
    ]


def strips_kernel(obj_hbm, col_even, col_odd, row_even, row_odd, col_buffer, row_buffer, sems):
    tile = obj_hbm.shape[1]
    half = row_even.shape[1]
    copies = []
    for pair in range(2):
        column = sides(COL, tile, half)[pair]
        row = sides(ROW, tile, half)[pair]
        copies.append(
            pltpu.make_async_copy(
                obj_hbm.at[:, :, pl.ds(column, half)], col_buffer.at[pair], sems.at[0, pair]
            )
        )
        copies.append(
            pltpu.make_async_copy(
                obj_hbm.at[:, pl.ds(row, half), :], row_buffer.at[pair], sems.at[1, pair]
            )
        )
    for copy in copies:
        copy.start()
    outputs = (col_even, row_even, col_odd, row_odd)
    buffers = (col_buffer, row_buffer) * 2
    for index, copy in enumerate(copies):
        copy.wait()
        outputs[index][...] = buffers[index][index // 2].astype(BF16)


def cut_strips(object_field, half):
    tile = object_field.shape[1]
    vmem = pl.BlockSpec(memory_space=pltpu.VMEM)
    columns = jax.ShapeDtypeStruct((2, tile, half), BF16)
    rows = jax.ShapeDtypeStruct((2, half, tile), BF16)
    return pl.pallas_call(
        strips_kernel,
        in_specs=[pl.BlockSpec(memory_space=pltpu.HBM)],
        out_specs=[vmem] * 4,
        out_shape=[columns, columns, rows, rows],
        scratch_shapes=[
            pltpu.VMEM((2, 2, tile, half), F32),
            pltpu.VMEM((2, 2, half, tile), F32),
            pltpu.SemaphoreType.DMA((2, 2)),
        ],
        compiler_params=pltpu.CompilerParams(vmem_limit_bytes=50 * 1024 * 1024),
        cost_estimate=pl.CostEstimate(
            flops=1024 * 1024, bytes_accessed=5 * 1024 * 1024, transcendentals=0
        ),
        name="strips",
    )(object_field)


def positions_kernel(with_border, *refs):
    counts, centers, obj_hbm, pat_hbm, probe = refs[:5]
    tables, row_halos = refs[5], refs[6:8]
    refs = refs[8:]
    if with_border:
        col_halos, end_halos = refs[0:2], refs[2:4]
        start_hbm, ring_in, sums_in = refs[4:7]
        out_hbm, g_rows, g_ends, g_mids = refs[7], refs[8:10], refs[10:12], refs[12:14]
        kept = refs[14]
        refs = refs[15:]
    else:
        out_hbm, ring_out, sums_out = refs[:3]
        refs = refs[3:]
    (obj, canvas, patterns, positive, negative, left_negative, low, waves, shifts, halves, backs,
     spectra, changes, patch, sums, order, piece_sems, out_sems, ring_sems, pat_sems,
     sums_sems) = refs
    size = probe.shape[-1]
    half = size // 2
    tile = obj_hbm.shape[1]
    inner = tile // LANES
    chunks = inner + 2
    modes = probe.shape[0]
    rows = slice(half, half + tile)
    near = [0, 1, inner - 2, inner - 1] if with_border else list(range(inner))
    pieces = [(comp, j) for comp in range(2) for j in near]

    def home(array, comp, j):
        return array.at[comp, :, pl.ds(j * LANES, LANES)]

    def held(array, comp, j):
        return array.at[comp * chunks + 1 + j, pl.ds(half, tile), :]

    def ring_pieces(array):
        for comp in range(2):
            for side, row in enumerate((0, half + tile)):
                yield (
                    array.at[pl.ds(comp * inner, inner), pl.ds(side * half, half), :],
                    canvas.at[pl.ds(comp * chunks + 1, inner), pl.ds(row, half), :],
                    ring_sems.at[side, comp],
                )

    def sums_pieces(array):
        step = array.shape[0] // sums_parts
        for part in range(sums_parts):
            here = pl.ds(part * step, step)
            yield array.at[here], sums.at[here], sums_sems.at[part]

    sums_parts = sums_sems.shape[0]
    obj_copies = [
        pltpu.make_async_copy(home(obj_hbm, *p), held(obj, *p), piece_sems.at[0, *p])
        for p in pieces
    ]
    out_copies = [
        pltpu.make_async_copy(held(canvas, *p), home(out_hbm, *p), out_sems.at[p]) for p in pieces
    ]
    later = []
    if with_border:
        later += [
            pltpu.make_async_copy(home(start_hbm, *p), held(canvas, *p), piece_sems.at[1, *p])
            for p in pieces
        ]
        later += [pltpu.make_async_copy(*each) for each in ring_pieces(ring_in)]
        later += [pltpu.make_async_copy(*each) for each in sums_pieces(sums_in)]
    for copy in obj_copies + later:
        copy.start()

    order[0] = 0
    count = counts[lax.axis_index(ROW), lax.axis_index("col")]

    def pattern_copy(slot):
        return pltpu.make_async_copy(pat_hbm.at[slot], patterns.at[slot], pat_sems.at[slot])

    def note(slot, found):
        column = centers[1, slot]
        inside = (column >= half) & (column <= tile - half)
        order[found] = slot
        return found + jnp.where(inside, 0 if with_border else 1, 1 if with_border else 0)

    def fetch(index, carry):
        pattern_copy(order[index]).start()
        return carry

    found = lax.fori_loop(0, count, note, 0)
    lax.fori_loop(0, found, fetch, 0)

    if not with_border:
        sums[...] = jnp.zeros_like(sums)
    intensity = jnp.zeros((size, size), F32)
    for m in range(modes):
        for comp in range(2):
            values = probe[m, comp]
            intensity = intensity + values * values
            low[2 * m + comp] = values.astype(BF16).astype(F32)
    scale = 1.0 / (jnp.max(intensity) + 1e-06)
    for turn, inverse in ((positive, True), (negative, False)):
        upper, lower = (2, 1) if inverse else (1, 2)
        turn[0:size, 0:size] = tables[0]
        turn[0:size, size:] = tables[upper]
        turn[size:, 0:size] = tables[lower]
        turn[size:, size:] = tables[0]
    for k in range(2):
        rows_here = slice(k * half, (k + 1) * half)
        first = k * size
        left_negative[first : first + half, 0:size] = tables[0, rows_here]
        left_negative[first : first + half, size:] = tables[1, rows_here]
        left_negative[first + half : first + size, 0:size] = tables[2, rows_here]
        left_negative[first + half : first + size, size:] = tables[0, rows_here]
    changes[...] = jnp.zeros_like(changes)
    patch[...] = jnp.zeros_like(patch)

    row_sides = sides(ROW, tile + size, half)
    col_sides = [offset // LANES for offset in sides(COL, tile + size, half)]
    blank = jnp.zeros((tile + size, LANES), F32)
    for comp in range(2):
        first = comp * chunks
        for pair in range(2):
            for j in near:
                columns = slice(j * LANES, (j + 1) * LANES)
                obj[first + 1 + j, pl.ds(row_sides[pair], half), :] = row_halos[pair][
                    comp, :, columns
                ].astype(F32)
            if with_border:
                beside = first + col_sides[pair]
                canvas[beside] = blank
                obj[beside, rows, :] = col_halos[pair][comp].astype(F32)
                for other in range(2):
                    obj[beside, pl.ds(row_sides[other], half), :] = end_halos[pair][
                        comp, other * half : (other + 1) * half, :
                    ].astype(F32)
        if not with_border:
            for j in range(inner):
                canvas[first + 1 + j, 0:half, :] = blank[0:half]
                canvas[first + 1 + j, half + tile :, :] = blank[0:half]

    block = 16
    groups = block // 8
    lane = lax.broadcasted_iota(jnp.int32, (block, LANES), 1)
    blocks = range(0, size, block)

    def place_of(index):
        slot = order[index]
        column = centers[1, slot]
        return slot, centers[0, slot], column >> 7, column & 127

    def cut(index, begin):
        _, row, chunk, offset = place_of(index)
        back_offset = (LANES - offset) & 127
        from_first = lane < LANES - offset
        here = slice(begin, begin + block)
        parts = []
        for comp in range(2):
            moved = [
                pltpu.roll(
                    obj[comp * chunks + chunk + k, pl.ds(row + begin, block), :], back_offset, 1
                )
                for k in range(3)
            ]
            window = jnp.concatenate(
                [
                    jnp.where(from_first, moved[0], moved[1]),
                    jnp.where(from_first, moved[1], moved[2]),
                ],
                1,
            ).astype(BF16).astype(F32)
            patch[index & 1, comp, here, :] = window
            parts.append(window)
        real, imag = parts
        for m in range(modes):
            probe_real = low[2 * m, here, :]
            probe_imag = low[2 * m + 1, here, :]
            there = slice(m * size + begin, m * size + begin + block)
            waves[there, 0:size] = (probe_real * real - probe_imag * imag).astype(BF16)
            waves[there, size:] = (probe_real * imag + probe_imag * real).astype(BF16)

    def forward_right(m, part):
        mode = slice(m * size, (m + 1) * size)
        columns = slice(part * size, (part + 1) * size)
        halves[columns, mode] = jnp.dot(
            waves[mode, :], positive[:, columns], preferred_element_type=F32
        ).astype(BF16)

    def forward_left(k):
        rows_here = slice(k * size, (k + 1) * size)
        spectra[rows_here, :] = jnp.dot(
            left_negative[rows_here, :], halves[...], preferred_element_type=F32
        )

    def reweigh(index, begin):
        slot = order[index]
        k, inside = divmod(begin, half)
        real_rows = slice(k * size + inside, k * size + inside + block)
        imag_rows = slice(k * size + half + inside, k * size + half + inside + block)
        amplitude = patterns[slot, begin : begin + block, :].astype(F32)
        mode_columns = [slice(m * size, (m + 1) * size) for m in range(modes)]
        parts = [(spectra[real_rows, mode], spectra[imag_rows, mode]) for mode in mode_columns]
        power = sum(real * real + imag * imag for real, imag in parts)
        factor = amplitude * lax.rsqrt(jnp.maximum(power, 0.5)) - 1.0
        for m, (real, imag) in enumerate(parts):
            first = k * size + m * half + inside
            there = slice(first, first + block)
            shifts[there, 0:size] = (factor * real).astype(BF16)
            shifts[there, size:] = (factor * imag).astype(BF16)

    def backward_right(k):
        product = jnp.dot(
            shifts[k * size : (k + 1) * size, :], negative[...],
            preferred_element_type=F32,
        ).astype(BF16)
        for m in range(modes):
            mode = slice(m * size, (m + 1) * size)
            for part in range(2):
                first = part * size + k * half
                backs[first : first + half, mode] = product[
                    m * half : (m + 1) * half, part * size : (part + 1) * size
                ]

    def backward_left(m, part):
        mode = slice(m * size, (m + 1) * size)
        rows_here = slice(part * size, (part + 1) * size)
        changes[rows_here, mode] = jnp.dot(
            positive[rows_here, :], backs[:, mode], preferred_element_type=F32
        )

    def deposit(index, buffer, begin):
        _, row, chunk, offset = place_of(index)
        past = lane >= offset
        here = slice(begin, begin + block)
        below = slice(size + begin, size + begin + block)
        start = begin // 8
        obj_real = patch[buffer, 0, here, :]
        obj_imag = patch[buffer, 1, here, :]

        def add(plane, value):
            sums[start : start + groups, plane] += value.reshape(groups, 8, size)

        add(2 * modes, obj_real * obj_real + obj_imag * obj_imag)
        term_real = term_imag = None
        for m in range(modes):
            mode = slice(m * size, (m + 1) * size)
            real = changes[here, mode]
            imag = changes[below, mode]
            probe_real = low[2 * m, here, :]
            probe_imag = low[2 * m + 1, here, :]
            more_real = probe_real * real + probe_imag * imag
            more_imag = probe_real * imag - probe_imag * real
            term_real = more_real if m == 0 else term_real + more_real
            term_imag = more_imag if m == 0 else term_imag + more_imag
            add(2 * m, obj_real * real + obj_imag * imag)
            add(2 * m + 1, obj_real * imag - obj_imag * real)
        for comp, term in enumerate((term_real, term_imag)):
            term = term.astype(BF16).astype(F32) * scale
            first = pltpu.roll(term[:, 0:LANES], offset, 1)
            second = pltpu.roll(term[:, LANES:], offset, 1)
            place = comp * chunks + chunk
            window = pl.ds(row + begin, block)
            values = [canvas[place + k, window, :] for k in range(3)]
            canvas[place, window, :] = values[0] + jnp.where(past, first, 0.0)
            canvas[place + 1, window, :] = values[1] + jnp.where(past, second, first)
            canvas[place + 2, window, :] = values[2] + jnp.where(past, 0.0, second)

    def step(index, carry):
        pattern_copy(order[index]).wait()
        previous = jnp.maximum(index - 1, 0)
        following = jnp.minimum(index + 1, found - 1)
        buffer = (index + 1) & 1
        starts = list(blocks)
        quarter = len(starts) // 4
        quarters = [starts[i * quarter : (i + 1) * quarter] for i in range(4)]
        for m in range(modes):
            for part in range(2):
                forward_right(m, part)
                for begin in quarters[2 * m + part]:
                    deposit(previous, buffer, begin)
        forward_left(0)
        forward_left(1)
        for begin in quarters[0] + quarters[1]:
            reweigh(index, begin)
        backward_right(0)
        for begin in quarters[2] + quarters[3]:
            reweigh(index, begin)
        for begin in quarters[0]:
            cut(following, begin)
        backward_right(1)
        for begin in quarters[1]:
            cut(following, begin)
        backward_left(0, 0)
        for begin in quarters[2]:
            cut(following, begin)
        backward_left(0, 1)
        for begin in quarters[3]:
            cut(following, begin)
        backward_left(1, 0)
        backward_left(1, 1)
        return carry

    for copy in obj_copies:
        copy.wait()

    @pl.when(found > 0)
    def _():
        for begin in blocks:
            cut(0, begin)

    if not with_border:
        for comp, j in pieces:
            index = comp * chunks + 1 + j
            canvas[index, rows, :] = obj[index, rows, :]
    for copy in later:
        copy.wait()

    @pl.when(found > 0)
    def _():
        lax.fori_loop(0, found, step, 0)
        for begin in blocks:
            deposit(found - 1, (found - 1) & 1, begin)

    last_copies = list(out_copies)
    if not with_border:
        last_copies += [
            pltpu.make_async_copy(here, there, sem) for there, here, sem in ring_pieces(ring_out)
        ]
        last_copies += [
            pltpu.make_async_copy(here, there, sem) for there, here, sem in sums_pieces(sums_out)
        ]
    for copy in last_copies:
        copy.start()
    if with_border:
        for pair in range(2):
            g_rows[pair][0 : 2 * chunks] = canvas[:, pl.ds(row_sides[pair], half), :].astype(BF16)
            for comp in range(2):
                beside = comp * chunks + col_sides[pair]
                low_end = half + tile
                g_ends[pair][comp, 0:half] = canvas[beside, half:size, :].astype(BF16)
                g_ends[pair][comp, half:] = canvas[beside, low_end - half : low_end, :].astype(BF16)
                g_mids[pair][comp] = canvas[beside, size : low_end - half, :].astype(BF16)
        core = lax.axis_index("core")
        count_of = kept.shape[0]
        kept[...] = sums[pl.ds(core * count_of, count_of)]
        for plane in range(2 * modes + 1):
            for side in range(2):
                columns = slice(side * half, (side + 1) * half)
                given = sums[pl.ds((1 - core) * count_of, count_of), plane, :, columns]
                g_rows[0][2 * chunks + 2 * plane + side] = given.reshape(half, LANES).astype(BF16)
    for copy in last_copies:
        copy.wait()


def run_positions(counts, centers, object_field, patterns, probe_modes, row_halos, border=None):
    size = probe_modes.shape[-1]
    half = size // 2
    modes = probe_modes.shape[0]
    tile = object_field.shape[1]
    inner = tile // LANES
    chunks = inner + 2
    slots = patterns.shape[0]
    smem = pl.BlockSpec(memory_space=pltpu.SMEM)
    vmem = pl.BlockSpec(memory_space=pltpu.VMEM)
    anywhere = pl.BlockSpec(memory_space=pl.ANY)
    shape = jax.ShapeDtypeStruct
    in_specs = [smem, smem, anywhere, anywhere] + [vmem] * 4
    operands = [counts, centers, object_field, patterns, probe_modes, dft_tables(size), *row_halos]
    sums_shape = (size // 8, 2 * modes + 1, 8, size)
    ring_shape = (2 * inner, size, LANES)
    aliases = {}
    if border is None:
        out_specs = [anywhere] * 3
        out_shape = [shape(each, F32) for each in (object_field.shape, ring_shape, sums_shape)]
    else:
        aliases = {len(operands) + 4: 0}
        in_specs += [vmem] * 4 + [anywhere] * 3
        operands += list(border)
        half_sums = (size // 16,) + sums_shape[1:]
        out_specs = [anywhere] + [vmem] * 7
        out_shape = [
            shape((2, tile, tile), F32),
            shape((2 * chunks + 4 * modes + 2, half, LANES), BF16),
            shape((2 * chunks, half, LANES), BF16),
            shape((2, size, LANES), BF16),
            shape((2, size, LANES), BF16),
            shape((2, tile - size, LANES), BF16),
            shape((2, tile - size, LANES), BF16),
            shape(half_sums, F32),
        ]
    table = pltpu.VMEM((2 * size, 2 * size), BF16)
    products = pltpu.VMEM((2 * size, modes * size), BF16)
    wide = pltpu.VMEM((2 * size, modes * size), F32)
    padded = pltpu.VMEM((2 * chunks, tile + size, LANES), F32)
    dma = pltpu.SemaphoreType.DMA
    return pl.pallas_call(
        functools.partial(positions_kernel, border is not None),
        in_specs=in_specs,
        out_specs=out_specs,
        out_shape=out_shape,
        input_output_aliases=aliases,
        scratch_shapes=[
            padded,
            padded,
            pltpu.VMEM(patterns.shape, BF16),
            table,
            table,
            table,
            pltpu.VMEM((2 * modes, size, size), F32),
            products,
            products,
            products,
            products,
            wide,
            wide,
            pltpu.VMEM((2, 2, size, size), F32),
            pltpu.VMEM(sums_shape, F32),
            pltpu.SMEM((slots + 1,), jnp.int32),
            dma((2, 2, inner)),
            dma((2, inner)),
            dma((2, 2)),
            dma((slots,)),
            dma((4,)),
        ],
        compiler_params=pltpu.CompilerParams(
            vmem_limit_bytes=(50 if border is None else 46) * 1024 * 1024
        ),
        cost_estimate=pl.CostEstimate(
            flops=slots * 16 * modes * size**3,
            bytes_accessed=24 * 1024 * 1024,
            transcendentals=0,
        ),
        name="border" if border is not None else "interior",
    )(*operands)


def corners_kernel(end_even, end_odd, row_even, row_odd, out_even, out_odd):
    half = row_even.shape[1]
    chunks = row_odd.shape[0] // 2
    row_sides = sides(ROW, 2 * half, half)
    col_sides = [offset // LANES for offset in sides(COL, chunks * LANES, half)]
    for pair, (strip, out) in enumerate(((end_even, out_even), (end_odd, out_odd))):
        for other, ring in enumerate((row_even, row_odd)):
            there = pl.ds(row_sides[other], half)
            for comp in range(2):
                extra = ring[comp * chunks + col_sides[pair]].astype(F32)
                out[comp, there, :] = (strip[comp, there, :].astype(F32) + extra).astype(BF16)


def add_corners(g_ends, from_rows):
    vmem = pl.BlockSpec(memory_space=pltpu.VMEM)
    shape = jax.ShapeDtypeStruct(g_ends[0].shape, BF16)
    return pl.pallas_call(
        corners_kernel,
        in_specs=[vmem] * 4,
        out_specs=[vmem] * 2,
        out_shape=[shape, shape],
        compiler_params=pltpu.CompilerParams(vmem_limit_bytes=8 * 1024 * 1024),
        cost_estimate=pl.CostEstimate(
            flops=256 * 1024, bytes_accessed=2 * 1024 * 1024, transcendentals=0
        ),
        name="corners",
    )(*g_ends, *from_rows)


def rims_kernel(
    partial, row_even, row_odd, end_even, end_odd, mid_even, mid_odd, out, row_buffer, col_buffer,
    sems,
):
    tile = partial.shape[1]
    half = row_even.shape[1]
    inner = tile // LANES
    chunks = inner + 2
    middle = tile - 2 * half
    row_sides = sides(ROW, tile, half)
    col_sides = sides(COL, tile, half)
    row_rings = (row_even, row_odd)
    end_sides = sides(ROW, 2 * half, half)
    end_strips = (end_even, end_odd)
    mid_strips = (mid_even, mid_odd)

    def copy(kind, pair, comp, inward):
        if kind == 0:
            here = row_buffer.at[pair, comp]
            place = (comp, pl.ds(row_sides[pair], half), slice(None))
        else:
            here = col_buffer.at[pair, comp]
            place = (comp, pl.ds(half, middle), pl.ds(col_sides[pair], half))
        source, target = (partial.at[place], here) if inward else (here, out.at[place])
        return pltpu.make_async_copy(
            source, target, sems.at[1 - int(inward), 2 * kind + pair, comp]
        )

    everything = [(kind, pair, comp) for kind in range(2) for pair in range(2) for comp in range(2)]
    for piece in everything:
        copy(*piece, True).start()
    for kind, pair, comp in everything:
        copy(kind, pair, comp, True).wait()
        if kind == 0:
            for j in range(inner):
                columns = slice(j * LANES, (j + 1) * LANES)
                ring = row_rings[pair][comp * chunks + 1 + j]
                row_buffer[pair, comp, :, columns] += ring.astype(F32)
            for other in range(2):
                columns = pl.ds(col_sides[other], half)
                strip = end_strips[other][comp, pl.ds(end_sides[pair], half), :]
                row_buffer[pair, comp, :, columns] += strip.astype(F32)
        else:
            col_buffer[pair, comp] += mid_strips[pair][comp].astype(F32)
        copy(kind, pair, comp, False).start()
    for piece in everything:
        copy(*piece, False).wait()


def add_rims(partial, from_rows, from_ends, from_mids):
    tile = partial.shape[1]
    half = from_rows[0].shape[1]
    vmem = pl.BlockSpec(memory_space=pltpu.VMEM)
    anywhere = pl.BlockSpec(memory_space=pl.ANY)
    return pl.pallas_call(
        rims_kernel,
        in_specs=[anywhere] + [vmem] * 6,
        out_specs=anywhere,
        out_shape=jax.ShapeDtypeStruct(partial.shape, F32),
        input_output_aliases={0: 0},
        scratch_shapes=[
            pltpu.VMEM((2, 2, half, tile), F32),
            pltpu.VMEM((2, 2, tile - 2 * half, half), F32),
            pltpu.SemaphoreType.DMA((2, 4, 2)),
        ],
        compiler_params=pltpu.CompilerParams(vmem_limit_bytes=16 * 1024 * 1024),
        cost_estimate=pl.CostEstimate(
            flops=1024 * 1024, bytes_accessed=6 * 1024 * 1024, transcendentals=0
        ),
        name="rims",
    )(partial, *from_rows, *from_ends, *from_mids)


def chip_sums_kernel(kept, received, out):
    groups, planes, height, size = kept.shape
    half = received.shape[1]
    first = received.shape[0] - 2 * planes
    for plane in range(planes):
        for side in range(2):
            columns = slice(side * half, (side + 1) * half)
            other = received[first + 2 * plane + side].astype(F32).reshape(groups, height, half)
            out[:, plane, :, columns] = (kept[:, plane, :, columns] + other).astype(BF16)


def chip_sums(kept, received):
    vmem = pl.BlockSpec(memory_space=pltpu.VMEM)
    return pl.pallas_call(
        chip_sums_kernel,
        in_specs=[vmem, vmem],
        out_specs=vmem,
        out_shape=jax.ShapeDtypeStruct(kept.shape, BF16),
        compiler_params=pltpu.CompilerParams(vmem_limit_bytes=8 * 1024 * 1024),
        cost_estimate=pl.CostEstimate(
            flops=32 * 1024**3, bytes_accessed=32 * 1024 * 1024, transcendentals=0
        ),
        name="chip_sums",
    )(kept, received)


def by_device(on_chip):
    devices = lax.axis_size("x") * lax.axis_size("col")
    groups, planes, _, size = on_chip.shape
    share = groups * 8 // devices
    if share < 8:
        on_chip = on_chip.reshape(groups, planes, 8 // share, share, size)
        return jnp.swapaxes(on_chip, 1, 2).reshape(devices, planes, share, size)
    return on_chip.reshape(devices, groups // devices, planes, 8, size)


def first_sums(parts):
    return lax.all_to_all(parts, ("x", "col"), 0, 0, tiled=True)


def update_kernel(received, copies):
    devices = received.shape[0]
    total = received[0].astype(F32)
    for device in range(1, devices):
        total = total + received[device].astype(F32)
    planes = total.shape[0]
    update = (total[: planes - 1] / jnp.sqrt(total[planes - 1])).astype(BF16)
    for device in range(devices):
        copies[device] = update


def shared_update(received):
    devices, planes, share, size = received.shape
    vmem = pl.BlockSpec(memory_space=pltpu.VMEM)
    return pl.pallas_call(
        update_kernel,
        in_specs=[vmem],
        out_specs=vmem,
        out_shape=jax.ShapeDtypeStruct((devices, planes - 1, share, size), BF16),
        compiler_params=pltpu.CompilerParams(vmem_limit_bytes=8 * 1024 * 1024),
        cost_estimate=pl.CostEstimate(
            flops=512 * 1024, bytes_accessed=1024 * 1024, transcendentals=0
        ),
        name="update",
    )(received)


def finish_kernel(probe, mine, other, out):
    core = lax.axis_index("core")
    groups, planes, height, _ = mine.shape
    for side, update in enumerate((mine, other)):
        first = jnp.where(core == side, 0, groups * height)
        for group in range(groups):
            place = pl.ds(pl.multiple_of(first + group * height, height), height)
            for plane in range(planes):
                m, comp = divmod(plane, 2)
                out[m, comp, place, :] = probe[m, comp, place, :] + update[group, plane].astype(F32)


def finish_probe(probe_modes, mine):
    devices, planes, share, size = mine.shape
    if share < 8:
        mine = mine.reshape(devices * share // 8, 8 // share, planes, share, size)
        mine = jnp.swapaxes(mine, 1, 2).reshape(-1, planes, 8, size)
    other = lax.ppermute(mine, "core", [(0, 1), (1, 0)])
    vmem = pl.BlockSpec(memory_space=pltpu.VMEM)
    return pl.pallas_call(
        finish_kernel,
        in_specs=[vmem] * 3,
        out_specs=vmem,
        out_shape=jax.ShapeDtypeStruct(probe_modes.shape, F32),
        compiler_params=pltpu.CompilerParams(vmem_limit_bytes=8 * 1024 * 1024),
        cost_estimate=pl.CostEstimate(
            flops=256 * 1024, bytes_accessed=3 * 1024 * 1024, transcendentals=0
        ),
        name="finish",
    )(probe_modes, mine, other)


def on_device(object_field, probe_modes, counts, centers, patterns):
    half = probe_modes.shape[-1] // 2

    col_even, col_odd, row_even, row_odd = cut_strips(object_field, half)
    go_on = lax.axis_index("col") < 4096
    row_halos = (swap_pairs(row_even, ROW, 0), swap_pairs(row_odd, ROW, 1))
    col_halos = (swap_pairs(col_even, COL, 0), swap_pairs(col_odd, COL, 1))
    is_even = (lax.axis_index("col") & 1) == 0
    first_ends = jnp.concatenate([halo[:, :, :half] for halo in row_halos], 1)
    last_ends = jnp.concatenate([halo[:, :, -half:] for halo in row_halos], 1)
    end_halos = (
        swap_pairs(jnp.where(is_even, last_ends, first_ends), COL, 0),
        swap_pairs(jnp.where(is_even, first_ends, last_ends), COL, 1),
    )

    inputs = (counts, centers[0, 0], object_field, patterns[0, 0], probe_modes, row_halos)
    started = run_positions(*inputs)
    border = (*col_halos, *end_halos, *started)
    partial, *rims, kept = run_positions(*inputs, border)
    g_row_even, g_row_odd, g_end_even, g_end_odd, g_mid_even, g_mid_odd = rims

    from_rows = (swap_pairs(g_row_even, ROW, 0), swap_pairs(g_row_odd, ROW, 1))
    from_mids = (swap_pairs(g_mid_even, COL, 0), swap_pairs(g_mid_odd, COL, 1))
    received = lax.cond(
        go_on, first_sums, jnp.zeros_like, by_device(chip_sums(kept, from_rows[0]))
    )
    row_odd, _ = lax.optimization_barrier((from_rows[1], received))
    from_rows = (from_rows[0], row_odd)
    to_even, to_odd = add_corners((g_end_even, g_end_odd), from_rows)
    received, from_mids, to_even, to_odd = lax.optimization_barrier(
        (received, from_mids, to_even, to_odd)
    )
    from_ends = (swap_pairs(to_even, COL, 0), swap_pairs(to_odd, COL, 1))
    if received.ndim == 5:
        received = received[:, 0]
    mine = lax.all_to_all(shared_update(received), ("x", "col"), 0, 0, tiled=True)
    mine, from_ends, partial = lax.optimization_barrier((mine, from_ends, partial))
    new_object = add_rims(partial, from_rows, from_ends, from_mids)
    return (new_object, finish_probe(probe_modes, mine))


def solution(mesh):
    rows, columns = mesh.devices.shape
    split = jax.sharding.Mesh(
        mesh.devices.reshape(rows // 2, 2, columns), ("x", "core", "col")
    )
    placed = (
        P(None, ROW, "col"),
        P(),
        P(),
        P(ROW, "col", None, None),
        P(ROW, "col", None, None, None),
    )
    return jax.shard_map(
        on_device,
        mesh=split,
        in_specs=placed,
        out_specs=(P(None, ROW, "col"), P()),
        check_vma=False,
    )
```

```python
import functools
import math

import jax
import jax.numpy as jnp
import ml_dtypes
import numpy as np
from jax import lax
from jax.experimental import pallas as pl
from jax.experimental.pallas import tpu as pltpu
from jax.sharding import PartitionSpec as P

LANES = 128
ROW = ("x", "core")
COL = ("col",)
F32 = jnp.float32
BF16 = jnp.bfloat16


def dft_tables(length):
    indices = np.arange(length)
    angles = (indices[:, None] * indices[None, :] % length) * (2.0 * np.pi / length)
    scale = 1.0 / np.sqrt(length)
    cosine = (np.cos(angles) * scale).astype(np.float32).astype(ml_dtypes.bfloat16)
    sine = (np.sin(angles) * scale).astype(np.float32).astype(ml_dtypes.bfloat16)
    return np.stack([cosine, sine, -sine])


def swap_pairs(array, axis, odd):
    devices = math.prod(lax.axis_size(name) for name in axis)
    firsts = range(odd, devices - 1, 2)
    return lax.ppermute(
        array, axis, [(i, i + 1) for i in firsts] + [(i + 1, i) for i in firsts]
    )


def sides(axis, length, width):
    even = (lax.axis_index(axis) & 1) == 0
    far = length - width
    return [
        pl.multiple_of(jnp.where(even, far, 0), width),
        pl.multiple_of(jnp.where(even, 0, far), width),
    ]


def strips_kernel(obj_hbm, col_even, col_odd, row_even, row_odd, col_buffer, row_buffer, sems):
    tile = obj_hbm.shape[1]
    half = row_even.shape[1]
    copies = []
    for pair in range(2):
        column = sides(COL, tile, half)[pair]
        row = sides(ROW, tile, half)[pair]
        copies.append(
            pltpu.make_async_copy(
                obj_hbm.at[:, :, pl.ds(column, half)], col_buffer.at[pair], sems.at[0, pair]
            )
        )
        copies.append(
            pltpu.make_async_copy(
                obj_hbm.at[:, pl.ds(row, half), :], row_buffer.at[pair], sems.at[1, pair]
            )
        )
    for copy in copies:
        copy.start()
    outputs = (col_even, row_even, col_odd, row_odd)
    buffers = (col_buffer, row_buffer) * 2
    for index, copy in enumerate(copies):
        copy.wait()
        outputs[index][...] = buffers[index][index // 2].astype(BF16)


def cut_strips(object_field, half):
    tile = object_field.shape[1]
    vmem = pl.BlockSpec(memory_space=pltpu.VMEM)
    columns = jax.ShapeDtypeStruct((2, tile, half), BF16)
    rows = jax.ShapeDtypeStruct((2, half, tile), BF16)
    return pl.pallas_call(
        strips_kernel,
        in_specs=[pl.BlockSpec(memory_space=pltpu.HBM)],
        out_specs=[vmem] * 4,
        out_shape=[columns, columns, rows, rows],
        scratch_shapes=[
            pltpu.VMEM((2, 2, tile, half), F32),
            pltpu.VMEM((2, 2, half, tile), F32),
            pltpu.SemaphoreType.DMA((2, 2)),
        ],
        compiler_params=pltpu.CompilerParams(vmem_limit_bytes=50 * 1024 * 1024),
        cost_estimate=pl.CostEstimate(
            flops=1024 * 1024, bytes_accessed=5 * 1024 * 1024, transcendentals=0
        ),
        name="strips",
    )(object_field)


def positions_kernel(with_border, *refs):
    counts, centers, obj_hbm, pat_hbm, probe = refs[:5]
    tables, row_halos = refs[5], refs[6:8]
    refs = refs[8:]
    if with_border:
        halos_in = refs[0:4]
        start_hbm, ring_in, sums_in = refs[4:7]
        out_hbm, g_rows, g_cols, kept = refs[7], refs[8:10], refs[10:12], refs[12]
        refs = refs[13:]
    else:
        out_hbm, ring_out, sums_out = refs[:3]
        refs = refs[3:]
    (obj, canvas, patterns, positive, negative, left_negative, low, waves, shifts, halves, backs,
     spectra, changes, patch, sums, col_halos, end_halos, order, piece_sems, out_sems, ring_sems, pat_sems,
     sums_sems, halo_sems) = refs
    size = probe.shape[-1]
    half = size // 2
    tile = obj_hbm.shape[1]
    inner = tile // LANES
    chunks = inner + 2
    modes = probe.shape[0]
    rows = slice(half, half + tile)
    near = [0, 1, inner - 2, inner - 1] if with_border else list(range(inner))
    pieces = [(comp, j) for comp in range(2) for j in near]

    def home(array, comp, j):
        return array.at[comp, :, pl.ds(j * LANES, LANES)]

    def held(array, comp, j):
        return array.at[comp * chunks + 1 + j, pl.ds(half, tile), :]

    def ring_pieces(array):
        for comp in range(2):
            for side, row in enumerate((0, half + tile)):
                yield (
                    array.at[pl.ds(comp * inner, inner), pl.ds(side * half, half), :],
                    canvas.at[pl.ds(comp * chunks + 1, inner), pl.ds(row, half), :],
                    ring_sems.at[side, comp],
                )

    def sums_pieces(array):
        step = array.shape[0] // sums_parts
        for part in range(sums_parts):
            here = pl.ds(part * step, step)
            yield array.at[here], sums.at[here], sums_sems.at[part]

    sums_parts = sums_sems.shape[0]
    obj_copies = [
        pltpu.make_async_copy(home(obj_hbm, *p), held(obj, *p), piece_sems.at[0, *p])
        for p in pieces
    ]
    out_copies = [
        pltpu.make_async_copy(held(canvas, *p), home(out_hbm, *p), out_sems.at[p]) for p in pieces
    ]
    later = []
    if with_border:
        later += [
            pltpu.make_async_copy(home(start_hbm, *p), held(canvas, *p), piece_sems.at[1, *p])
            for p in pieces
        ]
        later += [pltpu.make_async_copy(*each) for each in ring_pieces(ring_in)]
        later += [pltpu.make_async_copy(*each) for each in sums_pieces(sums_in)]
    halo_copies = []
    if with_border:
        targets = (col_halos.at[0], col_halos.at[1], end_halos.at[0], end_halos.at[1])
        halo_copies = [
            pltpu.make_async_copy(halos_in[i], targets[i], halo_sems.at[i]) for i in range(4)
        ]
    for copy in halo_copies + obj_copies + later:
        copy.start()

    order[0] = 0
    count = counts[lax.axis_index(ROW), lax.axis_index("col")]

    def pattern_copy(slot):
        return pltpu.make_async_copy(pat_hbm.at[slot], patterns.at[slot], pat_sems.at[slot])

    def note(slot, found):
        column = centers[1, slot]
        inside = (column >= half) & (column <= tile - half)
        order[found] = slot
        return found + jnp.where(inside, 0 if with_border else 1, 1 if with_border else 0)

    def fetch(index, carry):
        pattern_copy(order[index]).start()
        return carry

    found = lax.fori_loop(0, count, note, 0)
    lax.fori_loop(0, found, fetch, 0)

    if not with_border:
        sums[...] = jnp.zeros_like(sums)
    intensity = jnp.zeros((size, size), F32)
    for m in range(modes):
        for comp in range(2):
            values = probe[m, comp]
            intensity = intensity + values * values
            low[2 * m + comp] = values.astype(BF16).astype(F32)
    scale = 1.0 / (jnp.max(intensity) + 1e-06)
    for turn, inverse in ((positive, True), (negative, False)):
        upper, lower = (2, 1) if inverse else (1, 2)
        turn[0:size, 0:size] = tables[0]
        turn[0:size, size:] = tables[upper]
        turn[size:, 0:size] = tables[lower]
        turn[size:, size:] = tables[0]
    for k in range(2):
        rows_here = slice(k * half, (k + 1) * half)
        first = k * size
        left_negative[first : first + half, 0:size] = tables[0, rows_here]
        left_negative[first : first + half, size:] = tables[1, rows_here]
        left_negative[first + half : first + size, 0:size] = tables[2, rows_here]
        left_negative[first + half : first + size, size:] = tables[0, rows_here]
    changes[...] = jnp.zeros_like(changes)
    patch[...] = jnp.zeros_like(patch)

    for copy in halo_copies:
        copy.wait()
    row_sides = sides(ROW, tile + size, half)
    col_sides = [offset // LANES for offset in sides(COL, tile + size, half)]
    blank = jnp.zeros((tile + size, LANES), F32)
    for comp in range(2):
        first = comp * chunks
        for pair in range(2):
            for j in near:
                columns = slice(j * LANES, (j + 1) * LANES)
                obj[first + 1 + j, pl.ds(row_sides[pair], half), :] = row_halos[pair][
                    comp, :, columns
                ].astype(F32)
            if with_border:
                beside = first + col_sides[pair]
                canvas[beside] = blank
                obj[beside, rows, :] = col_halos[pair, comp].astype(F32)
                for other in range(2):
                    obj[beside, pl.ds(row_sides[other], half), :] = end_halos[
                        pair, comp, other * half : (other + 1) * half, :
                    ].astype(F32)
        if not with_border:
            for j in range(inner):
                canvas[first + 1 + j, 0:half, :] = blank[0:half]
                canvas[first + 1 + j, half + tile :, :] = blank[0:half]

    block = 16
    groups = block // 8
    lane = lax.broadcasted_iota(jnp.int32, (block, LANES), 1)
    blocks = range(0, size, block)

    def place_of(index):
        slot = order[index]
        column = centers[1, slot]
        return slot, centers[0, slot], column >> 7, column & 127

    def cut(index, begin):
        _, row, chunk, offset = place_of(index)
        back_offset = (LANES - offset) & 127
        from_first = lane < LANES - offset
        here = slice(begin, begin + block)
        parts = []
        for comp in range(2):
            moved = [
                pltpu.roll(
                    obj[comp * chunks + chunk + k, pl.ds(row + begin, block), :], back_offset, 1
                )
                for k in range(3)
            ]
            window = jnp.concatenate(
                [
                    jnp.where(from_first, moved[0], moved[1]),
                    jnp.where(from_first, moved[1], moved[2]),
                ],
                1,
            ).astype(BF16).astype(F32)
            patch[index & 1, comp, here, :] = window
            parts.append(window)
        real, imag = parts
        for m in range(modes):
            probe_real = low[2 * m, here, :]
            probe_imag = low[2 * m + 1, here, :]
            there = slice(m * size + begin, m * size + begin + block)
            waves[there, 0:size] = (probe_real * real - probe_imag * imag).astype(BF16)
            waves[there, size:] = (probe_real * imag + probe_imag * real).astype(BF16)

    def forward_right(m, part):
        mode = slice(m * size, (m + 1) * size)
        columns = slice(part * size, (part + 1) * size)
        halves[columns, mode] = jnp.dot(
            waves[mode, :], positive[:, columns], preferred_element_type=F32
        ).astype(BF16)

    def forward_left(k):
        rows_here = slice(k * size, (k + 1) * size)
        spectra[rows_here, :] = jnp.dot(
            left_negative[rows_here, :], halves[...], preferred_element_type=F32
        )

    def reweigh(index, begin):
        slot = order[index]
        k, inside = divmod(begin, half)
        real_rows = slice(k * size + inside, k * size + inside + block)
        imag_rows = slice(k * size + half + inside, k * size + half + inside + block)
        amplitude = patterns[slot, begin : begin + block, :].astype(F32)
        mode_columns = [slice(m * size, (m + 1) * size) for m in range(modes)]
        parts = [(spectra[real_rows, mode], spectra[imag_rows, mode]) for mode in mode_columns]
        power = sum(real * real + imag * imag for real, imag in parts)
        factor = amplitude * lax.rsqrt(jnp.maximum(power, 0.5)) - 1.0
        for m, (real, imag) in enumerate(parts):
            first = k * size + m * half + inside
            there = slice(first, first + block)
            shifts[there, 0:size] = (factor * real).astype(BF16)
            shifts[there, size:] = (factor * imag).astype(BF16)

    def backward_right(k):
        product = jnp.dot(
            shifts[k * size : (k + 1) * size, :], negative[...],
            preferred_element_type=F32,
        ).astype(BF16)
        for m in range(modes):
            mode = slice(m * size, (m + 1) * size)
            for part in range(2):
                first = part * size + k * half
                backs[first : first + half, mode] = product[
                    m * half : (m + 1) * half, part * size : (part + 1) * size
                ]

    def backward_left(m, part):
        mode = slice(m * size, (m + 1) * size)
        rows_here = slice(part * size, (part + 1) * size)
        changes[rows_here, mode] = jnp.dot(
            positive[rows_here, :], backs[:, mode], preferred_element_type=F32
        )

    def deposit(index, buffer, begin):
        _, row, chunk, offset = place_of(index)
        past = lane >= offset
        here = slice(begin, begin + block)
        below = slice(size + begin, size + begin + block)
        start = begin // 8
        obj_real = patch[buffer, 0, here, :]
        obj_imag = patch[buffer, 1, here, :]

        def add(plane, value):
            sums[start : start + groups, plane] += value.reshape(groups, 8, size)

        add(2 * modes, obj_real * obj_real + obj_imag * obj_imag)
        term_real = term_imag = None
        for m in range(modes):
            mode = slice(m * size, (m + 1) * size)
            real = changes[here, mode]
            imag = changes[below, mode]
            probe_real = low[2 * m, here, :]
            probe_imag = low[2 * m + 1, here, :]
            more_real = probe_real * real + probe_imag * imag
            more_imag = probe_real * imag - probe_imag * real
            term_real = more_real if m == 0 else term_real + more_real
            term_imag = more_imag if m == 0 else term_imag + more_imag
            add(2 * m, obj_real * real + obj_imag * imag)
            add(2 * m + 1, obj_real * imag - obj_imag * real)
        for comp, term in enumerate((term_real, term_imag)):
            term = term.astype(BF16).astype(F32) * scale
            first = pltpu.roll(term[:, 0:LANES], offset, 1)
            second = pltpu.roll(term[:, LANES:], offset, 1)
            place = comp * chunks + chunk
            window = pl.ds(row + begin, block)
            values = [canvas[place + k, window, :] for k in range(3)]
            canvas[place, window, :] = values[0] + jnp.where(past, first, 0.0)
            canvas[place + 1, window, :] = values[1] + jnp.where(past, second, first)
            canvas[place + 2, window, :] = values[2] + jnp.where(past, 0.0, second)

    def step(index, carry):
        pattern_copy(order[index]).wait()
        previous = jnp.maximum(index - 1, 0)
        following = jnp.minimum(index + 1, found - 1)
        buffer = (index + 1) & 1
        starts = list(blocks)
        quarter = len(starts) // 4
        quarters = [starts[i * quarter : (i + 1) * quarter] for i in range(4)]
        for m in range(modes):
            for part in range(2):
                forward_right(m, part)
                for begin in quarters[2 * m + part]:
                    deposit(previous, buffer, begin)
        forward_left(0)
        forward_left(1)
        for begin in quarters[0] + quarters[1]:
            reweigh(index, begin)
        backward_right(0)
        for begin in quarters[2] + quarters[3]:
            reweigh(index, begin)
        for begin in quarters[0]:
            cut(following, begin)
        backward_right(1)
        for begin in quarters[1]:
            cut(following, begin)
        backward_left(0, 0)
        for begin in quarters[2]:
            cut(following, begin)
        backward_left(0, 1)
        for begin in quarters[3]:
            cut(following, begin)
        backward_left(1, 0)
        backward_left(1, 1)
        return carry

    for copy in obj_copies:
        copy.wait()

    @pl.when(found > 0)
    def _():
        for begin in blocks:
            cut(0, begin)

    if not with_border:
        for comp, j in pieces:
            index = comp * chunks + 1 + j
            canvas[index, rows, :] = obj[index, rows, :]
    for copy in later:
        copy.wait()

    @pl.when(found > 0)
    def _():
        lax.fori_loop(0, found, step, 0)
        for begin in blocks:
            deposit(found - 1, (found - 1) & 1, begin)

    last_copies = list(out_copies)
    if not with_border:
        last_copies += [
            pltpu.make_async_copy(here, there, sem) for there, here, sem in ring_pieces(ring_out)
        ]
        last_copies += [
            pltpu.make_async_copy(here, there, sem) for there, here, sem in sums_pieces(sums_out)
        ]
    for copy in last_copies:
        copy.start()
    if with_border:
        for pair in range(2):
            g_rows[pair][0 : 2 * chunks] = canvas[:, pl.ds(row_sides[pair], half), :].astype(BF16)
            for comp in range(2):
                beside = comp * chunks + col_sides[pair]
                g_cols[pair][comp] = canvas[beside, rows, :].astype(BF16)
        core = lax.axis_index("core")
        count_of = kept.shape[0]
        kept[...] = sums[pl.ds(core * count_of, count_of)]
        for plane in range(2 * modes + 1):
            for side in range(2):
                columns = slice(side * half, (side + 1) * half)
                given = sums[pl.ds((1 - core) * count_of, count_of), plane, :, columns]
                g_rows[0][2 * chunks + 2 * plane + side] = given.reshape(half, LANES).astype(BF16)
    for copy in last_copies:
        copy.wait()


def run_positions(counts, centers, object_field, patterns, probe_modes, row_halos, border=None):
    size = probe_modes.shape[-1]
    half = size // 2
    modes = probe_modes.shape[0]
    tile = object_field.shape[1]
    inner = tile // LANES
    chunks = inner + 2
    slots = patterns.shape[0]
    smem = pl.BlockSpec(memory_space=pltpu.SMEM)
    vmem = pl.BlockSpec(memory_space=pltpu.VMEM)
    anywhere = pl.BlockSpec(memory_space=pl.ANY)
    shape = jax.ShapeDtypeStruct
    in_specs = [smem, smem, anywhere, anywhere] + [vmem] * 4
    operands = [counts, centers, object_field, patterns, probe_modes, dft_tables(size), *row_halos]
    sums_shape = (size // 8, 2 * modes + 1, 8, size)
    ring_shape = (2 * inner, size, LANES)
    aliases = {}
    if border is None:
        out_specs = [anywhere] * 3
        out_shape = [shape(each, F32) for each in (object_field.shape, ring_shape, sums_shape)]
    else:
        aliases = {len(operands) + 4: 0}
        in_specs += [anywhere] * 7
        operands += list(border)
        half_sums = (size // 16,) + sums_shape[1:]
        out_specs = [anywhere] + [vmem] * 5
        out_shape = [
            shape((2, tile, tile), F32),
            shape((2 * chunks + 4 * modes + 2, half, LANES), BF16),
            shape((2 * chunks, half, LANES), BF16),
            shape((2, tile, LANES), BF16),
            shape((2, tile, LANES), BF16),
            shape(half_sums, F32),
        ]
    table = pltpu.VMEM((2 * size, 2 * size), BF16)
    products = pltpu.VMEM((2 * size, modes * size), BF16)
    wide = pltpu.VMEM((2 * size, modes * size), F32)
    padded = pltpu.VMEM((2 * chunks, tile + size, LANES), F32)
    dma = pltpu.SemaphoreType.DMA
    return pl.pallas_call(
        functools.partial(positions_kernel, border is not None),
        in_specs=in_specs,
        out_specs=out_specs,
        out_shape=out_shape,
        input_output_aliases=aliases,
        scratch_shapes=[
            padded,
            padded,
            pltpu.VMEM(patterns.shape, BF16),
            table,
            table,
            table,
            pltpu.VMEM((2 * modes, size, size), F32),
            products,
            products,
            products,
            products,
            wide,
            wide,
            pltpu.VMEM((2, 2, size, size), F32),
            pltpu.VMEM(sums_shape, F32),
            pltpu.VMEM((2, 2, tile, LANES), BF16),
            pltpu.VMEM((2, 2, size, LANES), BF16),
            pltpu.SMEM((slots + 1,), jnp.int32),
            dma((2, 2, inner)),
            dma((2, inner)),
            dma((2, 2)),
            dma((slots,)),
            dma((4,)),
            dma((4,)),
        ],
        compiler_params=pltpu.CompilerParams(
            vmem_limit_bytes=(50 if border is None else 46) * 1024 * 1024
        ),
        cost_estimate=pl.CostEstimate(
            flops=slots * 16 * modes * size**3,
            bytes_accessed=24 * 1024 * 1024,
            transcendentals=0,
        ),
        name="border" if border is not None else "interior",
    )(*operands)


def corners_kernel(col_even, col_odd, row_even, row_odd, out_even, out_odd):
    tile = col_even.shape[1]
    half = row_even.shape[1]
    chunks = row_odd.shape[0] // 2
    row_sides = sides(ROW, tile, half)
    col_sides = [offset // LANES for offset in sides(COL, chunks * LANES, half)]
    for pair, (strip, out) in enumerate(((col_even, out_even), (col_odd, out_odd))):
        out[:, half : tile - half, :] = strip[:, half : tile - half, :]
        for other, ring in enumerate((row_even, row_odd)):
            there = pl.ds(row_sides[other], half)
            for comp in range(2):
                extra = ring[comp * chunks + col_sides[pair]].astype(F32)
                out[comp, there, :] = (strip[comp, there, :].astype(F32) + extra).astype(BF16)


def add_corners(g_cols, from_rows):
    vmem = pl.BlockSpec(memory_space=pltpu.VMEM)
    shape = jax.ShapeDtypeStruct(g_cols[0].shape, BF16)
    return pl.pallas_call(
        corners_kernel,
        in_specs=[vmem] * 4,
        out_specs=[vmem] * 2,
        out_shape=[shape, shape],
        compiler_params=pltpu.CompilerParams(vmem_limit_bytes=8 * 1024 * 1024),
        cost_estimate=pl.CostEstimate(
            flops=256 * 1024, bytes_accessed=2 * 1024 * 1024, transcendentals=0
        ),
        name="corners",
    )(*g_cols, *from_rows)


def rims_kernel(
    partial, row_even, row_odd, col_even, col_odd, out, row_buffer, col_buffer, sems
):
    tile = partial.shape[1]
    half = row_even.shape[1]
    inner = tile // LANES
    chunks = inner + 2
    middle = tile - 2 * half
    row_sides = sides(ROW, tile, half)
    col_sides = sides(COL, tile, half)
    row_rings = (row_even, row_odd)
    col_strips = (col_even, col_odd)

    def copy(kind, pair, comp, inward):
        if kind == 0:
            here = row_buffer.at[pair, comp]
            place = (comp, pl.ds(row_sides[pair], half), slice(None))
        else:
            here = col_buffer.at[pair, comp]
            place = (comp, pl.ds(half, middle), pl.ds(col_sides[pair], half))
        source, target = (partial.at[place], here) if inward else (here, out.at[place])
        return pltpu.make_async_copy(
            source, target, sems.at[1 - int(inward), 2 * kind + pair, comp]
        )

    everything = [(kind, pair, comp) for kind in range(2) for pair in range(2) for comp in range(2)]
    for piece in everything:
        copy(*piece, True).start()
    for kind, pair, comp in everything:
        copy(kind, pair, comp, True).wait()
        if kind == 0:
            for j in range(inner):
                columns = slice(j * LANES, (j + 1) * LANES)
                ring = row_rings[pair][comp * chunks + 1 + j]
                row_buffer[pair, comp, :, columns] += ring.astype(F32)
            for other in range(2):
                columns = pl.ds(col_sides[other], half)
                strip = col_strips[other][comp, pl.ds(row_sides[pair], half), :]
                row_buffer[pair, comp, :, columns] += strip.astype(F32)
        else:
            strip = col_strips[pair][comp, half : half + middle, :]
            col_buffer[pair, comp] += strip.astype(F32)
        copy(kind, pair, comp, False).start()
    for piece in everything:
        copy(*piece, False).wait()


def add_rims(partial, from_rows, from_cols):
    tile = partial.shape[1]
    half = from_rows[0].shape[1]
    vmem = pl.BlockSpec(memory_space=pltpu.VMEM)
    anywhere = pl.BlockSpec(memory_space=pl.ANY)
    return pl.pallas_call(
        rims_kernel,
        in_specs=[anywhere] + [vmem] * 4,
        out_specs=anywhere,
        out_shape=jax.ShapeDtypeStruct(partial.shape, F32),
        input_output_aliases={0: 0},
        scratch_shapes=[
            pltpu.VMEM((2, 2, half, tile), F32),
            pltpu.VMEM((2, 2, tile - 2 * half, half), F32),
            pltpu.SemaphoreType.DMA((2, 4, 2)),
        ],
        compiler_params=pltpu.CompilerParams(vmem_limit_bytes=16 * 1024 * 1024),
        cost_estimate=pl.CostEstimate(
            flops=1024 * 1024, bytes_accessed=6 * 1024 * 1024, transcendentals=0
        ),
        name="rims",
    )(partial, *from_rows, *from_cols)


def chip_sums_kernel(kept_in, received, out, kept, sems):
    groups, planes, height, size = kept.shape
    half = received.shape[1]
    first = received.shape[0] - 2 * planes
    step = groups // sems.shape[0]
    parts = [pl.ds(part * step, step) for part in range(sems.shape[0])]
    copies = [
        pltpu.make_async_copy(kept_in.at[here], kept.at[here], sems.at[part])
        for part, here in enumerate(parts)
    ]
    for copy in copies:
        copy.start()
    for copy in copies:
        copy.wait()
    for plane in range(planes):
        for side in range(2):
            columns = slice(side * half, (side + 1) * half)
            other = received[first + 2 * plane + side].astype(F32).reshape(groups, height, half)
            out[:, plane, :, columns] = (kept[:, plane, :, columns] + other).astype(BF16)


def chip_sums(kept, received):
    vmem = pl.BlockSpec(memory_space=pltpu.VMEM)
    return pl.pallas_call(
        chip_sums_kernel,
        in_specs=[pl.BlockSpec(memory_space=pl.ANY), vmem],
        out_specs=vmem,
        out_shape=jax.ShapeDtypeStruct(kept.shape, BF16),
        scratch_shapes=[pltpu.VMEM(kept.shape, F32), pltpu.SemaphoreType.DMA((4,))],
        compiler_params=pltpu.CompilerParams(vmem_limit_bytes=8 * 1024 * 1024),
        cost_estimate=pl.CostEstimate(
            flops=32 * 1024**3, bytes_accessed=32 * 1024 * 1024, transcendentals=0
        ),
        name="chip_sums",
    )(kept, received)


def by_device(on_chip):
    devices = lax.axis_size("x") * lax.axis_size("col")
    groups, planes, _, size = on_chip.shape
    share = groups * 8 // devices
    if share < 8:
        on_chip = on_chip.reshape(groups, planes, 8 // share, share, size)
        return jnp.swapaxes(on_chip, 1, 2).reshape(devices, planes, share, size)
    return on_chip.reshape(devices, groups // devices, planes, 8, size)


def exchange(parts):
    return lax.all_to_all(parts, ("x", "col"), 0, 0, tiled=True)


def update_kernel(received, copies):
    devices = received.shape[0]
    total = received[0].astype(F32)
    for device in range(1, devices):
        total = total + received[device].astype(F32)
    planes = total.shape[0]
    update = (total[: planes - 1] / jnp.sqrt(total[planes - 1])).astype(BF16)
    for device in range(devices):
        copies[device] = update


def shared_update(received):
    devices, planes, share, size = received.shape
    vmem = pl.BlockSpec(memory_space=pltpu.VMEM)
    return pl.pallas_call(
        update_kernel,
        in_specs=[vmem],
        out_specs=vmem,
        out_shape=jax.ShapeDtypeStruct((devices, planes - 1, share, size), BF16),
        compiler_params=pltpu.CompilerParams(vmem_limit_bytes=8 * 1024 * 1024),
        cost_estimate=pl.CostEstimate(
            flops=512 * 1024, bytes_accessed=1024 * 1024, transcendentals=0
        ),
        name="update",
    )(received)


def finish_kernel(probe, mine, other, out):
    core = lax.axis_index("core")
    groups, planes, height, _ = mine.shape
    for side, update in enumerate((mine, other)):
        first = jnp.where(core == side, 0, groups * height)
        for group in range(groups):
            place = pl.ds(pl.multiple_of(first + group * height, height), height)
            for plane in range(planes):
                m, comp = divmod(plane, 2)
                out[m, comp, place, :] = probe[m, comp, place, :] + update[group, plane].astype(F32)


def finish_probe(probe_modes, mine):
    devices, planes, share, size = mine.shape
    if share < 8:
        mine = mine.reshape(devices * share // 8, 8 // share, planes, share, size)
        mine = jnp.swapaxes(mine, 1, 2).reshape(-1, planes, 8, size)
    other = lax.ppermute(mine, "core", [(0, 1), (1, 0)])
    vmem = pl.BlockSpec(memory_space=pltpu.VMEM)
    return pl.pallas_call(
        finish_kernel,
        in_specs=[vmem] * 3,
        out_specs=vmem,
        out_shape=jax.ShapeDtypeStruct(probe_modes.shape, F32),
        compiler_params=pltpu.CompilerParams(vmem_limit_bytes=8 * 1024 * 1024),
        cost_estimate=pl.CostEstimate(
            flops=256 * 1024, bytes_accessed=3 * 1024 * 1024, transcendentals=0
        ),
        name="finish",
    )(probe_modes, mine, other)


def on_device(object_field, probe_modes, counts, centers, patterns):
    half = probe_modes.shape[-1] // 2

    col_even, col_odd, row_even, row_odd = cut_strips(object_field, half)
    go_on = lax.axis_index("col") < 4096
    row_halos = (swap_pairs(row_even, ROW, 0), swap_pairs(row_odd, ROW, 1))
    col_halos = (swap_pairs(col_even, COL, 0), swap_pairs(col_odd, COL, 1))
    is_even = (lax.axis_index("col") & 1) == 0
    first_ends = jnp.concatenate([halo[:, :, :half] for halo in row_halos], 1)
    last_ends = jnp.concatenate([halo[:, :, -half:] for halo in row_halos], 1)
    end_halos = (
        swap_pairs(jnp.where(is_even, last_ends, first_ends), COL, 0),
        swap_pairs(jnp.where(is_even, first_ends, last_ends), COL, 1),
    )

    inputs = (counts, centers[0, 0], object_field, patterns[0, 0], probe_modes, row_halos)
    started = run_positions(*inputs)
    border = (*col_halos, *end_halos, *started)
    partial, g_row_even, g_row_odd, g_col_even, g_col_odd, kept = run_positions(*inputs, border)

    from_rows = (swap_pairs(g_row_even, ROW, 0), swap_pairs(g_row_odd, ROW, 1))
    received = lax.cond(
        go_on, exchange, jnp.zeros_like, by_device(chip_sums(kept, from_rows[0]))
    )
    row_odd, _ = lax.optimization_barrier((from_rows[1], received))
    from_rows = (from_rows[0], row_odd)
    to_even, to_odd = add_corners((g_col_even, g_col_odd), from_rows)
    received, to_even, to_odd = lax.optimization_barrier((received, to_even, to_odd))
    from_cols = (swap_pairs(to_even, COL, 0), swap_pairs(to_odd, COL, 1))
    if received.ndim == 5:
        received = received[:, 0]
    mine = lax.cond(go_on, exchange, jnp.zeros_like, shared_update(received))
    mine, from_cols, partial = lax.optimization_barrier((mine, from_cols, partial))
    new_object = add_rims(partial, from_rows, from_cols)
    return (new_object, finish_probe(probe_modes, mine))


def solution(mesh):
    rows, columns = mesh.devices.shape
    split = jax.sharding.Mesh(
        mesh.devices.reshape(rows // 2, 2, columns), ("x", "core", "col")
    )
    placed = (
        P(None, ROW, "col"),
        P(),
        P(),
        P(ROW, "col", None, None),
        P(ROW, "col", None, None, None),
    )
    return jax.shard_map(
        on_device,
        mesh=split,
        in_specs=placed,
        out_specs=(P(None, ROW, "col"), P()),
        check_vma=False,
    )
```

```python
import functools
import math

import jax
import jax.numpy as jnp
import ml_dtypes
import numpy as np
from jax import lax
from jax.experimental import pallas as pl
from jax.experimental.pallas import tpu as pltpu
from jax.sharding import PartitionSpec as P

LANES = 128
ROW = ("x", "core")
COL = ("col",)
F32 = jnp.float32
BF16 = jnp.bfloat16


def dft_tables(length):
    indices = np.arange(length)
    angles = (indices[:, None] * indices[None, :] % length) * (2.0 * np.pi / length)
    scale = 1.0 / np.sqrt(length)
    cosine = (np.cos(angles) * scale).astype(np.float32).astype(ml_dtypes.bfloat16)
    sine = (np.sin(angles) * scale).astype(np.float32).astype(ml_dtypes.bfloat16)
    return np.stack([cosine, sine, -sine])


def swap_pairs(array, axis, odd):
    devices = math.prod(lax.axis_size(name) for name in axis)
    firsts = range(odd, devices - 1, 2)
    return lax.ppermute(
        array, axis, [(i, i + 1) for i in firsts] + [(i + 1, i) for i in firsts]
    )


def sides(axis, length, width):
    even = (lax.axis_index(axis) & 1) == 0
    far = length - width
    return [
        pl.multiple_of(jnp.where(even, far, 0), width),
        pl.multiple_of(jnp.where(even, 0, far), width),
    ]


def strips_kernel(obj_hbm, col_even, col_odd, row_even, row_odd, col_buffer, row_buffer, sems):
    tile = obj_hbm.shape[1]
    half = row_even.shape[1]
    copies = []
    for pair in range(2):
        column = sides(COL, tile, half)[pair]
        row = sides(ROW, tile, half)[pair]
        copies.append(
            pltpu.make_async_copy(
                obj_hbm.at[:, :, pl.ds(column, half)], col_buffer.at[pair], sems.at[0, pair]
            )
        )
        copies.append(
            pltpu.make_async_copy(
                obj_hbm.at[:, pl.ds(row, half), :], row_buffer.at[pair], sems.at[1, pair]
            )
        )
    for copy in copies:
        copy.start()
    outputs = (col_even, row_even, col_odd, row_odd)
    buffers = (col_buffer, row_buffer) * 2
    for index, copy in enumerate(copies):
        copy.wait()
        outputs[index][...] = buffers[index][index // 2].astype(BF16)


def cut_strips(object_field, half):
    tile = object_field.shape[1]
    vmem = pl.BlockSpec(memory_space=pltpu.VMEM)
    columns = jax.ShapeDtypeStruct((2, tile, half), BF16)
    rows = jax.ShapeDtypeStruct((2, half, tile), BF16)
    return pl.pallas_call(
        strips_kernel,
        in_specs=[pl.BlockSpec(memory_space=pltpu.HBM)],
        out_specs=[vmem] * 4,
        out_shape=[columns, columns, rows, rows],
        scratch_shapes=[
            pltpu.VMEM((2, 2, tile, half), F32),
            pltpu.VMEM((2, 2, half, tile), F32),
            pltpu.SemaphoreType.DMA((2, 2)),
        ],
        compiler_params=pltpu.CompilerParams(vmem_limit_bytes=50 * 1024 * 1024),
        cost_estimate=pl.CostEstimate(
            flops=1024 * 1024, bytes_accessed=5 * 1024 * 1024, transcendentals=0
        ),
        name="strips",
    )(object_field)


def positions_kernel(with_border, *refs):
    counts, centers, obj_hbm, pat_hbm, probe = refs[:5]
    tables, row_halos = refs[5], refs[6:8]
    refs = refs[8:]
    if with_border:
        col_halos = refs[0:2]
        start_hbm, ring_in, sums_in = refs[2:5]
        out_hbm, g_rows, g_cols, kept = refs[5], refs[6:8], refs[8:10], refs[10]
        refs = refs[11:]
    else:
        out_hbm, ring_out, sums_out = refs[:3]
        refs = refs[3:]
    (obj, canvas, patterns, positive, negative, low, waves, shifts, halves, backs,
     spectra, changes, patch, sums, order, piece_sems, out_sems, ring_sems, pat_sems,
     sums_sems) = refs
    size = probe.shape[-1]
    half = size // 2
    tile = obj_hbm.shape[1]
    inner = tile // LANES
    chunks = inner + 2
    modes = probe.shape[0]
    rows = slice(half, half + tile)
    near = [0, 1, inner - 2, inner - 1] if with_border else list(range(inner))
    pieces = [(comp, j) for comp in range(2) for j in near]

    def home(array, comp, j):
        return array.at[comp, :, pl.ds(j * LANES, LANES)]

    def held(array, comp, j):
        return array.at[comp * chunks + 1 + j, pl.ds(half, tile), :]

    def ring_pieces(array):
        for comp in range(2):
            for side, row in enumerate((0, half + tile)):
                yield (
                    array.at[pl.ds(comp * inner, inner), pl.ds(side * half, half), :],
                    canvas.at[pl.ds(comp * chunks + 1, inner), pl.ds(row, half), :],
                    ring_sems.at[side, comp],
                )

    def sums_pieces(array):
        step = array.shape[0] // sums_parts
        for part in range(sums_parts):
            here = pl.ds(part * step, step)
            yield array.at[here], sums.at[here], sums_sems.at[part]

    sums_parts = sums_sems.shape[0]
    obj_copies = [
        pltpu.make_async_copy(home(obj_hbm, *p), held(obj, *p), piece_sems.at[0, *p])
        for p in pieces
    ]
    out_copies = [
        pltpu.make_async_copy(held(canvas, *p), home(out_hbm, *p), out_sems.at[p]) for p in pieces
    ]
    later = []
    if with_border:
        later += [
            pltpu.make_async_copy(home(start_hbm, *p), held(canvas, *p), piece_sems.at[1, *p])
            for p in pieces
        ]
        later += [pltpu.make_async_copy(*each) for each in ring_pieces(ring_in)]
        later += [pltpu.make_async_copy(*each) for each in sums_pieces(sums_in)]
    for copy in obj_copies + later:
        copy.start()

    order[0] = 0
    count = counts[lax.axis_index(ROW), lax.axis_index("col")]

    def pattern_copy(slot):
        return pltpu.make_async_copy(pat_hbm.at[slot], patterns.at[slot], pat_sems.at[slot])

    def note(slot, found):
        column = centers[1, slot]
        inside = (column >= half) & (column <= tile - half)
        order[found] = slot
        return found + jnp.where(inside, 0 if with_border else 1, 1 if with_border else 0)

    def fetch(index, carry):
        pattern_copy(order[index]).start()
        return carry

    found = lax.fori_loop(0, count, note, 0)
    lax.fori_loop(0, found, fetch, 0)

    if not with_border:
        sums[...] = jnp.zeros_like(sums)
    intensity = jnp.zeros((size, size), F32)
    for m in range(modes):
        for comp in range(2):
            values = probe[m, comp]
            intensity = intensity + values * values
            low[2 * m + comp] = values.astype(BF16).astype(F32)
    scale = 1.0 / (jnp.max(intensity) + 1e-06)
    for turn, inverse in ((positive, True), (negative, False)):
        upper, lower = (2, 1) if inverse else (1, 2)
        turn[0:size, 0:size] = tables[0]
        turn[0:size, size:] = tables[upper]
        turn[size:, 0:size] = tables[lower]
        turn[size:, size:] = tables[0]
    changes[...] = jnp.zeros_like(changes)
    patch[...] = jnp.zeros_like(patch)

    row_sides = sides(ROW, tile + size, half)
    col_sides = [offset // LANES for offset in sides(COL, tile + size, half)]
    blank = jnp.zeros((tile + size, LANES), F32)
    for comp in range(2):
        first = comp * chunks
        for pair in range(2):
            for j in near:
                columns = slice(j * LANES, (j + 1) * LANES)
                obj[first + 1 + j, pl.ds(row_sides[pair], half), :] = row_halos[pair][
                    comp, :, columns
                ].astype(F32)
            if with_border:
                beside = first + col_sides[pair]
                canvas[beside] = blank
                obj[beside, rows, :] = col_halos[pair][comp, 0:tile, :].astype(F32)
                for other in range(2):
                    obj[beside, pl.ds(row_sides[other], half), :] = col_halos[pair][
                        comp, tile + other * half : tile + (other + 1) * half, :
                    ].astype(F32)
        if not with_border:
            for j in range(inner):
                canvas[first + 1 + j, 0:half, :] = blank[0:half]
                canvas[first + 1 + j, half + tile :, :] = blank[0:half]

    block = 16
    groups = block // 8
    lane = lax.broadcasted_iota(jnp.int32, (block, LANES), 1)
    blocks = range(0, size, block)

    def place_of(index):
        slot = order[index]
        column = centers[1, slot]
        return slot, centers[0, slot], column >> 7, column & 127

    def cut(index, begin):
        _, row, chunk, offset = place_of(index)
        back_offset = (LANES - offset) & 127
        from_first = lane < LANES - offset
        here = slice(begin, begin + block)
        parts = []
        for comp in range(2):
            moved = [
                pltpu.roll(
                    obj[comp * chunks + chunk + k, pl.ds(row + begin, block), :], back_offset, 1
                )
                for k in range(3)
            ]
            window = jnp.concatenate(
                [
                    jnp.where(from_first, moved[0], moved[1]),
                    jnp.where(from_first, moved[1], moved[2]),
                ],
                1,
            ).astype(BF16).astype(F32)
            patch[index & 1, comp, here, :] = window
            parts.append(window)
        real, imag = parts
        for m in range(modes):
            probe_real = low[2 * m, here, :]
            probe_imag = low[2 * m + 1, here, :]
            there = slice(m * size + begin, m * size + begin + block)
            waves[there, 0:size] = (probe_real * real - probe_imag * imag).astype(BF16)
            waves[there, size:] = (probe_real * imag + probe_imag * real).astype(BF16)

    def forward_right(part):
        columns = slice(part * size, (part + 1) * size)
        product = jnp.dot(
            waves[...], positive[:, columns], preferred_element_type=F32
        ).astype(BF16)
        for m in range(modes):
            mode = slice(m * size, (m + 1) * size)
            halves[columns, mode] = product[mode, :]

    def forward_left(m):
        mode = slice(m * size, (m + 1) * size)
        spectra[:, mode] = jnp.dot(
            negative[...], halves[:, mode], preferred_element_type=F32
        )

    def reweigh(index, begin):
        slot = order[index]
        here = slice(begin, begin + block)
        below = slice(size + begin, size + begin + block)
        amplitude = patterns[slot, here, :].astype(F32)
        mode_columns = [slice(m * size, (m + 1) * size) for m in range(modes)]
        parts = [(spectra[here, mode], spectra[below, mode]) for mode in mode_columns]
        power = sum(real * real + imag * imag for real, imag in parts)
        factor = amplitude * lax.rsqrt(jnp.maximum(power, 0.5)) - 1.0
        for m, (real, imag) in enumerate(parts):
            there = slice(m * size + begin, m * size + begin + block)
            shifts[there, 0:size] = (factor * real).astype(BF16)
            shifts[there, size:] = (factor * imag).astype(BF16)

    def backward_right(part):
        columns = slice(part * size, (part + 1) * size)
        product = jnp.dot(
            shifts[...], negative[:, columns], preferred_element_type=F32
        ).astype(BF16)
        for m in range(modes):
            mode = slice(m * size, (m + 1) * size)
            backs[columns, mode] = product[mode, :]

    def backward_left(m):
        mode = slice(m * size, (m + 1) * size)
        changes[:, mode] = jnp.dot(
            positive[...], backs[:, mode], preferred_element_type=F32
        )

    def deposit(index, buffer, begin):
        _, row, chunk, offset = place_of(index)
        past = lane >= offset
        here = slice(begin, begin + block)
        below = slice(size + begin, size + begin + block)
        start = begin // 8
        obj_real = patch[buffer, 0, here, :]
        obj_imag = patch[buffer, 1, here, :]

        def add(plane, value):
            sums[start : start + groups, plane] += value.reshape(groups, 8, size)

        add(2 * modes, obj_real * obj_real + obj_imag * obj_imag)
        term_real = term_imag = None
        for m in range(modes):
            mode = slice(m * size, (m + 1) * size)
            real = changes[here, mode]
            imag = changes[below, mode]
            probe_real = low[2 * m, here, :]
            probe_imag = low[2 * m + 1, here, :]
            more_real = probe_real * real + probe_imag * imag
            more_imag = probe_real * imag - probe_imag * real
            term_real = more_real if m == 0 else term_real + more_real
            term_imag = more_imag if m == 0 else term_imag + more_imag
            add(2 * m, obj_real * real + obj_imag * imag)
            add(2 * m + 1, obj_real * imag - obj_imag * real)
        for comp, term in enumerate((term_real, term_imag)):
            term = term.astype(BF16).astype(F32) * scale
            first = pltpu.roll(term[:, 0:LANES], offset, 1)
            second = pltpu.roll(term[:, LANES:], offset, 1)
            place = comp * chunks + chunk
            window = pl.ds(row + begin, block)
            values = [canvas[place + k, window, :] for k in range(3)]
            canvas[place, window, :] = values[0] + jnp.where(past, first, 0.0)
            canvas[place + 1, window, :] = values[1] + jnp.where(past, second, first)
            canvas[place + 2, window, :] = values[2] + jnp.where(past, 0.0, second)

    def step(index, carry):
        pattern_copy(order[index]).wait()
        previous = jnp.maximum(index - 1, 0)
        following = jnp.minimum(index + 1, found - 1)
        buffer = (index + 1) & 1
        starts = list(blocks)
        quarter = len(starts) // 4
        quarters = [starts[i * quarter : (i + 1) * quarter] for i in range(4)]
        forward_right(0)
        for begin in quarters[0] + quarters[1]:
            deposit(previous, buffer, begin)
        forward_right(1)
        for begin in quarters[2] + quarters[3]:
            deposit(previous, buffer, begin)
        for m in range(modes):
            forward_left(m)
        for begin in starts:
            reweigh(index, begin)
        for part in range(2):
            backward_right(part)
            for begin in quarters[part]:
                cut(following, begin)
        for m in range(modes):
            backward_left(m)
            for begin in quarters[2 + m]:
                cut(following, begin)
        return carry

    for copy in obj_copies:
        copy.wait()

    @pl.when(found > 0)
    def _():
        for begin in blocks:
            cut(0, begin)

    if not with_border:
        for comp, j in pieces:
            index = comp * chunks + 1 + j
            canvas[index, rows, :] = obj[index, rows, :]
    for copy in later:
        copy.wait()

    @pl.when(found > 0)
    def _():
        lax.fori_loop(0, found, step, 0)
        for begin in blocks:
            deposit(found - 1, (found - 1) & 1, begin)

    last_copies = list(out_copies)
    if not with_border:
        last_copies += [
            pltpu.make_async_copy(here, there, sem) for there, here, sem in ring_pieces(ring_out)
        ]
        last_copies += [
            pltpu.make_async_copy(here, there, sem) for there, here, sem in sums_pieces(sums_out)
        ]
    for copy in last_copies:
        copy.start()
    if with_border:
        for pair in range(2):
            g_rows[pair][0 : 2 * chunks] = canvas[:, pl.ds(row_sides[pair], half), :].astype(BF16)
            for comp in range(2):
                beside = comp * chunks + col_sides[pair]
                g_cols[pair][comp] = canvas[beside, rows, :].astype(BF16)
        core = lax.axis_index("core")
        count_of = kept.shape[0]
        kept[...] = sums[pl.ds(core * count_of, count_of)]
        for plane in range(2 * modes + 1):
            for side in range(2):
                columns = slice(side * half, (side + 1) * half)
                given = sums[pl.ds((1 - core) * count_of, count_of), plane, :, columns]
                g_rows[0][2 * chunks + 2 * plane + side] = given.reshape(half, LANES).astype(BF16)
    for copy in last_copies:
        copy.wait()


def run_positions(counts, centers, object_field, patterns, probe_modes, row_halos, border=None):
    size = probe_modes.shape[-1]
    half = size // 2
    modes = probe_modes.shape[0]
    tile = object_field.shape[1]
    inner = tile // LANES
    chunks = inner + 2
    slots = patterns.shape[0]
    smem = pl.BlockSpec(memory_space=pltpu.SMEM)
    vmem = pl.BlockSpec(memory_space=pltpu.VMEM)
    anywhere = pl.BlockSpec(memory_space=pl.ANY)
    shape = jax.ShapeDtypeStruct
    in_specs = [smem, smem, anywhere, anywhere] + [vmem] * 4
    operands = [counts, centers, object_field, patterns, probe_modes, dft_tables(size), *row_halos]
    sums_shape = (size // 8, 2 * modes + 1, 8, size)
    ring_shape = (2 * inner, size, LANES)
    aliases = {}
    if border is None:
        out_specs = [anywhere] * 3
        out_shape = [shape(each, F32) for each in (object_field.shape, ring_shape, sums_shape)]
    else:
        aliases = {len(operands) + 2: 0}
        in_specs += [vmem] * 2 + [anywhere] * 3
        operands += list(border)
        half_sums = (size // 16,) + sums_shape[1:]
        out_specs = [anywhere] + [vmem] * 5
        out_shape = [
            shape((2, tile, tile), F32),
            shape((2 * chunks + 4 * modes + 2, half, LANES), BF16),
            shape((2 * chunks, half, LANES), BF16),
            shape((2, tile, LANES), BF16),
            shape((2, tile, LANES), BF16),
            shape(half_sums, F32),
        ]
    table = pltpu.VMEM((2 * size, 2 * size), BF16)
    products = pltpu.VMEM((2 * size, modes * size), BF16)
    wide = pltpu.VMEM((2 * size, modes * size), F32)
    padded = pltpu.VMEM((2 * chunks, tile + size, LANES), F32)
    dma = pltpu.SemaphoreType.DMA
    return pl.pallas_call(
        functools.partial(positions_kernel, border is not None),
        in_specs=in_specs,
        out_specs=out_specs,
        out_shape=out_shape,
        input_output_aliases=aliases,
        scratch_shapes=[
            padded,
            padded,
            pltpu.VMEM(patterns.shape, BF16),
            table,
            table,
            pltpu.VMEM((2 * modes, size, size), F32),
            products,
            products,
            products,
            products,
            wide,
            wide,
            pltpu.VMEM((2, 2, size, size), F32),
            pltpu.VMEM(sums_shape, F32),
            pltpu.SMEM((slots + 1,), jnp.int32),
            dma((2, 2, inner)),
            dma((2, inner)),
            dma((2, 2)),
            dma((slots,)),
            dma((4,)),
        ],
        compiler_params=pltpu.CompilerParams(
            vmem_limit_bytes=(50 if border is None else 46) * 1024 * 1024
        ),
        cost_estimate=pl.CostEstimate(
            flops=slots * 16 * modes * size**3,
            bytes_accessed=24 * 1024 * 1024,
            transcendentals=0,
        ),
        name="border" if border is not None else "interior",
    )(*operands)


def corners_kernel(col_even, col_odd, row_even, row_odd, out_even, out_odd):
    tile = col_even.shape[1]
    half = row_even.shape[1]
    chunks = row_odd.shape[0] // 2
    row_sides = sides(ROW, tile, half)
    col_sides = [offset // LANES for offset in sides(COL, chunks * LANES, half)]
    for pair, (strip, out) in enumerate(((col_even, out_even), (col_odd, out_odd))):
        out[:, half : tile - half, :] = strip[:, half : tile - half, :]
        for other, ring in enumerate((row_even, row_odd)):
            there = pl.ds(row_sides[other], half)
            for comp in range(2):
                extra = ring[comp * chunks + col_sides[pair]].astype(F32)
                out[comp, there, :] = (strip[comp, there, :].astype(F32) + extra).astype(BF16)


def add_corners(g_cols, from_rows):
    vmem = pl.BlockSpec(memory_space=pltpu.VMEM)
    shape = jax.ShapeDtypeStruct(g_cols[0].shape, BF16)
    return pl.pallas_call(
        corners_kernel,
        in_specs=[vmem] * 4,
        out_specs=[vmem] * 2,
        out_shape=[shape, shape],
        compiler_params=pltpu.CompilerParams(vmem_limit_bytes=8 * 1024 * 1024),
        cost_estimate=pl.CostEstimate(
            flops=256 * 1024, bytes_accessed=2 * 1024 * 1024, transcendentals=0
        ),
        name="corners",
    )(*g_cols, *from_rows)


def rims_kernel(
    partial, row_even, row_odd, col_even, col_odd, out, row_buffer, col_buffer, sems
):
    tile = partial.shape[1]
    half = row_even.shape[1]
    inner = tile // LANES
    chunks = inner + 2
    middle = tile - 2 * half
    row_sides = sides(ROW, tile, half)
    col_sides = sides(COL, tile, half)
    row_rings = (row_even, row_odd)
    col_strips = (col_even, col_odd)

    def copy(kind, pair, comp, inward):
        if kind == 0:
            here = row_buffer.at[pair, comp]
            place = (comp, pl.ds(row_sides[pair], half), slice(None))
        else:
            here = col_buffer.at[pair, comp]
            place = (comp, pl.ds(half, middle), pl.ds(col_sides[pair], half))
        source, target = (partial.at[place], here) if inward else (here, out.at[place])
        return pltpu.make_async_copy(
            source, target, sems.at[1 - int(inward), 2 * kind + pair, comp]
        )

    everything = [(kind, pair, comp) for kind in range(2) for pair in range(2) for comp in range(2)]
    for piece in everything:
        copy(*piece, True).start()
    for kind, pair, comp in everything:
        copy(kind, pair, comp, True).wait()
        if kind == 0:
            for j in range(inner):
                columns = slice(j * LANES, (j + 1) * LANES)
                ring = row_rings[pair][comp * chunks + 1 + j]
                row_buffer[pair, comp, :, columns] += ring.astype(F32)
            for other in range(2):
                columns = pl.ds(col_sides[other], half)
                strip = col_strips[other][comp, pl.ds(row_sides[pair], half), :]
                row_buffer[pair, comp, :, columns] += strip.astype(F32)
        else:
            strip = col_strips[pair][comp, half : half + middle, :]
            col_buffer[pair, comp] += strip.astype(F32)
        copy(kind, pair, comp, False).start()
    for piece in everything:
        copy(*piece, False).wait()


def add_rims(partial, from_rows, from_cols):
    tile = partial.shape[1]
    half = from_rows[0].shape[1]
    vmem = pl.BlockSpec(memory_space=pltpu.VMEM)
    anywhere = pl.BlockSpec(memory_space=pl.ANY)
    return pl.pallas_call(
        rims_kernel,
        in_specs=[anywhere] + [vmem] * 4,
        out_specs=anywhere,
        out_shape=jax.ShapeDtypeStruct(partial.shape, F32),
        input_output_aliases={0: 0},
        scratch_shapes=[
            pltpu.VMEM((2, 2, half, tile), F32),
            pltpu.VMEM((2, 2, tile - 2 * half, half), F32),
            pltpu.SemaphoreType.DMA((2, 4, 2)),
        ],
        compiler_params=pltpu.CompilerParams(vmem_limit_bytes=16 * 1024 * 1024),
        cost_estimate=pl.CostEstimate(
            flops=1024 * 1024, bytes_accessed=6 * 1024 * 1024, transcendentals=0
        ),
        name="rims",
    )(partial, *from_rows, *from_cols)


def chip_sums_kernel(kept_in, received, out, kept, sems):
    groups, planes, height, size = kept.shape
    half = received.shape[1]
    first = received.shape[0] - 2 * planes
    step = groups // sems.shape[0]
    parts = [pl.ds(part * step, step) for part in range(sems.shape[0])]
    copies = [
        pltpu.make_async_copy(kept_in.at[here], kept.at[here], sems.at[part])
        for part, here in enumerate(parts)
    ]
    for copy in copies:
        copy.start()
    for copy in copies:
        copy.wait()
    for plane in range(planes):
        for side in range(2):
            columns = slice(side * half, (side + 1) * half)
            other = received[first + 2 * plane + side].astype(F32).reshape(groups, height, half)
            out[:, plane, :, columns] = (kept[:, plane, :, columns] + other).astype(BF16)


def chip_sums(kept, received):
    vmem = pl.BlockSpec(memory_space=pltpu.VMEM)
    return pl.pallas_call(
        chip_sums_kernel,
        in_specs=[pl.BlockSpec(memory_space=pl.ANY), vmem],
        out_specs=vmem,
        out_shape=jax.ShapeDtypeStruct(kept.shape, BF16),
        scratch_shapes=[pltpu.VMEM(kept.shape, F32), pltpu.SemaphoreType.DMA((4,))],
        compiler_params=pltpu.CompilerParams(vmem_limit_bytes=8 * 1024 * 1024),
        cost_estimate=pl.CostEstimate(
            flops=32 * 1024**3, bytes_accessed=32 * 1024 * 1024, transcendentals=0
        ),
        name="chip_sums",
    )(kept, received)


def by_device(on_chip):
    devices = lax.axis_size("x") * lax.axis_size("col")
    groups, planes, _, size = on_chip.shape
    share = groups * 8 // devices
    if share < 8:
        on_chip = on_chip.reshape(groups, planes, 8 // share, share, size)
        return jnp.swapaxes(on_chip, 1, 2).reshape(devices, planes, share, size)
    return on_chip.reshape(devices, groups // devices, planes, 8, size)


def exchange(parts):
    return lax.all_to_all(parts, ("x", "col"), 0, 0, tiled=True)


def update_kernel(received, copies):
    devices = received.shape[0]
    total = received[0].astype(F32)
    for device in range(1, devices):
        total = total + received[device].astype(F32)
    planes = total.shape[0]
    update = (total[: planes - 1] / jnp.sqrt(total[planes - 1])).astype(BF16)
    for device in range(devices):
        copies[device] = update


def shared_update(received):
    devices, planes, share, size = received.shape
    vmem = pl.BlockSpec(memory_space=pltpu.VMEM)
    return pl.pallas_call(
        update_kernel,
        in_specs=[vmem],
        out_specs=vmem,
        out_shape=jax.ShapeDtypeStruct((devices, planes - 1, share, size), BF16),
        compiler_params=pltpu.CompilerParams(vmem_limit_bytes=8 * 1024 * 1024),
        cost_estimate=pl.CostEstimate(
            flops=512 * 1024, bytes_accessed=1024 * 1024, transcendentals=0
        ),
        name="update",
    )(received)


def finish_kernel(probe, mine, other, out):
    core = lax.axis_index("core")
    groups, planes, height, _ = mine.shape
    for side, update in enumerate((mine, other)):
        first = jnp.where(core == side, 0, groups * height)
        for group in range(groups):
            place = pl.ds(pl.multiple_of(first + group * height, height), height)
            for plane in range(planes):
                m, comp = divmod(plane, 2)
                out[m, comp, place, :] = probe[m, comp, place, :] + update[group, plane].astype(F32)


def finish_probe(probe_modes, mine):
    devices, planes, share, size = mine.shape
    if share < 8:
        mine = mine.reshape(devices * share // 8, 8 // share, planes, share, size)
        mine = jnp.swapaxes(mine, 1, 2).reshape(-1, planes, 8, size)
    other = lax.ppermute(mine, "core", [(0, 1), (1, 0)])
    vmem = pl.BlockSpec(memory_space=pltpu.VMEM)
    return pl.pallas_call(
        finish_kernel,
        in_specs=[vmem] * 3,
        out_specs=vmem,
        out_shape=jax.ShapeDtypeStruct(probe_modes.shape, F32),
        compiler_params=pltpu.CompilerParams(vmem_limit_bytes=8 * 1024 * 1024),
        cost_estimate=pl.CostEstimate(
            flops=256 * 1024, bytes_accessed=3 * 1024 * 1024, transcendentals=0
        ),
        name="finish",
    )(probe_modes, mine, other)


def on_device(object_field, probe_modes, counts, centers, patterns):
    half = probe_modes.shape[-1] // 2

    col_even, col_odd, row_even, row_odd = cut_strips(object_field, half)
    go_on = lax.axis_index("col") < 4096
    row_halos = (swap_pairs(row_even, ROW, 0), swap_pairs(row_odd, ROW, 1))
    col_halos = (swap_pairs(col_even, COL, 0), swap_pairs(col_odd, COL, 1))
    is_even = (lax.axis_index("col") & 1) == 0
    first_ends = jnp.concatenate([halo[:, :, :half] for halo in row_halos], 1)
    last_ends = jnp.concatenate([halo[:, :, -half:] for halo in row_halos], 1)
    end_halos = (
        swap_pairs(jnp.where(is_even, last_ends, first_ends), COL, 0),
        swap_pairs(jnp.where(is_even, first_ends, last_ends), COL, 1),
    )

    inputs = (counts, centers[0, 0], object_field, patterns[0, 0], probe_modes, row_halos)
    started = run_positions(*inputs)
    joined = [jnp.concatenate(both, 1) for both in zip(col_halos, end_halos)]
    border = (*joined, *started)
    partial, g_row_even, g_row_odd, g_col_even, g_col_odd, kept = run_positions(*inputs, border)

    from_rows = (swap_pairs(g_row_even, ROW, 0), swap_pairs(g_row_odd, ROW, 1))
    received = lax.cond(
        go_on, exchange, jnp.zeros_like, by_device(chip_sums(kept, from_rows[0]))
    )
    row_odd, _ = lax.optimization_barrier((from_rows[1], received))
    from_rows = (from_rows[0], row_odd)
    to_even, to_odd = add_corners((g_col_even, g_col_odd), from_rows)
    received, to_even, to_odd = lax.optimization_barrier((received, to_even, to_odd))
    from_cols = (swap_pairs(to_even, COL, 0), swap_pairs(to_odd, COL, 1))
    if received.ndim == 5:
        received = received[:, 0]
    mine = lax.cond(go_on, exchange, jnp.zeros_like, shared_update(received))
    mine, from_cols, partial = lax.optimization_barrier((mine, from_cols, partial))
    new_object = add_rims(partial, from_rows, from_cols)
    return (new_object, finish_probe(probe_modes, mine))


def solution(mesh):
    rows, columns = mesh.devices.shape
    split = jax.sharding.Mesh(
        mesh.devices.reshape(rows // 2, 2, columns), ("x", "core", "col")
    )
    placed = (
        P(None, ROW, "col"),
        P(),
        P(),
        P(ROW, "col", None, None),
        P(ROW, "col", None, None, None),
    )
    return jax.shard_map(
        on_device,
        mesh=split,
        in_specs=placed,
        out_specs=(P(None, ROW, "col"), P()),
        check_vma=False,
    )
```

```python
import functools
import math

import jax
import jax.numpy as jnp
import ml_dtypes
import numpy as np
from jax import lax
from jax.experimental import pallas as pl
from jax.experimental.pallas import tpu as pltpu
from jax.sharding import PartitionSpec as P

LANES = 128
ROW = ("x", "core")
COL = ("col",)
F32 = jnp.float32
BF16 = jnp.bfloat16


def dft_tables(length):
    indices = np.arange(length)
    angles = (indices[:, None] * indices[None, :] % length) * (2.0 * np.pi / length)
    scale = 1.0 / np.sqrt(length)
    cosine = (np.cos(angles) * scale).astype(np.float32).astype(ml_dtypes.bfloat16)
    sine = (np.sin(angles) * scale).astype(np.float32).astype(ml_dtypes.bfloat16)
    return np.stack([cosine, sine, -sine])


def swap_pairs(array, axis, odd):
    devices = math.prod(lax.axis_size(name) for name in axis)
    firsts = range(odd, devices - 1, 2)
    return lax.ppermute(
        array, axis, [(i, i + 1) for i in firsts] + [(i + 1, i) for i in firsts]
    )


def sides(axis, length, width):
    even = (lax.axis_index(axis) & 1) == 0
    far = length - width
    return [
        pl.multiple_of(jnp.where(even, far, 0), width),
        pl.multiple_of(jnp.where(even, 0, far), width),
    ]


def strips_kernel(obj_hbm, col_even, col_odd, row_even, row_odd, col_buffer, row_buffer, sems):
    tile = obj_hbm.shape[1]
    half = row_even.shape[1]
    copies = []
    for pair in range(2):
        column = sides(COL, tile, half)[pair]
        row = sides(ROW, tile, half)[pair]
        copies.append(
            pltpu.make_async_copy(
                obj_hbm.at[:, :, pl.ds(column, half)], col_buffer.at[pair], sems.at[0, pair]
            )
        )
        copies.append(
            pltpu.make_async_copy(
                obj_hbm.at[:, pl.ds(row, half), :], row_buffer.at[pair], sems.at[1, pair]
            )
        )
    for copy in copies:
        copy.start()
    outputs = (col_even, row_even, col_odd, row_odd)
    buffers = (col_buffer, row_buffer) * 2
    for index, copy in enumerate(copies):
        copy.wait()
        outputs[index][...] = buffers[index][index // 2].astype(BF16)


def cut_strips(object_field, half):
    tile = object_field.shape[1]
    vmem = pl.BlockSpec(memory_space=pltpu.VMEM)
    columns = jax.ShapeDtypeStruct((2, tile, half), BF16)
    rows = jax.ShapeDtypeStruct((2, half, tile), BF16)
    return pl.pallas_call(
        strips_kernel,
        in_specs=[pl.BlockSpec(memory_space=pltpu.HBM)],
        out_specs=[vmem] * 4,
        out_shape=[columns, columns, rows, rows],
        scratch_shapes=[
            pltpu.VMEM((2, 2, tile, half), F32),
            pltpu.VMEM((2, 2, half, tile), F32),
            pltpu.SemaphoreType.DMA((2, 2)),
        ],
        compiler_params=pltpu.CompilerParams(vmem_limit_bytes=50 * 1024 * 1024),
        cost_estimate=pl.CostEstimate(
            flops=1024 * 1024, bytes_accessed=5 * 1024 * 1024, transcendentals=0
        ),
        name="strips",
    )(object_field)


def positions_kernel(with_border, *refs):
    counts, centers, obj_hbm, pat_hbm, probe = refs[:5]
    tables, row_halos = refs[5], refs[6:8]
    refs = refs[8:]
    if with_border:
        col_halos = refs[0:2]
        start_hbm, ring_in, sums_in = refs[2:5]
        out_hbm, g_rows, g_cols, kept = refs[5], refs[6:8], refs[8:10], refs[10]
        refs = refs[11:]
    else:
        out_hbm, ring_out, sums_out = refs[:3]
        refs = refs[3:]
    (obj, canvas, patterns, positive, negative, left_negative, low, waves, shifts, halves, backs,
     spectra, changes, patch, sums, order, piece_sems, out_sems, ring_sems, pat_sems,
     sums_sems) = refs
    size = probe.shape[-1]
    half = size // 2
    tile = obj_hbm.shape[1]
    inner = tile // LANES
    chunks = inner + 2
    modes = probe.shape[0]
    rows = slice(half, half + tile)
    near = [0, 1, inner - 2, inner - 1] if with_border else list(range(inner))
    pieces = [(comp, j) for comp in range(2) for j in near]

    def home(array, comp, j):
        return array.at[comp, :, pl.ds(j * LANES, LANES)]

    def held(array, comp, j):
        return array.at[comp * chunks + 1 + j, pl.ds(half, tile), :]

    def ring_pieces(array):
        for comp in range(2):
            for side, row in enumerate((0, half + tile)):
                yield (
                    array.at[pl.ds(comp * inner, inner), pl.ds(side * half, half), :],
                    canvas.at[pl.ds(comp * chunks + 1, inner), pl.ds(row, half), :],
                    ring_sems.at[side, comp],
                )

    def sums_pieces(array):
        step = array.shape[0] // sums_parts
        for part in range(sums_parts):
            here = pl.ds(part * step, step)
            yield array.at[here], sums.at[here], sums_sems.at[part]

    sums_parts = sums_sems.shape[0]
    obj_copies = [
        pltpu.make_async_copy(home(obj_hbm, *p), held(obj, *p), piece_sems.at[0, *p])
        for p in pieces
    ]
    out_copies = [
        pltpu.make_async_copy(held(canvas, *p), home(out_hbm, *p), out_sems.at[p]) for p in pieces
    ]
    later = []
    if with_border:
        later += [
            pltpu.make_async_copy(home(start_hbm, *p), held(canvas, *p), piece_sems.at[1, *p])
            for p in pieces
        ]
        later += [pltpu.make_async_copy(*each) for each in ring_pieces(ring_in)]
        later += [pltpu.make_async_copy(*each) for each in sums_pieces(sums_in)]
    for copy in obj_copies + later:
        copy.start()

    order[0] = 0
    count = counts[lax.axis_index(ROW), lax.axis_index("col")]

    def pattern_copy(slot):
        return pltpu.make_async_copy(pat_hbm.at[slot], patterns.at[slot], pat_sems.at[slot])

    def note(slot, found):
        column = centers[1, slot]
        inside = (column >= half) & (column <= tile - half)
        order[found] = slot
        return found + jnp.where(inside, 0 if with_border else 1, 1 if with_border else 0)

    def fetch(index, carry):
        pattern_copy(order[index]).start()
        return carry

    found = lax.fori_loop(0, count, note, 0)
    lax.fori_loop(0, found, fetch, 0)

    if not with_border:
        sums[...] = jnp.zeros_like(sums)
    intensity = jnp.zeros((size, size), F32)
    for m in range(modes):
        for comp in range(2):
            values = probe[m, comp]
            intensity = intensity + values * values
            low[2 * m + comp] = values.astype(BF16).astype(F32)
    scale = 1.0 / (jnp.max(intensity) + 1e-06)
    for turn, inverse in ((positive, True), (negative, False)):
        upper, lower = (2, 1) if inverse else (1, 2)
        turn[0:size, 0:size] = tables[0]
        turn[0:size, size:] = tables[upper]
        turn[size:, 0:size] = tables[lower]
        turn[size:, size:] = tables[0]
    for k in range(2):
        rows_here = slice(k * half, (k + 1) * half)
        first = k * size
        left_negative[first : first + half, 0:size] = tables[0, rows_here]
        left_negative[first : first + half, size:] = tables[1, rows_here]
        left_negative[first + half : first + size, 0:size] = tables[2, rows_here]
        left_negative[first + half : first + size, size:] = tables[0, rows_here]
    changes[...] = jnp.zeros_like(changes)
    patch[...] = jnp.zeros_like(patch)

    row_sides = sides(ROW, tile + size, half)
    col_sides = [offset // LANES for offset in sides(COL, tile + size, half)]
    blank = jnp.zeros((tile + size, LANES), F32)
    for comp in range(2):
        first = comp * chunks
        for pair in range(2):
            for j in near:
                columns = slice(j * LANES, (j + 1) * LANES)
                obj[first + 1 + j, pl.ds(row_sides[pair], half), :] = row_halos[pair][
                    comp, :, columns
                ].astype(F32)
            if with_border:
                beside = first + col_sides[pair]
                canvas[beside] = blank
                obj[beside, rows, :] = col_halos[pair][comp, 0:tile, :].astype(F32)
                for other in range(2):
                    obj[beside, pl.ds(row_sides[other], half), :] = col_halos[pair][
                        comp, tile + other * half : tile + (other + 1) * half, :
                    ].astype(F32)
        if not with_border:
            for j in range(inner):
                canvas[first + 1 + j, 0:half, :] = blank[0:half]
                canvas[first + 1 + j, half + tile :, :] = blank[0:half]

    block = 16
    groups = block // 8
    lane = lax.broadcasted_iota(jnp.int32, (block, LANES), 1)
    blocks = range(0, size, block)

    def place_of(index):
        slot = order[index]
        column = centers[1, slot]
        return slot, centers[0, slot], column >> 7, column & 127

    def cut(index, begin):
        _, row, chunk, offset = place_of(index)
        back_offset = (LANES - offset) & 127
        from_first = lane < LANES - offset
        here = slice(begin, begin + block)
        parts = []
        for comp in range(2):
            moved = [
                pltpu.roll(
                    obj[comp * chunks + chunk + k, pl.ds(row + begin, block), :], back_offset, 1
                )
                for k in range(3)
            ]
            window = jnp.concatenate(
                [
                    jnp.where(from_first, moved[0], moved[1]),
                    jnp.where(from_first, moved[1], moved[2]),
                ],
                1,
            ).astype(BF16).astype(F32)
            patch[index & 1, comp, here, :] = window
            parts.append(window)
        real, imag = parts
        for m in range(modes):
            probe_real = low[2 * m, here, :]
            probe_imag = low[2 * m + 1, here, :]
            there = slice(m * size + begin, m * size + begin + block)
            waves[there, 0:size] = (probe_real * real - probe_imag * imag).astype(BF16)
            waves[there, size:] = (probe_real * imag + probe_imag * real).astype(BF16)

    def forward_right(m, part):
        mode = slice(m * size, (m + 1) * size)
        columns = slice(part * size, (part + 1) * size)
        halves[columns, mode] = jnp.dot(
            waves[mode, :], positive[:, columns], preferred_element_type=F32
        ).astype(BF16)

    def forward_left(k, m):
        rows_here = slice(k * size, (k + 1) * size)
        mode = slice(m * size, (m + 1) * size)
        spectra[rows_here, mode] = jnp.dot(
            left_negative[rows_here, :], halves[:, mode], preferred_element_type=F32
        )

    def reweigh(index, begin):
        slot = order[index]
        k, inside = divmod(begin, half)
        real_rows = slice(k * size + inside, k * size + inside + block)
        imag_rows = slice(k * size + half + inside, k * size + half + inside + block)
        amplitude = patterns[slot, begin : begin + block, :].astype(F32)
        mode_columns = [slice(m * size, (m + 1) * size) for m in range(modes)]
        parts = [(spectra[real_rows, mode], spectra[imag_rows, mode]) for mode in mode_columns]
        power = sum(real * real + imag * imag for real, imag in parts)
        factor = amplitude * lax.rsqrt(jnp.maximum(power, 0.5)) - 1.0
        for m, (real, imag) in enumerate(parts):
            first = k * size + m * half + inside
            there = slice(first, first + block)
            shifts[there, 0:size] = (factor * real).astype(BF16)
            shifts[there, size:] = (factor * imag).astype(BF16)

    def backward_right(k, part):
        columns = slice(part * size, (part + 1) * size)
        product = jnp.dot(
            shifts[k * size : (k + 1) * size, :], negative[:, columns],
            preferred_element_type=F32,
        ).astype(BF16)
        first = part * size + k * half
        for m in range(modes):
            mode = slice(m * size, (m + 1) * size)
            backs[first : first + half, mode] = product[m * half : (m + 1) * half, :]

    def backward_left(m, part):
        mode = slice(m * size, (m + 1) * size)
        rows_here = slice(part * size, (part + 1) * size)
        changes[rows_here, mode] = jnp.dot(
            positive[rows_here, :], backs[:, mode], preferred_element_type=F32
        )

    def deposit(index, buffer, begin):
        _, row, chunk, offset = place_of(index)
        past = lane >= offset
        here = slice(begin, begin + block)
        below = slice(size + begin, size + begin + block)
        start = begin // 8
        obj_real = patch[buffer, 0, here, :]
        obj_imag = patch[buffer, 1, here, :]

        def add(plane, value):
            sums[start : start + groups, plane] += value.reshape(groups, 8, size)

        add(2 * modes, obj_real * obj_real + obj_imag * obj_imag)
        term_real = term_imag = None
        for m in range(modes):
            mode = slice(m * size, (m + 1) * size)
            real = changes[here, mode]
            imag = changes[below, mode]
            probe_real = low[2 * m, here, :]
            probe_imag = low[2 * m + 1, here, :]
            more_real = probe_real * real + probe_imag * imag
            more_imag = probe_real * imag - probe_imag * real
            term_real = more_real if m == 0 else term_real + more_real
            term_imag = more_imag if m == 0 else term_imag + more_imag
            add(2 * m, obj_real * real + obj_imag * imag)
            add(2 * m + 1, obj_real * imag - obj_imag * real)
        for comp, term in enumerate((term_real, term_imag)):
            term = term.astype(BF16).astype(F32) * scale
            first = pltpu.roll(term[:, 0:LANES], offset, 1)
            second = pltpu.roll(term[:, LANES:], offset, 1)
            place = comp * chunks + chunk
            window = pl.ds(row + begin, block)
            values = [canvas[place + k, window, :] for k in range(3)]
            canvas[place, window, :] = values[0] + jnp.where(past, first, 0.0)
            canvas[place + 1, window, :] = values[1] + jnp.where(past, second, first)
            canvas[place + 2, window, :] = values[2] + jnp.where(past, 0.0, second)

    def step(index, carry):
        pattern_copy(order[index]).wait()
        previous = jnp.maximum(index - 1, 0)
        following = jnp.minimum(index + 1, found - 1)
        buffer = (index + 1) & 1
        starts = list(blocks)
        middle = len(starts) // 2

        def between(pieces_of, blocks_of):
            given = 0
            for done, piece in enumerate(pieces_of):
                piece()
                until = (done + 1) * len(blocks_of) // len(pieces_of)
                for each in blocks_of[given:until]:
                    each()
                given = until

        bind = functools.partial
        pairs = [(first, second) for first in range(2) for second in range(2)]
        between(
            [bind(forward_right, *pair) for pair in pairs]
            + [bind(forward_left, 0, m) for m in range(modes)],
            [bind(deposit, previous, buffer, begin) for begin in starts],
        )
        between(
            [bind(forward_left, 1, m) for m in range(modes)],
            [bind(reweigh, index, begin) for begin in starts[:middle]],
        )
        between(
            [bind(backward_right, 0, part) for part in range(2)],
            [bind(reweigh, index, begin) for begin in starts[middle:]],
        )
        between(
            [bind(backward_right, 1, part) for part in range(2)]
            + [bind(backward_left, *pair) for pair in pairs],
            [bind(cut, following, begin) for begin in starts],
        )
        return carry

    for copy in obj_copies:
        copy.wait()

    @pl.when(found > 0)
    def _():
        for begin in blocks:
            cut(0, begin)

    if not with_border:
        for comp, j in pieces:
            index = comp * chunks + 1 + j
            canvas[index, rows, :] = obj[index, rows, :]
    for copy in later:
        copy.wait()

    @pl.when(found > 0)
    def _():
        lax.fori_loop(0, found, step, 0)
        for begin in blocks:
            deposit(found - 1, (found - 1) & 1, begin)

    last_copies = list(out_copies)
    if not with_border:
        last_copies += [
            pltpu.make_async_copy(here, there, sem) for there, here, sem in ring_pieces(ring_out)
        ]
        last_copies += [
            pltpu.make_async_copy(here, there, sem) for there, here, sem in sums_pieces(sums_out)
        ]
    for copy in last_copies:
        copy.start()
    if with_border:
        for pair in range(2):
            g_rows[pair][0 : 2 * chunks] = canvas[:, pl.ds(row_sides[pair], half), :].astype(BF16)
            for comp in range(2):
                beside = comp * chunks + col_sides[pair]
                g_cols[pair][comp] = canvas[beside, rows, :].astype(BF16)
        core = lax.axis_index("core")
        count_of = kept.shape[0]
        kept[...] = sums[pl.ds(core * count_of, count_of)]
        for plane in range(2 * modes + 1):
            for side in range(2):
                columns = slice(side * half, (side + 1) * half)
                given = sums[pl.ds((1 - core) * count_of, count_of), plane, :, columns]
                g_rows[0][2 * chunks + 2 * plane + side] = given.reshape(half, LANES).astype(BF16)
    for copy in last_copies:
        copy.wait()


def run_positions(counts, centers, object_field, patterns, probe_modes, row_halos, border=None):
    size = probe_modes.shape[-1]
    half = size // 2
    modes = probe_modes.shape[0]
    tile = object_field.shape[1]
    inner = tile // LANES
    chunks = inner + 2
    slots = patterns.shape[0]
    smem = pl.BlockSpec(memory_space=pltpu.SMEM)
    vmem = pl.BlockSpec(memory_space=pltpu.VMEM)
    anywhere = pl.BlockSpec(memory_space=pl.ANY)
    shape = jax.ShapeDtypeStruct
    in_specs = [smem, smem, anywhere, anywhere] + [vmem] * 4
    operands = [counts, centers, object_field, patterns, probe_modes, dft_tables(size), *row_halos]
    sums_shape = (size // 8, 2 * modes + 1, 8, size)
    ring_shape = (2 * inner, size, LANES)
    aliases = {}
    if border is None:
        out_specs = [anywhere] * 3
        out_shape = [shape(each, F32) for each in (object_field.shape, ring_shape, sums_shape)]
    else:
        aliases = {len(operands) + 2: 0}
        in_specs += [vmem] * 2 + [anywhere] * 3
        operands += list(border)
        half_sums = (size // 16,) + sums_shape[1:]
        out_specs = [anywhere] + [vmem] * 5
        out_shape = [
            shape((2, tile, tile), F32),
            shape((2 * chunks + 4 * modes + 2, half, LANES), BF16),
            shape((2 * chunks, half, LANES), BF16),
            shape((2, tile, LANES), BF16),
            shape((2, tile, LANES), BF16),
            shape(half_sums, F32),
        ]
    table = pltpu.VMEM((2 * size, 2 * size), BF16)
    products = pltpu.VMEM((2 * size, modes * size), BF16)
    wide = pltpu.VMEM((2 * size, modes * size), F32)
    padded = pltpu.VMEM((2 * chunks, tile + size, LANES), F32)
    dma = pltpu.SemaphoreType.DMA
    return pl.pallas_call(
        functools.partial(positions_kernel, border is not None),
        in_specs=in_specs,
        out_specs=out_specs,
        out_shape=out_shape,
        input_output_aliases=aliases,
        scratch_shapes=[
            padded,
            padded,
            pltpu.VMEM(patterns.shape, BF16),
            table,
            table,
            table,
            pltpu.VMEM((2 * modes, size, size), F32),
            products,
            products,
            products,
            products,
            wide,
            wide,
            pltpu.VMEM((2, 2, size, size), F32),
            pltpu.VMEM(sums_shape, F32),
            pltpu.SMEM((slots + 1,), jnp.int32),
            dma((2, 2, inner)),
            dma((2, inner)),
            dma((2, 2)),
            dma((slots,)),
            dma((4,)),
        ],
        compiler_params=pltpu.CompilerParams(
            vmem_limit_bytes=(50 if border is None else 46) * 1024 * 1024
        ),
        cost_estimate=pl.CostEstimate(
            flops=slots * 16 * modes * size**3,
            bytes_accessed=24 * 1024 * 1024,
            transcendentals=0,
        ),
        name="border" if border is not None else "interior",
    )(*operands)


def corners_kernel(col_even, col_odd, row_even, row_odd, out_even, out_odd):
    tile = col_even.shape[1]
    half = row_even.shape[1]
    chunks = row_odd.shape[0] // 2
    row_sides = sides(ROW, tile, half)
    col_sides = [offset // LANES for offset in sides(COL, chunks * LANES, half)]
    for pair, (strip, out) in enumerate(((col_even, out_even), (col_odd, out_odd))):
        out[:, half : tile - half, :] = strip[:, half : tile - half, :]
        for other, ring in enumerate((row_even, row_odd)):
            there = pl.ds(row_sides[other], half)
            for comp in range(2):
                extra = ring[comp * chunks + col_sides[pair]].astype(F32)
                out[comp, there, :] = (strip[comp, there, :].astype(F32) + extra).astype(BF16)


def add_corners(g_cols, from_rows):
    vmem = pl.BlockSpec(memory_space=pltpu.VMEM)
    shape = jax.ShapeDtypeStruct(g_cols[0].shape, BF16)
    return pl.pallas_call(
        corners_kernel,
        in_specs=[vmem] * 4,
        out_specs=[vmem] * 2,
        out_shape=[shape, shape],
        compiler_params=pltpu.CompilerParams(vmem_limit_bytes=8 * 1024 * 1024),
        cost_estimate=pl.CostEstimate(
            flops=256 * 1024, bytes_accessed=2 * 1024 * 1024, transcendentals=0
        ),
        name="corners",
    )(*g_cols, *from_rows)


def rims_kernel(
    partial, row_even, row_odd, col_even, col_odd, out, row_buffer, col_buffer, sems
):
    tile = partial.shape[1]
    half = row_even.shape[1]
    inner = tile // LANES
    chunks = inner + 2
    middle = tile - 2 * half
    row_sides = sides(ROW, tile, half)
    col_sides = sides(COL, tile, half)
    row_rings = (row_even, row_odd)
    col_strips = (col_even, col_odd)

    def copy(kind, pair, comp, inward):
        if kind == 0:
            here = row_buffer.at[pair, comp]
            place = (comp, pl.ds(row_sides[pair], half), slice(None))
        else:
            here = col_buffer.at[pair, comp]
            place = (comp, pl.ds(half, middle), pl.ds(col_sides[pair], half))
        source, target = (partial.at[place], here) if inward else (here, out.at[place])
        return pltpu.make_async_copy(
            source, target, sems.at[1 - int(inward), 2 * kind + pair, comp]
        )

    everything = [(kind, pair, comp) for kind in range(2) for pair in range(2) for comp in range(2)]
    for piece in everything:
        copy(*piece, True).start()
    for kind, pair, comp in everything:
        copy(kind, pair, comp, True).wait()
        if kind == 0:
            for j in range(inner):
                columns = slice(j * LANES, (j + 1) * LANES)
                ring = row_rings[pair][comp * chunks + 1 + j]
                row_buffer[pair, comp, :, columns] += ring.astype(F32)
            for other in range(2):
                columns = pl.ds(col_sides[other], half)
                strip = col_strips[other][comp, pl.ds(row_sides[pair], half), :]
                row_buffer[pair, comp, :, columns] += strip.astype(F32)
        else:
            strip = col_strips[pair][comp, half : half + middle, :]
            col_buffer[pair, comp] += strip.astype(F32)
        copy(kind, pair, comp, False).start()
    for piece in everything:
        copy(*piece, False).wait()


def add_rims(partial, from_rows, from_cols):
    tile = partial.shape[1]
    half = from_rows[0].shape[1]
    vmem = pl.BlockSpec(memory_space=pltpu.VMEM)
    anywhere = pl.BlockSpec(memory_space=pl.ANY)
    return pl.pallas_call(
        rims_kernel,
        in_specs=[anywhere] + [vmem] * 4,
        out_specs=anywhere,
        out_shape=jax.ShapeDtypeStruct(partial.shape, F32),
        input_output_aliases={0: 0},
        scratch_shapes=[
            pltpu.VMEM((2, 2, half, tile), F32),
            pltpu.VMEM((2, 2, tile - 2 * half, half), F32),
            pltpu.SemaphoreType.DMA((2, 4, 2)),
        ],
        compiler_params=pltpu.CompilerParams(vmem_limit_bytes=16 * 1024 * 1024),
        cost_estimate=pl.CostEstimate(
            flops=1024 * 1024, bytes_accessed=6 * 1024 * 1024, transcendentals=0
        ),
        name="rims",
    )(partial, *from_rows, *from_cols)


def chip_sums_kernel(kept_in, received, out, kept, sems):
    groups, planes, height, size = kept.shape
    half = received.shape[1]
    first = received.shape[0] - 2 * planes
    step = groups // sems.shape[0]
    parts = [pl.ds(part * step, step) for part in range(sems.shape[0])]
    copies = [
        pltpu.make_async_copy(kept_in.at[here], kept.at[here], sems.at[part])
        for part, here in enumerate(parts)
    ]
    for copy in copies:
        copy.start()
    for copy in copies:
        copy.wait()
    for plane in range(planes):
        for side in range(2):
            columns = slice(side * half, (side + 1) * half)
            other = received[first + 2 * plane + side].astype(F32).reshape(groups, height, half)
            out[:, plane, :, columns] = (kept[:, plane, :, columns] + other).astype(BF16)


def chip_sums(kept, received):
    vmem = pl.BlockSpec(memory_space=pltpu.VMEM)
    return pl.pallas_call(
        chip_sums_kernel,
        in_specs=[pl.BlockSpec(memory_space=pl.ANY), vmem],
        out_specs=vmem,
        out_shape=jax.ShapeDtypeStruct(kept.shape, BF16),
        scratch_shapes=[pltpu.VMEM(kept.shape, F32), pltpu.SemaphoreType.DMA((4,))],
        compiler_params=pltpu.CompilerParams(vmem_limit_bytes=8 * 1024 * 1024),
        cost_estimate=pl.CostEstimate(
            flops=32 * 1024**3, bytes_accessed=32 * 1024 * 1024, transcendentals=0
        ),
        name="chip_sums",
    )(kept, received)


def by_device(on_chip):
    devices = lax.axis_size("x") * lax.axis_size("col")
    groups, planes, _, size = on_chip.shape
    share = groups * 8 // devices
    if share < 8:
        on_chip = on_chip.reshape(groups, planes, 8 // share, share, size)
        return jnp.swapaxes(on_chip, 1, 2).reshape(devices, planes, share, size)
    return on_chip.reshape(devices, groups // devices, planes, 8, size)


def exchange(parts):
    return lax.all_to_all(parts, ("x", "col"), 0, 0, tiled=True)


def update_kernel(received, copies):
    devices = received.shape[0]
    total = received[0].astype(F32)
    for device in range(1, devices):
        total = total + received[device].astype(F32)
    planes = total.shape[0]
    update = (total[: planes - 1] / jnp.sqrt(total[planes - 1])).astype(BF16)
    for device in range(devices):
        copies[device] = update


def shared_update(received):
    devices, planes, share, size = received.shape
    vmem = pl.BlockSpec(memory_space=pltpu.VMEM)
    return pl.pallas_call(
        update_kernel,
        in_specs=[vmem],
        out_specs=vmem,
        out_shape=jax.ShapeDtypeStruct((devices, planes - 1, share, size), BF16),
        compiler_params=pltpu.CompilerParams(vmem_limit_bytes=8 * 1024 * 1024),
        cost_estimate=pl.CostEstimate(
            flops=512 * 1024, bytes_accessed=1024 * 1024, transcendentals=0
        ),
        name="update",
    )(received)


def finish_kernel(probe, mine, other, out):
    core = lax.axis_index("core")
    groups, planes, height, _ = mine.shape
    for side, update in enumerate((mine, other)):
        first = jnp.where(core == side, 0, groups * height)
        for group in range(groups):
            place = pl.ds(pl.multiple_of(first + group * height, height), height)
            for plane in range(planes):
                m, comp = divmod(plane, 2)
                out[m, comp, place, :] = probe[m, comp, place, :] + update[group, plane].astype(F32)


def finish_probe(probe_modes, mine):
    devices, planes, share, size = mine.shape
    if share < 8:
        mine = mine.reshape(devices * share // 8, 8 // share, planes, share, size)
        mine = jnp.swapaxes(mine, 1, 2).reshape(-1, planes, 8, size)
    other = lax.ppermute(mine, "core", [(0, 1), (1, 0)])
    vmem = pl.BlockSpec(memory_space=pltpu.VMEM)
    return pl.pallas_call(
        finish_kernel,
        in_specs=[vmem] * 3,
        out_specs=vmem,
        out_shape=jax.ShapeDtypeStruct(probe_modes.shape, F32),
        compiler_params=pltpu.CompilerParams(vmem_limit_bytes=8 * 1024 * 1024),
        cost_estimate=pl.CostEstimate(
            flops=256 * 1024, bytes_accessed=3 * 1024 * 1024, transcendentals=0
        ),
        name="finish",
    )(probe_modes, mine, other)


def on_device(object_field, probe_modes, counts, centers, patterns):
    half = probe_modes.shape[-1] // 2

    col_even, col_odd, row_even, row_odd = cut_strips(object_field, half)
    go_on = lax.axis_index("col") < 4096
    row_halos = (swap_pairs(row_even, ROW, 0), swap_pairs(row_odd, ROW, 1))
    col_halos = (swap_pairs(col_even, COL, 0), swap_pairs(col_odd, COL, 1))
    is_even = (lax.axis_index("col") & 1) == 0
    first_ends = jnp.concatenate([halo[:, :, :half] for halo in row_halos], 1)
    last_ends = jnp.concatenate([halo[:, :, -half:] for halo in row_halos], 1)
    end_halos = (
        swap_pairs(jnp.where(is_even, last_ends, first_ends), COL, 0),
        swap_pairs(jnp.where(is_even, first_ends, last_ends), COL, 1),
    )

    inputs = (counts, centers[0, 0], object_field, patterns[0, 0], probe_modes, row_halos)
    started = run_positions(*inputs)
    joined = [jnp.concatenate(both, 1) for both in zip(col_halos, end_halos)]
    border = (*joined, *started)
    partial, g_row_even, g_row_odd, g_col_even, g_col_odd, kept = run_positions(*inputs, border)

    from_rows = (swap_pairs(g_row_even, ROW, 0), swap_pairs(g_row_odd, ROW, 1))
    received = lax.cond(
        go_on, exchange, jnp.zeros_like, by_device(chip_sums(kept, from_rows[0]))
    )
    row_odd, _ = lax.optimization_barrier((from_rows[1], received))
    from_rows = (from_rows[0], row_odd)
    to_even, to_odd = add_corners((g_col_even, g_col_odd), from_rows)
    received, to_even, to_odd = lax.optimization_barrier((received, to_even, to_odd))
    from_cols = (swap_pairs(to_even, COL, 0), swap_pairs(to_odd, COL, 1))
    if received.ndim == 5:
        received = received[:, 0]
    mine = lax.cond(go_on, exchange, jnp.zeros_like, shared_update(received))
    mine, from_cols, partial = lax.optimization_barrier((mine, from_cols, partial))
    new_object = add_rims(partial, from_rows, from_cols)
    return (new_object, finish_probe(probe_modes, mine))


def solution(mesh):
    rows, columns = mesh.devices.shape
    split = jax.sharding.Mesh(
        mesh.devices.reshape(rows // 2, 2, columns), ("x", "core", "col")
    )
    placed = (
        P(None, ROW, "col"),
        P(),
        P(),
        P(ROW, "col", None, None),
        P(ROW, "col", None, None, None),
    )
    return jax.shard_map(
        on_device,
        mesh=split,
        in_specs=placed,
        out_specs=(P(None, ROW, "col"), P()),
        check_vma=False,
    )
```

```python
import functools
import math

import jax
import jax.numpy as jnp
import ml_dtypes
import numpy as np
from jax import lax
from jax.experimental import pallas as pl
from jax.experimental.pallas import tpu as pltpu
from jax.sharding import PartitionSpec as P

LANES = 128
ROW = ("x", "core")
COL = ("col",)
F32 = jnp.float32
BF16 = jnp.bfloat16


def dft_tables(length):
    indices = np.arange(length)
    angles = (indices[:, None] * indices[None, :] % length) * (2.0 * np.pi / length)
    scale = 1.0 / np.sqrt(length)
    cosine = (np.cos(angles) * scale).astype(np.float32).astype(ml_dtypes.bfloat16)
    sine = (np.sin(angles) * scale).astype(np.float32).astype(ml_dtypes.bfloat16)
    return np.stack([cosine, sine, -sine])


def swap_pairs(array, axis, odd):
    devices = math.prod(lax.axis_size(name) for name in axis)
    firsts = range(odd, devices - 1, 2)
    return lax.ppermute(
        array, axis, [(i, i + 1) for i in firsts] + [(i + 1, i) for i in firsts]
    )


def sides(axis, length, width):
    even = (lax.axis_index(axis) & 1) == 0
    far = length - width
    return [
        pl.multiple_of(jnp.where(even, far, 0), width),
        pl.multiple_of(jnp.where(even, 0, far), width),
    ]


def strips_kernel(obj_hbm, col_even, col_odd, row_even, row_odd, col_buffer, row_buffer, sems):
    tile = obj_hbm.shape[1]
    half = row_even.shape[1]
    copies = []
    for pair in range(2):
        column = sides(COL, tile, half)[pair]
        row = sides(ROW, tile, half)[pair]
        copies.append(
            pltpu.make_async_copy(
                obj_hbm.at[:, :, pl.ds(column, half)], col_buffer.at[pair], sems.at[0, pair]
            )
        )
        copies.append(
            pltpu.make_async_copy(
                obj_hbm.at[:, pl.ds(row, half), :], row_buffer.at[pair], sems.at[1, pair]
            )
        )
    for copy in copies:
        copy.start()
    outputs = (col_even, row_even, col_odd, row_odd)
    buffers = (col_buffer, row_buffer) * 2
    for index, copy in enumerate(copies):
        copy.wait()
        outputs[index][...] = buffers[index][index // 2].astype(BF16)


def cut_strips(object_field, half):
    tile = object_field.shape[1]
    vmem = pl.BlockSpec(memory_space=pltpu.VMEM)
    columns = jax.ShapeDtypeStruct((2, tile, half), BF16)
    rows = jax.ShapeDtypeStruct((2, half, tile), BF16)
    return pl.pallas_call(
        strips_kernel,
        in_specs=[pl.BlockSpec(memory_space=pltpu.HBM)],
        out_specs=[vmem] * 4,
        out_shape=[columns, columns, rows, rows],
        scratch_shapes=[
            pltpu.VMEM((2, 2, tile, half), F32),
            pltpu.VMEM((2, 2, half, tile), F32),
            pltpu.SemaphoreType.DMA((2, 2)),
        ],
        compiler_params=pltpu.CompilerParams(vmem_limit_bytes=50 * 1024 * 1024),
        cost_estimate=pl.CostEstimate(
            flops=1024 * 1024, bytes_accessed=5 * 1024 * 1024, transcendentals=0
        ),
        name="strips",
    )(object_field)


def positions_kernel(with_border, *refs):
    counts, centers, obj_hbm, pat_hbm, probe = refs[:5]
    tables, row_halos = refs[5], refs[6:8]
    refs = refs[8:]
    if with_border:
        col_halos = refs[0:2]
        start_hbm, ring_in, sums_in = refs[2:5]
        out_hbm, g_rows, g_cols, kept = refs[5], refs[6:8], refs[8:10], refs[10]
        refs = refs[11:]
    else:
        out_hbm, ring_out, sums_out = refs[:3]
        refs = refs[3:]
    (obj, canvas, patterns, positive, negative, folded, swapped, amplitudes, low, waves, shifts, halves, backs,
     spectra, changes, patch, sums, order, piece_sems, out_sems, ring_sems, pat_sems,
     sums_sems) = refs
    size = probe.shape[-1]
    half = size // 2
    tile = obj_hbm.shape[1]
    inner = tile // LANES
    chunks = inner + 2
    modes = probe.shape[0]
    rows = slice(half, half + tile)
    near = [0, 1, inner - 2, inner - 1] if with_border else list(range(inner))
    pieces = [(comp, j) for comp in range(2) for j in near]

    def home(array, comp, j):
        return array.at[comp, :, pl.ds(j * LANES, LANES)]

    def held(array, comp, j):
        return array.at[comp * chunks + 1 + j, pl.ds(half, tile), :]

    def ring_pieces(array):
        for comp in range(2):
            for side, row in enumerate((0, half + tile)):
                yield (
                    array.at[pl.ds(comp * inner, inner), pl.ds(side * half, half), :],
                    canvas.at[pl.ds(comp * chunks + 1, inner), pl.ds(row, half), :],
                    ring_sems.at[side, comp],
                )

    def sums_pieces(array):
        step = array.shape[0] // sums_parts
        for part in range(sums_parts):
            here = pl.ds(part * step, step)
            yield array.at[here], sums.at[here], sums_sems.at[part]

    sums_parts = sums_sems.shape[0]
    obj_copies = [
        pltpu.make_async_copy(home(obj_hbm, *p), held(obj, *p), piece_sems.at[0, *p])
        for p in pieces
    ]
    out_copies = [
        pltpu.make_async_copy(held(canvas, *p), home(out_hbm, *p), out_sems.at[p]) for p in pieces
    ]
    later = []
    if with_border:
        later += [
            pltpu.make_async_copy(home(start_hbm, *p), held(canvas, *p), piece_sems.at[1, *p])
            for p in pieces
        ]
        later += [pltpu.make_async_copy(*each) for each in ring_pieces(ring_in)]
        later += [pltpu.make_async_copy(*each) for each in sums_pieces(sums_in)]
    for copy in obj_copies + later:
        copy.start()

    order[0] = 0
    count = counts[lax.axis_index(ROW), lax.axis_index("col")]

    def pattern_copy(slot):
        return pltpu.make_async_copy(pat_hbm.at[slot], patterns.at[slot], pat_sems.at[slot])

    def note(slot, found):
        column = centers[1, slot]
        inside = (column >= half) & (column <= tile - half)
        order[found] = slot
        return found + jnp.where(inside, 0 if with_border else 1, 1 if with_border else 0)

    def fetch(index, carry):
        pattern_copy(order[index]).start()
        return carry

    found = lax.fori_loop(0, count, note, 0)
    lax.fori_loop(0, found, fetch, 0)

    if not with_border:
        sums[...] = jnp.zeros_like(sums)
    intensity = jnp.zeros((size, size), F32)
    for m in range(modes):
        for comp in range(2):
            values = probe[m, comp]
            intensity = intensity + values * values
            low[2 * m + comp] = values.astype(BF16).astype(F32)
    scale = 1.0 / (jnp.max(intensity) + 1e-06)
    cosine, sine = tables[0], tables[1]
    index_row = lax.broadcasted_iota(jnp.int32, (size, size), 0)
    index_column = lax.broadcasted_iota(jnp.int32, (size, size), 1)
    target = jnp.where(index_row > half, size + half - index_row, index_row)
    swapped[...] = jnp.where(index_column == target, 1.0, 0.0).astype(BF16)
    first_lane = lax.broadcasted_iota(jnp.int32, (size, half), 1) == 0
    first_row = lax.broadcasted_iota(jnp.int32, (half, size), 0) == 0
    wide_cosine = cosine.astype(F32)
    wide_sine = sine.astype(F32)
    folded[0, :, 0:half] = cosine[:, 0:half]
    folded[0, :, half:] = jnp.where(
        first_lane, wide_cosine[:, half:], wide_sine[:, 0:half]
    ).astype(BF16)
    folded[1, 0:half, :] = cosine[0:half, :]
    folded[1, half:, :] = jnp.where(
        first_row, wide_cosine[half:, :], wide_sine[0:half, :]
    ).astype(BF16)

    def reordered(left_side, right_side):
        return jnp.dot(left_side, right_side, preferred_element_type=F32).astype(BF16)

    turns = [reordered(swapped[...], tables[i]) for i in range(3)]
    negative[0:size, 0:size] = turns[0]
    negative[0:size, size:] = turns[1]
    negative[size:, 0:size] = turns[2]
    negative[size:, size:] = turns[0]
    turns = [reordered(tables[i], swapped[...]) for i in range(3)]
    positive[0:size, 0:size] = turns[0]
    positive[0:size, size:] = turns[2]
    positive[size:, 0:size] = turns[1]
    positive[size:, size:] = turns[0]
    changes[...] = jnp.zeros_like(changes)
    patch[...] = jnp.zeros_like(patch)

    row_sides = sides(ROW, tile + size, half)
    col_sides = [offset // LANES for offset in sides(COL, tile + size, half)]
    blank = jnp.zeros((tile + size, LANES), F32)
    for comp in range(2):
        first = comp * chunks
        for pair in range(2):
            for j in near:
                columns = slice(j * LANES, (j + 1) * LANES)
                obj[first + 1 + j, pl.ds(row_sides[pair], half), :] = row_halos[pair][
                    comp, :, columns
                ].astype(F32)
            if with_border:
                beside = first + col_sides[pair]
                canvas[beside] = blank
                obj[beside, rows, :] = col_halos[pair][comp, 0:tile, :].astype(F32)
                for other in range(2):
                    obj[beside, pl.ds(row_sides[other], half), :] = col_halos[pair][
                        comp, tile + other * half : tile + (other + 1) * half, :
                    ].astype(F32)
        if not with_border:
            for j in range(inner):
                canvas[first + 1 + j, 0:half, :] = blank[0:half]
                canvas[first + 1 + j, half + tile :, :] = blank[0:half]

    block = 16
    groups = block // 8
    lane = lax.broadcasted_iota(jnp.int32, (block, LANES), 1)
    blocks = range(0, size, block)

    def place_of(index):
        slot = order[index]
        column = centers[1, slot]
        return slot, centers[0, slot], column >> 7, column & 127

    def cut(index, begin):
        _, row, chunk, offset = place_of(index)
        back_offset = (LANES - offset) & 127
        from_first = lane < LANES - offset
        here = slice(begin, begin + block)
        parts = []
        for comp in range(2):
            moved = [
                pltpu.roll(
                    obj[comp * chunks + chunk + k, pl.ds(row + begin, block), :], back_offset, 1
                )
                for k in range(3)
            ]
            window = jnp.concatenate(
                [
                    jnp.where(from_first, moved[0], moved[1]),
                    jnp.where(from_first, moved[1], moved[2]),
                ],
                1,
            ).astype(BF16).astype(F32)
            patch[index & 1, comp, here, :] = window
            parts.append(window)
        real, imag = parts
        for m in range(modes):
            probe_real = low[2 * m, here, :]
            probe_imag = low[2 * m + 1, here, :]
            there = slice(m * size + begin, m * size + begin + block)
            waves[there, 0:size] = (probe_real * real - probe_imag * imag).astype(BF16)
            waves[there, size:] = (probe_real * imag + probe_imag * real).astype(BF16)

    def forward_right(m):
        mode = slice(m * size, (m + 1) * size)
        real = jnp.dot(waves[mode, 0:size], folded[0], preferred_element_type=F32)
        imag = jnp.dot(waves[mode, size:], folded[0], preferred_element_type=F32)
        real_cos, real_sin = real[:, 0:half], real[:, half:]
        imag_cos, imag_sin = imag[:, 0:half], imag[:, half:]
        plus = slice(m * size, m * size + half)
        minus = slice(m * size + half, (m + 1) * size)
        halves[0:size, plus] = (real_cos + jnp.where(first_lane, 0.0, imag_sin)).astype(BF16)
        halves[size:, plus] = (imag_cos - jnp.where(first_lane, 0.0, real_sin)).astype(BF16)
        halves[0:size, minus] = jnp.where(first_lane, real_sin, real_cos - imag_sin).astype(BF16)
        halves[size:, minus] = jnp.where(first_lane, imag_sin, imag_cos + real_sin).astype(BF16)

    def forward_left(m):
        mode = slice(m * size, (m + 1) * size)
        real = jnp.dot(folded[1], halves[0:size, mode], preferred_element_type=F32)
        imag = jnp.dot(folded[1], halves[size:, mode], preferred_element_type=F32)
        real_cos, real_sin = real[0:half], real[half:]
        imag_cos, imag_sin = imag[0:half], imag[half:]
        spectra[0:half, mode] = real_cos + jnp.where(first_row, 0.0, imag_sin)
        spectra[size : size + half, mode] = imag_cos - jnp.where(first_row, 0.0, real_sin)
        spectra[half:size, mode] = jnp.where(first_row, real_sin, real_cos - imag_sin)
        spectra[size + half :, mode] = jnp.where(first_row, imag_sin, imag_cos + real_sin)

    def fold_amplitudes(index):
        rows_folded = reordered(swapped[...], patterns[order[index]])
        amplitudes[...] = jnp.dot(rows_folded, swapped[...], preferred_element_type=F32)

    def reweigh(begin):
        k, inside = divmod(begin, half)
        here = slice(begin, begin + block)
        below = slice(size + begin, size + begin + block)
        mode_columns = [slice(m * size, (m + 1) * size) for m in range(modes)]
        parts = [(spectra[here, mode], spectra[below, mode]) for mode in mode_columns]
        power = sum(real * real + imag * imag for real, imag in parts)
        factor = amplitudes[here, :] * lax.rsqrt(jnp.maximum(power, 0.5)) - 1.0
        for m, (real, imag) in enumerate(parts):
            first = k * size + m * half + inside
            there = slice(first, first + block)
            shifts[there, 0:size] = (factor * real).astype(BF16)
            shifts[there, size:] = (factor * imag).astype(BF16)

    def backward_right(k, part):
        columns = slice(part * size, (part + 1) * size)
        product = jnp.dot(
            shifts[k * size : (k + 1) * size, :], negative[:, columns],
            preferred_element_type=F32,
        ).astype(BF16)
        first = part * size + k * half
        for m in range(modes):
            mode = slice(m * size, (m + 1) * size)
            backs[first : first + half, mode] = product[m * half : (m + 1) * half, :]

    def backward_left(m, part):
        mode = slice(m * size, (m + 1) * size)
        rows_here = slice(part * size, (part + 1) * size)
        changes[rows_here, mode] = jnp.dot(
            positive[rows_here, :], backs[:, mode], preferred_element_type=F32
        )

    def deposit(index, buffer, begin):
        _, row, chunk, offset = place_of(index)
        past = lane >= offset
        here = slice(begin, begin + block)
        below = slice(size + begin, size + begin + block)
        start = begin // 8
        obj_real = patch[buffer, 0, here, :]
        obj_imag = patch[buffer, 1, here, :]

        def add(plane, value):
            sums[start : start + groups, plane] += value.reshape(groups, 8, size)

        add(2 * modes, obj_real * obj_real + obj_imag * obj_imag)
        term_real = term_imag = None
        for m in range(modes):
            mode = slice(m * size, (m + 1) * size)
            real = changes[here, mode]
            imag = changes[below, mode]
            probe_real = low[2 * m, here, :]
            probe_imag = low[2 * m + 1, here, :]
            more_real = probe_real * real + probe_imag * imag
            more_imag = probe_real * imag - probe_imag * real
            term_real = more_real if m == 0 else term_real + more_real
            term_imag = more_imag if m == 0 else term_imag + more_imag
            add(2 * m, obj_real * real + obj_imag * imag)
            add(2 * m + 1, obj_real * imag - obj_imag * real)
        for comp, term in enumerate((term_real, term_imag)):
            term = term.astype(BF16).astype(F32) * scale
            first = pltpu.roll(term[:, 0:LANES], offset, 1)
            second = pltpu.roll(term[:, LANES:], offset, 1)
            place = comp * chunks + chunk
            window = pl.ds(row + begin, block)
            values = [canvas[place + k, window, :] for k in range(3)]
            canvas[place, window, :] = values[0] + jnp.where(past, first, 0.0)
            canvas[place + 1, window, :] = values[1] + jnp.where(past, second, first)
            canvas[place + 2, window, :] = values[2] + jnp.where(past, 0.0, second)

    def step(index, carry):
        pattern_copy(order[index]).wait()
        previous = jnp.maximum(index - 1, 0)
        following = jnp.minimum(index + 1, found - 1)
        buffer = (index + 1) & 1
        starts = list(blocks)
        middle = len(starts) // 2

        def between(pieces_of, blocks_of):
            given = 0
            for done, piece in enumerate(pieces_of):
                piece()
                until = (done + 1) * len(blocks_of) // len(pieces_of)
                for each in blocks_of[given:until]:
                    each()
                given = until

        bind = functools.partial
        pairs = [(first, second) for first in range(2) for second in range(2)]
        between(
            [bind(forward_right, 0), bind(fold_amplitudes, index), bind(forward_right, 1)]
            + [bind(forward_left, m) for m in range(modes)],
            [bind(deposit, previous, buffer, begin) for begin in starts],
        )
        for begin in starts[:middle]:
            reweigh(begin)
        between(
            [bind(backward_right, 0, part) for part in range(2)],
            [bind(reweigh, begin) for begin in starts[middle:]],
        )
        between(
            [bind(backward_right, 1, part) for part in range(2)]
            + [bind(backward_left, *pair) for pair in pairs],
            [bind(cut, following, begin) for begin in starts],
        )
        return carry

    for copy in obj_copies:
        copy.wait()

    @pl.when(found > 0)
    def _():
        for begin in blocks:
            cut(0, begin)

    if not with_border:
        for comp, j in pieces:
            index = comp * chunks + 1 + j
            canvas[index, rows, :] = obj[index, rows, :]
    for copy in later:
        copy.wait()

    @pl.when(found > 0)
    def _():
        lax.fori_loop(0, found, step, 0)
        for begin in blocks:
            deposit(found - 1, (found - 1) & 1, begin)

    last_copies = list(out_copies)
    if not with_border:
        last_copies += [
            pltpu.make_async_copy(here, there, sem) for there, here, sem in ring_pieces(ring_out)
        ]
        last_copies += [
            pltpu.make_async_copy(here, there, sem) for there, here, sem in sums_pieces(sums_out)
        ]
    for copy in last_copies:
        copy.start()
    if with_border:
        for pair in range(2):
            g_rows[pair][0 : 2 * chunks] = canvas[:, pl.ds(row_sides[pair], half), :].astype(BF16)
            for comp in range(2):
                beside = comp * chunks + col_sides[pair]
                g_cols[pair][comp] = canvas[beside, rows, :].astype(BF16)
        core = lax.axis_index("core")
        count_of = kept.shape[0]
        kept[...] = sums[pl.ds(core * count_of, count_of)]
        for plane in range(2 * modes + 1):
            for side in range(2):
                columns = slice(side * half, (side + 1) * half)
                given = sums[pl.ds((1 - core) * count_of, count_of), plane, :, columns]
                g_rows[0][2 * chunks + 2 * plane + side] = given.reshape(half, LANES).astype(BF16)
    for copy in last_copies:
        copy.wait()


def run_positions(counts, centers, object_field, patterns, probe_modes, row_halos, border=None):
    size = probe_modes.shape[-1]
    half = size // 2
    modes = probe_modes.shape[0]
    tile = object_field.shape[1]
    inner = tile // LANES
    chunks = inner + 2
    slots = patterns.shape[0]
    smem = pl.BlockSpec(memory_space=pltpu.SMEM)
    vmem = pl.BlockSpec(memory_space=pltpu.VMEM)
    anywhere = pl.BlockSpec(memory_space=pl.ANY)
    shape = jax.ShapeDtypeStruct
    in_specs = [smem, smem, anywhere, anywhere] + [vmem] * 4
    operands = [counts, centers, object_field, patterns, probe_modes, dft_tables(size), *row_halos]
    sums_shape = (size // 8, 2 * modes + 1, 8, size)
    ring_shape = (2 * inner, size, LANES)
    aliases = {}
    if border is None:
        out_specs = [anywhere] * 3
        out_shape = [shape(each, F32) for each in (object_field.shape, ring_shape, sums_shape)]
    else:
        aliases = {len(operands) + 2: 0}
        in_specs += [vmem] * 2 + [anywhere] * 3
        operands += list(border)
        half_sums = (size // 16,) + sums_shape[1:]
        out_specs = [anywhere] + [vmem] * 5
        out_shape = [
            shape((2, tile, tile), F32),
            shape((2 * chunks + 4 * modes + 2, half, LANES), BF16),
            shape((2 * chunks, half, LANES), BF16),
            shape((2, tile, LANES), BF16),
            shape((2, tile, LANES), BF16),
            shape(half_sums, F32),
        ]
    table = pltpu.VMEM((2 * size, 2 * size), BF16)
    products = pltpu.VMEM((2 * size, modes * size), BF16)
    wide = pltpu.VMEM((2 * size, modes * size), F32)
    padded = pltpu.VMEM((2 * chunks, tile + size, LANES), F32)
    dma = pltpu.SemaphoreType.DMA
    return pl.pallas_call(
        functools.partial(positions_kernel, border is not None),
        in_specs=in_specs,
        out_specs=out_specs,
        out_shape=out_shape,
        input_output_aliases=aliases,
        scratch_shapes=[
            padded,
            padded,
            pltpu.VMEM(patterns.shape, BF16),
            table,
            table,
            pltpu.VMEM((2, size, size), BF16),
            pltpu.VMEM((size, size), BF16),
            pltpu.VMEM((size, size), F32),
            pltpu.VMEM((2 * modes, size, size), F32),
            products,
            products,
            products,
            products,
            wide,
            wide,
            pltpu.VMEM((2, 2, size, size), F32),
            pltpu.VMEM(sums_shape, F32),
            pltpu.SMEM((slots + 1,), jnp.int32),
            dma((2, 2, inner)),
            dma((2, inner)),
            dma((2, 2)),
            dma((slots,)),
            dma((4,)),
        ],
        compiler_params=pltpu.CompilerParams(
            vmem_limit_bytes=(50 if border is None else 46) * 1024 * 1024
        ),
        cost_estimate=pl.CostEstimate(
            flops=slots * 16 * modes * size**3,
            bytes_accessed=24 * 1024 * 1024,
            transcendentals=0,
        ),
        name="border" if border is not None else "interior",
    )(*operands)


def corners_kernel(col_even, col_odd, row_even, row_odd, out_even, out_odd):
    tile = col_even.shape[1]
    half = row_even.shape[1]
    chunks = row_odd.shape[0] // 2
    row_sides = sides(ROW, tile, half)
    col_sides = [offset // LANES for offset in sides(COL, chunks * LANES, half)]
    for pair, (strip, out) in enumerate(((col_even, out_even), (col_odd, out_odd))):
        out[:, half : tile - half, :] = strip[:, half : tile - half, :]
        for other, ring in enumerate((row_even, row_odd)):
            there = pl.ds(row_sides[other], half)
            for comp in range(2):
                extra = ring[comp * chunks + col_sides[pair]].astype(F32)
                out[comp, there, :] = (strip[comp, there, :].astype(F32) + extra).astype(BF16)


def add_corners(g_cols, from_rows):
    vmem = pl.BlockSpec(memory_space=pltpu.VMEM)
    shape = jax.ShapeDtypeStruct(g_cols[0].shape, BF16)
    return pl.pallas_call(
        corners_kernel,
        in_specs=[vmem] * 4,
        out_specs=[vmem] * 2,
        out_shape=[shape, shape],
        compiler_params=pltpu.CompilerParams(vmem_limit_bytes=8 * 1024 * 1024),
        cost_estimate=pl.CostEstimate(
            flops=256 * 1024, bytes_accessed=2 * 1024 * 1024, transcendentals=0
        ),
        name="corners",
    )(*g_cols, *from_rows)


def rims_kernel(
    partial, row_even, row_odd, col_even, col_odd, out, row_buffer, col_buffer, sems
):
    tile = partial.shape[1]
    half = row_even.shape[1]
    inner = tile // LANES
    chunks = inner + 2
    middle = tile - 2 * half
    row_sides = sides(ROW, tile, half)
    col_sides = sides(COL, tile, half)
    row_rings = (row_even, row_odd)
    col_strips = (col_even, col_odd)

    def copy(kind, pair, comp, inward):
        if kind == 0:
            here = row_buffer.at[pair, comp]
            place = (comp, pl.ds(row_sides[pair], half), slice(None))
        else:
            here = col_buffer.at[pair, comp]
            place = (comp, pl.ds(half, middle), pl.ds(col_sides[pair], half))
        source, target = (partial.at[place], here) if inward else (here, out.at[place])
        return pltpu.make_async_copy(
            source, target, sems.at[1 - int(inward), 2 * kind + pair, comp]
        )

    everything = [(kind, pair, comp) for kind in range(2) for pair in range(2) for comp in range(2)]
    for piece in everything:
        copy(*piece, True).start()
    for kind, pair, comp in everything:
        copy(kind, pair, comp, True).wait()
        if kind == 0:
            for j in range(inner):
                columns = slice(j * LANES, (j + 1) * LANES)
                ring = row_rings[pair][comp * chunks + 1 + j]
                row_buffer[pair, comp, :, columns] += ring.astype(F32)
            for other in range(2):
                columns = pl.ds(col_sides[other], half)
                strip = col_strips[other][comp, pl.ds(row_sides[pair], half), :]
                row_buffer[pair, comp, :, columns] += strip.astype(F32)
        else:
            strip = col_strips[pair][comp, half : half + middle, :]
            col_buffer[pair, comp] += strip.astype(F32)
        copy(kind, pair, comp, False).start()
    for piece in everything:
        copy(*piece, False).wait()


def add_rims(partial, from_rows, from_cols):
    tile = partial.shape[1]
    half = from_rows[0].shape[1]
    vmem = pl.BlockSpec(memory_space=pltpu.VMEM)
    anywhere = pl.BlockSpec(memory_space=pl.ANY)
    return pl.pallas_call(
        rims_kernel,
        in_specs=[anywhere] + [vmem] * 4,
        out_specs=anywhere,
        out_shape=jax.ShapeDtypeStruct(partial.shape, F32),
        input_output_aliases={0: 0},
        scratch_shapes=[
            pltpu.VMEM((2, 2, half, tile), F32),
            pltpu.VMEM((2, 2, tile - 2 * half, half), F32),
            pltpu.SemaphoreType.DMA((2, 4, 2)),
        ],
        compiler_params=pltpu.CompilerParams(vmem_limit_bytes=16 * 1024 * 1024),
        cost_estimate=pl.CostEstimate(
            flops=1024 * 1024, bytes_accessed=6 * 1024 * 1024, transcendentals=0
        ),
        name="rims",
    )(partial, *from_rows, *from_cols)


def chip_sums_kernel(kept, received, out):
    groups, planes, height, size = kept.shape
    half = received.shape[1]
    first = received.shape[0] - 2 * planes
    for plane in range(planes):
        for side in range(2):
            columns = slice(side * half, (side + 1) * half)
            other = received[first + 2 * plane + side].astype(F32).reshape(groups, height, half)
            out[:, plane, :, columns] = (kept[:, plane, :, columns] + other).astype(BF16)


def chip_sums(kept, received):
    vmem = pl.BlockSpec(memory_space=pltpu.VMEM)
    return pl.pallas_call(
        chip_sums_kernel,
        in_specs=[vmem, vmem],
        out_specs=vmem,
        out_shape=jax.ShapeDtypeStruct(kept.shape, BF16),
        compiler_params=pltpu.CompilerParams(vmem_limit_bytes=8 * 1024 * 1024),
        cost_estimate=pl.CostEstimate(
            flops=32 * 1024**3, bytes_accessed=32 * 1024 * 1024, transcendentals=0
        ),
        name="chip_sums",
    )(kept, received)


def by_device(on_chip):
    devices = lax.axis_size("x") * lax.axis_size("col")
    groups, planes, _, size = on_chip.shape
    share = groups * 8 // devices
    if share < 8:
        on_chip = on_chip.reshape(groups, planes, 8 // share, share, size)
        return jnp.swapaxes(on_chip, 1, 2).reshape(devices, planes, share, size)
    return on_chip.reshape(devices, groups // devices, planes, 8, size)


def exchange(parts):
    return lax.all_to_all(parts, ("x", "col"), 0, 0, tiled=True)


def update_kernel(received, copies):
    devices = received.shape[0]
    total = received[0].astype(F32)
    for device in range(1, devices):
        total = total + received[device].astype(F32)
    planes = total.shape[0]
    update = (total[: planes - 1] / jnp.sqrt(total[planes - 1])).astype(BF16)
    for device in range(devices):
        copies[device] = update


def shared_update(received):
    devices, planes, share, size = received.shape
    vmem = pl.BlockSpec(memory_space=pltpu.VMEM)
    return pl.pallas_call(
        update_kernel,
        in_specs=[vmem],
        out_specs=vmem,
        out_shape=jax.ShapeDtypeStruct((devices, planes - 1, share, size), BF16),
        compiler_params=pltpu.CompilerParams(vmem_limit_bytes=8 * 1024 * 1024),
        cost_estimate=pl.CostEstimate(
            flops=512 * 1024, bytes_accessed=1024 * 1024, transcendentals=0
        ),
        name="update",
    )(received)


def finish_kernel(probe, mine, other, out):
    core = lax.axis_index("core")
    groups, planes, height, _ = mine.shape
    for side, update in enumerate((mine, other)):
        first = jnp.where(core == side, 0, groups * height)
        for group in range(groups):
            place = pl.ds(pl.multiple_of(first + group * height, height), height)
            for plane in range(planes):
                m, comp = divmod(plane, 2)
                out[m, comp, place, :] = probe[m, comp, place, :] + update[group, plane].astype(F32)


def finish_probe(probe_modes, mine):
    devices, planes, share, size = mine.shape
    if share < 8:
        mine = mine.reshape(devices * share // 8, 8 // share, planes, share, size)
        mine = jnp.swapaxes(mine, 1, 2).reshape(-1, planes, 8, size)
    other = lax.ppermute(mine, "core", [(0, 1), (1, 0)])
    vmem = pl.BlockSpec(memory_space=pltpu.VMEM)
    return pl.pallas_call(
        finish_kernel,
        in_specs=[vmem] * 3,
        out_specs=vmem,
        out_shape=jax.ShapeDtypeStruct(probe_modes.shape, F32),
        compiler_params=pltpu.CompilerParams(vmem_limit_bytes=8 * 1024 * 1024),
        cost_estimate=pl.CostEstimate(
            flops=256 * 1024, bytes_accessed=3 * 1024 * 1024, transcendentals=0
        ),
        name="finish",
    )(probe_modes, mine, other)


def on_device(object_field, probe_modes, counts, centers, patterns):
    half = probe_modes.shape[-1] // 2

    col_even, col_odd, row_even, row_odd = cut_strips(object_field, half)
    go_on = lax.axis_index("col") < 4096
    row_halos = (swap_pairs(row_even, ROW, 0), swap_pairs(row_odd, ROW, 1))
    col_halos = (swap_pairs(col_even, COL, 0), swap_pairs(col_odd, COL, 1))
    is_even = (lax.axis_index("col") & 1) == 0
    first_ends = jnp.concatenate([halo[:, :, :half] for halo in row_halos], 1)
    last_ends = jnp.concatenate([halo[:, :, -half:] for halo in row_halos], 1)
    end_halos = (
        swap_pairs(jnp.where(is_even, last_ends, first_ends), COL, 0),
        swap_pairs(jnp.where(is_even, first_ends, last_ends), COL, 1),
    )

    inputs = (counts, centers[0, 0], object_field, patterns[0, 0], probe_modes, row_halos)
    started = run_positions(*inputs)
    joined = [jnp.concatenate(both, 1) for both in zip(col_halos, end_halos)]
    border = (*joined, *started)
    partial, g_row_even, g_row_odd, g_col_even, g_col_odd, kept = run_positions(*inputs, border)

    from_rows = (swap_pairs(g_row_even, ROW, 0), swap_pairs(g_row_odd, ROW, 1))
    received = lax.cond(
        go_on, exchange, jnp.zeros_like, by_device(chip_sums(kept, from_rows[0]))
    )
    row_odd, _ = lax.optimization_barrier((from_rows[1], received))
    from_rows = (from_rows[0], row_odd)
    to_even, to_odd = add_corners((g_col_even, g_col_odd), from_rows)
    received, to_even, to_odd = lax.optimization_barrier((received, to_even, to_odd))
    from_cols = (swap_pairs(to_even, COL, 0), swap_pairs(to_odd, COL, 1))
    if received.ndim == 5:
        received = received[:, 0]
    mine = lax.cond(go_on, exchange, jnp.zeros_like, shared_update(received))
    mine, from_cols, partial = lax.optimization_barrier((mine, from_cols, partial))
    new_object = add_rims(partial, from_rows, from_cols)
    return (new_object, finish_probe(probe_modes, mine))


def solution(mesh):
    rows, columns = mesh.devices.shape
    split = jax.sharding.Mesh(
        mesh.devices.reshape(rows // 2, 2, columns), ("x", "core", "col")
    )
    placed = (
        P(None, ROW, "col"),
        P(),
        P(),
        P(ROW, "col", None, None),
        P(ROW, "col", None, None, None),
    )
    return jax.shard_map(
        on_device,
        mesh=split,
        in_specs=placed,
        out_specs=(P(None, ROW, "col"), P()),
        check_vma=False,
    )
```

```python
import functools
import math

import jax
import jax.numpy as jnp
import ml_dtypes
import numpy as np
from jax import lax
from jax.experimental import pallas as pl
from jax.experimental.pallas import tpu as pltpu
from jax.sharding import PartitionSpec as P

LANES = 128
ROW = ("x", "core")
COL = ("col",)
F32 = jnp.float32
BF16 = jnp.bfloat16


def dft_tables(length):
    indices = np.arange(length)
    angles = (indices[:, None] * indices[None, :] % length) * (2.0 * np.pi / length)
    scale = 1.0 / np.sqrt(length)
    cosine = (np.cos(angles) * scale).astype(np.float32).astype(ml_dtypes.bfloat16)
    sine = (np.sin(angles) * scale).astype(np.float32).astype(ml_dtypes.bfloat16)
    return np.stack([cosine, sine, -sine])


def swap_pairs(array, axis, odd):
    devices = math.prod(lax.axis_size(name) for name in axis)
    firsts = range(odd, devices - 1, 2)
    return lax.ppermute(
        array, axis, [(i, i + 1) for i in firsts] + [(i + 1, i) for i in firsts]
    )


def sides(axis, length, width):
    even = (lax.axis_index(axis) & 1) == 0
    far = length - width
    return [
        pl.multiple_of(jnp.where(even, far, 0), width),
        pl.multiple_of(jnp.where(even, 0, far), width),
    ]


def strips_kernel(obj_hbm, col_even, col_odd, row_even, row_odd, col_buffer, row_buffer, sems):
    tile = obj_hbm.shape[1]
    half = row_even.shape[1]
    copies = []
    for pair in range(2):
        column = sides(COL, tile, half)[pair]
        row = sides(ROW, tile, half)[pair]
        copies.append(
            pltpu.make_async_copy(
                obj_hbm.at[:, :, pl.ds(column, half)], col_buffer.at[pair], sems.at[0, pair]
            )
        )
        copies.append(
            pltpu.make_async_copy(
                obj_hbm.at[:, pl.ds(row, half), :], row_buffer.at[pair], sems.at[1, pair]
            )
        )
    for copy in copies:
        copy.start()
    outputs = (col_even, row_even, col_odd, row_odd)
    buffers = (col_buffer, row_buffer) * 2
    for index, copy in enumerate(copies):
        copy.wait()
        outputs[index][...] = buffers[index][index // 2].astype(BF16)


def cut_strips(object_field, half):
    tile = object_field.shape[1]
    vmem = pl.BlockSpec(memory_space=pltpu.VMEM)
    columns = jax.ShapeDtypeStruct((2, tile, half), BF16)
    rows = jax.ShapeDtypeStruct((2, half, tile), BF16)
    return pl.pallas_call(
        strips_kernel,
        in_specs=[pl.BlockSpec(memory_space=pltpu.HBM)],
        out_specs=[vmem] * 4,
        out_shape=[columns, columns, rows, rows],
        scratch_shapes=[
            pltpu.VMEM((2, 2, tile, half), F32),
            pltpu.VMEM((2, 2, half, tile), F32),
            pltpu.SemaphoreType.DMA((2, 2)),
        ],
        compiler_params=pltpu.CompilerParams(vmem_limit_bytes=50 * 1024 * 1024),
        cost_estimate=pl.CostEstimate(
            flops=1024 * 1024, bytes_accessed=5 * 1024 * 1024, transcendentals=0
        ),
        name="strips",
    )(object_field)


def positions_kernel(with_border, *refs):
    counts, centers, obj_hbm, pat_hbm, probe = refs[:5]
    tables, row_halos = refs[5], refs[6:8]
    refs = refs[8:]
    if with_border:
        col_halos = refs[0:2]
        start_hbm, ring_in, sums_in = refs[2:5]
        out_hbm, g_rows, g_ends, g_mids, kept = refs[5], refs[6:8], refs[8:10], refs[10:12], refs[12]
        refs = refs[13:]
    else:
        out_hbm, ring_out, sums_out = refs[:3]
        refs = refs[3:]
    (obj, canvas, patterns, positive, negative, folded, swapped, amplitudes, low, waves, shifts, halves, backs,
     spectra, changes, patch, sums, order, piece_sems, out_sems, ring_sems, pat_sems,
     sums_sems) = refs
    size = probe.shape[-1]
    half = size // 2
    tile = obj_hbm.shape[1]
    inner = tile // LANES
    chunks = inner + 2
    modes = probe.shape[0]
    rows = slice(half, half + tile)
    near = [0, 1, inner - 2, inner - 1] if with_border else list(range(inner))
    pieces = [(comp, j) for comp in range(2) for j in near]

    def home(array, comp, j):
        return array.at[comp, :, pl.ds(j * LANES, LANES)]

    def held(array, comp, j):
        return array.at[comp * chunks + 1 + j, pl.ds(half, tile), :]

    def ring_pieces(array):
        for comp in range(2):
            for side, row in enumerate((0, half + tile)):
                yield (
                    array.at[pl.ds(comp * inner, inner), pl.ds(side * half, half), :],
                    canvas.at[pl.ds(comp * chunks + 1, inner), pl.ds(row, half), :],
                    ring_sems.at[side, comp],
                )

    def sums_pieces(array):
        step = array.shape[0] // sums_parts
        for part in range(sums_parts):
            here = pl.ds(part * step, step)
            yield array.at[here], sums.at[here], sums_sems.at[part]

    sums_parts = sums_sems.shape[0]
    obj_copies = [
        pltpu.make_async_copy(home(obj_hbm, *p), held(obj, *p), piece_sems.at[0, *p])
        for p in pieces
    ]
    out_copies = [
        pltpu.make_async_copy(held(canvas, *p), home(out_hbm, *p), out_sems.at[p]) for p in pieces
    ]
    later = []
    if with_border:
        later += [
            pltpu.make_async_copy(home(start_hbm, *p), held(canvas, *p), piece_sems.at[1, *p])
            for p in pieces
        ]
        later += [pltpu.make_async_copy(*each) for each in ring_pieces(ring_in)]
        later += [pltpu.make_async_copy(*each) for each in sums_pieces(sums_in)]
    for copy in obj_copies + later:
        copy.start()

    order[0] = 0
    count = counts[lax.axis_index(ROW), lax.axis_index("col")]

    def pattern_copy(slot):
        return pltpu.make_async_copy(pat_hbm.at[slot], patterns.at[slot], pat_sems.at[slot])

    def note(slot, found):
        column = centers[1, slot]
        inside = (column >= half) & (column <= tile - half)
        order[found] = slot
        return found + jnp.where(inside, 0 if with_border else 1, 1 if with_border else 0)

    def fetch(index, carry):
        pattern_copy(order[index]).start()
        return carry

    found = lax.fori_loop(0, count, note, 0)
    lax.fori_loop(0, found, fetch, 0)

    if not with_border:
        sums[...] = jnp.zeros_like(sums)
    intensity = jnp.zeros((size, size), F32)
    for m in range(modes):
        for comp in range(2):
            values = probe[m, comp]
            intensity = intensity + values * values
            low[2 * m + comp] = values.astype(BF16).astype(F32)
    scale = 1.0 / (jnp.max(intensity) + 1e-06)
    cosine, sine = tables[0], tables[1]
    index_row = lax.broadcasted_iota(jnp.int32, (size, size), 0)
    index_column = lax.broadcasted_iota(jnp.int32, (size, size), 1)
    target = jnp.where(index_row > half, size + half - index_row, index_row)
    swapped[...] = jnp.where(index_column == target, 1.0, 0.0).astype(BF16)
    first_lane = lax.broadcasted_iota(jnp.int32, (size, half), 1) == 0
    first_row = lax.broadcasted_iota(jnp.int32, (half, size), 0) == 0
    wide_cosine = cosine.astype(F32)
    wide_sine = sine.astype(F32)
    folded[0, :, 0:half] = cosine[:, 0:half]
    folded[0, :, half:] = jnp.where(
        first_lane, wide_cosine[:, half:], wide_sine[:, 0:half]
    ).astype(BF16)
    folded[1, 0:half, :] = cosine[0:half, :]
    folded[1, half:, :] = jnp.where(
        first_row, wide_cosine[half:, :], wide_sine[0:half, :]
    ).astype(BF16)

    def reordered(left_side, right_side):
        return jnp.dot(left_side, right_side, preferred_element_type=F32).astype(BF16)

    turns = [reordered(swapped[...], tables[i]) for i in range(3)]
    negative[0:size, 0:size] = turns[0]
    negative[0:size, size:] = turns[1]
    negative[size:, 0:size] = turns[2]
    negative[size:, size:] = turns[0]
    turns = [reordered(tables[i], swapped[...]) for i in range(3)]
    positive[0:size, 0:size] = turns[0]
    positive[0:size, size:] = turns[2]
    positive[size:, 0:size] = turns[1]
    positive[size:, size:] = turns[0]
    changes[...] = jnp.zeros_like(changes)
    patch[...] = jnp.zeros_like(patch)

    row_sides = sides(ROW, tile + size, half)
    col_sides = [offset // LANES for offset in sides(COL, tile + size, half)]
    blank = jnp.zeros((tile + size, LANES), F32)
    for comp in range(2):
        first = comp * chunks
        for pair in range(2):
            for j in near:
                columns = slice(j * LANES, (j + 1) * LANES)
                obj[first + 1 + j, pl.ds(row_sides[pair], half), :] = row_halos[pair][
                    comp, :, columns
                ].astype(F32)
            if with_border:
                beside = first + col_sides[pair]
                canvas[beside] = blank
                obj[beside, rows, :] = col_halos[pair][comp, 0:tile, :].astype(F32)
                for other in range(2):
                    obj[beside, pl.ds(row_sides[other], half), :] = col_halos[pair][
                        comp, tile + other * half : tile + (other + 1) * half, :
                    ].astype(F32)
        if not with_border:
            for j in range(inner):
                canvas[first + 1 + j, 0:half, :] = blank[0:half]
                canvas[first + 1 + j, half + tile :, :] = blank[0:half]

    block = 16
    groups = block // 8
    lane = lax.broadcasted_iota(jnp.int32, (block, LANES), 1)
    blocks = range(0, size, block)

    def place_of(index):
        slot = order[index]
        column = centers[1, slot]
        return slot, centers[0, slot], column >> 7, column & 127

    def cut(index, begin):
        _, row, chunk, offset = place_of(index)
        back_offset = (LANES - offset) & 127
        from_first = lane < LANES - offset
        here = slice(begin, begin + block)
        parts = []
        for comp in range(2):
            moved = [
                pltpu.roll(
                    obj[comp * chunks + chunk + k, pl.ds(row + begin, block), :], back_offset, 1
                )
                for k in range(3)
            ]
            window = jnp.concatenate(
                [
                    jnp.where(from_first, moved[0], moved[1]),
                    jnp.where(from_first, moved[1], moved[2]),
                ],
                1,
            ).astype(BF16).astype(F32)
            patch[index & 1, comp, here, :] = window
            parts.append(window)
        real, imag = parts
        for m in range(modes):
            probe_real = low[2 * m, here, :]
            probe_imag = low[2 * m + 1, here, :]
            there = slice(m * size + begin, m * size + begin + block)
            waves[there, 0:size] = (probe_real * real - probe_imag * imag).astype(BF16)
            waves[there, size:] = (probe_real * imag + probe_imag * real).astype(BF16)

    def forward_right(m):
        mode = slice(m * size, (m + 1) * size)
        real = jnp.dot(waves[mode, 0:size], folded[0], preferred_element_type=F32)
        imag = jnp.dot(waves[mode, size:], folded[0], preferred_element_type=F32)
        real_cos, real_sin = real[:, 0:half], real[:, half:]
        imag_cos, imag_sin = imag[:, 0:half], imag[:, half:]
        plus = slice(m * size, m * size + half)
        minus = slice(m * size + half, (m + 1) * size)
        halves[0:size, plus] = (real_cos + jnp.where(first_lane, 0.0, imag_sin)).astype(BF16)
        halves[size:, plus] = (imag_cos - jnp.where(first_lane, 0.0, real_sin)).astype(BF16)
        halves[0:size, minus] = jnp.where(first_lane, real_sin, real_cos - imag_sin).astype(BF16)
        halves[size:, minus] = jnp.where(first_lane, imag_sin, imag_cos + real_sin).astype(BF16)

    def forward_left(m):
        mode = slice(m * size, (m + 1) * size)
        real = jnp.dot(folded[1], halves[0:size, mode], preferred_element_type=F32)
        imag = jnp.dot(folded[1], halves[size:, mode], preferred_element_type=F32)
        real_cos, real_sin = real[0:half], real[half:]
        imag_cos, imag_sin = imag[0:half], imag[half:]
        spectra[0:half, mode] = real_cos + jnp.where(first_row, 0.0, imag_sin)
        spectra[size : size + half, mode] = imag_cos - jnp.where(first_row, 0.0, real_sin)
        spectra[half:size, mode] = jnp.where(first_row, real_sin, real_cos - imag_sin)
        spectra[size + half :, mode] = jnp.where(first_row, imag_sin, imag_cos + real_sin)

    def fold_amplitudes(index):
        rows_folded = reordered(swapped[...], patterns[order[index]])
        amplitudes[...] = jnp.dot(rows_folded, swapped[...], preferred_element_type=F32)

    def reweigh(begin):
        k, inside = divmod(begin, half)
        here = slice(begin, begin + block)
        below = slice(size + begin, size + begin + block)
        mode_columns = [slice(m * size, (m + 1) * size) for m in range(modes)]
        parts = [(spectra[here, mode], spectra[below, mode]) for mode in mode_columns]
        power = sum(real * real + imag * imag for real, imag in parts)
        factor = amplitudes[here, :] * lax.rsqrt(jnp.maximum(power, 0.5)) - 1.0
        for m, (real, imag) in enumerate(parts):
            first = k * size + m * half + inside
            there = slice(first, first + block)
            shifts[there, 0:size] = (factor * real).astype(BF16)
            shifts[there, size:] = (factor * imag).astype(BF16)

    def backward_right(k, part):
        columns = slice(part * size, (part + 1) * size)
        product = jnp.dot(
            shifts[k * size : (k + 1) * size, :], negative[:, columns],
            preferred_element_type=F32,
        ).astype(BF16)
        first = part * size + k * half
        for m in range(modes):
            mode = slice(m * size, (m + 1) * size)
            backs[first : first + half, mode] = product[m * half : (m + 1) * half, :]

    def backward_left(m, part):
        mode = slice(m * size, (m + 1) * size)
        rows_here = slice(part * size, (part + 1) * size)
        changes[rows_here, mode] = jnp.dot(
            positive[rows_here, :], backs[:, mode], preferred_element_type=F32
        )

    def deposit(index, buffer, begin):
        _, row, chunk, offset = place_of(index)
        past = lane >= offset
        here = slice(begin, begin + block)
        below = slice(size + begin, size + begin + block)
        start = begin // 8
        obj_real = patch[buffer, 0, here, :]
        obj_imag = patch[buffer, 1, here, :]

        def add(plane, value):
            sums[start : start + groups, plane] += value.reshape(groups, 8, size)

        add(2 * modes, obj_real * obj_real + obj_imag * obj_imag)
        term_real = term_imag = None
        for m in range(modes):
            mode = slice(m * size, (m + 1) * size)
            real = changes[here, mode]
            imag = changes[below, mode]
            probe_real = low[2 * m, here, :]
            probe_imag = low[2 * m + 1, here, :]
            more_real = probe_real * real + probe_imag * imag
            more_imag = probe_real * imag - probe_imag * real
            term_real = more_real if m == 0 else term_real + more_real
            term_imag = more_imag if m == 0 else term_imag + more_imag
            add(2 * m, obj_real * real + obj_imag * imag)
            add(2 * m + 1, obj_real * imag - obj_imag * real)
        for comp, term in enumerate((term_real, term_imag)):
            term = term.astype(BF16).astype(F32) * scale
            first = pltpu.roll(term[:, 0:LANES], offset, 1)
            second = pltpu.roll(term[:, LANES:], offset, 1)
            place = comp * chunks + chunk
            window = pl.ds(row + begin, block)
            values = [canvas[place + k, window, :] for k in range(3)]
            canvas[place, window, :] = values[0] + jnp.where(past, first, 0.0)
            canvas[place + 1, window, :] = values[1] + jnp.where(past, second, first)
            canvas[place + 2, window, :] = values[2] + jnp.where(past, 0.0, second)

    def step(index, carry):
        pattern_copy(order[index]).wait()
        previous = jnp.maximum(index - 1, 0)
        following = jnp.minimum(index + 1, found - 1)
        buffer = (index + 1) & 1
        starts = list(blocks)
        middle = len(starts) // 2

        def between(pieces_of, blocks_of):
            given = 0
            for done, piece in enumerate(pieces_of):
                piece()
                until = (done + 1) * len(blocks_of) // len(pieces_of)
                for each in blocks_of[given:until]:
                    each()
                given = until

        bind = functools.partial
        pairs = [(first, second) for first in range(2) for second in range(2)]
        between(
            [bind(forward_right, 0), bind(fold_amplitudes, index), bind(forward_right, 1)]
            + [bind(forward_left, m) for m in range(modes)],
            [bind(deposit, previous, buffer, begin) for begin in starts],
        )
        for begin in starts[:middle]:
            reweigh(begin)
        between(
            [bind(backward_right, 0, part) for part in range(2)],
            [bind(reweigh, begin) for begin in starts[middle:]],
        )
        between(
            [bind(backward_right, 1, part) for part in range(2)]
            + [bind(backward_left, *pair) for pair in pairs],
            [bind(cut, following, begin) for begin in starts],
        )
        return carry

    for copy in obj_copies:
        copy.wait()

    @pl.when(found > 0)
    def _():
        for begin in blocks:
            cut(0, begin)

    if not with_border:
        for comp, j in pieces:
            index = comp * chunks + 1 + j
            canvas[index, rows, :] = obj[index, rows, :]
    for copy in later:
        copy.wait()

    @pl.when(found > 0)
    def _():
        lax.fori_loop(0, found, step, 0)
        for begin in blocks:
            deposit(found - 1, (found - 1) & 1, begin)

    last_copies = list(out_copies)
    if not with_border:
        last_copies += [
            pltpu.make_async_copy(here, there, sem) for there, here, sem in ring_pieces(ring_out)
        ]
        last_copies += [
            pltpu.make_async_copy(here, there, sem) for there, here, sem in sums_pieces(sums_out)
        ]
    for copy in last_copies:
        copy.start()
    if with_border:
        for pair in range(2):
            g_rows[pair][0 : 2 * chunks] = canvas[:, pl.ds(row_sides[pair], half), :].astype(BF16)
            for comp in range(2):
                beside = comp * chunks + col_sides[pair]
                low_end = half + tile
                g_ends[pair][comp, 0:half] = canvas[beside, half:size, :].astype(BF16)
                g_ends[pair][comp, half:] = canvas[beside, low_end - half : low_end, :].astype(BF16)
                g_mids[pair][comp] = canvas[beside, size : low_end - half, :].astype(BF16)
        core = lax.axis_index("core")
        count_of = kept.shape[0]
        kept[...] = sums[pl.ds(core * count_of, count_of)]
        for plane in range(2 * modes + 1):
            for side in range(2):
                columns = slice(side * half, (side + 1) * half)
                given = sums[pl.ds((1 - core) * count_of, count_of), plane, :, columns]
                g_rows[0][2 * chunks + 2 * plane + side] = given.reshape(half, LANES).astype(BF16)
    for copy in last_copies:
        copy.wait()


def run_positions(counts, centers, object_field, patterns, probe_modes, row_halos, border=None):
    size = probe_modes.shape[-1]
    half = size // 2
    modes = probe_modes.shape[0]
    tile = object_field.shape[1]
    inner = tile // LANES
    chunks = inner + 2
    slots = patterns.shape[0]
    smem = pl.BlockSpec(memory_space=pltpu.SMEM)
    vmem = pl.BlockSpec(memory_space=pltpu.VMEM)
    anywhere = pl.BlockSpec(memory_space=pl.ANY)
    shape = jax.ShapeDtypeStruct
    in_specs = [smem, smem, anywhere, anywhere] + [vmem] * 4
    operands = [counts, centers, object_field, patterns, probe_modes, dft_tables(size), *row_halos]
    sums_shape = (size // 8, 2 * modes + 1, 8, size)
    ring_shape = (2 * inner, size, LANES)
    aliases = {}
    if border is None:
        out_specs = [anywhere] * 3
        out_shape = [shape(each, F32) for each in (object_field.shape, ring_shape, sums_shape)]
    else:
        aliases = {len(operands) + 2: 0}
        in_specs += [vmem] * 2 + [anywhere] * 3
        operands += list(border)
        half_sums = (size // 16,) + sums_shape[1:]
        out_specs = [anywhere] + [vmem] * 7
        out_shape = [
            shape((2, tile, tile), F32),
            shape((2 * chunks + 4 * modes + 2, half, LANES), BF16),
            shape((2 * chunks, half, LANES), BF16),
            shape((2, size, LANES), BF16),
            shape((2, size, LANES), BF16),
            shape((2, tile - size, LANES), BF16),
            shape((2, tile - size, LANES), BF16),
            shape(half_sums, F32),
        ]
    table = pltpu.VMEM((2 * size, 2 * size), BF16)
    products = pltpu.VMEM((2 * size, modes * size), BF16)
    wide = pltpu.VMEM((2 * size, modes * size), F32)
    padded = pltpu.VMEM((2 * chunks, tile + size, LANES), F32)
    dma = pltpu.SemaphoreType.DMA
    return pl.pallas_call(
        functools.partial(positions_kernel, border is not None),
        in_specs=in_specs,
        out_specs=out_specs,
        out_shape=out_shape,
        input_output_aliases=aliases,
        scratch_shapes=[
            padded,
            padded,
            pltpu.VMEM(patterns.shape, BF16),
            table,
            table,
            pltpu.VMEM((2, size, size), BF16),
            pltpu.VMEM((size, size), BF16),
            pltpu.VMEM((size, size), F32),
            pltpu.VMEM((2 * modes, size, size), F32),
            products,
            products,
            products,
            products,
            wide,
            wide,
            pltpu.VMEM((2, 2, size, size), F32),
            pltpu.VMEM(sums_shape, F32),
            pltpu.SMEM((slots + 1,), jnp.int32),
            dma((2, 2, inner)),
            dma((2, inner)),
            dma((2, 2)),
            dma((slots,)),
            dma((4,)),
        ],
        compiler_params=pltpu.CompilerParams(
            vmem_limit_bytes=(50 if border is None else 46) * 1024 * 1024
        ),
        cost_estimate=pl.CostEstimate(
            flops=slots * 16 * modes * size**3,
            bytes_accessed=24 * 1024 * 1024,
            transcendentals=0,
        ),
        name="border" if border is not None else "interior",
    )(*operands)


def corners_kernel(end_even, end_odd, row_even, row_odd, out_even, out_odd):
    half = row_even.shape[1]
    chunks = row_odd.shape[0] // 2
    row_sides = sides(ROW, 2 * half, half)
    col_sides = [offset // LANES for offset in sides(COL, chunks * LANES, half)]
    for pair, (strip, out) in enumerate(((end_even, out_even), (end_odd, out_odd))):
        for other, ring in enumerate((row_even, row_odd)):
            there = pl.ds(row_sides[other], half)
            for comp in range(2):
                extra = ring[comp * chunks + col_sides[pair]].astype(F32)
                out[comp, there, :] = (strip[comp, there, :].astype(F32) + extra).astype(BF16)


def add_corners(g_ends, from_rows):
    vmem = pl.BlockSpec(memory_space=pltpu.VMEM)
    shape = jax.ShapeDtypeStruct(g_ends[0].shape, BF16)
    return pl.pallas_call(
        corners_kernel,
        in_specs=[vmem] * 4,
        out_specs=[vmem] * 2,
        out_shape=[shape, shape],
        compiler_params=pltpu.CompilerParams(vmem_limit_bytes=8 * 1024 * 1024),
        cost_estimate=pl.CostEstimate(
            flops=256 * 1024, bytes_accessed=2 * 1024 * 1024, transcendentals=0
        ),
        name="corners",
    )(*g_ends, *from_rows)


def rims_kernel(
    partial, row_even, row_odd, end_even, end_odd, mid_even, mid_odd, out, row_buffer, col_buffer,
    sems,
):
    tile = partial.shape[1]
    half = row_even.shape[1]
    inner = tile // LANES
    chunks = inner + 2
    middle = tile - 2 * half
    row_sides = sides(ROW, tile, half)
    col_sides = sides(COL, tile, half)
    row_rings = (row_even, row_odd)
    end_sides = sides(ROW, 2 * half, half)
    end_strips = (end_even, end_odd)
    mid_strips = (mid_even, mid_odd)

    def copy(kind, pair, comp, inward):
        if kind == 0:
            here = row_buffer.at[pair, comp]
            place = (comp, pl.ds(row_sides[pair], half), slice(None))
        else:
            here = col_buffer.at[pair, comp]
            place = (comp, pl.ds(half, middle), pl.ds(col_sides[pair], half))
        source, target = (partial.at[place], here) if inward else (here, out.at[place])
        return pltpu.make_async_copy(
            source, target, sems.at[1 - int(inward), 2 * kind + pair, comp]
        )

    everything = [(kind, pair, comp) for kind in range(2) for pair in range(2) for comp in range(2)]
    for piece in everything:
        copy(*piece, True).start()
    for kind, pair, comp in everything:
        copy(kind, pair, comp, True).wait()
        if kind == 0:
            for j in range(inner):
                columns = slice(j * LANES, (j + 1) * LANES)
                ring = row_rings[pair][comp * chunks + 1 + j]
                row_buffer[pair, comp, :, columns] += ring.astype(F32)
            for other in range(2):
                columns = pl.ds(col_sides[other], half)
                strip = end_strips[other][comp, pl.ds(end_sides[pair], half), :]
                row_buffer[pair, comp, :, columns] += strip.astype(F32)
        else:
            col_buffer[pair, comp] += mid_strips[pair][comp].astype(F32)
        copy(kind, pair, comp, False).start()
    for piece in everything:
        copy(*piece, False).wait()


def add_rims(partial, from_rows, from_ends, from_mids):
    tile = partial.shape[1]
    half = from_rows[0].shape[1]
    vmem = pl.BlockSpec(memory_space=pltpu.VMEM)
    anywhere = pl.BlockSpec(memory_space=pl.ANY)
    return pl.pallas_call(
        rims_kernel,
        in_specs=[anywhere] + [vmem] * 6,
        out_specs=anywhere,
        out_shape=jax.ShapeDtypeStruct(partial.shape, F32),
        input_output_aliases={0: 0},
        scratch_shapes=[
            pltpu.VMEM((2, 2, half, tile), F32),
            pltpu.VMEM((2, 2, tile - 2 * half, half), F32),
            pltpu.SemaphoreType.DMA((2, 4, 2)),
        ],
        compiler_params=pltpu.CompilerParams(vmem_limit_bytes=16 * 1024 * 1024),
        cost_estimate=pl.CostEstimate(
            flops=1024 * 1024, bytes_accessed=6 * 1024 * 1024, transcendentals=0
        ),
        name="rims",
    )(partial, *from_rows, *from_ends, *from_mids)


def chip_sums_kernel(kept, received, out):
    groups, planes, height, size = kept.shape
    half = received.shape[1]
    first = received.shape[0] - 2 * planes
    for plane in range(planes):
        for side in range(2):
            columns = slice(side * half, (side + 1) * half)
            other = received[first + 2 * plane + side].astype(F32).reshape(groups, height, half)
            out[:, plane, :, columns] = (kept[:, plane, :, columns] + other).astype(BF16)


def chip_sums(kept, received):
    vmem = pl.BlockSpec(memory_space=pltpu.VMEM)
    return pl.pallas_call(
        chip_sums_kernel,
        in_specs=[vmem, vmem],
        out_specs=vmem,
        out_shape=jax.ShapeDtypeStruct(kept.shape, BF16),
        compiler_params=pltpu.CompilerParams(vmem_limit_bytes=8 * 1024 * 1024),
        cost_estimate=pl.CostEstimate(
            flops=32 * 1024**3, bytes_accessed=32 * 1024 * 1024, transcendentals=0
        ),
        name="chip_sums",
    )(kept, received)


def by_device(on_chip):
    devices = lax.axis_size("x") * lax.axis_size("col")
    groups, planes, _, size = on_chip.shape
    share = groups * 8 // devices
    if share < 8:
        on_chip = on_chip.reshape(groups, planes, 8 // share, share, size)
        return jnp.swapaxes(on_chip, 1, 2).reshape(devices, planes, share, size)
    return on_chip.reshape(devices, groups // devices, planes, 8, size)


def exchange(parts):
    return lax.all_to_all(parts, ("x", "col"), 0, 0, tiled=True)


def update_kernel(received, copies):
    devices = received.shape[0]
    total = received[0].astype(F32)
    for device in range(1, devices):
        total = total + received[device].astype(F32)
    planes = total.shape[0]
    update = (total[: planes - 1] / jnp.sqrt(total[planes - 1])).astype(BF16)
    for device in range(devices):
        copies[device] = update


def shared_update(received):
    devices, planes, share, size = received.shape
    vmem = pl.BlockSpec(memory_space=pltpu.VMEM)
    return pl.pallas_call(
        update_kernel,
        in_specs=[vmem],
        out_specs=vmem,
        out_shape=jax.ShapeDtypeStruct((devices, planes - 1, share, size), BF16),
        compiler_params=pltpu.CompilerParams(vmem_limit_bytes=8 * 1024 * 1024),
        cost_estimate=pl.CostEstimate(
            flops=512 * 1024, bytes_accessed=1024 * 1024, transcendentals=0
        ),
        name="update",
    )(received)


def finish_kernel(probe, mine, other, out):
    core = lax.axis_index("core")
    groups, planes, height, _ = mine.shape
    for side, update in enumerate((mine, other)):
        first = jnp.where(core == side, 0, groups * height)
        for group in range(groups):
            place = pl.ds(pl.multiple_of(first + group * height, height), height)
            for plane in range(planes):
                m, comp = divmod(plane, 2)
                out[m, comp, place, :] = probe[m, comp, place, :] + update[group, plane].astype(F32)


def finish_probe(probe_modes, mine):
    devices, planes, share, size = mine.shape
    if share < 8:
        mine = mine.reshape(devices * share // 8, 8 // share, planes, share, size)
        mine = jnp.swapaxes(mine, 1, 2).reshape(-1, planes, 8, size)
    other = lax.ppermute(mine, "core", [(0, 1), (1, 0)])
    vmem = pl.BlockSpec(memory_space=pltpu.VMEM)
    return pl.pallas_call(
        finish_kernel,
        in_specs=[vmem] * 3,
        out_specs=vmem,
        out_shape=jax.ShapeDtypeStruct(probe_modes.shape, F32),
        compiler_params=pltpu.CompilerParams(vmem_limit_bytes=8 * 1024 * 1024),
        cost_estimate=pl.CostEstimate(
            flops=256 * 1024, bytes_accessed=3 * 1024 * 1024, transcendentals=0
        ),
        name="finish",
    )(probe_modes, mine, other)


def on_device(object_field, probe_modes, counts, centers, patterns):
    half = probe_modes.shape[-1] // 2

    col_even, col_odd, row_even, row_odd = cut_strips(object_field, half)
    go_on = lax.axis_index("col") < 4096
    row_halos = (swap_pairs(row_even, ROW, 0), swap_pairs(row_odd, ROW, 1))
    col_halos = (swap_pairs(col_even, COL, 0), swap_pairs(col_odd, COL, 1))
    is_even = (lax.axis_index("col") & 1) == 0
    first_ends = jnp.concatenate([halo[:, :, :half] for halo in row_halos], 1)
    last_ends = jnp.concatenate([halo[:, :, -half:] for halo in row_halos], 1)
    end_halos = (
        swap_pairs(jnp.where(is_even, last_ends, first_ends), COL, 0),
        swap_pairs(jnp.where(is_even, first_ends, last_ends), COL, 1),
    )

    inputs = (counts, centers[0, 0], object_field, patterns[0, 0], probe_modes, row_halos)
    started = run_positions(*inputs)
    joined = [jnp.concatenate(both, 1) for both in zip(col_halos, end_halos)]
    border = (*joined, *started)
    partial, *rims, kept = run_positions(*inputs, border)
    g_row_even, g_row_odd, g_end_even, g_end_odd, g_mid_even, g_mid_odd = rims

    from_rows = (swap_pairs(g_row_even, ROW, 0), swap_pairs(g_row_odd, ROW, 1))
    from_mids = (swap_pairs(g_mid_even, COL, 0), swap_pairs(g_mid_odd, COL, 1))
    received = lax.cond(
        go_on, exchange, jnp.zeros_like, by_device(chip_sums(kept, from_rows[0]))
    )
    row_odd, _ = lax.optimization_barrier((from_rows[1], received))
    from_rows = (from_rows[0], row_odd)
    to_even, to_odd = add_corners((g_end_even, g_end_odd), from_rows)
    received, from_mids, to_even, to_odd = lax.optimization_barrier(
        (received, from_mids, to_even, to_odd)
    )
    from_ends = (swap_pairs(to_even, COL, 0), swap_pairs(to_odd, COL, 1))
    if received.ndim == 5:
        received = received[:, 0]
    mine = lax.cond(go_on, exchange, jnp.zeros_like, shared_update(received))
    mine, from_ends, partial = lax.optimization_barrier((mine, from_ends, partial))
    new_object = add_rims(partial, from_rows, from_ends, from_mids)
    return (new_object, finish_probe(probe_modes, mine))


def solution(mesh):
    rows, columns = mesh.devices.shape
    split = jax.sharding.Mesh(
        mesh.devices.reshape(rows // 2, 2, columns), ("x", "core", "col")
    )
    placed = (
        P(None, ROW, "col"),
        P(),
        P(),
        P(ROW, "col", None, None),
        P(ROW, "col", None, None, None),
    )
    return jax.shard_map(
        on_device,
        mesh=split,
        in_specs=placed,
        out_specs=(P(None, ROW, "col"), P()),
        check_vma=False,
    )
```

```python
import functools
import math

import jax
import jax.numpy as jnp
import ml_dtypes
import numpy as np
from jax import lax
from jax.experimental import pallas as pl
from jax.experimental.pallas import tpu as pltpu
from jax.sharding import PartitionSpec as P

LANES = 128
ROW = ("x", "core")
COL = ("col",)
F32 = jnp.float32
BF16 = jnp.bfloat16


def dft_tables(length):
    indices = np.arange(length)
    angles = (indices[:, None] * indices[None, :] % length) * (2.0 * np.pi / length)
    scale = 1.0 / np.sqrt(length)
    cosine = (np.cos(angles) * scale).astype(np.float32).astype(ml_dtypes.bfloat16)
    sine = (np.sin(angles) * scale).astype(np.float32).astype(ml_dtypes.bfloat16)
    return np.stack([cosine, sine, -sine])


def swap_pairs(array, axis, odd):
    devices = math.prod(lax.axis_size(name) for name in axis)
    firsts = range(odd, devices - 1, 2)
    return lax.ppermute(
        array, axis, [(i, i + 1) for i in firsts] + [(i + 1, i) for i in firsts]
    )


def sides(axis, length, width):
    even = (lax.axis_index(axis) & 1) == 0
    far = length - width
    return [
        pl.multiple_of(jnp.where(even, far, 0), width),
        pl.multiple_of(jnp.where(even, 0, far), width),
    ]


def strips_kernel(obj_hbm, col_even, col_odd, row_even, row_odd, col_buffer, row_buffer, sems):
    tile = obj_hbm.shape[1]
    half = row_even.shape[1]
    copies = []
    for pair in range(2):
        column = sides(COL, tile, half)[pair]
        row = sides(ROW, tile, half)[pair]
        copies.append(
            pltpu.make_async_copy(
                obj_hbm.at[:, :, pl.ds(column, half)], col_buffer.at[pair], sems.at[0, pair]
            )
        )
        copies.append(
            pltpu.make_async_copy(
                obj_hbm.at[:, pl.ds(row, half), :], row_buffer.at[pair], sems.at[1, pair]
            )
        )
    for copy in copies:
        copy.start()
    outputs = (col_even, row_even, col_odd, row_odd)
    buffers = (col_buffer, row_buffer) * 2
    for index, copy in enumerate(copies):
        copy.wait()
        outputs[index][...] = buffers[index][index // 2].astype(BF16)


def cut_strips(object_field, half):
    tile = object_field.shape[1]
    vmem = pl.BlockSpec(memory_space=pltpu.VMEM)
    columns = jax.ShapeDtypeStruct((2, tile, half), BF16)
    rows = jax.ShapeDtypeStruct((2, half, tile), BF16)
    return pl.pallas_call(
        strips_kernel,
        in_specs=[pl.BlockSpec(memory_space=pltpu.HBM)],
        out_specs=[vmem] * 4,
        out_shape=[columns, columns, rows, rows],
        scratch_shapes=[
            pltpu.VMEM((2, 2, tile, half), F32),
            pltpu.VMEM((2, 2, half, tile), F32),
            pltpu.SemaphoreType.DMA((2, 2)),
        ],
        compiler_params=pltpu.CompilerParams(vmem_limit_bytes=50 * 1024 * 1024),
        cost_estimate=pl.CostEstimate(
            flops=1024 * 1024, bytes_accessed=5 * 1024 * 1024, transcendentals=0
        ),
        name="strips",
    )(object_field)


def positions_kernel(with_border, *refs):
    counts, centers, obj_hbm, pat_hbm, probe = refs[:5]
    tables, row_halos = refs[5], refs[6:8]
    refs = refs[8:]
    if with_border:
        col_halos = refs[0:2]
        start_hbm, ring_in, sums_in = refs[2:5]
        out_hbm, g_rows, g_cols, kept = refs[5], refs[6:8], refs[8:10], refs[10]
        refs = refs[11:]
    else:
        out_hbm, ring_out, sums_out = refs[:3]
        refs = refs[3:]
    (obj, canvas, patterns, positive, negative, folded, swapped, amplitudes, low, waves, shifts, halves, backs,
     spectra, changes, patch, sums, order, piece_sems, out_sems, ring_sems, pat_sems,
     sums_sems) = refs
    size = probe.shape[-1]
    half = size // 2
    tile = obj_hbm.shape[1]
    inner = tile // LANES
    chunks = inner + 2
    modes = probe.shape[0]
    rows = slice(half, half + tile)
    near = [0, 1, inner - 2, inner - 1] if with_border else list(range(inner))
    pieces = [(comp, j) for comp in range(2) for j in near]

    def home(array, comp, j):
        return array.at[comp, :, pl.ds(j * LANES, LANES)]

    def held(array, comp, j):
        return array.at[comp * chunks + 1 + j, pl.ds(half, tile), :]

    def ring_pieces(array):
        for comp in range(2):
            for side, row in enumerate((0, half + tile)):
                yield (
                    array.at[pl.ds(comp * inner, inner), pl.ds(side * half, half), :],
                    canvas.at[pl.ds(comp * chunks + 1, inner), pl.ds(row, half), :],
                    ring_sems.at[side, comp],
                )

    def sums_pieces(array):
        step = array.shape[0] // sums_parts
        for part in range(sums_parts):
            here = pl.ds(part * step, step)
            yield array.at[here], sums.at[here], sums_sems.at[part]

    sums_parts = sums_sems.shape[0]
    obj_copies = [
        pltpu.make_async_copy(home(obj_hbm, *p), held(obj, *p), piece_sems.at[0, *p])
        for p in pieces
    ]
    out_copies = [
        pltpu.make_async_copy(held(canvas, *p), home(out_hbm, *p), out_sems.at[p]) for p in pieces
    ]
    later = []
    if with_border:
        later += [
            pltpu.make_async_copy(home(start_hbm, *p), held(canvas, *p), piece_sems.at[1, *p])
            for p in pieces
        ]
        later += [pltpu.make_async_copy(*each) for each in ring_pieces(ring_in)]
        later += [pltpu.make_async_copy(*each) for each in sums_pieces(sums_in)]
    for copy in obj_copies + later:
        copy.start()

    order[0] = 0
    count = counts[lax.axis_index(ROW), lax.axis_index("col")]

    def pattern_copy(slot):
        return pltpu.make_async_copy(pat_hbm.at[slot], patterns.at[slot], pat_sems.at[slot])

    def note(slot, found):
        column = centers[1, slot]
        inside = (column >= half) & (column <= tile - half)
        order[found] = slot
        return found + jnp.where(inside, 0 if with_border else 1, 1 if with_border else 0)

    def fetch(index, carry):
        pattern_copy(order[index]).start()
        return carry

    found = lax.fori_loop(0, count, note, 0)
    lax.fori_loop(0, found, fetch, 0)

    if not with_border:
        sums[...] = jnp.zeros_like(sums)
    intensity = jnp.zeros((size, size), F32)
    for m in range(modes):
        for comp in range(2):
            values = probe[m, comp]
            intensity = intensity + values * values
            low[2 * m + comp] = values.astype(BF16).astype(F32)
    scale = 1.0 / (jnp.max(intensity) + 1e-06)
    cosine, sine = tables[0], tables[1]
    index_row = lax.broadcasted_iota(jnp.int32, (size, size), 0)
    index_column = lax.broadcasted_iota(jnp.int32, (size, size), 1)
    target = jnp.where(index_row > half, size + half - index_row, index_row)
    swapped[...] = jnp.where(index_column == target, 1.0, 0.0).astype(BF16)
    first_lane = lax.broadcasted_iota(jnp.int32, (half, half), 1) == 0
    quarter = half // 2
    first_row = lax.broadcasted_iota(jnp.int32, (quarter, size), 0) == 0
    wide_cosine = cosine.astype(F32)
    wide_sine = sine.astype(F32)
    folded[0, :, 0:half] = cosine[:, 0:half]
    for part in range(2):
        here = slice(part * half, (part + 1) * half)
        folded[0, here, half:] = jnp.where(
            first_lane, wide_cosine[here, half:], wide_sine[here, 0:half]
        ).astype(BF16)
    for part in range(2):
        first = part * quarter
        sines = wide_sine[first : first + quarter, :]
        if part == 0:
            sines = jnp.where(first_row, wide_cosine[half : half + quarter, :], sines)
        folded[1, part * half : part * half + quarter, :] = cosine[first : first + quarter, :]
        folded[1, part * half + quarter : (part + 1) * half, :] = sines.astype(BF16)

    def reordered(left_side, right_side):
        return jnp.dot(left_side, right_side, preferred_element_type=F32).astype(BF16)

    turns = [reordered(swapped[...], tables[i]) for i in range(3)]
    negative[0:size, 0:size] = turns[0]
    negative[0:size, size:] = turns[1]
    negative[size:, 0:size] = turns[2]
    negative[size:, size:] = turns[0]
    turns = [reordered(tables[i], swapped[...]) for i in range(3)]
    positive[0:size, 0:size] = turns[0]
    positive[0:size, size:] = turns[2]
    positive[size:, 0:size] = turns[1]
    positive[size:, size:] = turns[0]
    changes[...] = jnp.zeros_like(changes)
    patch[...] = jnp.zeros_like(patch)

    row_sides = sides(ROW, tile + size, half)
    col_sides = [offset // LANES for offset in sides(COL, tile + size, half)]
    blank = jnp.zeros((tile + size, LANES), F32)
    for comp in range(2):
        first = comp * chunks
        for pair in range(2):
            for j in near:
                columns = slice(j * LANES, (j + 1) * LANES)
                obj[first + 1 + j, pl.ds(row_sides[pair], half), :] = row_halos[pair][
                    comp, :, columns
                ].astype(F32)
            if with_border:
                beside = first + col_sides[pair]
                canvas[beside] = blank
                obj[beside, rows, :] = col_halos[pair][comp, 0:tile, :].astype(F32)
                for other in range(2):
                    obj[beside, pl.ds(row_sides[other], half), :] = col_halos[pair][
                        comp, tile + other * half : tile + (other + 1) * half, :
                    ].astype(F32)
        if not with_border:
            for j in range(inner):
                canvas[first + 1 + j, 0:half, :] = blank[0:half]
                canvas[first + 1 + j, half + tile :, :] = blank[0:half]

    block = 16
    groups = block // 8
    lane = lax.broadcasted_iota(jnp.int32, (block, LANES), 1)
    blocks = range(0, size, block)

    def place_of(index):
        slot = order[index]
        column = centers[1, slot]
        return slot, centers[0, slot], column >> 7, column & 127

    def cut(index, begin):
        _, row, chunk, offset = place_of(index)
        back_offset = (LANES - offset) & 127
        from_first = lane < LANES - offset
        here = slice(begin, begin + block)
        parts = []
        for comp in range(2):
            moved = [
                pltpu.roll(
                    obj[comp * chunks + chunk + k, pl.ds(row + begin, block), :], back_offset, 1
                )
                for k in range(3)
            ]
            window = jnp.concatenate(
                [
                    jnp.where(from_first, moved[0], moved[1]),
                    jnp.where(from_first, moved[1], moved[2]),
                ],
                1,
            ).astype(BF16).astype(F32)
            patch[index & 1, comp, here, :] = window
            parts.append(window)
        real, imag = parts
        for m in range(modes):
            probe_real = low[2 * m, here, :]
            probe_imag = low[2 * m + 1, here, :]
            there = slice(m * size + begin, m * size + begin + block)
            waves[there, 0:size] = (probe_real * real - probe_imag * imag).astype(BF16)
            waves[there, size:] = (probe_real * imag + probe_imag * real).astype(BF16)

    def forward_right(m, part):
        here = slice(m * size + part * half, m * size + (part + 1) * half)
        real = jnp.dot(waves[here, 0:size], folded[0], preferred_element_type=F32)
        imag = jnp.dot(waves[here, size:], folded[0], preferred_element_type=F32)
        real_cos, real_sin = real[:, 0:half], real[:, half:]
        imag_cos, imag_sin = imag[:, 0:half], imag[:, half:]
        up = slice(part * half, (part + 1) * half)
        down = slice(size + part * half, size + (part + 1) * half)
        plus = slice(m * size, m * size + half)
        minus = slice(m * size + half, (m + 1) * size)
        halves[up, plus] = (real_cos + jnp.where(first_lane, 0.0, imag_sin)).astype(BF16)
        halves[down, plus] = (imag_cos - jnp.where(first_lane, 0.0, real_sin)).astype(BF16)
        halves[up, minus] = jnp.where(first_lane, real_sin, real_cos - imag_sin).astype(BF16)
        halves[down, minus] = jnp.where(first_lane, imag_sin, imag_cos + real_sin).astype(BF16)

    def forward_left(m, part):
        mode = slice(m * size, (m + 1) * size)
        table = folded[1, part * half : (part + 1) * half, :]
        real = jnp.dot(table, halves[0:size, mode], preferred_element_type=F32)
        imag = jnp.dot(table, halves[size:, mode], preferred_element_type=F32)
        real_cos, real_sin = real[0:quarter], real[quarter:]
        imag_cos, imag_sin = imag[0:quarter], imag[quarter:]
        real_more, imag_more, real_less, imag_less = (
            imag_sin, real_sin, real_cos - imag_sin, imag_cos + real_sin
        )
        if part == 0:
            real_more = jnp.where(first_row, 0.0, imag_sin)
            imag_more = jnp.where(first_row, 0.0, real_sin)
            real_less = jnp.where(first_row, real_sin, real_less)
            imag_less = jnp.where(first_row, imag_sin, imag_less)
        first = part * quarter
        spectra[first : first + quarter, mode] = real_cos + real_more
        spectra[size + first : size + first + quarter, mode] = imag_cos - imag_more
        spectra[half + first : half + first + quarter, mode] = real_less
        spectra[size + half + first : size + half + first + quarter, mode] = imag_less

    def fold_amplitudes(index):
        rows_folded = reordered(swapped[...], patterns[order[index]])
        amplitudes[...] = jnp.dot(rows_folded, swapped[...], preferred_element_type=F32)

    def reweigh(begin):
        k, inside = divmod(begin, half)
        here = slice(begin, begin + block)
        below = slice(size + begin, size + begin + block)
        mode_columns = [slice(m * size, (m + 1) * size) for m in range(modes)]
        parts = [(spectra[here, mode], spectra[below, mode]) for mode in mode_columns]
        power = sum(real * real + imag * imag for real, imag in parts)
        factor = amplitudes[here, :] * lax.rsqrt(jnp.maximum(power, 0.5)) - 1.0
        for m, (real, imag) in enumerate(parts):
            first = k * size + m * half + inside
            there = slice(first, first + block)
            shifts[there, 0:size] = (factor * real).astype(BF16)
            shifts[there, size:] = (factor * imag).astype(BF16)

    def backward_right(k, m, part):
        columns = slice(part * size, (part + 1) * size)
        first = k * size + m * half
        target = part * size + k * half
        backs[target : target + half, m * size : (m + 1) * size] = jnp.dot(
            shifts[first : first + half, :], negative[:, columns], preferred_element_type=F32
        ).astype(BF16)

    def backward_left(m, part):
        mode = slice(m * size, (m + 1) * size)
        rows_here = slice(part * half, (part + 1) * half)
        changes[rows_here, mode] = jnp.dot(
            positive[rows_here, :], backs[:, mode], preferred_element_type=F32
        )

    def deposit(index, buffer, begin):
        _, row, chunk, offset = place_of(index)
        past = lane >= offset
        here = slice(begin, begin + block)
        below = slice(size + begin, size + begin + block)
        start = begin // 8
        obj_real = patch[buffer, 0, here, :]
        obj_imag = patch[buffer, 1, here, :]

        def add(plane, value):
            sums[start : start + groups, plane] += value.reshape(groups, 8, size)

        add(2 * modes, obj_real * obj_real + obj_imag * obj_imag)
        term_real = term_imag = None
        for m in range(modes):
            mode = slice(m * size, (m + 1) * size)
            real = changes[here, mode]
            imag = changes[below, mode]
            probe_real = low[2 * m, here, :]
            probe_imag = low[2 * m + 1, here, :]
            more_real = probe_real * real + probe_imag * imag
            more_imag = probe_real * imag - probe_imag * real
            term_real = more_real if m == 0 else term_real + more_real
            term_imag = more_imag if m == 0 else term_imag + more_imag
            add(2 * m, obj_real * real + obj_imag * imag)
            add(2 * m + 1, obj_real * imag - obj_imag * real)
        for comp, term in enumerate((term_real, term_imag)):
            term = term.astype(BF16).astype(F32) * scale
            first = pltpu.roll(term[:, 0:LANES], offset, 1)
            second = pltpu.roll(term[:, LANES:], offset, 1)
            place = comp * chunks + chunk
            window = pl.ds(row + begin, block)
            values = [canvas[place + k, window, :] for k in range(3)]
            canvas[place, window, :] = values[0] + jnp.where(past, first, 0.0)
            canvas[place + 1, window, :] = values[1] + jnp.where(past, second, first)
            canvas[place + 2, window, :] = values[2] + jnp.where(past, 0.0, second)

    def step(index, carry):
        pattern_copy(order[index]).wait()
        previous = jnp.maximum(index - 1, 0)
        following = jnp.minimum(index + 1, found - 1)
        buffer = (index + 1) & 1
        starts = list(blocks)
        middle = len(starts) // 2

        def between(pieces_of, blocks_of):
            given = 0
            for done, piece in enumerate(pieces_of):
                piece()
                until = (done + 1) * len(blocks_of) // len(pieces_of)
                for each in blocks_of[given:until]:
                    each()
                given = until

        bind = functools.partial
        pairs = [(first, second) for first in range(2) for second in range(2)]
        between(
            [bind(fold_amplitudes, index)]
            + [bind(forward_right, *pair) for pair in pairs]
            + [bind(forward_left, *pair) for pair in pairs],
            [bind(deposit, previous, buffer, begin) for begin in starts],
        )
        for begin in starts[:middle]:
            reweigh(begin)
        between(
            [bind(backward_right, 0, *pair) for pair in pairs],
            [bind(reweigh, begin) for begin in starts[middle:]],
        )
        between(
            [bind(backward_right, 1, *pair) for pair in pairs]
            + [bind(backward_left, m, part) for m in range(modes) for part in range(4)],
            [bind(cut, following, begin) for begin in starts],
        )
        return carry

    for copy in obj_copies:
        copy.wait()

    @pl.when(found > 0)
    def _():
        for begin in blocks:
            cut(0, begin)

    if not with_border:
        for comp, j in pieces:
            index = comp * chunks + 1 + j
            canvas[index, rows, :] = obj[index, rows, :]
    for copy in later:
        copy.wait()

    @pl.when(found > 0)
    def _():
        lax.fori_loop(0, found, step, 0)
        for begin in blocks:
            deposit(found - 1, (found - 1) & 1, begin)

    last_copies = list(out_copies)
    if not with_border:
        last_copies += [
            pltpu.make_async_copy(here, there, sem) for there, here, sem in ring_pieces(ring_out)
        ]
        last_copies += [
            pltpu.make_async_copy(here, there, sem) for there, here, sem in sums_pieces(sums_out)
        ]
    for copy in last_copies:
        copy.start()
    if with_border:
        for pair in range(2):
            g_rows[pair][0 : 2 * chunks] = canvas[:, pl.ds(row_sides[pair], half), :].astype(BF16)
            for comp in range(2):
                beside = comp * chunks + col_sides[pair]
                g_cols[pair][comp] = canvas[beside, rows, :].astype(BF16)
        core = lax.axis_index("core")
        count_of = kept.shape[0]
        kept[...] = sums[pl.ds(core * count_of, count_of)]
        for plane in range(2 * modes + 1):
            for side in range(2):
                columns = slice(side * half, (side + 1) * half)
                given = sums[pl.ds((1 - core) * count_of, count_of), plane, :, columns]
                g_rows[0][2 * chunks + 2 * plane + side] = given.reshape(half, LANES).astype(BF16)
    for copy in last_copies:
        copy.wait()


def run_positions(counts, centers, object_field, patterns, probe_modes, row_halos, border=None):
    size = probe_modes.shape[-1]
    half = size // 2
    modes = probe_modes.shape[0]
    tile = object_field.shape[1]
    inner = tile // LANES
    chunks = inner + 2
    slots = patterns.shape[0]
    smem = pl.BlockSpec(memory_space=pltpu.SMEM)
    vmem = pl.BlockSpec(memory_space=pltpu.VMEM)
    anywhere = pl.BlockSpec(memory_space=pl.ANY)
    shape = jax.ShapeDtypeStruct
    in_specs = [smem, smem, anywhere, anywhere] + [vmem] * 4
    operands = [counts, centers, object_field, patterns, probe_modes, dft_tables(size), *row_halos]
    sums_shape = (size // 8, 2 * modes + 1, 8, size)
    ring_shape = (2 * inner, size, LANES)
    aliases = {}
    if border is None:
        out_specs = [anywhere] * 3
        out_shape = [shape(each, F32) for each in (object_field.shape, ring_shape, sums_shape)]
    else:
        aliases = {len(operands) + 2: 0}
        in_specs += [vmem] * 2 + [anywhere] * 3
        operands += list(border)
        half_sums = (size // 16,) + sums_shape[1:]
        out_specs = [anywhere] + [vmem] * 5
        out_shape = [
            shape((2, tile, tile), F32),
            shape((2 * chunks + 4 * modes + 2, half, LANES), BF16),
            shape((2 * chunks, half, LANES), BF16),
            shape((2, tile, LANES), BF16),
            shape((2, tile, LANES), BF16),
            shape(half_sums, F32),
        ]
    table = pltpu.VMEM((2 * size, 2 * size), BF16)
    products = pltpu.VMEM((2 * size, modes * size), BF16)
    wide = pltpu.VMEM((2 * size, modes * size), F32)
    padded = pltpu.VMEM((2 * chunks, tile + size, LANES), F32)
    dma = pltpu.SemaphoreType.DMA
    return pl.pallas_call(
        functools.partial(positions_kernel, border is not None),
        in_specs=in_specs,
        out_specs=out_specs,
        out_shape=out_shape,
        input_output_aliases=aliases,
        scratch_shapes=[
            padded,
            padded,
            pltpu.VMEM(patterns.shape, BF16),
            table,
            table,
            pltpu.VMEM((2, size, size), BF16),
            pltpu.VMEM((size, size), BF16),
            pltpu.VMEM((size, size), F32),
            pltpu.VMEM((2 * modes, size, size), F32),
            products,
            products,
            products,
            products,
            wide,
            wide,
            pltpu.VMEM((2, 2, size, size), F32),
            pltpu.VMEM(sums_shape, F32),
            pltpu.SMEM((slots + 1,), jnp.int32),
            dma((2, 2, inner)),
            dma((2, inner)),
            dma((2, 2)),
            dma((slots,)),
            dma((4,)),
        ],
        compiler_params=pltpu.CompilerParams(
            vmem_limit_bytes=(50 if border is None else 46) * 1024 * 1024
        ),
        cost_estimate=pl.CostEstimate(
            flops=slots * 16 * modes * size**3,
            bytes_accessed=24 * 1024 * 1024,
            transcendentals=0,
        ),
        name="border" if border is not None else "interior",
    )(*operands)


def corners_kernel(col_even, col_odd, row_even, row_odd, out_even, out_odd):
    tile = col_even.shape[1]
    half = row_even.shape[1]
    chunks = row_odd.shape[0] // 2
    row_sides = sides(ROW, tile, half)
    col_sides = [offset // LANES for offset in sides(COL, chunks * LANES, half)]
    for pair, (strip, out) in enumerate(((col_even, out_even), (col_odd, out_odd))):
        out[:, half : tile - half, :] = strip[:, half : tile - half, :]
        for other, ring in enumerate((row_even, row_odd)):
            there = pl.ds(row_sides[other], half)
            for comp in range(2):
                extra = ring[comp * chunks + col_sides[pair]].astype(F32)
                out[comp, there, :] = (strip[comp, there, :].astype(F32) + extra).astype(BF16)


def add_corners(g_cols, from_rows):
    vmem = pl.BlockSpec(memory_space=pltpu.VMEM)
    shape = jax.ShapeDtypeStruct(g_cols[0].shape, BF16)
    return pl.pallas_call(
        corners_kernel,
        in_specs=[vmem] * 4,
        out_specs=[vmem] * 2,
        out_shape=[shape, shape],
        compiler_params=pltpu.CompilerParams(vmem_limit_bytes=8 * 1024 * 1024),
        cost_estimate=pl.CostEstimate(
            flops=256 * 1024, bytes_accessed=2 * 1024 * 1024, transcendentals=0
        ),
        name="corners",
    )(*g_cols, *from_rows)


def rims_kernel(
    partial, row_even, row_odd, col_even, col_odd, out, row_buffer, col_buffer, sems
):
    tile = partial.shape[1]
    half = row_even.shape[1]
    inner = tile // LANES
    chunks = inner + 2
    middle = tile - 2 * half
    row_sides = sides(ROW, tile, half)
    col_sides = sides(COL, tile, half)
    row_rings = (row_even, row_odd)
    col_strips = (col_even, col_odd)

    def copy(kind, pair, comp, inward):
        if kind == 0:
            here = row_buffer.at[pair, comp]
            place = (comp, pl.ds(row_sides[pair], half), slice(None))
        else:
            here = col_buffer.at[pair, comp]
            place = (comp, pl.ds(half, middle), pl.ds(col_sides[pair], half))
        source, target = (partial.at[place], here) if inward else (here, out.at[place])
        return pltpu.make_async_copy(
            source, target, sems.at[1 - int(inward), 2 * kind + pair, comp]
        )

    everything = [(kind, pair, comp) for kind in range(2) for pair in range(2) for comp in range(2)]
    for piece in everything:
        copy(*piece, True).start()
    for kind, pair, comp in everything:
        copy(kind, pair, comp, True).wait()
        if kind == 0:
            for j in range(inner):
                columns = slice(j * LANES, (j + 1) * LANES)
                ring = row_rings[pair][comp * chunks + 1 + j]
                row_buffer[pair, comp, :, columns] += ring.astype(F32)
            for other in range(2):
                columns = pl.ds(col_sides[other], half)
                strip = col_strips[other][comp, pl.ds(row_sides[pair], half), :]
                row_buffer[pair, comp, :, columns] += strip.astype(F32)
        else:
            strip = col_strips[pair][comp, half : half + middle, :]
            col_buffer[pair, comp] += strip.astype(F32)
        copy(kind, pair, comp, False).start()
    for piece in everything:
        copy(*piece, False).wait()


def add_rims(partial, from_rows, from_cols):
    tile = partial.shape[1]
    half = from_rows[0].shape[1]
    vmem = pl.BlockSpec(memory_space=pltpu.VMEM)
    anywhere = pl.BlockSpec(memory_space=pl.ANY)
    return pl.pallas_call(
        rims_kernel,
        in_specs=[anywhere] + [vmem] * 4,
        out_specs=anywhere,
        out_shape=jax.ShapeDtypeStruct(partial.shape, F32),
        input_output_aliases={0: 0},
        scratch_shapes=[
            pltpu.VMEM((2, 2, half, tile), F32),
            pltpu.VMEM((2, 2, tile - 2 * half, half), F32),
            pltpu.SemaphoreType.DMA((2, 4, 2)),
        ],
        compiler_params=pltpu.CompilerParams(vmem_limit_bytes=16 * 1024 * 1024),
        cost_estimate=pl.CostEstimate(
            flops=1024 * 1024, bytes_accessed=6 * 1024 * 1024, transcendentals=0
        ),
        name="rims",
    )(partial, *from_rows, *from_cols)


def chip_sums_kernel(kept, received, out):
    groups, planes, height, size = kept.shape
    half = received.shape[1]
    first = received.shape[0] - 2 * planes
    for plane in range(planes):
        for side in range(2):
            columns = slice(side * half, (side + 1) * half)
            other = received[first + 2 * plane + side].astype(F32).reshape(groups, height, half)
            out[:, plane, :, columns] = (kept[:, plane, :, columns] + other).astype(BF16)


def chip_sums(kept, received):
    vmem = pl.BlockSpec(memory_space=pltpu.VMEM)
    return pl.pallas_call(
        chip_sums_kernel,
        in_specs=[vmem, vmem],
        out_specs=vmem,
        out_shape=jax.ShapeDtypeStruct(kept.shape, BF16),
        compiler_params=pltpu.CompilerParams(vmem_limit_bytes=8 * 1024 * 1024),
        cost_estimate=pl.CostEstimate(
            flops=32 * 1024**3, bytes_accessed=32 * 1024 * 1024, transcendentals=0
        ),
        name="chip_sums",
    )(kept, received)


def by_device(on_chip):
    devices = lax.axis_size("x") * lax.axis_size("col")
    groups, planes, _, size = on_chip.shape
    share = groups * 8 // devices
    if share < 8:
        on_chip = on_chip.reshape(groups, planes, 8 // share, share, size)
        return jnp.swapaxes(on_chip, 1, 2).reshape(devices, planes, share, size)
    return on_chip.reshape(devices, groups // devices, planes, 8, size)


def exchange(parts):
    return lax.all_to_all(parts, ("x", "col"), 0, 0, tiled=True)


def update_kernel(received, copies):
    devices = received.shape[0]
    total = received[0].astype(F32)
    for device in range(1, devices):
        total = total + received[device].astype(F32)
    planes = total.shape[0]
    update = (total[: planes - 1] / jnp.sqrt(total[planes - 1])).astype(BF16)
    for device in range(devices):
        copies[device] = update


def shared_update(received):
    devices, planes, share, size = received.shape
    vmem = pl.BlockSpec(memory_space=pltpu.VMEM)
    return pl.pallas_call(
        update_kernel,
        in_specs=[vmem],
        out_specs=vmem,
        out_shape=jax.ShapeDtypeStruct((devices, planes - 1, share, size), BF16),
        compiler_params=pltpu.CompilerParams(vmem_limit_bytes=8 * 1024 * 1024),
        cost_estimate=pl.CostEstimate(
            flops=512 * 1024, bytes_accessed=1024 * 1024, transcendentals=0
        ),
        name="update",
    )(received)


def finish_kernel(probe, mine, other, out):
    core = lax.axis_index("core")
    groups, planes, height, _ = mine.shape
    for side, update in enumerate((mine, other)):
        first = jnp.where(core == side, 0, groups * height)
        for group in range(groups):
            place = pl.ds(pl.multiple_of(first + group * height, height), height)
            for plane in range(planes):
                m, comp = divmod(plane, 2)
                out[m, comp, place, :] = probe[m, comp, place, :] + update[group, plane].astype(F32)


def finish_probe(probe_modes, mine):
    devices, planes, share, size = mine.shape
    if share < 8:
        mine = mine.reshape(devices * share // 8, 8 // share, planes, share, size)
        mine = jnp.swapaxes(mine, 1, 2).reshape(-1, planes, 8, size)
    other = lax.ppermute(mine, "core", [(0, 1), (1, 0)])
    vmem = pl.BlockSpec(memory_space=pltpu.VMEM)
    return pl.pallas_call(
        finish_kernel,
        in_specs=[vmem] * 3,
        out_specs=vmem,
        out_shape=jax.ShapeDtypeStruct(probe_modes.shape, F32),
        compiler_params=pltpu.CompilerParams(vmem_limit_bytes=8 * 1024 * 1024),
        cost_estimate=pl.CostEstimate(
            flops=256 * 1024, bytes_accessed=3 * 1024 * 1024, transcendentals=0
        ),
        name="finish",
    )(probe_modes, mine, other)


def on_device(object_field, probe_modes, counts, centers, patterns):
    half = probe_modes.shape[-1] // 2

    col_even, col_odd, row_even, row_odd = cut_strips(object_field, half)
    go_on = lax.axis_index("col") < 4096
    row_halos = (swap_pairs(row_even, ROW, 0), swap_pairs(row_odd, ROW, 1))
    col_halos = (swap_pairs(col_even, COL, 0), swap_pairs(col_odd, COL, 1))
    is_even = (lax.axis_index("col") & 1) == 0
    first_ends = jnp.concatenate([halo[:, :, :half] for halo in row_halos], 1)
    last_ends = jnp.concatenate([halo[:, :, -half:] for halo in row_halos], 1)
    end_halos = (
        swap_pairs(jnp.where(is_even, last_ends, first_ends), COL, 0),
        swap_pairs(jnp.where(is_even, first_ends, last_ends), COL, 1),
    )

    inputs = (counts, centers[0, 0], object_field, patterns[0, 0], probe_modes, row_halos)
    started = run_positions(*inputs)
    joined = [jnp.concatenate(both, 1) for both in zip(col_halos, end_halos)]
    border = (*joined, *started)
    partial, g_row_even, g_row_odd, g_col_even, g_col_odd, kept = run_positions(*inputs, border)

    from_rows = (swap_pairs(g_row_even, ROW, 0), swap_pairs(g_row_odd, ROW, 1))
    received = lax.cond(
        go_on, exchange, jnp.zeros_like, by_device(chip_sums(kept, from_rows[0]))
    )
    row_odd, _ = lax.optimization_barrier((from_rows[1], received))
    from_rows = (from_rows[0], row_odd)
    to_even, to_odd = add_corners((g_col_even, g_col_odd), from_rows)
    received, to_even, to_odd = lax.optimization_barrier((received, to_even, to_odd))
    from_cols = (swap_pairs(to_even, COL, 0), swap_pairs(to_odd, COL, 1))
    if received.ndim == 5:
        received = received[:, 0]
    mine = lax.cond(go_on, exchange, jnp.zeros_like, shared_update(received))
    mine, from_cols, partial = lax.optimization_barrier((mine, from_cols, partial))
    new_object = add_rims(partial, from_rows, from_cols)
    return (new_object, finish_probe(probe_modes, mine))


def solution(mesh):
    rows, columns = mesh.devices.shape
    split = jax.sharding.Mesh(
        mesh.devices.reshape(rows // 2, 2, columns), ("x", "core", "col")
    )
    placed = (
        P(None, ROW, "col"),
        P(),
        P(),
        P(ROW, "col", None, None),
        P(ROW, "col", None, None, None),
    )
    return jax.shard_map(
        on_device,
        mesh=split,
        in_specs=placed,
        out_specs=(P(None, ROW, "col"), P()),
        check_vma=False,
    )
```

```python
import functools
import math

import jax
import jax.numpy as jnp
import ml_dtypes
import numpy as np
from jax import lax
from jax.experimental import pallas as pl
from jax.experimental.pallas import tpu as pltpu
from jax.sharding import PartitionSpec as P

LANES = 128
ROW = ("x", "core")
COL = ("col",)
F32 = jnp.float32
BF16 = jnp.bfloat16


def dft_tables(length):
    indices = np.arange(length)
    angles = (indices[:, None] * indices[None, :] % length) * (2.0 * np.pi / length)
    scale = 1.0 / np.sqrt(length)
    cosine = (np.cos(angles) * scale).astype(np.float32).astype(ml_dtypes.bfloat16)
    sine = (np.sin(angles) * scale).astype(np.float32).astype(ml_dtypes.bfloat16)
    return np.stack([cosine, sine, -sine])


def swap_pairs(array, axis, odd):
    devices = math.prod(lax.axis_size(name) for name in axis)
    firsts = range(odd, devices - 1, 2)
    return lax.ppermute(
        array, axis, [(i, i + 1) for i in firsts] + [(i + 1, i) for i in firsts]
    )


def sides(axis, length, width):
    even = (lax.axis_index(axis) & 1) == 0
    far = length - width
    return [
        pl.multiple_of(jnp.where(even, far, 0), width),
        pl.multiple_of(jnp.where(even, 0, far), width),
    ]


def strips_kernel(obj_hbm, col_even, col_odd, row_even, row_odd, col_buffer, row_buffer, sems):
    tile = obj_hbm.shape[1]
    half = row_even.shape[1]
    copies = []
    for pair in range(2):
        column = sides(COL, tile, half)[pair]
        row = sides(ROW, tile, half)[pair]
        copies.append(
            pltpu.make_async_copy(
                obj_hbm.at[:, :, pl.ds(column, half)], col_buffer.at[pair], sems.at[0, pair]
            )
        )
        copies.append(
            pltpu.make_async_copy(
                obj_hbm.at[:, pl.ds(row, half), :], row_buffer.at[pair], sems.at[1, pair]
            )
        )
    for copy in copies:
        copy.start()
    outputs = (col_even, row_even, col_odd, row_odd)
    buffers = (col_buffer, row_buffer) * 2
    for index, copy in enumerate(copies):
        copy.wait()
        outputs[index][...] = buffers[index][index // 2].astype(BF16)


def cut_strips(object_field, half):
    tile = object_field.shape[1]
    vmem = pl.BlockSpec(memory_space=pltpu.VMEM)
    columns = jax.ShapeDtypeStruct((2, tile, half), BF16)
    rows = jax.ShapeDtypeStruct((2, half, tile), BF16)
    return pl.pallas_call(
        strips_kernel,
        in_specs=[pl.BlockSpec(memory_space=pltpu.HBM)],
        out_specs=[vmem] * 4,
        out_shape=[columns, columns, rows, rows],
        scratch_shapes=[
            pltpu.VMEM((2, 2, tile, half), F32),
            pltpu.VMEM((2, 2, half, tile), F32),
            pltpu.SemaphoreType.DMA((2, 2)),
        ],
        compiler_params=pltpu.CompilerParams(vmem_limit_bytes=50 * 1024 * 1024),
        cost_estimate=pl.CostEstimate(
            flops=1024 * 1024, bytes_accessed=5 * 1024 * 1024, transcendentals=0
        ),
        name="strips",
    )(object_field)


def positions_kernel(with_border, *refs):
    counts, centers, obj_hbm, pat_hbm, probe = refs[:5]
    tables, row_halos = refs[5], refs[6:8]
    refs = refs[8:]
    if with_border:
        col_halos = refs[0:2]
        start_hbm, ring_in, sums_in = refs[2:5]
        out_hbm, g_rows, g_cols, kept = refs[5], refs[6:8], refs[8:10], refs[10]
        refs = refs[11:]
    else:
        out_hbm, ring_out, sums_out = refs[:3]
        refs = refs[3:]
    (obj, canvas, patterns, positive, negative, folded, swapped, amplitudes, low, waves, shifts, halves, backs,
     spectra, changes, patch, sums, order, piece_sems, out_sems, ring_sems, pat_sems,
     sums_sems) = refs
    size = probe.shape[-1]
    half = size // 2
    tile = obj_hbm.shape[1]
    inner = tile // LANES
    chunks = inner + 2
    modes = probe.shape[0]
    rows = slice(half, half + tile)
    near = [0, 1, inner - 2, inner - 1] if with_border else list(range(inner))
    pieces = [(comp, j) for comp in range(2) for j in near]

    def home(array, comp, j):
        return array.at[comp, :, pl.ds(j * LANES, LANES)]

    def held(array, comp, j):
        return array.at[comp * chunks + 1 + j, pl.ds(half, tile), :]

    def ring_pieces(array):
        for comp in range(2):
            for side, row in enumerate((0, half + tile)):
                yield (
                    array.at[pl.ds(comp * inner, inner), pl.ds(side * half, half), :],
                    canvas.at[pl.ds(comp * chunks + 1, inner), pl.ds(row, half), :],
                    ring_sems.at[side, comp],
                )

    def sums_pieces(array):
        step = array.shape[0] // sums_parts
        for part in range(sums_parts):
            here = pl.ds(part * step, step)
            yield array.at[here], sums.at[here], sums_sems.at[part]

    sums_parts = sums_sems.shape[0]
    obj_copies = [
        pltpu.make_async_copy(home(obj_hbm, *p), held(obj, *p), piece_sems.at[0, *p])
        for p in pieces
    ]
    out_copies = [
        pltpu.make_async_copy(held(canvas, *p), home(out_hbm, *p), out_sems.at[p]) for p in pieces
    ]
    later = []
    if with_border:
        later += [
            pltpu.make_async_copy(home(start_hbm, *p), held(canvas, *p), piece_sems.at[1, *p])
            for p in pieces
        ]
        later += [pltpu.make_async_copy(*each) for each in ring_pieces(ring_in)]
        later += [pltpu.make_async_copy(*each) for each in sums_pieces(sums_in)]
    for copy in obj_copies + later:
        copy.start()

    order[0] = 0
    count = counts[lax.axis_index(ROW), lax.axis_index("col")]

    def pattern_copy(slot):
        return pltpu.make_async_copy(pat_hbm.at[slot], patterns.at[slot], pat_sems.at[slot])

    def note(slot, found):
        column = centers[1, slot]
        inside = (column >= half) & (column <= tile - half)
        order[found] = slot
        return found + jnp.where(inside, 0 if with_border else 1, 1 if with_border else 0)

    def fetch(index, carry):
        pattern_copy(order[index]).start()
        return carry

    found = lax.fori_loop(0, count, note, 0)
    lax.fori_loop(0, found, fetch, 0)

    if not with_border:
        sums[...] = jnp.zeros_like(sums)
    intensity = jnp.zeros((size, size), F32)
    for m in range(modes):
        for comp in range(2):
            values = probe[m, comp]
            intensity = intensity + values * values
            low[2 * m + comp] = values.astype(BF16).astype(F32)
    scale = 1.0 / (jnp.max(intensity) + 1e-06)
    cosine, sine = tables[0], tables[1]
    index_row = lax.broadcasted_iota(jnp.int32, (size, size), 0)
    index_column = lax.broadcasted_iota(jnp.int32, (size, size), 1)
    target = jnp.where(index_row > half, size + half - index_row, index_row)
    swapped[...] = jnp.where(index_column == target, 1.0, 0.0).astype(BF16)
    first_lane = lax.broadcasted_iota(jnp.int32, (size, half), 1) == 0
    first_row = lax.broadcasted_iota(jnp.int32, (half, size), 0) == 0
    wide_cosine = cosine.astype(F32)
    wide_sine = sine.astype(F32)
    folded[0, :, 0:half] = cosine[:, 0:half]
    folded[0, :, half:] = jnp.where(
        first_lane, wide_cosine[:, half:], wide_sine[:, 0:half]
    ).astype(BF16)
    folded[1, 0:half, :] = cosine[0:half, :]
    folded[1, half:, :] = jnp.where(
        first_row, wide_cosine[half:, :], wide_sine[0:half, :]
    ).astype(BF16)

    def reordered(left_side, right_side):
        return jnp.dot(left_side, right_side, preferred_element_type=F32).astype(BF16)

    turns = [reordered(swapped[...], tables[i]) for i in range(3)]
    negative[0:size, 0:size] = turns[0]
    negative[0:size, size:] = turns[1]
    negative[size:, 0:size] = turns[2]
    negative[size:, size:] = turns[0]
    turns = [reordered(tables[i], swapped[...]) for i in range(3)]
    positive[0:size, 0:size] = turns[0]
    positive[0:size, size:] = turns[2]
    positive[size:, 0:size] = turns[1]
    positive[size:, size:] = turns[0]
    changes[...] = jnp.zeros_like(changes)
    patch[...] = jnp.zeros_like(patch)

    row_sides = sides(ROW, tile + size, half)
    col_sides = [offset // LANES for offset in sides(COL, tile + size, half)]
    blank = jnp.zeros((tile + size, LANES), F32)
    for comp in range(2):
        first = comp * chunks
        for pair in range(2):
            for j in near:
                columns = slice(j * LANES, (j + 1) * LANES)
                obj[first + 1 + j, pl.ds(row_sides[pair], half), :] = row_halos[pair][
                    comp, :, columns
                ].astype(F32)
            if with_border:
                beside = first + col_sides[pair]
                canvas[beside] = blank
                obj[beside, rows, :] = col_halos[pair][comp, 0:tile, :].astype(F32)
                for other in range(2):
                    obj[beside, pl.ds(row_sides[other], half), :] = col_halos[pair][
                        comp, tile + other * half : tile + (other + 1) * half, :
                    ].astype(F32)
        if not with_border:
            for j in range(inner):
                canvas[first + 1 + j, 0:half, :] = blank[0:half]
                canvas[first + 1 + j, half + tile :, :] = blank[0:half]

    block = 16
    groups = block // 8
    lane = lax.broadcasted_iota(jnp.int32, (block, LANES), 1)
    blocks = range(0, size, block)

    def place_of(index):
        slot = order[index]
        column = centers[1, slot]
        return slot, centers[0, slot], column >> 7, column & 127

    def cut(index, begin):
        _, row, chunk, offset = place_of(index)
        back_offset = (LANES - offset) & 127
        from_first = lane < LANES - offset
        here = slice(begin, begin + block)
        parts = []
        for comp in range(2):
            moved = [
                pltpu.roll(
                    obj[comp * chunks + chunk + k, pl.ds(row + begin, block), :], back_offset, 1
                )
                for k in range(3)
            ]
            window = jnp.concatenate(
                [
                    jnp.where(from_first, moved[0], moved[1]),
                    jnp.where(from_first, moved[1], moved[2]),
                ],
                1,
            ).astype(BF16).astype(F32)
            patch[index & 1, comp, here, :] = window
            parts.append(window)
        real, imag = parts
        for m in range(modes):
            probe_real = low[2 * m, here, :]
            probe_imag = low[2 * m + 1, here, :]
            there = slice(m * size + begin, m * size + begin + block)
            waves[there, 0:size] = (probe_real * real - probe_imag * imag).astype(BF16)
            waves[there, size:] = (probe_real * imag + probe_imag * real).astype(BF16)

    def forward_right(m):
        mode = slice(m * size, (m + 1) * size)
        real = jnp.dot(waves[mode, 0:size], folded[0], preferred_element_type=F32)
        imag = jnp.dot(waves[mode, size:], folded[0], preferred_element_type=F32)
        real_cos, real_sin = real[:, 0:half], real[:, half:]
        imag_cos, imag_sin = imag[:, 0:half], imag[:, half:]
        plus = slice(m * size, m * size + half)
        minus = slice(m * size + half, (m + 1) * size)
        halves[0:size, plus] = (real_cos + jnp.where(first_lane, 0.0, imag_sin)).astype(BF16)
        halves[size:, plus] = (imag_cos - jnp.where(first_lane, 0.0, real_sin)).astype(BF16)
        halves[0:size, minus] = jnp.where(first_lane, real_sin, real_cos - imag_sin).astype(BF16)
        halves[size:, minus] = jnp.where(first_lane, imag_sin, imag_cos + real_sin).astype(BF16)

    def forward_left(m):
        mode = slice(m * size, (m + 1) * size)
        real = jnp.dot(folded[1], halves[0:size, mode], preferred_element_type=F32)
        imag = jnp.dot(folded[1], halves[size:, mode], preferred_element_type=F32)
        real_cos, real_sin = real[0:half], real[half:]
        imag_cos, imag_sin = imag[0:half], imag[half:]
        spectra[0:half, mode] = real_cos + jnp.where(first_row, 0.0, imag_sin)
        spectra[size : size + half, mode] = imag_cos - jnp.where(first_row, 0.0, real_sin)
        spectra[half:size, mode] = jnp.where(first_row, real_sin, real_cos - imag_sin)
        spectra[size + half :, mode] = jnp.where(first_row, imag_sin, imag_cos + real_sin)

    def fold_amplitudes(index):
        rows_folded = reordered(swapped[...], patterns[order[index]])
        amplitudes[...] = jnp.dot(rows_folded, swapped[...], preferred_element_type=F32)

    def reweigh(begin):
        k, inside = divmod(begin, half)
        here = slice(begin, begin + block)
        below = slice(size + begin, size + begin + block)
        mode_columns = [slice(m * size, (m + 1) * size) for m in range(modes)]
        parts = [(spectra[here, mode], spectra[below, mode]) for mode in mode_columns]
        power = sum(real * real + imag * imag for real, imag in parts)
        factor = amplitudes[here, :] * lax.rsqrt(jnp.maximum(power, 0.5)) - 1.0
        for m, (real, imag) in enumerate(parts):
            first = k * size + m * half + inside
            there = slice(first, first + block)
            shifts[there, 0:size] = (factor * real).astype(BF16)
            shifts[there, size:] = (factor * imag).astype(BF16)

    def backward_right(k, part):
        columns = slice(part * size, (part + 1) * size)
        product = jnp.dot(
            shifts[k * size : (k + 1) * size, :], negative[:, columns],
            preferred_element_type=F32,
        ).astype(BF16)
        first = part * size + k * half
        for m in range(modes):
            mode = slice(m * size, (m + 1) * size)
            backs[first : first + half, mode] = product[m * half : (m + 1) * half, :]

    def backward_left(m, part):
        mode = slice(m * size, (m + 1) * size)
        rows_here = slice(part * size, (part + 1) * size)
        changes[rows_here, mode] = jnp.dot(
            positive[rows_here, :], backs[:, mode], preferred_element_type=F32
        )

    def deposit(index, buffer, begin):
        _, row, chunk, offset = place_of(index)
        past = lane >= offset
        here = slice(begin, begin + block)
        below = slice(size + begin, size + begin + block)
        start = begin // 8
        obj_real = patch[buffer, 0, here, :]
        obj_imag = patch[buffer, 1, here, :]

        def add(plane, value):
            sums[start : start + groups, plane] += value.reshape(groups, 8, size)

        add(2 * modes, obj_real * obj_real + obj_imag * obj_imag)
        term_real = term_imag = None
        for m in range(modes):
            mode = slice(m * size, (m + 1) * size)
            real = changes[here, mode]
            imag = changes[below, mode]
            probe_real = low[2 * m, here, :]
            probe_imag = low[2 * m + 1, here, :]
            more_real = probe_real * real + probe_imag * imag
            more_imag = probe_real * imag - probe_imag * real
            term_real = more_real if m == 0 else term_real + more_real
            term_imag = more_imag if m == 0 else term_imag + more_imag
            add(2 * m, obj_real * real + obj_imag * imag)
            add(2 * m + 1, obj_real * imag - obj_imag * real)
        for comp, term in enumerate((term_real, term_imag)):
            term = term.astype(BF16).astype(F32) * scale
            first = pltpu.roll(term[:, 0:LANES], offset, 1)
            second = pltpu.roll(term[:, LANES:], offset, 1)
            place = comp * chunks + chunk
            window = pl.ds(row + begin, block)
            values = [canvas[place + k, window, :] for k in range(3)]
            canvas[place, window, :] = values[0] + jnp.where(past, first, 0.0)
            canvas[place + 1, window, :] = values[1] + jnp.where(past, second, first)
            canvas[place + 2, window, :] = values[2] + jnp.where(past, 0.0, second)

    def step(index, carry):
        pattern_copy(order[index]).wait()
        previous = jnp.maximum(index - 1, 0)
        following = jnp.minimum(index + 1, found - 1)
        buffer = (index + 1) & 1
        starts = list(blocks)
        middle = len(starts) // 2

        def between(pieces_of, blocks_of):
            given = 0
            for done, piece in enumerate(pieces_of):
                piece()
                until = (done + 1) * len(blocks_of) // len(pieces_of)
                for each in blocks_of[given:until]:
                    each()
                given = until

        bind = functools.partial
        pairs = [(first, second) for first in range(2) for second in range(2)]
        between(
            [bind(forward_right, 0), bind(fold_amplitudes, index), bind(forward_right, 1)]
            + [bind(forward_left, m) for m in range(modes)],
            [bind(deposit, previous, buffer, begin) for begin in starts],
        )
        for begin in starts[:middle]:
            reweigh(begin)
        between(
            [bind(backward_right, 0, part) for part in range(2)],
            [bind(reweigh, begin) for begin in starts[middle:]],
        )
        between(
            [bind(backward_right, 1, part) for part in range(2)]
            + [bind(backward_left, *pair) for pair in pairs],
            [bind(cut, following, begin) for begin in starts],
        )
        return carry

    for copy in obj_copies:
        copy.wait()

    @pl.when(found > 0)
    def _():
        for begin in blocks:
            cut(0, begin)

    if not with_border:
        for comp, j in pieces:
            index = comp * chunks + 1 + j
            canvas[index, rows, :] = obj[index, rows, :]
    for copy in later:
        copy.wait()

    @pl.when(found > 0)
    def _():
        lax.fori_loop(0, found, step, 0)
        for begin in blocks:
            deposit(found - 1, (found - 1) & 1, begin)

    last_copies = list(out_copies)
    if not with_border:
        last_copies += [
            pltpu.make_async_copy(here, there, sem) for there, here, sem in ring_pieces(ring_out)
        ]
        last_copies += [
            pltpu.make_async_copy(here, there, sem) for there, here, sem in sums_pieces(sums_out)
        ]
    for copy in last_copies:
        copy.start()
    if with_border:
        for pair in range(2):
            g_rows[pair][0 : 2 * chunks] = canvas[:, pl.ds(row_sides[pair], half), :].astype(BF16)
            for comp in range(2):
                beside = comp * chunks + col_sides[pair]
                g_cols[pair][comp] = canvas[beside, rows, :].astype(BF16)
        core = lax.axis_index("core")
        count_of = kept.shape[0]
        kept[...] = sums[pl.ds(core * count_of, count_of)]
        for plane in range(2 * modes + 1):
            for side in range(2):
                columns = slice(side * half, (side + 1) * half)
                given = sums[pl.ds((1 - core) * count_of, count_of), plane, :, columns]
                g_rows[0][2 * chunks + 2 * plane + side] = given.reshape(half, LANES).astype(BF16)
    for copy in last_copies:
        copy.wait()


def run_positions(counts, centers, object_field, patterns, probe_modes, row_halos, border=None):
    size = probe_modes.shape[-1]
    half = size // 2
    modes = probe_modes.shape[0]
    tile = object_field.shape[1]
    inner = tile // LANES
    chunks = inner + 2
    slots = patterns.shape[0]
    smem = pl.BlockSpec(memory_space=pltpu.SMEM)
    vmem = pl.BlockSpec(memory_space=pltpu.VMEM)
    anywhere = pl.BlockSpec(memory_space=pl.ANY)
    shape = jax.ShapeDtypeStruct
    in_specs = [smem, smem, anywhere, anywhere] + [vmem] * 4
    operands = [counts, centers, object_field, patterns, probe_modes, dft_tables(size), *row_halos]
    sums_shape = (size // 8, 2 * modes + 1, 8, size)
    ring_shape = (2 * inner, size, LANES)
    aliases = {}
    if border is None:
        out_specs = [anywhere] * 3
        out_shape = [shape(each, F32) for each in (object_field.shape, ring_shape, sums_shape)]
    else:
        aliases = {len(operands) + 2: 0}
        in_specs += [vmem] * 2 + [anywhere] * 3
        operands += list(border)
        half_sums = (size // 16,) + sums_shape[1:]
        out_specs = [anywhere] + [vmem] * 5
        out_shape = [
            shape((2, tile, tile), F32),
            shape((2 * chunks + 4 * modes + 2, half, LANES), BF16),
            shape((2 * chunks, half, LANES), BF16),
            shape((2, tile, LANES), BF16),
            shape((2, tile, LANES), BF16),
            shape(half_sums, F32),
        ]
    table = pltpu.VMEM((2 * size, 2 * size), BF16)
    products = pltpu.VMEM((2 * size, modes * size), BF16)
    wide = pltpu.VMEM((2 * size, modes * size), F32)
    padded = pltpu.VMEM((2 * chunks, tile + size, LANES), F32)
    dma = pltpu.SemaphoreType.DMA
    return pl.pallas_call(
        functools.partial(positions_kernel, border is not None),
        in_specs=in_specs,
        out_specs=out_specs,
        out_shape=out_shape,
        input_output_aliases=aliases,
        scratch_shapes=[
            padded,
            padded,
            pltpu.VMEM(patterns.shape, BF16),
            table,
            table,
            pltpu.VMEM((2, size, size), BF16),
            pltpu.VMEM((size, size), BF16),
            pltpu.VMEM((size, size), F32),
            pltpu.VMEM((2 * modes, size, size), F32),
            products,
            products,
            products,
            products,
            wide,
            wide,
            pltpu.VMEM((2, 2, size, size), F32),
            pltpu.VMEM(sums_shape, F32),
            pltpu.SMEM((slots + 1,), jnp.int32),
            dma((2, 2, inner)),
            dma((2, inner)),
            dma((2, 2)),
            dma((slots,)),
            dma((4,)),
        ],
        compiler_params=pltpu.CompilerParams(
            vmem_limit_bytes=(50 if border is None else 46) * 1024 * 1024
        ),
        cost_estimate=pl.CostEstimate(
            flops=slots * 16 * modes * size**3,
            bytes_accessed=24 * 1024 * 1024,
            transcendentals=0,
        ),
        name="border" if border is not None else "interior",
    )(*operands)


def join_kernel(col_even, col_odd, end_even, end_odd, out_even, out_odd):
    tile = col_even.shape[1]
    for strip, end, out in ((col_even, end_even, out_even), (col_odd, end_odd, out_odd)):
        out[:, 0:tile, :] = strip[...]
        out[:, tile:, :] = end[...]


def join_halos(col_halos, end_halos):
    vmem = pl.BlockSpec(memory_space=pltpu.VMEM)
    planes, tile, width = col_halos[0].shape
    shape = jax.ShapeDtypeStruct((planes, tile + end_halos[0].shape[1], width), BF16)
    return pl.pallas_call(
        join_kernel,
        in_specs=[vmem] * 4,
        out_specs=[vmem] * 2,
        out_shape=[shape, shape],
        compiler_params=pltpu.CompilerParams(vmem_limit_bytes=8 * 1024 * 1024),
        cost_estimate=pl.CostEstimate(
            flops=0, bytes_accessed=2 * 1024 * 1024, transcendentals=0
        ),
        name="join",
    )(*col_halos, *end_halos)


def corners_kernel(col_even, col_odd, row_even, row_odd, out_even, out_odd):
    tile = col_even.shape[1]
    half = row_even.shape[1]
    chunks = row_odd.shape[0] // 2
    row_sides = sides(ROW, tile, half)
    col_sides = [offset // LANES for offset in sides(COL, chunks * LANES, half)]
    for pair, (strip, out) in enumerate(((col_even, out_even), (col_odd, out_odd))):
        out[:, half : tile - half, :] = strip[:, half : tile - half, :]
        for other, ring in enumerate((row_even, row_odd)):
            there = pl.ds(row_sides[other], half)
            for comp in range(2):
                extra = ring[comp * chunks + col_sides[pair]].astype(F32)
                out[comp, there, :] = (strip[comp, there, :].astype(F32) + extra).astype(BF16)


def add_corners(g_cols, from_rows):
    vmem = pl.BlockSpec(memory_space=pltpu.VMEM)
    shape = jax.ShapeDtypeStruct(g_cols[0].shape, BF16)
    return pl.pallas_call(
        corners_kernel,
        in_specs=[vmem] * 4,
        out_specs=[vmem] * 2,
        out_shape=[shape, shape],
        compiler_params=pltpu.CompilerParams(vmem_limit_bytes=8 * 1024 * 1024),
        cost_estimate=pl.CostEstimate(
            flops=256 * 1024, bytes_accessed=2 * 1024 * 1024, transcendentals=0
        ),
        name="corners",
    )(*g_cols, *from_rows)


def rims_kernel(
    partial, row_even, row_odd, col_even, col_odd, out, row_buffer, col_buffer, sems
):
    tile = partial.shape[1]
    half = row_even.shape[1]
    inner = tile // LANES
    chunks = inner + 2
    middle = tile - 2 * half
    row_sides = sides(ROW, tile, half)
    col_sides = sides(COL, tile, half)
    row_rings = (row_even, row_odd)
    col_strips = (col_even, col_odd)

    def copy(kind, pair, comp, inward):
        if kind == 0:
            here = row_buffer.at[pair, comp]
            place = (comp, pl.ds(row_sides[pair], half), slice(None))
        else:
            here = col_buffer.at[pair, comp]
            place = (comp, pl.ds(half, middle), pl.ds(col_sides[pair], half))
        source, target = (partial.at[place], here) if inward else (here, out.at[place])
        return pltpu.make_async_copy(
            source, target, sems.at[1 - int(inward), 2 * kind + pair, comp]
        )

    everything = [(kind, pair, comp) for kind in range(2) for pair in range(2) for comp in range(2)]
    for piece in everything:
        copy(*piece, True).start()
    for kind, pair, comp in everything:
        copy(kind, pair, comp, True).wait()
        if kind == 0:
            for j in range(inner):
                columns = slice(j * LANES, (j + 1) * LANES)
                ring = row_rings[pair][comp * chunks + 1 + j]
                row_buffer[pair, comp, :, columns] += ring.astype(F32)
            for other in range(2):
                columns = pl.ds(col_sides[other], half)
                strip = col_strips[other][comp, pl.ds(row_sides[pair], half), :]
                row_buffer[pair, comp, :, columns] += strip.astype(F32)
        else:
            strip = col_strips[pair][comp, half : half + middle, :]
            col_buffer[pair, comp] += strip.astype(F32)
        copy(kind, pair, comp, False).start()
    for piece in everything:
        copy(*piece, False).wait()


def add_rims(partial, from_rows, from_cols):
    tile = partial.shape[1]
    half = from_rows[0].shape[1]
    vmem = pl.BlockSpec(memory_space=pltpu.VMEM)
    anywhere = pl.BlockSpec(memory_space=pl.ANY)
    return pl.pallas_call(
        rims_kernel,
        in_specs=[anywhere] + [vmem] * 4,
        out_specs=anywhere,
        out_shape=jax.ShapeDtypeStruct(partial.shape, F32),
        input_output_aliases={0: 0},
        scratch_shapes=[
            pltpu.VMEM((2, 2, half, tile), F32),
            pltpu.VMEM((2, 2, tile - 2 * half, half), F32),
            pltpu.SemaphoreType.DMA((2, 4, 2)),
        ],
        compiler_params=pltpu.CompilerParams(vmem_limit_bytes=16 * 1024 * 1024),
        cost_estimate=pl.CostEstimate(
            flops=1024 * 1024, bytes_accessed=6 * 1024 * 1024, transcendentals=0
        ),
        name="rims",
    )(partial, *from_rows, *from_cols)


def chip_sums_kernel(kept, received, out):
    groups, planes, height, size = kept.shape
    half = received.shape[1]
    first = received.shape[0] - 2 * planes
    for plane in range(planes):
        for side in range(2):
            columns = slice(side * half, (side + 1) * half)
            other = received[first + 2 * plane + side].astype(F32).reshape(groups, height, half)
            out[:, plane, :, columns] = (kept[:, plane, :, columns] + other).astype(BF16)


def chip_sums(kept, received):
    vmem = pl.BlockSpec(memory_space=pltpu.VMEM)
    return pl.pallas_call(
        chip_sums_kernel,
        in_specs=[vmem, vmem],
        out_specs=vmem,
        out_shape=jax.ShapeDtypeStruct(kept.shape, BF16),
        compiler_params=pltpu.CompilerParams(vmem_limit_bytes=8 * 1024 * 1024),
        cost_estimate=pl.CostEstimate(
            flops=32 * 1024**3, bytes_accessed=32 * 1024 * 1024, transcendentals=0
        ),
        name="chip_sums",
    )(kept, received)


def by_device(on_chip):
    devices = lax.axis_size("x") * lax.axis_size("col")
    groups, planes, _, size = on_chip.shape
    share = groups * 8 // devices
    if share < 8:
        on_chip = on_chip.reshape(groups, planes, 8 // share, share, size)
        return jnp.swapaxes(on_chip, 1, 2).reshape(devices, planes, share, size)
    return on_chip.reshape(devices, groups // devices, planes, 8, size)


def exchange(parts):
    return lax.all_to_all(parts, ("x", "col"), 0, 0, tiled=True)


def update_kernel(received, copies):
    devices = received.shape[0]
    total = received[0].astype(F32)
    for device in range(1, devices):
        total = total + received[device].astype(F32)
    planes = total.shape[0]
    update = (total[: planes - 1] / jnp.sqrt(total[planes - 1])).astype(BF16)
    for device in range(devices):
        copies[device] = update


def shared_update(received):
    devices, planes, share, size = received.shape
    vmem = pl.BlockSpec(memory_space=pltpu.VMEM)
    return pl.pallas_call(
        update_kernel,
        in_specs=[vmem],
        out_specs=vmem,
        out_shape=jax.ShapeDtypeStruct((devices, planes - 1, share, size), BF16),
        compiler_params=pltpu.CompilerParams(vmem_limit_bytes=8 * 1024 * 1024),
        cost_estimate=pl.CostEstimate(
            flops=512 * 1024, bytes_accessed=1024 * 1024, transcendentals=0
        ),
        name="update",
    )(received)


def finish_kernel(probe, mine, other, out):
    core = lax.axis_index("core")
    groups, planes, height, _ = mine.shape
    for side, update in enumerate((mine, other)):
        first = jnp.where(core == side, 0, groups * height)
        for group in range(groups):
            place = pl.ds(pl.multiple_of(first + group * height, height), height)
            for plane in range(planes):
                m, comp = divmod(plane, 2)
                out[m, comp, place, :] = probe[m, comp, place, :] + update[group, plane].astype(F32)


def finish_probe(probe_modes, mine):
    devices, planes, share, size = mine.shape
    if share < 8:
        mine = mine.reshape(devices * share // 8, 8 // share, planes, share, size)
        mine = jnp.swapaxes(mine, 1, 2).reshape(-1, planes, 8, size)
    other = lax.ppermute(mine, "core", [(0, 1), (1, 0)])
    vmem = pl.BlockSpec(memory_space=pltpu.VMEM)
    return pl.pallas_call(
        finish_kernel,
        in_specs=[vmem] * 3,
        out_specs=vmem,
        out_shape=jax.ShapeDtypeStruct(probe_modes.shape, F32),
        compiler_params=pltpu.CompilerParams(vmem_limit_bytes=8 * 1024 * 1024),
        cost_estimate=pl.CostEstimate(
            flops=256 * 1024, bytes_accessed=3 * 1024 * 1024, transcendentals=0
        ),
        name="finish",
    )(probe_modes, mine, other)


def on_device(object_field, probe_modes, counts, centers, patterns):
    half = probe_modes.shape[-1] // 2

    col_even, col_odd, row_even, row_odd = cut_strips(object_field, half)
    go_on = lax.axis_index("col") < 4096
    row_halos = (swap_pairs(row_even, ROW, 0), swap_pairs(row_odd, ROW, 1))
    col_halos = (swap_pairs(col_even, COL, 0), swap_pairs(col_odd, COL, 1))
    is_even = (lax.axis_index("col") & 1) == 0
    first_ends = jnp.concatenate([halo[:, :, :half] for halo in row_halos], 1)
    last_ends = jnp.concatenate([halo[:, :, -half:] for halo in row_halos], 1)
    end_halos = (
        swap_pairs(jnp.where(is_even, last_ends, first_ends), COL, 0),
        swap_pairs(jnp.where(is_even, first_ends, last_ends), COL, 1),
    )

    inputs = (counts, centers[0, 0], object_field, patterns[0, 0], probe_modes, row_halos)
    started = run_positions(*inputs)
    joined = join_halos(col_halos, end_halos)
    border = (*joined, *started)
    partial, g_row_even, g_row_odd, g_col_even, g_col_odd, kept = run_positions(*inputs, border)

    from_rows = (swap_pairs(g_row_even, ROW, 0), swap_pairs(g_row_odd, ROW, 1))
    received = lax.cond(
        go_on, exchange, jnp.zeros_like, by_device(chip_sums(kept, from_rows[0]))
    )
    row_odd, _ = lax.optimization_barrier((from_rows[1], received))
    from_rows = (from_rows[0], row_odd)
    to_even, to_odd = add_corners((g_col_even, g_col_odd), from_rows)
    received, to_even, to_odd = lax.optimization_barrier((received, to_even, to_odd))
    from_cols = (swap_pairs(to_even, COL, 0), swap_pairs(to_odd, COL, 1))
    if received.ndim == 5:
        received = received[:, 0]
    mine = lax.cond(go_on, exchange, jnp.zeros_like, shared_update(received))
    mine, from_cols, partial = lax.optimization_barrier((mine, from_cols, partial))
    new_object = add_rims(partial, from_rows, from_cols)
    return (new_object, finish_probe(probe_modes, mine))


def solution(mesh):
    rows, columns = mesh.devices.shape
    split = jax.sharding.Mesh(
        mesh.devices.reshape(rows // 2, 2, columns), ("x", "core", "col")
    )
    placed = (
        P(None, ROW, "col"),
        P(),
        P(),
        P(ROW, "col", None, None),
        P(ROW, "col", None, None, None),
    )
    return jax.shard_map(
        on_device,
        mesh=split,
        in_specs=placed,
        out_specs=(P(None, ROW, "col"), P()),
        check_vma=False,
    )
```
